32 devices in a mesh: batch: 8 (over z, y), seq: 4 (over x, core).
Axes of the slice: x: 2, y: 2, z: 4, core: 2. Of those that a mesh axis runs over, the one named last changes fastest.
Arguments:
- byte_inputs: bfloat16 [32, 1024, 768], P('batch', 'seq'), may hold values from -6 to 6
- language: int32 [32], P('batch'), may hold values from 0 to 15
- lang_table: bfloat16 [16, 768], replicated, may hold values from -3 to 3
- latents: bfloat16 [32, 256, 1280], P('batch'), may hold values from -6 to 6
- gain_in: float32 [768], replicated, may hold values from 0.25 to 1.75
- gain_lat: float32 [1280], replicated, may hold values from 0.25 to 1.75
- gain_mlp: float32 [1280], replicated, may hold values from 0.25 to 1.75
- w_query: bfloat16 [1280, 256], replicated, may hold values from -0.25 to 0.25
- w_key: bfloat16 [768, 256], replicated, may hold values from -0.3125 to 0.3125
- w_value: bfloat16 [768, 1280], replicated, may hold values from -0.21875 to 0.21875
- w_out: bfloat16 [1280, 1280], replicated, may hold values from -1 to 1
- w_up: bfloat16 [1280, 1280], replicated, may hold values from -0.15625 to 0.15625
- w_down: bfloat16 [1280, 1280], replicated, may hold values from -0.15625 to 0.15625
- cotangent: bfloat16 [32, 256, 1280], P('batch'), may hold values from -6 to 6
Outputs:
- latents_out: bfloat16 [32, 256, 1280], P('batch')
- grad_latents: float32 [32, 256, 1280], P('batch')
- grad_bytes: float32 [32, 1024, 768], P('batch', 'seq')
- grad_lang_table: float32 [16, 768], P(None, ('batch', 'seq'))
- grad_gain_in: float32 [768], P(('batch', 'seq'))
- grad_gain_lat: float32 [1280], P(('batch', 'seq'))
- grad_gain_mlp: float32 [1280], P(('batch', 'seq'))
- grad_w_query: float32 [1280, 256], P(('batch', 'seq'))
- grad_w_key: float32 [768, 256], P(('batch', 'seq'))
- grad_w_value: float32 [768, 1280], P(('batch', 'seq'))
- grad_w_out: float32 [1280, 1280], P(('batch', 'seq'))
- grad_w_up: float32 [1280, 1280], P(('batch', 'seq'))
- grad_w_down: float32 [1280, 1280], P(('batch', 'seq'))
The draws below stay inside these ranges and needn't reach their ends.
All inputs are finite; a program needn't handle non-finite values.
Results may differ from the reference program's by a relative error of at most 0.035.
Values may be sent and summed in bfloat16 or wider, within the bound.
No kernel may reach another device: no remote copies, remote signals or barrier semaphores. Data moves between devices by JAX's collectives and lax.ppermute only.
A program may use at most 192 MiB of HBM per device.

```python
import math
import jax
import jax.numpy as jnp
from jax import lax

D_IN = 768
D_LAT = 1280
QK = 256
FF = 1280
HEADS = 8
LAT = 256
LANGS = 16
ITEMS = 32
BYTES = 1024
N_SEQ = 4


def with_ends(entries, rng, least, high):
    extent = entries.shape
    index_at = [jax.random.randint(jax.random.fold_in(rng, axis), (), 0, extent[axis]) for axis in range(len(extent))]
    entries = entries.at[tuple(index_at)].set(least)
    longest = extent.index(max(extent))
    index_at[longest] = (index_at[longest] + 1) % extent[longest]
    return entries.at[tuple(index_at)].set(high)


def steps_of(key, extent, split, smallest, high):
    level = 1.0
    for dim, blocks in split:
        steps = jax.random.uniform(jax.random.fold_in(jax.random.fold_in(key, 6), dim), (blocks,), jnp.float32, smallest / len(split), high / len(split))
        level = level * jnp.repeat(jnp.exp(steps), extent[dim] // blocks).reshape((-1,) + (1,) * (len(extent) - 1 - dim))
    return level


def scatter_about(key, extent, deviation, bound, split=(), held_as=jnp.bfloat16):
    loudness = steps_of(key, extent, split, -0.22, 0.18) if split else 1.0
    values = jax.random.normal(key, extent, jnp.float32) * deviation * loudness
    return jnp.minimum(jnp.maximum(values, -bound), bound).astype(held_as)


def setup_inputs(seed: int = 0) -> dict:
    arg_keys = jax.random.split(jax.random.key(seed), 15)
    byte_inputs = scatter_about(arg_keys[0], (ITEMS, BYTES, D_IN), 1.0, 6.0, ((0, 8), (1, 4)))
    language = with_ends(jax.random.randint(arg_keys[1], (ITEMS,), 0, LANGS), jax.random.fold_in(arg_keys[1], 1), 0, LANGS - 1).astype(jnp.int32)
    lang_table = scatter_about(arg_keys[2], (LANGS, D_IN), 0.5, 3.0)
    latents = scatter_about(arg_keys[3], (ITEMS, LAT, D_LAT), 1.0, 6.0, ((0, 8),))
    gain_in = jnp.clip(1.0 + 0.15 * jax.random.normal(arg_keys[4], (D_IN,), jnp.float32), 0.25, 1.75)
    gain_lat = jnp.clip(1.0 + 0.15 * jax.random.normal(arg_keys[5], (D_LAT,), jnp.float32), 0.25, 1.75)
    gain_mlp = jnp.clip(1.0 + 0.15 * jax.random.normal(arg_keys[6], (D_LAT,), jnp.float32), 0.25, 1.75)
    w_query = scatter_about(arg_keys[7], (D_LAT, QK), (D_LAT // 2) ** -0.5, 0.25)
    w_key = scatter_about(arg_keys[8], (D_IN, QK), (D_IN // 2) ** -0.5, 0.3125)
    w_value = scatter_about(arg_keys[9], (D_IN, D_LAT), D_IN ** -0.5, 0.21875)
    w_out = scatter_about(arg_keys[10], (D_LAT, D_LAT), (D_LAT // 32) ** -0.5, 1.0)
    w_up = scatter_about(arg_keys[11], (D_LAT, FF), D_LAT ** -0.5, 0.15625)
    w_down = scatter_about(arg_keys[12], (FF, D_LAT), FF ** -0.5, 0.15625)
    cotangent = scatter_about(arg_keys[13], (ITEMS, LAT, D_LAT), 1.0, 6.0, ((0, 8),))
    return dict(byte_inputs=byte_inputs, language=language, lang_table=lang_table, latents=latents, gain_in=gain_in, gain_lat=gain_lat, gain_mlp=gain_mlp, w_query=w_query, w_key=w_key, w_value=w_value, w_out=w_out, w_up=w_up, w_down=w_down, cotangent=cotangent)


@jax.custom_vjp
def low(v):
    return lax.optimization_barrier(v.astype(jnp.bfloat16)).astype(jnp.float32)

@jax.custom_vjp
def low_back(v):
    return v

def low_keep(v):
    return (low(v), None)

def low_pass(kept, grad):
    return (grad,)

def back_keep(v):
    return (v, None)

def back_low(kept, grad):
    return (low(grad),)
low.defvjp(low_keep, low_pass)
low_back.defvjp(back_keep, back_low)
EPS = 1e-05
HIGH = lax.Precision.HIGHEST

def layer_norm(values_in, gains):
    centre = values_in - lax.optimization_barrier(jnp.mean(values_in, -1, keepdims=True))
    spread = lax.optimization_barrier(jnp.mean(centre * centre, -1, keepdims=True))
    return centre * lax.rsqrt(spread + EPS) * gains

def matmul_high(left, right):
    return jnp.dot(left, right, precision=HIGH)

def item_block(params, byte_rows, lang_row, latent_rows):
    gain_in, gain_lat, gain_mlp, w_query, w_key, w_value, w_out, w_up, w_down = params
    qk_head = QK // HEADS
    v_head = D_LAT // HEADS
    score_scale = 1.0 / math.sqrt(qk_head)
    inputs_x = byte_rows + lang_row[None, :]
    normed_in = low(layer_norm(inputs_x, gain_in))
    key_rows = low(low_back(matmul_high(normed_in, w_key)))
    value_rows = low(low_back(matmul_high(normed_in, w_value)))
    normed_lat = low(layer_norm(latent_rows, gain_lat))
    query_rows = low(low_back(matmul_high(normed_lat, w_query)))
    query_heads = query_rows.reshape(LAT, HEADS, qk_head)
    key_heads = key_rows.reshape(BYTES, HEADS, qk_head)
    value_heads = value_rows.reshape(N_SEQ, BYTES // N_SEQ, HEADS, v_head)
    scores = low_back(jnp.einsum('qhd,khd->hqk', query_heads, key_heads, precision=HIGH) * score_scale)
    row_top = lax.optimization_barrier(jnp.max(scores, -1, keepdims=True))
    log_total = row_top + jnp.log(lax.optimization_barrier(jnp.sum(jnp.exp(scores - row_top), -1, keepdims=True)))
    attn_probs = low(jnp.exp(scores - log_total)).reshape(HEADS, LAT, N_SEQ, BYTES // N_SEQ)
    block_sums = low(jnp.einsum('hqsk,skhd->sqhd', attn_probs, value_heads, precision=HIGH))
    mixture = lax.optimization_barrier(jnp.sum(block_sums, 0)).reshape(LAT, D_LAT)
    attended = low(low_back(mixture))
    residual = latent_rows + low_back(matmul_high(attended, w_out))
    hidden_rows = low(layer_norm(residual, gain_mlp))
    activated = low(jax.nn.gelu(low_back(matmul_high(hidden_rows, w_up))))
    return residual + matmul_high(activated, w_down)

def reference(byte_inputs, language, lang_table, latents, gain_in, gain_lat, gain_mlp, w_query, w_key, w_value, w_out, w_up, w_down, cotangent):
    params = (gain_in, gain_lat, gain_mlp, w_query.astype(jnp.float32), w_key.astype(jnp.float32), w_value.astype(jnp.float32), w_out.astype(jnp.float32), w_up.astype(jnp.float32), w_down.astype(jnp.float32))

    def forward(weights, table, byte_rows, latent_rows):
        lang_rows = table[language]

        def step(carry, item):
            return (carry, jax.checkpoint(item_block)(weights, item[0], item[1], item[2]))
        _, outputs = lax.scan(step, jnp.zeros((), jnp.float32), (byte_rows, lang_rows, latent_rows))
        return outputs
    result, pull = jax.vjp(forward, params, lang_table.astype(jnp.float32), byte_inputs.astype(jnp.float32), latents.astype(jnp.float32))
    grad_params, grad_table, grad_bytes, grad_latents = pull(cotangent.astype(jnp.float32))
    return (result.astype(jnp.bfloat16), grad_latents, grad_bytes, grad_table, grad_params[0], grad_params[1], grad_params[2], grad_params[3], grad_params[4], grad_params[5], grad_params[6], grad_params[7], grad_params[8])
```

```python
import functools
import math

import jax
import jax.numpy as jnp
from jax import lax
from jax.experimental import pallas as pl
from jax.experimental.pallas import tpu as pltpu
from jax.sharding import PartitionSpec as P

HEADS = 8
CORES = 2
EPS = 1e-05
F32 = jnp.float32
BF = jnp.bfloat16
VMEM_LIMIT = 50 * 1024 * 1024


def nn(a, b):
    return lax.dot_general(a, b, (((1,), (0,)), ((), ())), preferred_element_type=F32)


def nt(a, b):
    return lax.dot_general(a, b, (((1,), (1,)), ((), ())), preferred_element_type=F32)


def tn(a, b):
    return lax.dot_general(a, b, (((0,), (0,)), ((), ())), preferred_element_type=F32)


def standardise(x):
    centre = x - jnp.mean(x, -1, keepdims=True)
    inverse = lax.rsqrt(jnp.mean(centre * centre, -1, keepdims=True) + EPS)
    return centre * inverse, inverse


def standardise_back(unit, inverse, grad):
    return inverse * (
        grad - jnp.mean(grad, -1, keepdims=True) - unit * jnp.mean(grad * unit, -1, keepdims=True)
    )


def params():
    return pltpu.CompilerParams(vmem_limit_bytes=VMEM_LIMIT)


def whole(shape):
    return pl.BlockSpec(shape, lambda *_: (0,) * len(shape))


def sds(shape, dtype):
    return jax.ShapeDtypeStruct(shape, dtype)


def query_kernel(where, lat_ref, gain_ref, wq_ref, q_ref, qt_ref):
    unit, _ = standardise(lat_ref[0].astype(F32))
    rows = nn((unit * gain_ref[...]).astype(BF), wq_ref[...])
    q_ref[0] = rows.astype(BF)
    qt_ref[0] = rows.T.astype(BF)


def queries(where, latents, gain, w_query, items):
    _, count, width = latents.shape
    qk = w_query.shape[1]
    return pl.pallas_call(
        query_kernel,
        grid_spec=pltpu.PrefetchScalarGridSpec(
            num_scalar_prefetch=1,
            grid=(items,),
            in_specs=[
                pl.BlockSpec((1, count, width), lambda i, w: (w[0] * items + i, 0, 0)),
                whole((1, width)),
                whole((width, qk)),
            ],
            out_specs=[
                pl.BlockSpec((1, count, qk), lambda i, w: (i, 0, 0)),
                pl.BlockSpec((1, qk, count), lambda i, w: (i, 0, 0)),
            ],
        ),
        out_shape=[sds((items, count, qk), BF), sds((items, qk, count), BF)],
        compiler_params=params(),
        name="queries",
    )(where, latents, gain, w_query)


def language_row(table_ref, language):
    at = lax.broadcasted_iota(jnp.int32, table_ref.shape, 0)
    return jnp.sum(jnp.where(at == language, table_ref[...], 0.0), 0, keepdims=True)


def attend_kernel(
    item, score_unit, where, own_ref, far_ref, table_ref, gain_ref, wk_ref, wv_ref, qt_ref,
    ot_ref, lse_ref, xn_ref, k_ref, kt_ref, v_ref, vt_ref,
):
    count = own_ref.shape[1]
    row = language_row(table_ref, where[2 + item])
    gain = gain_ref[...]
    for part, ref in enumerate((own_ref, far_ref)):
        unit, _ = standardise(ref[0].astype(F32) + row)
        xn_ref[part * count : (part + 1) * count] = (unit * gain).astype(BF)
    xn = xn_ref[...]
    k = nn(xn, wk_ref[...]).astype(BF)
    k_ref[...] = k
    kt_ref[...] = k.T
    v = nn(xn, wv_ref[...]).astype(BF)
    v_ref[...] = v
    vt_ref[...] = v.T
    qt = qt_ref[0]
    qk = qt.shape[0]
    depth = qk // HEADS
    wide = vt_ref.shape[0] // HEADS
    at = lax.broadcasted_iota(jnp.int32, qt.shape, 0) // depth
    for h in range(HEADS):
        score = nn(k, jnp.where(at == h, qt, jnp.zeros_like(qt))) * score_unit
        top = jnp.max(score, 0, keepdims=True)
        weight = jnp.exp2(score - top)
        total = jnp.sum(weight, 0, keepdims=True)
        out = nn(vt_ref[h * wide : (h + 1) * wide], weight.astype(BF))
        ot_ref[h * wide : (h + 1) * wide] = (out * (1.0 / total)).astype(BF)
        lse_ref[h : h + 1] = top + jnp.log2(total)


def attend(item, items, where, own, far, table, gain, w_key, w_value, qt, score_unit):
    _, count, width = own.shape
    qk, lat = w_key.shape[1], qt.shape[2]
    wide = w_value.shape[1]
    return pl.pallas_call(
        functools.partial(attend_kernel, item, score_unit),
        grid_spec=pltpu.PrefetchScalarGridSpec(
            num_scalar_prefetch=1,
            grid=(1,),
            in_specs=[
                pl.BlockSpec((1, count, width), lambda g, w: (w[0] * items + item, 0, 0)),
                pl.BlockSpec((1, count, width), lambda g, w: (item, 0, 0)),
                whole(table.shape),
                whole((1, width)),
                whole((width, qk)),
                whole((width, wide)),
                pl.BlockSpec((1, qk, lat), lambda g, w: (item, 0, 0)),
            ],
            out_specs=[
                whole((wide, lat)),
                whole((HEADS, lat)),
                whole((2 * count, width)),
                whole((2 * count, qk)),
                whole((qk, 2 * count)),
                whole((2 * count, wide)),
            ],
            scratch_shapes=[pltpu.VMEM((wide, 2 * count), BF)],
        ),
        out_shape=[
            sds((wide, lat), BF),
            sds((HEADS, lat), F32),
            sds((2 * count, width), BF),
            sds((2 * count, qk), BF),
            sds((qk, 2 * count), BF),
            sds((2 * count, wide), BF),
        ],
        compiler_params=params(),
        name="attend",
    )(where, own, far, table, gain, w_key, w_value, qt)


GELU_A = math.sqrt(2.0 / math.pi)
GELU_B = 0.044715


def latent_kernel(
    where, oa_ref, ob_ref, la_ref, lb_ref, lat_ref, cot_ref, gain_ref, wo_ref, wu_ref, wd_ref,
    out_ref, gres_ref, gatt_ref, dot_ref, lse_ref, att_ref, hid_ref, act_ref, gpre_ref, glow_ref,
    ggain_ref,
):
    first = where[1] == 0
    wide = oa_ref.shape[0] // HEADS
    ours, theirs = la_ref[...], lb_ref[...]
    left = jnp.where(first, ours, theirs)
    right = jnp.where(first, theirs, ours)
    top = jnp.maximum(left, right)
    e_left, e_right = jnp.exp2(left - top), jnp.exp2(right - top)
    total = e_left + e_right
    lse_ref[...] = top + jnp.log2(total)
    scale = 1.0 / total
    e_left, e_right = e_left * scale, e_right * scale
    merged = []
    for h in range(HEADS):
        a = oa_ref[h * wide : (h + 1) * wide].astype(F32)
        b = ob_ref[h * wide : (h + 1) * wide].astype(F32)
        low, high = jnp.where(first, a, b), jnp.where(first, b, a)
        merged.append(low * e_left[h : h + 1] + high * e_right[h : h + 1])
        att_ref[h * wide : (h + 1) * wide] = merged[-1].astype(BF)
    resid = lat_ref[0].astype(F32) + tn(att_ref[...], wo_ref[...])
    unit, inverse = standardise(resid)
    gain = gain_ref[...]
    hidden = (unit * gain).astype(BF)
    hid_ref[...] = hidden.T
    pre = nn(hidden, wu_ref[...])
    square = pre * pre
    slope = jnp.tanh(GELU_A * pre * (1.0 + GELU_B * square))
    act = (0.5 * pre * (1.0 + slope)).astype(BF)
    act_ref[...] = act.T
    out_ref[0] = (resid + nn(act, wd_ref[...])).astype(BF)
    cot = cot_ref[0]
    gelu_slope = 0.5 * (1.0 + slope) + 0.5 * pre * (1.0 - slope * slope) * GELU_A * (
        1.0 + 3.0 * GELU_B * square
    )
    gpre = (nt(cot, wd_ref[...]) * gelu_slope).astype(BF)
    gpre_ref[...] = gpre
    ghid = nt(gpre, wu_ref[...])
    ggain_ref[...] = jnp.sum(ghid * unit, 0, keepdims=True)
    gres = cot.astype(F32) + standardise_back(unit, inverse, ghid * gain)
    gres_ref[...] = gres
    glow = gres.astype(BF)
    glow_ref[...] = glow
    gatt = nt(wo_ref[...], glow)
    gatt_ref[...] = gatt.astype(BF)
    for h in range(HEADS):
        dot_ref[h : h + 1] = jnp.sum(
            gatt_ref[h * wide : (h + 1) * wide].astype(F32) * merged[h], 0, keepdims=True
        )


def latent_side(item, items, where, oa, ob, la, lb, latents, cot, gain, w_out, w_up, w_down):
    _, lat, width = latents.shape
    feed = w_up.shape[1]
    return pl.pallas_call(
        latent_kernel,
        grid_spec=pltpu.PrefetchScalarGridSpec(
            num_scalar_prefetch=1,
            grid=(1,),
            in_specs=[
                whole(oa.shape),
                whole(ob.shape),
                whole(la.shape),
                whole(lb.shape),
                pl.BlockSpec((1, lat, width), lambda g, w: (w[0] * items + item, 0, 0)),
                pl.BlockSpec((1, lat, width), lambda g, w: (w[0] * items + item, 0, 0)),
                whole((1, width)),
                whole(w_out.shape),
                whole(w_up.shape),
                whole(w_down.shape),
            ],
            out_specs=[
                whole((1, lat, width)),
                whole((lat, width)),
                whole((width, lat)),
                whole((HEADS, lat)),
                whole((HEADS, lat)),
                whole((width, lat)),
                whole((width, lat)),
                whole((feed, lat)),
                whole((lat, feed)),
                whole((lat, width)),
                whole((1, width)),
            ],
        ),
        out_shape=[
            sds((1, lat, width), BF),
            sds((lat, width), F32),
            sds((width, lat), BF),
            sds((HEADS, lat), F32),
            sds((HEADS, lat), F32),
            sds((width, lat), BF),
            sds((width, lat), BF),
            sds((feed, lat), BF),
            sds((lat, feed), BF),
            sds((lat, width), BF),
            sds((1, width), F32),
        ],
        compiler_params=params(),
        name="latent_side",
    )(where, oa, ob, la, lb, latents, cot, gain, w_out, w_up, w_down)


def product_kernel(*refs):
    count = (len(refs) - 1) // 2
    total = nn(refs[0][...], refs[1][...])
    for i in range(1, count):
        total += nn(refs[2 * i][...], refs[2 * i + 1][...])
    refs[-1][...] = total.astype(refs[-1].dtype)


def rows_product(lefts, rights, name):
    flat = [a for pair in zip(lefts, rights) for a in pair]
    shape = (lefts[0].shape[0], rights[0].shape[1])
    return pl.pallas_call(
        product_kernel,
        grid=(1,),
        in_specs=[whole(a.shape) for a in flat],
        out_specs=whole(shape),
        out_shape=sds(shape, BF),
        compiler_params=params(),
        name=name,
    )(*flat)


def attend_back_kernel(
    score_unit, score_scale, q_ref, qt_ref, k_ref, kt_ref, v_ref, gatt_ref, lse_ref, dot_ref,
    dqt_ref, dkv_ref, dvt_ref,
):
    q, qt, k = q_ref[0], qt_ref[0], k_ref[...]
    qk = qt.shape[0]
    depth = qk // HEADS
    wide = gatt_ref.shape[0] // HEADS
    lat = qt.shape[1]
    span = 2 * 128
    at = lax.broadcasted_iota(jnp.int32, qt.shape, 0) // depth
    across = lax.broadcasted_iota(jnp.int32, q.shape, 1) // depth
    dk = jnp.zeros(k.shape, F32)
    for h in range(HEADS):
        score = nn(k, jnp.where(at == h, qt, jnp.zeros_like(qt))) * score_unit
        prob = jnp.exp2(score - lse_ref[h : h + 1])
        grad = gatt_ref[h * wide : (h + 1) * wide]
        begin = h * wide // 128 * 128
        ahead = h * wide - begin
        after = span - ahead - wide
        pieces = [grad]
        if ahead:
            pieces = [jnp.zeros((ahead, lat), BF)] + pieces
        if after:
            pieces = pieces + [jnp.zeros((after, lat), BF)]
        grad_prob = nn(v_ref[:, begin : begin + span], jnp.concatenate(pieces, 0))
        grad_score = (prob * (grad_prob - dot_ref[h : h + 1])).astype(BF)
        dvt_ref[h * wide : (h + 1) * wide] = nt(grad, prob.astype(BF)).astype(BF)
        dk += nn(grad_score, jnp.where(across == h, q, jnp.zeros_like(q)))
        dqt_ref[h * depth : (h + 1) * depth] = nn(
            kt_ref[h * depth : (h + 1) * depth], grad_score
        ).astype(BF)
    dkv_ref[:, :qk] = (dk * score_scale).astype(BF)
    dkv_ref[:, qk:] = dvt_ref[...].T


def attend_back(item, q, qt, k, kt, v, gatt, lse, dot, score_unit, score_scale):
    _, lat, qk = q.shape
    count, wide = v.shape
    return pl.pallas_call(
        functools.partial(attend_back_kernel, score_unit, score_scale),
        grid=(1,),
        in_specs=[
            pl.BlockSpec((1, lat, qk), lambda g: (item, 0, 0)),
            pl.BlockSpec((1, qk, lat), lambda g: (item, 0, 0)),
            whole(k.shape),
            whole(kt.shape),
            whole(v.shape),
            whole(gatt.shape),
            whole(lse.shape),
            whole(dot.shape),
        ],
        out_specs=[whole((qk, lat)), whole((count, qk + wide))],
        out_shape=[sds((qk, lat), BF), sds((count, qk + wide), BF)],
        scratch_shapes=[pltpu.VMEM((wide, count), BF)],
        compiler_params=params(),
        name="attend_back",
    )(q, qt, k, kt, v, gatt, lse, dot)


def byte_weights_kernel(*refs):
    count = (len(refs) - 1) // 2
    total = tn(refs[0][...], refs[1][...])
    for i in range(1, count):
        total += tn(refs[2 * i][...], refs[2 * i + 1][...])
    refs[-1][...] = total.astype(BF)


def byte_weights(xns, dkvs):
    flat = [a for pair in zip(xns, dkvs) for a in pair]
    shape = (xns[0].shape[1], dkvs[0].shape[1])
    return pl.pallas_call(
        byte_weights_kernel,
        grid=(1,),
        in_specs=[whole(a.shape) for a in flat],
        out_specs=whole(shape),
        out_shape=sds(shape, BF),
        compiler_params=params(),
        name="byte_weights",
    )(*flat)


def bytes_back_kernel(
    item, where, own_ref, far_ref, table_ref, gain_ref, wk_ref, wv_ref, dkv_ref,
    gown_ref, gfar_ref, small_ref,
):
    count = own_ref.shape[1]
    qk = wk_ref.shape[1]
    language = where[2 + item]
    row = language_row(table_ref, language)
    gain = gain_ref[...]
    grads = nt(dkv_ref[:, :qk], wk_ref[...]) + nt(dkv_ref[:, qk:], wv_ref[...])
    gain_sum = jnp.zeros_like(row)
    byte_sum = jnp.zeros_like(row)
    for part, ref, out in ((0, own_ref, gown_ref), (1, far_ref, gfar_ref)):
        unit, inverse = standardise(ref[0].astype(F32) + row)
        grad = grads[part * count : (part + 1) * count]
        gain_sum += jnp.sum(grad * unit, 0, keepdims=True)
        back = standardise_back(unit, inverse, grad * gain)
        byte_sum += jnp.sum(back, 0, keepdims=True)
        out[0] = back.astype(out.dtype)
    langs = table_ref.shape[0]
    at = lax.broadcasted_iota(jnp.int32, table_ref.shape, 0)
    small_ref[0:langs] = jnp.where(at == language, byte_sum, 0.0)
    at = lax.broadcasted_iota(jnp.int32, (8, row.shape[1]), 0)
    small_ref[langs : langs + 8] = jnp.where(at == 0, gain_sum, 0.0)


def bytes_back(item, items, where, own, far, table, gain, w_key, w_value, dkv):
    _, count, width = own.shape
    langs = table.shape[0]
    return pl.pallas_call(
        functools.partial(bytes_back_kernel, item),
        grid_spec=pltpu.PrefetchScalarGridSpec(
            num_scalar_prefetch=1,
            grid=(1,),
            in_specs=[
                pl.BlockSpec((1, count, width), lambda g, w: (w[0] * items + item, 0, 0)),
                pl.BlockSpec((1, count, width), lambda g, w: (item, 0, 0)),
                whole(table.shape),
                whole((1, width)),
                whole(w_key.shape),
                whole(w_value.shape),
                whole(dkv.shape),
            ],
            out_specs=[
                whole((1, count, width)),
                whole((1, count, width)),
                whole((langs + 8, width)),
            ],
        ),
        out_shape=[
            sds((1, count, width), F32),
            sds((1, count, width), BF),
            sds((langs + 8, width), F32),
        ],
        compiler_params=params(),
        name="bytes_back",
    )(where, own, far, table, gain, w_key, w_value, dkv)


def latents_back_kernel(
    score_scale, where, da_ref, db_ref, gres_ref, lat_ref, gain_ref, wq_ref,
    glat_ref, gw_ref, ggain_ref,
):
    total = (da_ref[...].astype(F32) + db_ref[...].astype(F32)) * score_scale
    grad = total.T.astype(BF)
    unit, inverse = standardise(lat_ref[0].astype(F32))
    gain = gain_ref[...]
    gln = nt(grad, wq_ref[...])
    ggain_ref[...] = jnp.sum(gln * unit, 0, keepdims=True)
    glat_ref[0] = (gres_ref[...] + standardise_back(unit, inverse, gln * gain)).astype(BF)
    gw_ref[...] = tn((unit * gain).astype(BF), grad)


def latents_back(item, items, where, da, db, gres, latents, gain, w_query, score_scale):
    _, lat, width = latents.shape
    qk = w_query.shape[1]
    return pl.pallas_call(
        functools.partial(latents_back_kernel, score_scale),
        grid_spec=pltpu.PrefetchScalarGridSpec(
            num_scalar_prefetch=1,
            grid=(1,),
            in_specs=[
                whole(da.shape),
                whole(db.shape),
                whole(gres.shape),
                pl.BlockSpec((1, lat, width), lambda g, w: (w[0] * items + item, 0, 0)),
                whole((1, width)),
                whole(w_query.shape),
            ],
            out_specs=[whole((1, lat, width)), whole((width, qk)), whole((1, width))],
        ),
        out_shape=[sds((1, lat, width), BF), sds((width, qk), F32), sds((1, width), F32)],
        compiler_params=params(),
        name="latents_back",
    )(where, da, db, gres, latents, gain, w_query)


def swap(value, axis, bit):
    size = lax.axis_size(axis)
    return jax.tree.map(
        lambda a: lax.ppermute(a, axis, [(i, i ^ bit) for i in range(size)]), value
    )


def bits_of(size, start=1):
    bit = start
    while bit < size:
        yield bit
        bit *= 2


def halve(value, dim, axis, bit, dtype=BF):
    mine = (lax.axis_index(axis) // bit) % 2
    keep = lax.dynamic_index_in_dim(value, mine, dim, keepdims=False)
    send = lax.dynamic_index_in_dim(value, 1 - mine, dim, keepdims=False)
    return (keep.astype(F32) + swap(send, axis, bit).astype(F32)).astype(dtype)


def scatter_batch(value):
    parts = value.shape[0]
    for bit in bits_of(parts):
        rest = value.shape[1:]
        value = halve(value.reshape((value.shape[0] // 2, 2) + rest), 1, "batch", bit)
    return value[0].astype(F32)


def scatter_latent(value):
    spots, chips = lax.axis_size("batch"), lax.axis_size("seq") // CORES
    rows = value.shape[0] // (spots * CORES)
    blocks = value.reshape(spots, CORES, rows, value.shape[1])
    return scatter_batch(halve(blocks, 1, "seq", 1))


def scatter_bytes(value):
    spots, chips = lax.axis_size("batch"), lax.axis_size("seq") // CORES
    rows = value.shape[0] // (spots * chips * CORES)
    blocks = value.reshape(spots, chips, CORES, rows, value.shape[1])
    blocks = halve(blocks, 2, "seq", 1)
    for bit in bits_of(chips):
        rest = blocks.shape[2:]
        blocks = blocks.reshape((spots, blocks.shape[1] // 2, 2) + rest)
        blocks = halve(blocks, 2, "seq", CORES * bit)
    return scatter_batch(blocks[:, 0])


def own_side(value):
    spots, chips = lax.axis_size("batch"), lax.axis_size("seq") // CORES
    rows = value.shape[0] // (spots * chips)
    blocks = value.reshape(spots, chips, rows, value.shape[1])
    side = lax.axis_index("seq") // CORES
    return lax.dynamic_index_in_dim(blocks, side, 1, keepdims=False).reshape(-1, value.shape[1])


def both_cores(own, far, core):
    return jnp.where(
        core == 0, jnp.concatenate([own, far], 0), jnp.concatenate([far, own], 0)
    )


def everywhere(value):
    for bit in bits_of(lax.axis_size("seq")):
        value = value + swap(value, "seq", bit)
    for bit in bits_of(lax.axis_size("batch")):
        value = value + swap(value, "batch", bit)
    return value


def merge(pair_a, pair_b):
    oa, la = pair_a
    ob, lb = pair_b
    top = jnp.maximum(la, lb)
    ea, eb = jnp.exp2(la - top), jnp.exp2(lb - top)
    total = ea + eb
    wide = oa.shape[0] // HEADS
    weight = lambda e: jnp.repeat(e / total, wide, 0)
    out = oa.astype(F32) * weight(ea) + ob.astype(F32) * weight(eb)
    return out.astype(BF), top + jnp.log2(total)


def local(
    byte_inputs,
    language,
    lang_table,
    latents,
    gain_in,
    gain_lat,
    gain_mlp,
    w_query,
    w_key,
    w_value,
    w_out,
    w_up,
    w_down,
    cotangent,
):
    items = byte_inputs.shape[0] // CORES
    width_in, width_lat = byte_inputs.shape[2], latents.shape[2]
    depth = w_query.shape[1] // HEADS
    score_scale = 1.0 / math.sqrt(depth)
    score_unit = score_scale * math.log2(math.e)
    seq_at = lax.axis_index("seq")
    core, side = seq_at % CORES, seq_at // CORES
    chips = lax.axis_size("seq") // CORES
    place = lax.axis_index("batch") * lax.axis_size("seq") + seq_at
    own_languages = lax.dynamic_slice_in_dim(language, core * items, items, 0)
    where = jnp.concatenate([jnp.stack([core, side]).astype(jnp.int32), own_languages])
    table = lang_table.astype(F32)
    gain_in, gain_lat, gain_mlp = gain_in[None], gain_lat[None], gain_mlp[None]

    send = lax.dynamic_slice_in_dim(byte_inputs, (1 - core) * items, items, 0)
    far = swap(send, "seq", 1)
    q, qt = queries(where, latents, gain_lat, w_query, items)

    kept, pairs = [], []
    for item in range(items):
        ot, lse, xn, k, kt, v = attend(
            item, items, where, byte_inputs, far, table, gain_in, w_key, w_value, qt, score_unit
        )
        kept.append((xn, k, kt, v))
        bits = list(bits_of(chips))
        for bit in bits[:-1]:
            ot, lse = merge((ot, lse), swap((ot, lse), "seq", CORES * bit))
        pairs.append(((ot, lse), swap((ot, lse), "seq", CORES * bits[-1]), bits[-1]))

    sides = []
    dqs, dkvs = [], []
    for item in range(items):
        (oa, la), (ob, lb), bit = pairs[item]
        order = jnp.stack([core, side // bit % 2]).astype(jnp.int32)
        side_out = latent_side(
            item, items, order, oa, ob, la, lb, latents, cotangent, gain_mlp, w_out, w_up, w_down
        )
        sides.append(side_out)
        gatt, dot, lse = side_out[2], side_out[3], side_out[4]
        xn, k, kt, v = kept[item]
        dqt, dkv = attend_back(item, q, qt, k, kt, v, gatt, lse, dot, score_unit, score_scale)
        for bit in list(bits_of(chips))[:-1]:
            dqt = (dqt.astype(F32) + swap(dqt, "seq", CORES * bit).astype(F32)).astype(BF)
        dqs.append((dqt, swap(dqt, "seq", CORES * list(bits_of(chips))[-1])))
        dkvs.append(dkv)

    pick = lambda at: [s[at] for s in sides]
    cots = lax.dynamic_slice_in_dim(cotangent, core * items, items, 0)
    g_down = rows_product(
        [own_side(a) for a in pick(7)], [cots[i] for i in range(items)], "down_weights"
    )
    g_up = rows_product([own_side(a) for a in pick(6)], pick(8), "up_weights")
    g_out = rows_product([own_side(a) for a in pick(5)], pick(9), "out_weights")
    g_down, g_up, g_out = scatter_latent(g_down), scatter_latent(g_up), scatter_latent(g_out)

    g_bytes = scatter_bytes(byte_weights([k[0] for k in kept], dkvs))

    gown, gfar, small = [], [], 0.0
    for item in range(items):
        a, b, s = bytes_back(
            item, items, where, byte_inputs, far, table, gain_in, w_key, w_value, dkvs[item]
        )
        gown.append(a)
        gfar.append(b)
        small = small + s
    gfar = swap(jnp.concatenate(gfar, 0), "seq", 1)
    grad_bytes = both_cores(jnp.concatenate(gown, 0), gfar.astype(F32), core)

    glats, g_query, g_gain_lat = [], 0.0, 0.0
    for item in range(items):
        a, b, s = latents_back(
            item, items, where, dqs[item][0], dqs[item][1], sides[item][1], latents, gain_lat,
            w_query, score_scale,
        )
        glats.append(a)
        g_query = g_query + b
        g_gain_lat = g_gain_lat + s
    glats = jnp.concatenate(glats, 0)
    grad_latents = both_cores(glats, swap(glats, "seq", 1), core).astype(F32)
    g_query = scatter_latent(own_side(g_query.astype(BF)))

    outs = jnp.concatenate(pick(0), 0)
    latents_out = both_cores(outs, swap(outs, "seq", 1), core)

    g_gain_mlp = functools.reduce(jnp.add, pick(10))
    share = 1.0 / chips
    pack = jnp.concatenate(
        [
            jnp.pad(small[: lang_table.shape[0] + 1], ((0, 0), (0, width_lat - width_in))),
            g_gain_lat * share,
            g_gain_mlp * share,
        ],
        0,
    )
    pack = everywhere(pack)
    langs = lang_table.shape[0]
    devices = lax.axis_size("batch") * lax.axis_size("seq")
    cut_in, cut_lat = width_in // devices, width_lat // devices
    byte_cut = lax.dynamic_slice_in_dim(pack, place * cut_in, cut_in, 1)
    lat_cut = lax.dynamic_slice_in_dim(pack, place * cut_lat, cut_lat, 1)
    qk = w_query.shape[1]
    return (
        latents_out,
        grad_latents,
        grad_bytes,
        byte_cut[:langs],
        byte_cut[langs],
        lat_cut[langs + 1],
        lat_cut[langs + 2],
        g_query,
        g_bytes[:, :qk],
        g_bytes[:, qk:],
        g_out,
        g_up,
        g_down,
    )


def solution(mesh):
    return jax.shard_map(
        local,
        mesh=mesh,
        in_specs=(
            P("batch", "seq", None),
            P("batch"),
            P(),
            P("batch", None, None),
            P(),
            P(),
            P(),
            P(),
            P(),
            P(),
            P(),
            P(),
            P(),
            P("batch", None, None),
        ),
        out_specs=(
            P("batch", None, None),
            P("batch", None, None),
            P("batch", "seq", None),
            P(None, ("batch", "seq")),
            P(("batch", "seq")),
            P(("batch", "seq")),
            P(("batch", "seq")),
            P(("batch", "seq"), None),
            P(("batch", "seq"), None),
            P(("batch", "seq"), None),
            P(("batch", "seq"), None),
            P(("batch", "seq"), None),
            P(("batch", "seq"), None),
        ),
        check_vma=False,
    )
```

```python
import functools
import math

import jax
import jax.numpy as jnp
from jax import lax
from jax.experimental import pallas as pl
from jax.experimental.pallas import tpu as pltpu
from jax.sharding import PartitionSpec as P

HEADS = 8
CORES = 2
EPS = 1e-05
F32 = jnp.float32
BF = jnp.bfloat16
VMEM_LIMIT = 50 * 1024 * 1024


def nn(a, b):
    return lax.dot_general(a, b, (((1,), (0,)), ((), ())), preferred_element_type=F32)


def nt(a, b):
    return lax.dot_general(a, b, (((1,), (1,)), ((), ())), preferred_element_type=F32)


def tn(a, b):
    return lax.dot_general(a, b, (((0,), (0,)), ((), ())), preferred_element_type=F32)


def standardise(x):
    centre = x - jnp.mean(x, -1, keepdims=True)
    inverse = lax.rsqrt(jnp.mean(centre * centre, -1, keepdims=True) + EPS)
    return centre * inverse, inverse


def standardise_back(unit, inverse, grad):
    return inverse * (
        grad - jnp.mean(grad, -1, keepdims=True) - unit * jnp.mean(grad * unit, -1, keepdims=True)
    )


def whole(shape):
    return pl.BlockSpec(shape, lambda *_: (0,) * len(shape))


def block(shape, at):
    return pl.BlockSpec(shape, lambda g, w: (at(g, w),) + (0,) * (len(shape) - 1))


ANY = pl.BlockSpec(memory_space=pl.ANY)


def launch(body, name, where, ins, outs, scratch=(), deps=(), alias=None, grid=1):
    count, extra = len(ins), len(deps)

    def kernel(where_ref, *refs):
        body(where_ref, *refs[:count], *refs[count + extra :])

    return pl.pallas_call(
        kernel,
        grid_spec=pltpu.PrefetchScalarGridSpec(
            num_scalar_prefetch=1,
            grid=(grid,),
            in_specs=[whole(a.shape) if s is None else s for a, s in ins] + [ANY] * extra,
            out_specs=[whole(shape) if s is None else s for shape, _, s in outs],
            scratch_shapes=list(scratch),
        ),
        out_shape=[jax.ShapeDtypeStruct(shape, dtype) for shape, dtype, _ in outs],
        input_output_aliases={1 + i: o for i, o in (alias or {}).items()},
        compiler_params=pltpu.CompilerParams(vmem_limit_bytes=VMEM_LIMIT),
        cost_estimate=pl.CostEstimate(flops=1, bytes_accessed=1, transcendentals=0),
        name=name,
    )(where, *[a for a, _ in ins], *deps)


def query_kernel(where, lat_ref, gain_ref, wq_ref, q_ref, qt_ref):
    unit, _ = standardise(lat_ref[0].astype(F32))
    rows = nn((unit * gain_ref[...]).astype(BF), wq_ref[...])
    q_ref[0] = rows.astype(BF)
    qt_ref[0] = rows.T.astype(BF)


def queries(where, latents, gain, w_query, items):
    _, count, width = latents.shape
    qk = w_query.shape[1]
    return launch(
        query_kernel,
        "queries",
        where,
        [
            (latents, block((1, count, width), lambda g, w: w[0] * items + g)),
            (gain, None),
            (w_query, None),
        ],
        [
            ((items, count, qk), BF, block((1, count, qk), lambda g, w: g)),
            ((items, qk, count), BF, block((1, qk, count), lambda g, w: g)),
        ],
        grid=items,
    )


def language_row(table_ref, language):
    at = lax.broadcasted_iota(jnp.int32, table_ref.shape, 0)
    return jnp.sum(jnp.where(at == language, table_ref[...], 0.0), 0, keepdims=True)


def attend_kernel(
    item, score_unit, where, own_ref, far_ref, table_ref, gain_ref, wk_ref, wv_ref, qt_ref,
    *refs,
):
    ot_ref, xn_ref, k_ref, kt_ref, v_ref, vt_ref = refs[-6:]
    count = own_ref.shape[1]
    row = language_row(table_ref, where[LANG_AT + item])
    gain = gain_ref[...]
    for part, ref in enumerate((own_ref, far_ref)):
        unit, _ = standardise(ref[0].astype(F32) + row)
        xn_ref[0, part * count : (part + 1) * count] = (unit * gain).astype(BF)
    xn = xn_ref[0]
    k = nn(xn, wk_ref[...]).astype(BF)
    k_ref[...] = k
    kt_ref[...] = k.T
    v = nn(xn, wv_ref[...]).astype(BF)
    v_ref[...] = v
    vt_ref[...] = v.T
    qt = qt_ref[0]
    depth = qt.shape[0] // HEADS
    wide = vt_ref.shape[0] // HEADS
    at = lax.broadcasted_iota(jnp.int32, qt.shape, 0) // depth
    lse = []
    for h in range(HEADS):
        score = nn(k, jnp.where(at == h, qt, jnp.zeros_like(qt))) * score_unit
        top = jnp.max(score, 0, keepdims=True)
        weight = jnp.exp2(score - top)
        total = jnp.sum(weight, 0, keepdims=True)
        out = nn(vt_ref[h * wide : (h + 1) * wide], weight.astype(BF))
        ot_ref[h * wide : (h + 1) * wide] = (out * (1.0 / total)).astype(BF)
        lse.append(top + jnp.log2(total))
    lse = jnp.concatenate(lse, 0)
    high = lse.astype(BF)
    low = (lse - high.astype(F32)).astype(BF)
    ot_ref[HEADS * wide :] = jnp.concatenate([high, low], 0)


def attend(item, items, where, own, far, table, gain, w_key, w_value, qt, score_unit, before, deps):
    _, count, width = own.shape
    qk, lat = w_key.shape[1], qt.shape[2]
    wide = w_value.shape[1]
    ins = [
        (own, block((1, count, width), lambda g, w: w[0] * items + item)),
        (far, block((1, count, width), lambda g, w: item)),
        (table, None),
        (gain, None),
        (w_key, None),
        (w_value, None),
        (qt, block((1, qk, lat), lambda g, w: item)),
    ]
    alias = {}
    if before is not None:
        alias[len(ins)] = 1
        ins.append((before, ANY))
    return launch(
        functools.partial(attend_kernel, item, score_unit),
        "attend",
        where,
        ins,
        [
            ((wide + 2 * HEADS, lat), BF, None),
            ((items, 2 * count, width), BF, block((1, 2 * count, width), lambda g, w: item)),
            ((2 * count, qk), BF, None),
            ((qk, 2 * count), BF, None),
            ((2 * count, wide), BF, None),
        ],
        scratch=[pltpu.VMEM((wide, 2 * count), BF)],
        alias=alias,
        deps=deps,
    )


GELU_A = math.sqrt(2.0 / math.pi)
GELU_B = 0.044715


def latent_kernel(
    where, oa_ref, ob_ref, lat_ref, cot_ref, gain_ref, wo_ref, wu_ref, wd_ref, *refs
):
    (
        out_ref, outs_ref, gres_ref, gatt_ref, dot_ref, lse_ref, att_ref, hid_ref, act_ref,
        gpre_ref, glow_ref, ggain_ref,
    ) = refs[-12:]
    first = where[1] == 0
    rows = gatt_ref.shape[0]
    wide = rows // HEADS
    ours = oa_ref[rows : rows + HEADS].astype(F32) + oa_ref[rows + HEADS :].astype(F32)
    theirs = ob_ref[rows : rows + HEADS].astype(F32) + ob_ref[rows + HEADS :].astype(F32)
    left = jnp.where(first, ours, theirs)
    right = jnp.where(first, theirs, ours)
    top = jnp.maximum(left, right)
    e_left, e_right = jnp.exp2(left - top), jnp.exp2(right - top)
    total = e_left + e_right
    lse_ref[...] = top + jnp.log2(total)
    scale = 1.0 / total
    e_left, e_right = e_left * scale, e_right * scale
    merged = []
    for h in range(HEADS):
        a = oa_ref[h * wide : (h + 1) * wide].astype(F32)
        b = ob_ref[h * wide : (h + 1) * wide].astype(F32)
        low, high = jnp.where(first, a, b), jnp.where(first, b, a)
        merged.append(low * e_left[h : h + 1] + high * e_right[h : h + 1])
        att_ref[h * wide : (h + 1) * wide] = merged[-1].astype(BF)
    resid = lat_ref[0].astype(F32) + tn(att_ref[...], wo_ref[...])
    unit, inverse = standardise(resid)
    gain = gain_ref[...]
    hidden = (unit * gain).astype(BF)
    hid_ref[...] = hidden.T
    pre = nn(hidden, wu_ref[...])
    square = pre * pre
    slope = jnp.tanh(GELU_A * pre * (1.0 + GELU_B * square))
    act = (0.5 * pre * (1.0 + slope)).astype(BF)
    act_ref[...] = act.T
    out = (resid + nn(act, wd_ref[...])).astype(BF)
    out_ref[0] = out
    outs_ref[0] = out
    cot = cot_ref[0]
    gelu_slope = 0.5 * (1.0 + slope) + 0.5 * pre * (1.0 - slope * slope) * GELU_A * (
        1.0 + 3.0 * GELU_B * square
    )
    gpre = (nt(cot, wd_ref[...]) * gelu_slope).astype(BF)
    gpre_ref[...] = gpre
    ghid = nt(gpre, wu_ref[...])
    ggain_ref[...] = jnp.sum(ghid * unit, 0, keepdims=True)
    gres = cot.astype(F32) + standardise_back(unit, inverse, ghid * gain)
    gres_ref[...] = gres
    glow = gres.astype(BF)
    glow_ref[...] = glow
    gatt_ref[...] = nt(wo_ref[...], glow).astype(BF)
    for h in range(HEADS):
        dot_ref[h : h + 1] = jnp.sum(
            gatt_ref[h * wide : (h + 1) * wide].astype(F32) * merged[h], 0, keepdims=True
        )


def latent_side(
    item, items, where, oa, ob, latents, cot, gain, w_out, w_up, w_down, before, deps
):
    total, lat, width = latents.shape
    feed = w_up.shape[1]
    own = block((1, lat, width), lambda g, w: w[0] * items + item)
    ins = [
        (oa, None),
        (ob, None),
        (latents, own),
        (cot, own),
        (gain, None),
        (w_out, None),
        (w_up, None),
        (w_down, None),
    ]
    alias = {}
    for spot, array in enumerate(before):
        alias[len(ins)] = spot
        ins.append((array, ANY))
    return launch(
        latent_kernel,
        "latent_side",
        where,
        ins,
        [
            ((total, lat, width), BF, own),
            ((items, lat, width), BF, block((1, lat, width), lambda g, w: item)),
            ((lat, width), F32, None),
            ((width, lat), BF, None),
            ((HEADS, lat), F32, None),
            ((HEADS, lat), F32, None),
            ((width, lat), BF, None),
            ((width, lat), BF, None),
            ((feed, lat), BF, None),
            ((lat, feed), BF, None),
            ((lat, width), BF, None),
            ((1, width), F32, None),
        ],
        alias=alias,
        deps=deps,
    )


def flipped(at, bits):
    return sum(((at >> (len(bits) - 1 - t)) & 1) * bit for t, bit in enumerate(bits))


def pick_rows(where, source, lhs_ref, lane, rows, chips, bits):
    lat = source.shape[1]
    for j in range(2 ** len(bits)):
        spot = where[2] ^ flipped(j, bits)
        begin = pl.multiple_of((spot * chips + where[1]) * rows, 16)
        lhs_ref[j * rows : (j + 1) * rows, lane : lane + lat] = source[pl.ds(begin, rows)]


def latent_weights_kernel(group, items, chips, bits, where, *refs):
    ins, keep_ref, send_ref, lhs_ref = refs[:-3], refs[-3], refs[-2], refs[-1]
    half = keep_ref.shape[2]
    for w in range(group):
        lefts = ins[2 * items * w : 2 * items * w + items]
        rights = ins[2 * items * w + items : 2 * items * (w + 1)]
        total = 0.0
        for i in range(items):
            lat = lefts[i].shape[1]
            pick_rows(where, lefts[i], lhs_ref, i * lat, 2 * half, chips, bits)
            right = rights[i][0] if len(rights[i].shape) == 3 else rights[i][...]
            total += nn(lhs_ref[:, i * lat : (i + 1) * lat], right)
        for j in range(keep_ref.shape[0]):
            low = total[2 * j * half : (2 * j + 1) * half]
            high = total[(2 * j + 1) * half : (2 * j + 2) * half]
            keep_ref[j, w] = jnp.where(where[0] == 0, low, high).astype(BF)
            send_ref[j, w] = jnp.where(where[0] == 0, high, low).astype(BF)


def latent_weights(where, groups, chips, bits, name, deps):
    items = len(groups[0][0])
    ins = []
    for lefts, rights in groups:
        ins += [(a, None) for a in lefts] + list(rights)
    width, lat = groups[0][0][0].shape
    count = 2 ** len(bits)
    half = width // (count * chips * CORES)
    wide = groups[0][1][0][0].shape[-1]
    shape = (count, len(groups), half, wide)
    return launch(
        functools.partial(latent_weights_kernel, len(groups), items, chips, bits),
        name,
        where,
        ins,
        [(shape, BF, None), (shape, BF, None)],
        scratch=[pltpu.VMEM((width // chips, items * lat), BF)],
        deps=deps,
    )


def attend_back_kernel(
    score_unit, score_scale, where, q_ref, qt_ref, k_ref, kt_ref, v_ref, gatt_ref, lse_ref,
    dot_ref, *refs,
):
    dqt_ref, dkv_ref, dvt_ref = refs[-3:]
    q, qt, k = q_ref[0], qt_ref[0], k_ref[...]
    qk = qt.shape[0]
    depth = qk // HEADS
    wide = gatt_ref.shape[0] // HEADS
    lat = qt.shape[1]
    span = 2 * 128
    at = lax.broadcasted_iota(jnp.int32, qt.shape, 0) // depth
    across = lax.broadcasted_iota(jnp.int32, q.shape, 1) // depth
    dk = jnp.zeros(k.shape, F32)
    for h in range(HEADS):
        score = nn(k, jnp.where(at == h, qt, jnp.zeros_like(qt))) * score_unit
        prob = jnp.exp2(score - lse_ref[h : h + 1])
        grad = gatt_ref[h * wide : (h + 1) * wide]
        begin = h * wide // 128 * 128
        ahead = h * wide - begin
        after = span - ahead - wide
        pieces = [grad]
        if ahead:
            pieces = [jnp.zeros((ahead, lat), BF)] + pieces
        if after:
            pieces = pieces + [jnp.zeros((after, lat), BF)]
        grad_prob = nn(v_ref[:, begin : begin + span], jnp.concatenate(pieces, 0))
        grad_score = (prob * (grad_prob - dot_ref[h : h + 1])).astype(BF)
        dvt_ref[h * wide : (h + 1) * wide] = nt(grad, prob.astype(BF)).astype(BF)
        dk += nn(grad_score, jnp.where(across == h, q, jnp.zeros_like(q)))
        dqt_ref[0, h * depth : (h + 1) * depth] = nn(
            kt_ref[h * depth : (h + 1) * depth], grad_score
        ).astype(BF)
    dkv_ref[0, :, :qk] = (dk * score_scale).astype(BF)
    dkv_ref[0, :, qk:] = dvt_ref[...].T


def attend_back(
    item, where, q, qt, k, kt, v, gatt, lse, dot, score_unit, score_scale, before, deps
):
    items, lat, qk = q.shape
    count, wide = v.shape
    ins = [
        (q, block((1, lat, qk), lambda g, w: item)),
        (qt, block((1, qk, lat), lambda g, w: item)),
    ] + [(a, None) for a in (k, kt, v, gatt, lse, dot)]
    alias = {}
    for spot, array in enumerate(before):
        alias[len(ins)] = spot
        ins.append((array, ANY))
    return launch(
        functools.partial(attend_back_kernel, score_unit, score_scale),
        "attend_back",
        where,
        ins,
        [
            ((items, qk, lat), BF, block((1, qk, lat), lambda g, w: item)),
            (
                (items, count, qk + wide),
                BF,
                block((1, count, qk + wide), lambda g, w: item),
            ),
        ],
        scratch=[pltpu.VMEM((wide, count), BF)],
        alias=alias,
        deps=deps,
    )


def byte_product(xn_ref, dkv_ref):
    total = tn(xn_ref[0], dkv_ref[0])
    for i in range(1, xn_ref.shape[0]):
        total += tn(xn_ref[i], dkv_ref[i])
    return total


def byte_weights_kernel(bits, where, xn_ref, dkv_ref, keep_ref, send_ref, all_ref):
    all_ref[...] = byte_product(xn_ref, dkv_ref)
    rows = keep_ref.shape[1]
    mine = where[2] * 2 + where[1]
    for j in range(keep_ref.shape[0]):
        spot = (mine ^ flipped(j, bits)) * CORES
        keep = pl.multiple_of((spot + where[0]) * rows, 8)
        send = pl.multiple_of((spot + 1 - where[0]) * rows, 8)
        keep_ref[j] = all_ref[pl.ds(keep, rows)].astype(BF)
        send_ref[j] = all_ref[pl.ds(send, rows)].astype(BF)


def byte_weights(where, xn, dkv, bits, deps):
    width, wide = xn.shape[2], dkv.shape[2]
    count = 2 ** len(bits)
    shape = (count, width // (count * CORES), wide)
    return launch(
        functools.partial(byte_weights_kernel, bits),
        "byte_weights",
        where,
        [(xn, None), (dkv, None)],
        [(shape, BF, None), (shape, BF, None)],
        scratch=[pltpu.VMEM((width, wide), F32)],
        deps=deps,
    )


def bytes_back_kernel(
    where, own_ref, far_ref, table_ref, gain_ref, wk_ref, wv_ref, dkv_ref, gown_ref, gfar_ref,
    small_ref,
):
    count = own_ref.shape[1]
    qk = wk_ref.shape[1]
    item = pl.program_id(0)
    language = where[LANG_AT + item]
    row = language_row(table_ref, language)
    gain = gain_ref[...]
    grads = nt(dkv_ref[0, :, :qk], wk_ref[...]) + nt(dkv_ref[0, :, qk:], wv_ref[...])
    gain_sum = jnp.zeros_like(row)
    byte_sum = jnp.zeros_like(row)
    for part, ref, out in ((0, own_ref, gown_ref), (1, far_ref, gfar_ref)):
        unit, inverse = standardise(ref[0].astype(F32) + row)
        grad = grads[part * count : (part + 1) * count]
        gain_sum += jnp.sum(grad * unit, 0, keepdims=True)
        back = standardise_back(unit, inverse, grad * gain)
        byte_sum += jnp.sum(back, 0, keepdims=True)
        out[0] = back.astype(out.dtype)
    langs = table_ref.shape[0]
    at = lax.broadcasted_iota(jnp.int32, small_ref.shape, 0)

    @pl.when(item == 0)
    def _():
        small_ref[...] = jnp.zeros_like(small_ref)

    small_ref[...] += jnp.where(at == language, byte_sum, 0.0) + jnp.where(
        at == langs, gain_sum, 0.0
    )


def bytes_back(where, own, far, table, gain, w_key, w_value, dkv, deps):
    total, count, width = own.shape
    items = far.shape[0]
    langs = table.shape[0]
    spot = block((1, count, width), lambda g, w: w[0] * items + g)
    here = block((1, count, width), lambda g, w: g)
    return launch(
        bytes_back_kernel,
        "bytes_back",
        where,
        [
            (own, spot),
            (far, here),
            (table, None),
            (gain, None),
            (w_key, None),
            (w_value, None),
            (dkv, block((1,) + dkv.shape[1:], lambda g, w: g)),
        ],
        [
            ((total, count, width), F32, spot),
            ((items, count, width), BF, here),
            ((langs + 8, width), F32, None),
        ],
        deps=deps,
        grid=items,
    )


def latents_back_kernel(
    score_scale, chips, bits, where, da_ref, db_ref, *refs
):
    items = da_ref.shape[0]
    gres_refs = refs[:items]
    lat_ref, gain_ref, wq_ref, glat_ref, gsend_ref, keep_ref, send_ref, ggain_ref = refs[
        items : items + 8
    ]
    lhs_ref, rhs_ref, turn_ref = refs[items + 8 :]
    lat = lat_ref.shape[1]
    gain = gain_ref[...]
    gain_sum = jnp.zeros_like(gain)
    half = keep_ref.shape[1]
    for i in range(items):
        total = (da_ref[i].astype(F32) + db_ref[i].astype(F32)) * score_scale
        grad = total.T.astype(BF)
        rhs_ref[i * lat : (i + 1) * lat] = grad
        unit, inverse = standardise(lat_ref[i].astype(F32))
        turn_ref[i] = (unit * gain).astype(BF).T
        gln = nt(grad, wq_ref[...])
        gain_sum += jnp.sum(gln * unit, 0, keepdims=True)
        out = (gres_refs[i][...] + standardise_back(unit, inverse, gln * gain)).astype(BF)
        gsend_ref[i] = out
        glat_ref[i] = out.astype(F32)
    ggain_ref[...] = gain_sum
    for i in range(items):
        pick_rows(where, turn_ref.at[i], lhs_ref, i * lat, 2 * half, chips, bits)
    total = nn(lhs_ref[...], rhs_ref[...])
    for j in range(keep_ref.shape[0]):
        low = total[2 * j * half : (2 * j + 1) * half]
        high = total[(2 * j + 1) * half : (2 * j + 2) * half]
        keep_ref[j] = jnp.where(where[0] == 0, low, high).astype(BF)
        send_ref[j] = jnp.where(where[0] == 0, high, low).astype(BF)


def latents_back(where, da, db, gres, latents, gain, w_query, score_scale, chips, bits, deps):
    all_items, lat, width = latents.shape
    items = da.shape[0]
    qk = w_query.shape[1]
    count = 2 ** len(bits)
    half = width // (count * chips * CORES)
    own = block((items, lat, width), lambda g, w: w[0])
    return launch(
        functools.partial(latents_back_kernel, score_scale, chips, bits),
        "latents_back",
        where,
        [(da, None), (db, None)]
        + [(g, None) for g in gres]
        + [(latents, own), (gain, None), (w_query, None)],
        [
            ((all_items, lat, width), F32, own),
            ((items, lat, width), BF, None),
            ((count, half, qk), BF, None),
            ((count, half, qk), BF, None),
            ((1, width), F32, None),
        ],
        scratch=[
            pltpu.VMEM((width // chips, items * lat), BF),
            pltpu.VMEM((items * lat, qk), BF),
            pltpu.VMEM((items, width, lat), BF),
        ],
        deps=deps,
    )


def fold_kernel(where, keep_ref, far_ref, *outs):
    half = keep_ref.shape[0] // 2
    if len(outs) == 1:
        outs[0][...] = keep_ref[0].astype(F32) + far_ref[0].astype(F32)
        return
    for spot, out in enumerate(outs):
        for j in range(half):
            at = spot * half + j
            out[j] = (keep_ref[at].astype(F32) + far_ref[at].astype(F32)).astype(BF)


def fold(where, keep, far, deps):
    if keep.shape[0] == 1:
        outs = [(keep.shape[1:], F32, None)]
    else:
        shape = (keep.shape[0] // 2,) + keep.shape[1:]
        outs = [(shape, BF, None), (shape, BF, None)]
    return launch(fold_kernel, "fold", where, [(keep, None), (far, None)], outs, deps=deps)


def pack_kernel(share, langs, where, small_ref, glat_ref, *refs):
    gmlp_refs, (gq_ref, own_ref, send_ref, turn_ref) = refs[:-4], refs[-4:]
    rows = small_ref.shape[0]
    wide = own_ref.shape[2]
    at = lax.broadcasted_iota(jnp.int32, (rows, wide), 0)
    gmlp = functools.reduce(jnp.add, [r[...] for r in gmlp_refs])
    for g in range(glat_ref.shape[1] // wide):
        cut = slice(g * wide, (g + 1) * wide)
        piece = jnp.where(at == langs + 1, glat_ref[:, cut] * share, 0.0) + jnp.where(
            at == langs + 2, gmlp[:, cut] * share, 0.0
        )
        if (g + 1) * wide <= small_ref.shape[1]:
            piece += small_ref[:, cut]
        turn_ref[g * rows : (g + 1) * rows] = piece
    count, half = gq_ref.shape[:2]
    for j in range(count):
        send_ref[j] = gq_ref[j]
    for j in range(own_ref.shape[0]):
        own_ref[j] = turn_ref[j * half : (j + 1) * half]
        send_ref[count + j] = turn_ref[j * half : (j + 1) * half].astype(BF)


def pack(where, small, glat, gmlps, gq_send, share, langs, deps):
    count, half, wide = gq_send.shape
    groups = glat.shape[1] // wide
    blocks = groups * small.shape[0] // half
    return launch(
        functools.partial(pack_kernel, share, langs),
        "pack",
        where,
        [(small, None), (glat, None)] + [(g, None) for g in gmlps] + [(gq_send, None)],
        [((blocks, half, wide), F32, None), ((count + blocks, half, wide), BF, None)],
        scratch=[pltpu.VMEM((groups * small.shape[0], wide), F32)],
        deps=deps,
    )


def late_kernel(where, keep_ref, far_ref, own_ref, keep_out, send_out, own_out):
    blocks = own_ref.shape[0]
    count = keep_ref.shape[0]
    half = count // 2
    for j in range(blocks):
        own = own_ref[j] + far_ref[count + j].astype(F32)
        own_out[j] = own
        send_out[half + j] = own.astype(BF)
    for j in range(half):
        keep_out[j] = (keep_ref[j].astype(F32) + far_ref[j].astype(F32)).astype(BF)
        send_out[j] = (keep_ref[half + j].astype(F32) + far_ref[half + j].astype(F32)).astype(BF)


def late_side_kernel(where, far_ref, own_ref, send_ref, own_out, send_out):
    half = send_ref.shape[0] - own_ref.shape[0]
    for j in range(half):
        send_out[j] = send_ref[j]
    for j in range(own_ref.shape[0]):
        own = own_ref[j] + far_ref[j].astype(F32)
        own_out[j] = own
        send_out[half + j] = own.astype(BF)


def late_last_kernel(where, keep_ref, far_ref, own_ref, gq_ref, small_ref, turn_ref):
    gq_ref[...] = keep_ref[0].astype(F32) + far_ref[0].astype(F32)
    blocks, half, wide = own_ref.shape
    for j in range(blocks):
        turn_ref[j * half : (j + 1) * half] = own_ref[j] + far_ref[1 + j].astype(F32)
    rows = small_ref.shape[0]
    for g in range(small_ref.shape[1] // wide):
        small_ref[:, g * wide : (g + 1) * wide] = turn_ref[g * rows : (g + 1) * rows]


def late(where, keep, far, own, deps):
    count, half, wide = keep.shape
    blocks = own.shape[0]
    return launch(
        late_kernel,
        "late",
        where,
        [(keep, None), (far, None), (own, None)],
        [
            ((count // 2, half, wide), BF, None),
            ((count // 2 + blocks, half, wide), BF, None),
            ((blocks, half, wide), F32, None),
        ],
        deps=deps,
    )


def late_side(where, far, own, send, deps):
    return launch(
        late_side_kernel,
        "late_side",
        where,
        [(far, None), (own, None), (send, None)],
        [(own.shape, F32, None), (send.shape, BF, None)],
        deps=deps,
    )


def late_last(where, keep, far, own, rows, width, deps):
    return launch(
        late_last_kernel,
        "late_last",
        where,
        [(keep, None), (far, None), (own, None)],
        [(keep.shape[1:], F32, None), ((rows, width), F32, None)],
        scratch=[pltpu.VMEM((own.shape[0] * own.shape[1], own.shape[2]), F32)],
        deps=deps,
    )


def place_kernel(where, out_ref, glat_ref, gbyte_ref, *refs):
    out, glat, gbyte = refs[-3:]
    out[...] = out_ref[...]
    glat[...] = glat_ref[...].astype(F32)
    gbyte[...] = gbyte_ref[...].astype(F32)


def place(where, arrived, holders, deps):
    items = arrived[0].shape[0]
    ins = [(a, block((1,) + a.shape[1:], lambda g, w: g)) for a in arrived]
    ins += [(a, ANY) for a in holders]
    other = lambda g, w: (1 - w[0]) * items + g
    outs = [(a.shape, a.dtype, block((1,) + a.shape[1:], other)) for a in holders]
    alias = {len(arrived) + i: i for i in range(len(holders))}
    return launch(
        place_kernel, "place", where, ins, outs, alias=alias, deps=deps, grid=items
    )


def swap(value, axis, bit):
    size = lax.axis_size(axis)
    return lax.ppermute(value, axis, [(i, i ^ bit) for i in range(size)])


def bits_of(size):
    return [2**t for t in range(size.bit_length() - 1)]


def halve(value, dim, axis, bit):
    mine = (lax.axis_index(axis) // bit) % 2
    keep = lax.dynamic_index_in_dim(value, mine, dim, keepdims=False)
    send = lax.dynamic_index_in_dim(value, 1 - mine, dim, keepdims=False)
    return (keep.astype(F32) + swap(send, axis, bit).astype(F32)).astype(BF)


def scatter_rows(value):
    spots, chips = lax.axis_size("batch"), lax.axis_size("seq") // CORES
    rows = value.shape[0] // (spots * chips * CORES)
    blocks = value.astype(BF).reshape(spots, chips, CORES, rows, value.shape[1])
    blocks = halve(blocks, 2, "seq", 1)
    for bit in bits_of(chips):
        rest = blocks.shape[2:]
        blocks = blocks.reshape((spots, blocks.shape[1] // 2, 2) + rest)
        blocks = halve(blocks, 2, "seq", CORES * bit)
    blocks = blocks[:, 0]
    for bit in bits_of(spots):
        blocks = blocks.reshape((blocks.shape[0] // 2, 2) + blocks.shape[1:])
        blocks = halve(blocks, 1, "batch", bit)
    return blocks[0].astype(F32)


def everywhere(value):
    for axis in ("seq", "batch"):
        for bit in bits_of(lax.axis_size(axis)):
            value = value + swap(value, axis, bit)
    return value


def merge(oa, ob):
    rows = oa.shape[0] - 2 * HEADS
    wide = rows // HEADS
    la = oa[rows : rows + HEADS].astype(F32) + oa[rows + HEADS :].astype(F32)
    lb = ob[rows : rows + HEADS].astype(F32) + ob[rows + HEADS :].astype(F32)
    top = jnp.maximum(la, lb)
    ea, eb = jnp.exp2(la - top), jnp.exp2(lb - top)
    total = ea + eb
    lse = top + jnp.log2(total)
    out = oa[:rows].astype(F32) * jnp.repeat(ea / total, wide, 0)
    out = out + ob[:rows].astype(F32) * jnp.repeat(eb / total, wide, 0)
    high = lse.astype(BF)
    return jnp.concatenate([out.astype(BF), high, (lse - high.astype(F32)).astype(BF)], 0)


LANG_AT = 3


def local(
    byte_inputs,
    language,
    lang_table,
    latents,
    gain_in,
    gain_lat,
    gain_mlp,
    w_query,
    w_key,
    w_value,
    w_out,
    w_up,
    w_down,
    cotangent,
):
    items = byte_inputs.shape[0] // CORES
    width_in, width_lat = byte_inputs.shape[2], latents.shape[2]
    lat, qk = latents.shape[1], w_query.shape[1]
    langs = lang_table.shape[0]
    score_scale = 1.0 / math.sqrt(qk // HEADS)
    score_unit = score_scale * math.log2(math.e)
    spots, chips = lax.axis_size("batch"), lax.axis_size("seq") // CORES
    devices = spots * chips * CORES
    seq_at, spot = lax.axis_index("seq"), lax.axis_index("batch")
    core, side = seq_at % CORES, seq_at // CORES
    device = spot * (chips * CORES) + seq_at
    chip_bits, spot_bits = bits_of(chips), bits_of(spots)
    rows_in, rows_lat = width_in // devices, width_lat // devices
    direct = chips == 2 and rows_in % 8 == 0 and rows_lat % 8 == 0
    own_languages = lax.dynamic_slice_in_dim(language, core * items, items, 0)
    where = jnp.concatenate([jnp.stack([core, side, spot]).astype(jnp.int32), own_languages])
    last_bit = chip_bits[-1]
    order = where.at[1].set(side // last_bit % 2)
    table = lang_table.astype(F32)
    gain_in, gain_lat, gain_mlp = gain_in[None], gain_lat[None], gain_mlp[None]

    send = lax.dynamic_slice_in_dim(byte_inputs, (1 - core) * items, items, 0)
    far = swap(send, "seq", 1)
    q, qt = queries(where, latents, gain_lat, w_query, items)

    xn, kept, pairs, token = None, [], [], ()
    for item in range(items):
        ot, xn, k, kt, v = attend(
            item, items, where, byte_inputs, far, table, gain_in, w_key, w_value, qt, score_unit,
            xn, token,
        )
        kept.append((k, kt, v))
        token = (k,)
        for bit in chip_bits[:-1]:
            ot = merge(ot, swap(ot, "seq", CORES * bit))
        pairs.append((ot, swap(ot, "seq", CORES * last_bit)))

    sides, held, dqkv = [], (), ()

    def back(item, deps):
        gatt, dot, lse = sides[item][3:6]
        return attend_back(
            item, where, q, qt, *kept[item], gatt, lse, dot, score_unit, score_scale, dqkv, deps
        )

    for item in range(items):
        if item:
            dqkv = back(item - 1, token)
            token = (dqkv[0],)
        side_out = latent_side(
            item, items, order if chips > 2 else where, *pairs[item], latents, cotangent,
            gain_mlp, w_out, w_up, w_down, held, token,
        )
        held = side_out[:2]
        sides.append(side_out)
        token = (side_out[4],)
    latents_out, outs = held
    outs_far = swap(outs, "seq", 1)

    pick = lambda at: [s[at] for s in sides]
    cots = [
        (cotangent, block((1, lat, width_lat), lambda g, w, i=i: w[0] * items + i))
        for i in range(items)
    ]
    whole_arrays = lambda arrays: [(a, None) for a in arrays]
    down = (pick(8), cots)
    up = (pick(7), whole_arrays(pick(9)))
    out = (pick(6), whole_arrays(pick(10)))

    if direct:
        keep_a, send_a = latent_weights(where, [down], chips, spot_bits, "down_weights", token)
        far_a = swap(send_a, "seq", 1)
        keep_b, send_b = latent_weights(where, [up, out], chips, spot_bits, "up_weights", (keep_a,))
        far_b = swap(send_b, "seq", 1)
        keep_a, send_a = fold(where, keep_a, far_a, (keep_b,))
        far_a = swap(send_a, "batch", spot_bits[0])
        dqt, dkv = back(items - 1, (keep_a,))
        dqt_far = swap(dqt, "seq", CORES)
        keep_b, send_b = fold(where, keep_b, far_b, (dqt,))
        far_b = swap(send_b, "batch", spot_bits[0])
        byte_bits = [1] + [2 * b for b in spot_bits]
        keep_c, send_c = byte_weights(where, xn, dkv, byte_bits, (keep_b,))
        far_c = swap(send_c, "seq", 1)
        keep_a, send_a = fold(where, keep_a, far_a, (keep_c,))
        far_a = swap(send_a, "batch", spot_bits[1])
        grad_latents, glats, keep_q, send_q, ggain_lat = latents_back(
            where, dqt, dqt_far, pick(2), latents, gain_lat, w_query, score_scale, chips, spot_bits,
            (keep_a,),
        )
        glats_far = swap(glats, "seq", 1)
        keep_c, send_c = fold(where, keep_c, far_c, (ggain_lat,))
        far_c = swap(send_c, "seq", CORES)
        grad_bytes, gfar, small = bytes_back(
            where, byte_inputs, far, table, gain_in, w_key, w_value, dkv, (keep_c,)
        )
        gfar_far = swap(gfar, "seq", 1)
        own_s, send_q = pack(where, small, ggain_lat, pick(11), send_q, 1.0 / chips, langs, ())
        far_q = swap(send_q, "seq", 1)
        keep_a, send_a = fold(where, keep_a, far_a, (own_s,))
        far_a = swap(send_a, "batch", spot_bits[2])
        keep_q, send_q, own_s = late(where, keep_q, far_q, own_s, (keep_a,))
        far_s = swap(send_q[keep_q.shape[0] :], "seq", CORES)
        keep_c, send_c = fold(where, keep_c, far_c, (own_s,))
        far_c = swap(send_c, "batch", spot_bits[0])
        own_s, send_q = late_side(where, far_s, own_s, send_q, (keep_c,))
        far_q = swap(send_q, "batch", spot_bits[0])
        keep_b, send_b = fold(where, keep_b, far_b, (own_s,))
        far_b = swap(send_b, "batch", spot_bits[1])
        keep_c, send_c = fold(where, keep_c, far_c, (keep_b,))
        far_c = swap(send_c, "batch", spot_bits[1])
        keep_q, send_q, own_s = late(where, keep_q, far_q, own_s, (keep_c,))
        far_q = swap(send_q, "batch", spot_bits[1])
        latents_out, grad_latents, grad_bytes = place(
            where, [outs_far, glats_far, gfar_far], [latents_out, grad_latents, grad_bytes], (keep_q,)
        )
        (g_a,) = fold(where, keep_a, far_a, (keep_q,))
        keep_c, send_c = fold(where, keep_c, far_c, (g_a,))
        far_c = swap(send_c, "batch", spot_bits[2])
        keep_q, send_q, own_s = late(where, keep_q, far_q, own_s, (keep_c,))
        far_q = swap(send_q, "batch", spot_bits[2])
        keep_b, send_b = fold(where, keep_b, far_b, (own_s,))
        far_b = swap(send_b, "batch", spot_bits[2])
        (g_c,) = fold(where, keep_c, far_c, (keep_b,))
        g_query, small = late_last(where, keep_q, far_q, own_s, langs + 8, width_lat, (g_c,))
        (g_b,) = fold(where, keep_b, far_b, (small,))
        g_down, g_up, g_out = g_a[0], g_b[0], g_b[1]
        g_bytes = g_c
    else:
        dqt, dkv = back(items - 1, token)
        for bit in chip_bits:
            dqt = (dqt.astype(F32) + swap(dqt, "seq", CORES * bit).astype(F32)).astype(BF)
        grad_bytes, gfar, small = bytes_back(
            where, byte_inputs, far, table, gain_in, w_key, w_value, dkv, ()
        )
        gfar_far = swap(gfar, "seq", 1)
        own_cut = lambda a: lax.dynamic_slice_in_dim(a, core * items, items, 0)
        grad_q = (dqt.astype(F32) * score_scale).swapaxes(1, 2).astype(BF)
        unit, inverse = standardise(own_cut(latents).astype(F32))
        gln = lax.dot_general(
            grad_q, w_query, (((2,), (1,)), ((), ())), preferred_element_type=F32
        )
        glats = jnp.stack(pick(2)) + standardise_back(unit, inverse, gln * gain_lat)
        glats = glats.astype(BF)
        glats_far = swap(glats, "seq", 1)
        flat = lambda a: a.reshape(-1, a.shape[-1])
        share = 1.0 / chips
        g_query = scatter_rows(tn(flat((unit * gain_lat).astype(BF)), flat(grad_q)) * share)
        rows = lambda lefts, rights: scatter_rows(
            sum(nn(x, y) for x, y in zip(lefts, rights)) * share
        )
        g_down = rows(pick(8), own_cut(cotangent))
        g_up, g_out = rows(pick(7), pick(9)), rows(pick(6), pick(10))
        g_bytes = scatter_rows(sum(tn(xn[i], dkv[i]) for i in range(items)))
        pad = ((0, 0), (0, width_lat - width_in))
        small = jnp.concatenate(
            [
                jnp.pad(small[: langs + 1], pad),
                jnp.sum(gln * unit, (0, 1))[None] * share,
                sum(pick(11)) * share,
            ],
            0,
        )
        small = everywhere(small)
        grad_latents = lax.dynamic_update_slice(
            jnp.zeros(latents.shape, F32), glats.astype(F32), (core * items, 0, 0)
        )
        latents_out, grad_latents, grad_bytes = place(
            where,
            [outs_far, glats_far, gfar_far],
            [latents_out, grad_latents, grad_bytes],
            (),
        )

    byte_cut = lax.dynamic_slice_in_dim(small, device * rows_in, rows_in, 1)
    lat_cut = lax.dynamic_slice_in_dim(small, device * rows_lat, rows_lat, 1)
    return (
        latents_out,
        grad_latents,
        grad_bytes,
        byte_cut[:langs],
        byte_cut[langs],
        lat_cut[langs + 1],
        lat_cut[langs + 2],
        g_query,
        g_bytes[:, :qk],
        g_bytes[:, qk:],
        g_out,
        g_up,
        g_down,
    )


def solution(mesh):
    return jax.shard_map(
        local,
        mesh=mesh,
        in_specs=(
            P("batch", "seq", None),
            P("batch"),
            P(),
            P("batch", None, None),
            P(),
            P(),
            P(),
            P(),
            P(),
            P(),
            P(),
            P(),
            P(),
            P("batch", None, None),
        ),
        out_specs=(
            P("batch", None, None),
            P("batch", None, None),
            P("batch", "seq", None),
            P(None, ("batch", "seq")),
            P(("batch", "seq")),
            P(("batch", "seq")),
            P(("batch", "seq")),
            P(("batch", "seq"), None),
            P(("batch", "seq"), None),
            P(("batch", "seq"), None),
            P(("batch", "seq"), None),
            P(("batch", "seq"), None),
            P(("batch", "seq"), None),
        ),
        check_vma=False,
    )
```

```python
import functools
import math

import jax
import jax.numpy as jnp
from jax import lax
from jax.experimental import pallas as pl
from jax.experimental.pallas import tpu as pltpu
from jax.sharding import PartitionSpec as P

HEADS = 8
CORES = 2
EPS = 1e-05
F32 = jnp.float32
BF = jnp.bfloat16
VMEM_LIMIT = 16 * 1024 * 1024
PEAK = 1.15e9
SHORT, LONG = 0.001, 40


def nn(a, b):
    return lax.dot_general(a, b, (((1,), (0,)), ((), ())), preferred_element_type=F32)


def nt(a, b):
    return lax.dot_general(a, b, (((1,), (1,)), ((), ())), preferred_element_type=F32)


def tn(a, b):
    return lax.dot_general(a, b, (((0,), (0,)), ((), ())), preferred_element_type=F32)


def standardise(x):
    centre = x - jnp.mean(x, -1, keepdims=True)
    inverse = lax.rsqrt(jnp.mean(centre * centre, -1, keepdims=True) + EPS)
    return centre * inverse, inverse


def standardise_back(unit, inverse, grad):
    return inverse * (
        grad - jnp.mean(grad, -1, keepdims=True) - unit * jnp.mean(grad * unit, -1, keepdims=True)
    )


def block(shape, at):
    return pl.BlockSpec(shape, lambda g, w: (at(g, w),) + (0,) * (len(shape) - 1))


ANY = pl.BlockSpec(memory_space=pl.ANY)
FAST = pl.BlockSpec(memory_space=pltpu.VMEM)


def launch(body, name, micros, where, ins, outs, scratch=(), deps=(), alias=None, grid=1, far=False):
    count, extra = len(ins), len(deps)

    def kernel(where_ref, *refs):
        body(where_ref, *refs[:count], *refs[count + extra :])

    return pl.pallas_call(
        kernel,
        grid_spec=pltpu.PrefetchScalarGridSpec(
            num_scalar_prefetch=1,
            grid=(grid,),
            in_specs=[FAST if s is None else s for _, s in ins] + [ANY] * extra,
            out_specs=[FAST if s is None else s for _, _, s in outs],
            scratch_shapes=list(scratch),
        ),
        out_shape=[
            (pltpu.HBM if far else jax.ShapeDtypeStruct)(shape, dtype) for shape, dtype, _ in outs
        ],
        input_output_aliases={1 + i: o for i, o in (alias or {}).items()},
        compiler_params=pltpu.CompilerParams(vmem_limit_bytes=VMEM_LIMIT),
        cost_estimate=pl.CostEstimate(
            flops=int(micros * PEAK), bytes_accessed=1, transcendentals=0
        ),
        name=name,
    )(where, *[a for a, _ in ins], *deps)


def query_kernel(where, lat_ref, gain_ref, wq_ref, q_ref, qt_ref):
    items = q_ref.shape[0]
    for i in range(items):
        unit, _ = standardise(lat_ref[where[0] * items + i].astype(F32))
        rows = nn((unit * gain_ref[...]).astype(BF), wq_ref[...])
        q_ref[i] = rows.astype(BF)
        qt_ref[i] = rows.T.astype(BF)


def queries(where, latents, gain, w_query, items):
    _, count, width = latents.shape
    qk = w_query.shape[1]
    return launch(
        query_kernel,
        "queries",
        2,
        where,
        [
            (latents, None),
            (gain, None),
            (w_query, None),
        ],
        [((items, count, qk), BF, None), ((items, qk, count), BF, None)],
    )


SPAN = 256


def head_span(h, wide):
    begin = h * wide // 128 * 128
    return begin, h * wide - begin


def language_row(table_ref, language):
    at = lax.broadcasted_iota(jnp.int32, table_ref.shape, 0)
    return jnp.sum(jnp.where(at == language, table_ref[...], 0.0), 0, keepdims=True)


def attend_kernel(
    item, score_unit, where, own_ref, far_ref, table_ref, gain_ref, wk_ref, wv_ref, qt_ref,
    ot_ref, xn_ref, k_ref, kt_ref, v_ref,
):
    items, count = far_ref.shape[:2]
    row = language_row(table_ref, where[LANG_AT + item])
    gain = gain_ref[...]
    for part, rows in enumerate((own_ref[where[0] * items + item], far_ref[item])):
        unit, _ = standardise(rows.astype(F32) + row)
        xn_ref[part * count : (part + 1) * count] = (unit * gain).astype(BF)
    xn = xn_ref[...]
    k = nn(xn, wk_ref[...]).astype(BF)
    k_ref[...] = k
    kt_ref[...] = k.T
    v = nn(xn, wv_ref[...]).astype(BF)
    v_ref[...] = v
    qt = qt_ref[item]
    depth = qt.shape[0] // HEADS
    wide = v.shape[1] // HEADS
    at = lax.broadcasted_iota(jnp.int32, qt.shape, 0) // depth

    def score_of(h):
        return nn(k, jnp.where(at == h, qt, jnp.zeros_like(qt)))

    def finish(h, weight, total):
        begin, ahead = head_span(h, wide)
        out = tn(v[:, begin : begin + SPAN], weight)[ahead : ahead + wide]
        ot_ref[h * wide : (h + 1) * wide] = (out * (1.0 / total)).astype(BF)

    lse = []
    coming, waiting = score_of(0), None
    for h in range(HEADS):
        score = coming * score_unit
        if h + 1 < HEADS:
            coming = score_of(h + 1)
        if waiting is not None:
            finish(*waiting)
        top = jnp.max(score, 0, keepdims=True)
        weight = jnp.exp2(score - top)
        total = jnp.sum(weight, 0, keepdims=True)
        lse.append(top + jnp.log2(total))
        waiting = (h, weight.astype(BF), total)
    finish(*waiting)
    lse = jnp.concatenate(lse, 0)
    high = lse.astype(BF)
    low = (lse - high.astype(F32)).astype(BF)
    ot_ref[HEADS * wide :] = jnp.concatenate([high, low], 0)


def attend(item, items, where, own, far, table, gain, w_key, w_value, qt, score_unit, deps):
    _, count, width = own.shape
    qk, lat = w_key.shape[1], qt.shape[2]
    wide = w_value.shape[1]
    return launch(
        functools.partial(attend_kernel, item, score_unit),
        "attend",
        5.7,
        where,
        [(a, None) for a in (own, far, table, gain, w_key, w_value, qt)],
        [
            ((wide + 2 * HEADS, lat), BF, None),
            ((2 * count, width), BF, None),
            ((2 * count, qk), BF, None),
            ((qk, 2 * count), BF, None),
            ((2 * count, wide), BF, None),
        ],
        deps=deps,
    )


def act_back_kernel(where, cot_ref, wd_ref, gact_ref):
    items = gact_ref.shape[0]
    for i in range(items):
        gact_ref[i] = nt(cot_ref[where[0] * items + i], wd_ref[...])


def act_back(where, cot, w_down, items, deps):
    return launch(
        act_back_kernel,
        "act_back",
        2.5,
        where,
        [(cot, None), (w_down, None)],
        [((items, cot.shape[1], w_down.shape[0]), F32, None)],
        deps=deps,
    )[0]


GELU_A = math.sqrt(2.0 / math.pi)
GELU_B = 0.044715


def latent_kernel(
    item, items, where, oa_ref, ob_ref, lat_ref, cot_ref, gact_ref, gain_ref, wo_ref, wu_ref, wd_ref,
    *refs,
):
    (
        outs_ref, gres_ref, gatt_ref, dot_ref, lse_ref, att_ref, hid_ref, act_ref, gpre_ref,
        glow_ref, ggain_ref,
    ) = refs[-11:]
    at = where[0] * items + item
    first = where[1] == 0
    rows = gatt_ref.shape[0]
    wide = rows // HEADS
    ours = oa_ref[rows : rows + HEADS].astype(F32) + oa_ref[rows + HEADS :].astype(F32)
    theirs = ob_ref[rows : rows + HEADS].astype(F32) + ob_ref[rows + HEADS :].astype(F32)
    left = jnp.where(first, ours, theirs)
    right = jnp.where(first, theirs, ours)
    top = jnp.maximum(left, right)
    e_left, e_right = jnp.exp2(left - top), jnp.exp2(right - top)
    total = e_left + e_right
    lse_ref[...] = top + jnp.log2(total)
    scale = 1.0 / total
    e_left, e_right = e_left * scale, e_right * scale
    merged = []
    for h in range(HEADS):
        a = oa_ref[h * wide : (h + 1) * wide].astype(F32)
        b = ob_ref[h * wide : (h + 1) * wide].astype(F32)
        low, high = jnp.where(first, a, b), jnp.where(first, b, a)
        merged.append(low * e_left[h : h + 1] + high * e_right[h : h + 1])
        att_ref[h * wide : (h + 1) * wide] = merged[-1].astype(BF)
    resid = lat_ref[at].astype(F32) + tn(att_ref[...], wo_ref[...])
    unit, inverse = standardise(resid)
    gain = gain_ref[...]
    hidden = (unit * gain).astype(BF)
    hid_ref[...] = hidden.T
    pre = nn(hidden, wu_ref[...])
    square = pre * pre
    slope = jnp.tanh(GELU_A * pre * (1.0 + GELU_B * square))
    act = (0.5 * pre * (1.0 + slope)).astype(BF)
    act_ref[...] = act.T
    outs_ref[item] = (resid + nn(act, wd_ref[...])).astype(BF)
    cot = cot_ref[at]
    gelu_slope = 0.5 * (1.0 + slope) + 0.5 * pre * (1.0 - slope * slope) * GELU_A * (
        1.0 + 3.0 * GELU_B * square
    )
    gpre = (gact_ref[item] * gelu_slope).astype(BF)
    gpre_ref[...] = gpre
    ghid = nt(gpre, wu_ref[...])
    ggain_ref[...] = jnp.sum(ghid * unit, 0, keepdims=True)
    gres = cot.astype(F32) + standardise_back(unit, inverse, ghid * gain)
    gres_ref[...] = gres
    glow = gres.astype(BF)
    glow_ref[...] = glow
    gatt_ref[...] = nt(wo_ref[...], glow).astype(BF)
    for h in range(HEADS):
        dot_ref[h : h + 1] = jnp.sum(
            gatt_ref[h * wide : (h + 1) * wide].astype(F32) * merged[h], 0, keepdims=True
        )


def latent_side(
    item, items, where, oa, ob, latents, cot, gact, gain, w_out, w_up, w_down, before, deps
):
    total, lat, width = latents.shape
    feed = w_up.shape[1]
    ins = [(a, None) for a in (oa, ob, latents, cot, gact, gain, w_out, w_up, w_down)]
    alias = {}
    if before is not None:
        alias[len(ins)] = 0
        ins.append((before, None))
    return launch(
        functools.partial(latent_kernel, item, items),
        "latent_side",
        7,
        where,
        ins,
        [
            ((items, lat, width), BF, None),
            ((lat, width), F32, None),
            ((width, lat), BF, None),
            ((HEADS, lat), F32, None),
            ((HEADS, lat), F32, None),
            ((width, lat), BF, None),
            ((width, lat), BF, None),
            ((feed, lat), BF, None),
            ((lat, feed), BF, None),
            ((lat, width), BF, None),
            ((1, width), F32, None),
        ],
        alias=alias,
        deps=deps,
    )


def flipped(at, bits):
    return sum(((at >> (len(bits) - 1 - t)) & 1) * bit for t, bit in enumerate(bits))


def pick_rows(where, source, lhs_ref, lane, rows, chips, bits):
    lat = source.shape[1]
    for j in range(2 ** len(bits)):
        spot = where[2] ^ flipped(j, bits)
        begin = pl.multiple_of((spot * chips + where[1]) * rows, 16)
        lhs_ref[j * rows : (j + 1) * rows, lane : lane + lat] = source[pl.ds(begin, rows)]


def latent_weights_kernel(plan, items, chips, bits, where, *refs):
    ins, keep_ref, send_ref, lhs_ref = refs[:-3], refs[-3], refs[-2], refs[-1]
    half = keep_ref.shape[1]
    column = 0
    for w, (begin, width) in enumerate(plan):
        lefts = ins[2 * items * w : 2 * items * w + items]
        rights = ins[2 * items * w + items : 2 * items * (w + 1)]
        total = 0.0
        for i in range(items):
            lat = lefts[i].shape[1]
            pick_rows(where, lefts[i], lhs_ref, i * lat, 2 * half, chips, bits)
            right = rights[i]
            if len(right.shape) == 3:
                right = right.at[where[0] * items + i]
            total += nn(lhs_ref[:, i * lat : (i + 1) * lat], right[:, begin : begin + width])
        out = slice(column, column + width)
        for j in range(keep_ref.shape[0]):
            low = total[2 * j * half : (2 * j + 1) * half]
            high = total[(2 * j + 1) * half : (2 * j + 2) * half]
            keep_ref[j, :, out] = jnp.where(where[0] == 0, low, high).astype(BF)
            send_ref[j, :, out] = jnp.where(where[0] == 0, high, low).astype(BF)
        column += width


def latent_weights(where, groups, plan, chips, bits, name, deps):
    items = len(groups[0][0])
    ins = []
    for lefts, rights in groups:
        ins += [(a, None) for a in lefts + rights]
    width, lat = groups[0][0][0].shape
    count = 2 ** len(bits)
    half = width // (count * chips * CORES)
    shape = (count, half, sum(w for _, w in plan))
    return launch(
        functools.partial(latent_weights_kernel, plan, items, chips, bits),
        name,
        SHORT,
        where,
        ins,
        [(shape, BF, None), (shape, BF, None)],
        scratch=[pltpu.VMEM((width // chips, items * lat), BF)],
        deps=deps,
    )


def attend_back_kernel(
    item, score_unit, score_scale, where, q_ref, qt_ref, k_ref, kt_ref, v_ref, gatt_ref, lse_ref,
    dot_ref, *refs,
):
    dqt_ref, dkv_ref, dvt_ref = refs[-3:]
    q, qt, k = q_ref[item], qt_ref[item], k_ref[...]
    qk = qt.shape[0]
    depth = qk // HEADS
    wide = gatt_ref.shape[0] // HEADS
    lat = qt.shape[1]
    at = lax.broadcasted_iota(jnp.int32, qt.shape, 0) // depth
    across = lax.broadcasted_iota(jnp.int32, q.shape, 1) // depth

    def begin_head(h):
        score = nn(k, jnp.where(at == h, qt, jnp.zeros_like(qt)))
        grad = gatt_ref[h * wide : (h + 1) * wide]
        begin, ahead = head_span(h, wide)
        after = SPAN - ahead - wide
        pieces = [grad]
        if ahead:
            pieces = [jnp.zeros((ahead, lat), BF)] + pieces
        if after:
            pieces = pieces + [jnp.zeros((after, lat), BF)]
        return score, grad, nn(v_ref[:, begin : begin + SPAN], jnp.concatenate(pieces, 0))

    def finish(h, grad, prob, grad_score):
        dvt_ref[h * wide : (h + 1) * wide] = nt(grad, prob).astype(BF)
        dqt_ref[item, h * depth : (h + 1) * depth] = nn(
            kt_ref[h * depth : (h + 1) * depth], grad_score
        ).astype(BF)
        return nn(grad_score, jnp.where(across == h, q, jnp.zeros_like(q)))

    dk = jnp.zeros(k.shape, F32)
    coming, waiting = begin_head(0), None
    for h in range(HEADS):
        score, grad, grad_prob = coming
        if h + 1 < HEADS:
            coming = begin_head(h + 1)
        if waiting is not None:
            dk += finish(*waiting)
        prob = jnp.exp2(score * score_unit - lse_ref[h : h + 1])
        grad_score = (prob * (grad_prob - dot_ref[h : h + 1])).astype(BF)
        waiting = (h, grad, prob.astype(BF), grad_score)
    dk += finish(*waiting)
    dkv_ref[item, :, :qk] = (dk * score_scale).astype(BF)
    dkv_ref[item, :, qk:] = dvt_ref[...].T


def attend_back(
    item, where, q, qt, k, kt, v, gatt, lse, dot, score_unit, score_scale, before, deps
):
    items, lat, qk = q.shape
    count, wide = v.shape
    ins = [(a, None) for a in (q, qt, k, kt, v, gatt, lse, dot)]
    alias = {}
    for spot, array in enumerate(before):
        alias[len(ins)] = spot
        ins.append((array, None))
    return launch(
        functools.partial(attend_back_kernel, item, score_unit, score_scale),
        "attend_back",
        3.8 if item + 1 < items else SHORT,
        where,
        ins,
        [
            ((items, qk, lat), BF, None),
            ((items, count, qk + wide), BF, None),
        ],
        scratch=[pltpu.VMEM((wide, count), BF)],
        alias=alias,
        deps=deps,
    )


def byte_weights_kernel(bits, where, *refs):
    xn_refs, (dkv_ref, keep_ref, send_ref, all_ref) = refs[:-4], refs[-4:]
    total = 0.0
    for i, ref in enumerate(xn_refs):
        total += tn(ref[...], dkv_ref[i])
    all_ref[...] = total
    count, rows, wide = keep_ref.shape
    mine = where[2] * 2 + where[1]
    for j in range(count):
        spot = (mine ^ flipped(j, bits)) * CORES
        keep = pl.multiple_of((spot + where[0]) * rows, 8)
        send = pl.multiple_of((spot + 1 - where[0]) * rows, 8)
        keep_ref[j] = all_ref[pl.ds(keep, rows)].astype(BF)
        send_ref[j] = all_ref[pl.ds(send, rows)].astype(BF)


def byte_weights(where, xn, dkv, bits, deps):
    width, wide = xn[0].shape[1], dkv.shape[2]
    count = 2 ** len(bits)
    rows = width // (count * CORES)
    return launch(
        functools.partial(byte_weights_kernel, bits),
        "byte_weights",
        SHORT,
        where,
        [(a, None) for a in xn] + [(dkv, None)],
        [
            ((count, rows, wide), BF, None),
            ((count, rows, wide), BF, None),
        ],
        scratch=[pltpu.VMEM((width, wide), F32)],
        deps=deps,
    )


def bytes_back_kernel(
    where, own_ref, far_ref, table_ref, gain_ref, wk_ref, wv_ref, dkv_ref, gown_ref, gfar_ref,
    small_ref,
):
    items, count = far_ref.shape[:2]
    qk = wk_ref.shape[1]
    langs = table_ref.shape[0]
    gain = gain_ref[...]
    at = lax.broadcasted_iota(jnp.int32, small_ref.shape, 0)
    small = jnp.zeros(small_ref.shape, F32)
    for i in range(items):
        language = where[LANG_AT + i]
        row = language_row(table_ref, language)
        grads = nt(dkv_ref[i, :, :qk], wk_ref[...]) + nt(dkv_ref[i, :, qk:], wv_ref[...])
        gain_sum = jnp.zeros_like(row)
        byte_sum = jnp.zeros_like(row)
        for part, rows, out in (
            (0, own_ref[where[0] * items + i], gown_ref),
            (1, far_ref[i], gfar_ref),
        ):
            unit, inverse = standardise(rows.astype(F32) + row)
            grad = grads[part * count : (part + 1) * count]
            gain_sum += jnp.sum(grad * unit, 0, keepdims=True)
            back = standardise_back(unit, inverse, grad * gain)
            byte_sum += jnp.sum(back, 0, keepdims=True)
            out[i] = back.astype(out.dtype)
        small += jnp.where(at == language, byte_sum, 0.0) + jnp.where(at == langs, gain_sum, 0.0)
    small_ref[...] = small


def bytes_back(where, own, far, table, gain, w_key, w_value, dkv, deps):
    return launch(
        bytes_back_kernel,
        "bytes_back",
        SHORT,
        where,
        [(a, None) for a in (own, far, table, gain, w_key, w_value, dkv)],
        [
            (far.shape, F32, None),
            (far.shape, BF, None),
            ((table.shape[0] + 8, far.shape[2]), F32, None),
        ],
        deps=deps,
    )


def latents_back_kernel(
    score_scale, chips, bits, where, da_ref, db_ref, *refs
):
    items = da_ref.shape[0]
    gres_refs, gmlp_refs, refs = refs[:items], refs[items : 2 * items], refs[2 * items :]
    gfar_ref, small_ref, lat_ref, gain_ref, wq_ref = refs[:5]
    glat_ref, keep_ref, send_ref, own_ref = refs[5:9]
    lhs_ref, rhs_ref, turn_ref = refs[9:]
    lat = lat_ref.shape[1]
    gain = gain_ref[...]
    gain_sum = jnp.zeros_like(gain)
    half = keep_ref.shape[1]
    for i in range(items):
        total = (da_ref[i].astype(F32) + db_ref[i].astype(F32)) * score_scale
        grad = total.T.astype(BF)
        rhs_ref[i * lat : (i + 1) * lat] = grad
        unit, inverse = standardise(lat_ref[where[0] * items + i].astype(F32))
        turn_ref[i] = (unit * gain).astype(BF).T
        gln = nt(grad, wq_ref[...])
        gain_sum += jnp.sum(gln * unit, 0, keepdims=True)
        out = gres_refs[i][...] + standardise_back(unit, inverse, gln * gain)
        glat_ref[i, :, : out.shape[1]] = out.astype(BF)
        glat_ref[i, :, out.shape[1] :] = gfar_ref[i]
    gmlp = functools.reduce(jnp.add, [r[...] for r in gmlp_refs])
    wide = own_ref.shape[1]
    at = lax.broadcasted_iota(jnp.int32, (8, wide), 0)
    own = jnp.concatenate(
        [
            jnp.where(at == 1, gain_sum[:, g : g + wide], 0.0)
            + jnp.where(at == 2, gmlp[:, g : g + wide], 0.0)
            for g in range(0, gain.shape[1], wide)
        ],
        0,
    )
    own_ref[...] = own
    count = keep_ref.shape[0]
    send_ref[count] = own.astype(BF)
    tall = [small_ref[:, g : g + wide] for g in range(0, small_ref.shape[1], wide)]
    rest = (send_ref.shape[0] - count - 1) * half - len(tall) * small_ref.shape[0]
    tall = jnp.concatenate(tall + [jnp.zeros((rest, wide), F32)], 0)
    for j in range(count + 1, send_ref.shape[0]):
        send_ref[j] = tall[(j - count - 1) * half : (j - count) * half].astype(BF)
    for i in range(items):
        pick_rows(where, turn_ref.at[i], lhs_ref, i * lat, 2 * half, chips, bits)
    total = nn(lhs_ref[...], rhs_ref[...])
    for j in range(keep_ref.shape[0]):
        low = total[2 * j * half : (2 * j + 1) * half]
        high = total[(2 * j + 1) * half : (2 * j + 2) * half]
        keep_ref[j] = jnp.where(where[0] == 0, low, high).astype(BF)
        send_ref[j] = jnp.where(where[0] == 0, high, low).astype(BF)


def latents_back(where, da, db, gres, gmlps, gfar, small, latents, gain, w_query, score_scale, chips, bits, deps):
    _, lat, width = latents.shape
    items = da.shape[0]
    qk = w_query.shape[1]
    count = 2 ** len(bits)
    half = width // (count * chips * CORES)
    small_blocks = -(-small.size // (half * qk))
    return launch(
        functools.partial(latents_back_kernel, score_scale, chips, bits),
        "latents_back",
        SHORT,
        where,
        [(da, None), (db, None)]
        + [(g, None) for g in gres + gmlps]
        + [(a, None) for a in (gfar, small, latents, gain, w_query)],
        [
            ((items, lat, width + gfar.shape[2]), BF, None),
            ((count, half, qk), BF, None),
            ((count + 1 + small_blocks, half, qk), BF, None),
            ((half, qk), F32, None),
        ],
        scratch=[
            pltpu.VMEM((width // chips, items * lat), BF),
            pltpu.VMEM((items * lat, qk), BF),
            pltpu.VMEM((items, width, lat), BF),
        ],
        deps=deps,
    )


def fold_kernel(where, keep_ref, far_ref, *outs):
    half = keep_ref.shape[0] // 2
    if len(outs) == 1:
        outs[0][...] = keep_ref[0].astype(F32) + far_ref[0].astype(F32)
        return
    for spot, out in enumerate(outs):
        for j in range(half):
            at = spot * half + j
            out[j] = (keep_ref[at].astype(F32) + far_ref[at].astype(F32)).astype(BF)


def fold(where, keep, far, deps, micros=SHORT):
    if keep.shape[0] == 1:
        outs = [(keep.shape[1:], F32, None)]
    else:
        shape = (keep.shape[0] // 2,) + keep.shape[1:]
        outs = [(shape, BF, None), (shape, BF, None)]
    return launch(fold_kernel, "fold", micros, where, [(keep, None), (far, None)], outs, deps=deps)


def side_kernel(begin, where, far_ref, small_ref, own_ref, send_ref):
    rows, width = small_ref.shape
    tall = jnp.concatenate([far_ref[j].astype(F32) for j in range(begin, far_ref.shape[0])], 0)
    pieces = [tall[rows * g : rows * (g + 1)] for g in range(width // far_ref.shape[2])]
    own = small_ref[...] + jnp.concatenate(pieces, 1)
    own_ref[...] = own
    send_ref[...] = own.astype(BF)


def side_sum(where, far, small, begin, deps):
    return launch(
        functools.partial(side_kernel, begin),
        "side_sum",
        1,
        where,
        [(far, None), (small, None)],
        [(small.shape, F32, None), (small.shape, BF, None)],
        deps=deps,
    )


def join_kernel(
    langs, chips, bits, where, keep_ref, far_ref, own_ref, side_ref, qkeep_ref, qfar_ref, qown_ref,
    keep_out, send_out,
):
    count, rows, wide = keep_ref.shape
    qrows, qwide = qown_ref.shape

    def across(tall):
        return jnp.concatenate([tall[r : r + 8] for r in range(0, qrows, 8)], 1)

    own = own_ref[...] + side_ref[...].astype(F32)
    gains = across(qown_ref[...] + qfar_ref[count].astype(F32))
    at = lax.broadcasted_iota(jnp.int32, (8, qwide), 1)
    half = count // 2
    for j in range(count):
        spot = where[2] ^ flipped(j, bits)
        device = (spot * chips + where[1]) * CORES + where[0]
        byte_cut = pltpu.roll(own, own.shape[1] - device * rows, 1)[:, :qwide]
        lat_cut = pltpu.roll(gains, gains.shape[1] - device * qrows, 1)[:, :qwide]
        spare = jnp.where(at < rows, byte_cut[:8], 0.0)
        for n in range(1, langs // 8 + 1):
            piece = jnp.where(at < rows, byte_cut[8 * n : 8 * n + 8], 0.0)
            spare += pltpu.roll(piece, n * rows, 1)
        spare += pltpu.roll(jnp.where(at < qrows, lat_cut, 0.0), (langs // 8 + 1) * rows, 1)
        byte = keep_ref[j].astype(F32) + far_ref[j].astype(F32)
        query = across(qkeep_ref[j].astype(F32) + qfar_ref[j].astype(F32))
        out = keep_out if j < half else send_out
        below = jnp.concatenate([query, spare], 1)
        out[j % half] = jnp.concatenate([byte, below], 0).astype(BF)


def join(where, keep, far, own, side, qkeep, qfar, qown, langs, chips, bits, deps):
    count, rows, wide = keep.shape
    shape = (count // 2, rows + 8, wide)
    return launch(
        functools.partial(join_kernel, langs, chips, bits),
        "join",
        LONG,
        where,
        [(a, None) for a in (keep, far, own, side, qkeep, qfar, qown)],
        [(shape, BF, None), (shape, BF, None)],
        deps=deps,
    )


def part_kernel(
    where, keep_ref, far_ref, key_ref, value_ref, query_ref, lang_ref, gin_ref, glat_ref, gmlp_ref
):
    total = keep_ref[0].astype(F32) + far_ref[0].astype(F32)
    rows, qk = key_ref.shape
    qrows, langs = query_ref.shape[0], lang_ref.shape[0]
    key_ref[...] = total[:rows, :qk]
    value_ref[...] = total[:rows, qk:]
    for r in range(0, qrows, 8):
        query_ref[r : r + 8] = total[rows:, r // 8 * qk : (r // 8 + 1) * qk]
    spare = total[rows:, qrows // 8 * qk : (qrows // 8 + 1) * qk]
    groups = langs // 8
    for n in range(groups):
        lang_ref[8 * n : 8 * n + 8] = spare[:, n * rows : (n + 1) * rows]
    gin_ref[...] = spare[:1, groups * rows : (groups + 1) * rows]
    begin = (groups + 1) * rows
    glat_ref[...] = spare[1:2, begin : begin + qrows]
    gmlp_ref[...] = spare[2:3, begin : begin + qrows]


def part(where, keep, far, qk, qrows, langs, deps):
    rows, wide = keep.shape[1] - 8, keep.shape[2]
    shapes = [(rows, qk), (rows, wide - qk), (qrows, qk), (langs, rows)]
    shapes += [(1, rows), (1, qrows), (1, qrows)]
    return launch(
        part_kernel,
        "part",
        SHORT,
        where,
        [(keep, None), (far, None)],
        [(shape, F32, None) for shape in shapes],
        deps=deps,
    )


def last_kernel(where, keep_a, far_a, keep_b, far_b, up_ref, down_ref, out_ref):
    wide = up_ref.shape[1]
    split = out_ref.shape[1] // 2
    first = keep_a[0].astype(F32) + far_a[0].astype(F32)
    second = keep_b[0].astype(F32) + far_b[0].astype(F32)
    up_ref[...] = first[:, :wide]
    down_ref[...] = second[:, :wide]
    out_ref[:, :split] = first[:, wide:]
    out_ref[:, split:] = second[:, wide:]


def last(where, keep_a, far_a, keep_b, far_b, width, deps):
    shape = (keep_a.shape[1], width)
    return launch(
        last_kernel,
        "last",
        SHORT,
        where,
        [(a, None) for a in (keep_a, far_a, keep_b, far_b)],
        [(shape, F32, None)] * 3,
        deps=deps,
    )


def place_kernel(columns, where, *refs):
    count = len(columns)
    items = pl.num_programs(0) // 2
    ours = pl.program_id(0) // items == where[0]
    for n, (left, right) in enumerate(columns):
        out = refs[2 * count + n]
        wide = out.shape[2]
        own = refs[n][:, :, left : left + wide].astype(out.dtype)
        far = refs[count + n][:, :, right : right + wide].astype(out.dtype)
        out[...] = jnp.where(ours, own, far)
    refs[-1][...] = jnp.zeros_like(refs[-1])


def place(where, pairs, deps):
    items = pairs[0][0].shape[0]
    one = lambda a: (1,) + a.shape[1:]
    rows = lambda p: p[0].shape[1]
    outs = [
        ((2 * items, rows(p), p[4]), p[5], block((1, rows(p), p[4]), lambda g, w: g))
        for p in pairs
    ]
    return launch(
        functools.partial(place_kernel, [(p[1], p[3]) for p in pairs]),
        "place",
        LONG,
        where,
        [(a, block(one(a), lambda g, w: g % items)) for a in [p[0] for p in pairs]]
        + [(a, block(one(a), lambda g, w: g % items)) for a in [p[2] for p in pairs]],
        outs + [((8, 128), F32, None)],
        deps=deps,
        grid=2 * items,
        far=True,
    )


def swap(value, axis, bit):
    size = lax.axis_size(axis)
    return lax.ppermute(value, axis, [(i, i ^ bit) for i in range(size)])


def bits_of(size):
    return [2**t for t in range(size.bit_length() - 1)]


def halve(value, dim, axis, bit):
    mine = (lax.axis_index(axis) // bit) % 2
    keep = lax.dynamic_index_in_dim(value, mine, dim, keepdims=False)
    send = lax.dynamic_index_in_dim(value, 1 - mine, dim, keepdims=False)
    return (keep.astype(F32) + swap(send, axis, bit).astype(F32)).astype(BF)


def scatter_rows(value):
    spots, chips = lax.axis_size("batch"), lax.axis_size("seq") // CORES
    rows = value.shape[0] // (spots * chips * CORES)
    blocks = value.astype(BF).reshape(spots, chips, CORES, rows, value.shape[1])
    blocks = halve(blocks, 2, "seq", 1)
    for bit in bits_of(chips):
        rest = blocks.shape[2:]
        blocks = blocks.reshape((spots, blocks.shape[1] // 2, 2) + rest)
        blocks = halve(blocks, 2, "seq", CORES * bit)
    blocks = blocks[:, 0]
    for bit in bits_of(spots):
        blocks = blocks.reshape((blocks.shape[0] // 2, 2) + blocks.shape[1:])
        blocks = halve(blocks, 1, "batch", bit)
    return blocks[0].astype(F32)


def everywhere(value):
    for axis in ("seq", "batch"):
        for bit in bits_of(lax.axis_size(axis)):
            value = value + swap(value, axis, bit)
    return value


def merge(oa, ob):
    rows = oa.shape[0] - 2 * HEADS
    wide = rows // HEADS
    la = oa[rows : rows + HEADS].astype(F32) + oa[rows + HEADS :].astype(F32)
    lb = ob[rows : rows + HEADS].astype(F32) + ob[rows + HEADS :].astype(F32)
    top = jnp.maximum(la, lb)
    ea, eb = jnp.exp2(la - top), jnp.exp2(lb - top)
    total = ea + eb
    lse = top + jnp.log2(total)
    out = oa[:rows].astype(F32) * jnp.repeat(ea / total, wide, 0)
    out = out + ob[:rows].astype(F32) * jnp.repeat(eb / total, wide, 0)
    high = lse.astype(BF)
    return jnp.concatenate([out.astype(BF), high, (lse - high.astype(F32)).astype(BF)], 0)


LANG_AT = 3


def local(
    byte_inputs,
    language,
    lang_table,
    latents,
    gain_in,
    gain_lat,
    gain_mlp,
    w_query,
    w_key,
    w_value,
    w_out,
    w_up,
    w_down,
    cotangent,
):
    items = byte_inputs.shape[0] // CORES
    width_in, width_lat = byte_inputs.shape[2], latents.shape[2]
    lat, qk = latents.shape[1], w_query.shape[1]
    langs = lang_table.shape[0]
    score_scale = 1.0 / math.sqrt(qk // HEADS)
    score_unit = score_scale * math.log2(math.e)
    spots, chips = lax.axis_size("batch"), lax.axis_size("seq") // CORES
    devices = spots * chips * CORES
    seq_at, spot = lax.axis_index("seq"), lax.axis_index("batch")
    core, side = seq_at % CORES, seq_at // CORES
    device = spot * (chips * CORES) + seq_at
    chip_bits, spot_bits = bits_of(chips), bits_of(spots)
    rows_in, rows_lat = width_in // devices, width_lat // devices
    direct = (
        chips == 2
        and rows_in == langs + 8
        and rows_lat * qk == 8 * width_lat
        and width_lat % qk == 0
        and langs % 8 == 0
        and byte_inputs.shape[1] == lat
    )
    own_languages = lax.dynamic_slice_in_dim(language, core * items, items, 0)
    where = jnp.concatenate([jnp.stack([core, side, spot]).astype(jnp.int32), own_languages])
    last_bit = chip_bits[-1]
    order = where.at[1].set(side // last_bit % 2)
    table = lang_table.astype(F32)
    gain_in, gain_lat, gain_mlp = gain_in[None], gain_lat[None], gain_mlp[None]

    send = lax.dynamic_slice_in_dim(byte_inputs, (1 - core) * items, items, 0)
    far = swap(send, "seq", 1)
    q, qt = queries(where, latents, gain_lat, w_query, items)

    xns, kept, pairs, token = [], [], [], ()
    for item in range(items):
        ot, xn, k, kt, v = attend(
            item, items, where, byte_inputs, far, table, gain_in, w_key, w_value, qt, score_unit,
            token,
        )
        xns.append(xn)
        kept.append((k, kt, v))
        token = (k,)
        for bit in chip_bits[:-1]:
            ot = merge(ot, swap(ot, "seq", CORES * bit))
        pairs.append((ot, swap(ot, "seq", CORES * last_bit)))

    gact = act_back(where, cotangent, w_down, items, token)
    token = (gact,)
    sides, outs, dqkv = [], None, ()

    def back(item, deps):
        gatt, dot, lse = sides[item][2:5]
        return attend_back(
            item, where, q, qt, *kept[item], gatt, lse, dot, score_unit, score_scale, dqkv, deps
        )

    for item in range(items):
        if item:
            dqkv = back(item - 1, token)
            token = (dqkv[0],)
        side_out = latent_side(
            item, items, order if chips > 2 else where, *pairs[item], latents, cotangent,
            gact, gain_mlp, w_out, w_up, w_down, outs, token,
        )
        outs = side_out[0]
        sides.append(side_out)
        token = (side_out[3],)
    outs_far = swap(outs, "seq", 1)

    pick = lambda at: [s[at] for s in sides]
    down = (pick(7), [cotangent] * items)
    up = (pick(6), pick(8))
    out = (pick(5), pick(9))

    if direct:
        y_bit, z_bit, far_bit = spot_bits
        a_bits, b_bits = [y_bit, z_bit, far_bit], [z_bit, far_bit, y_bit]
        c_bits = [1] + [2 * b for b in a_bits]
        split = width_lat // 2
        keep_a, send_a = latent_weights(
            where, [up, out], [(0, width_lat), (0, split)], chips, a_bits, "weights_a", token
        )
        far_a = swap(send_a, "seq", 1)
        keep_b, send_b = latent_weights(
            where, [down, out], [(0, width_lat), (split, split)], chips, b_bits, "weights_b",
            (keep_a,),
        )
        far_b = swap(send_b, "seq", 1)
        dqt, dkv = back(items - 1, (keep_b,))
        dqt_far = swap(dqt, "seq", CORES)
        keep_a, send_a = fold(where, keep_a, far_a, (dqt, outs_far))
        far_a = swap(send_a, "batch", a_bits[0])
        keep_b, send_b = fold(where, keep_b, far_b, (keep_a,))
        far_b = swap(send_b, "batch", b_bits[0])
        keep_c, send_c = byte_weights(where, xns, dkv, c_bits, (keep_b,))
        far_c = swap(send_c, "seq", 1)
        gown, gfar, small = bytes_back(
            where, byte_inputs, far, table, gain_in, w_key, w_value, dkv, (keep_c,)
        )
        keep_c, send_c = fold(where, keep_c, far_c, (small,))
        far_c = swap(send_c, "seq", CORES)
        glats, keep_q, send_q, own_q = latents_back(
            where, dqt, dqt_far, pick(1), pick(10), gfar, small, latents, gain_lat, w_query,
            score_scale, chips, a_bits, (keep_c,),
        )
        glats_far = swap(glats, "seq", 1)
        far_q = swap(send_q, "seq", 1)
        own_s, send_s = side_sum(where, far_q, small, keep_q.shape[0] + 1, ())
        far_s = swap(send_s, "seq", CORES)
        keep_b, send_b = fold(where, keep_b, far_b, (own_s,))
        far_b = swap(send_b, "batch", b_bits[1])
        keep_a, send_a = fold(where, keep_a, far_a, (keep_b,))
        far_a = swap(send_a, "batch", a_bits[1])
        keep_c, send_c = join(
            where, keep_c, far_c, own_s, far_s, keep_q, far_q, own_q, langs, chips, a_bits,
            (keep_a,),
        )
        far_c = swap(send_c, "batch", a_bits[0])
        latents_out, grad_bytes, token = place(
            where,
            [
                (outs, 0, outs_far, 0, width_lat, BF),
                (gown, 0, glats_far, width_lat, width_in, F32),
            ],
            (keep_c,),
        )
        keep_b, send_b = fold(where, keep_b, far_b, (token,))
        far_b = swap(send_b, "batch", b_bits[2])
        keep_a, send_a = fold(where, keep_a, far_a, (keep_b,))
        far_a = swap(send_a, "batch", a_bits[2])
        keep_c, send_c = fold(where, keep_c, far_c, (keep_a,))
        far_c = swap(send_c, "batch", a_bits[1])
        grad_latents, token = place(
            where, [(glats, 0, glats_far, 0, width_lat, F32)], (keep_c,)
        )
        keep_c, send_c = fold(where, keep_c, far_c, (token,))
        far_c = swap(send_c, "batch", a_bits[2])
        g_up, g_down, g_out = last(where, keep_a, far_a, keep_b, far_b, width_lat, (keep_c,))
        g_key, g_value, g_query, g_table, *gains = part(
            where, keep_c, far_c, qk, rows_lat, langs, ()
        )
        g_in, g_lat, g_mlp = [g[0] for g in gains]
    else:
        dqt, dkv = back(items - 1, token)
        for bit in chip_bits:
            dqt = (dqt.astype(F32) + swap(dqt, "seq", CORES * bit).astype(F32)).astype(BF)
        gown, gfar, small = bytes_back(
            where, byte_inputs, far, table, gain_in, w_key, w_value, dkv, ()
        )
        gfar_far = swap(gfar, "seq", 1)
        own_cut = lambda a: lax.dynamic_slice_in_dim(a, core * items, items, 0)
        grad_q = (dqt.astype(F32) * score_scale).swapaxes(1, 2).astype(BF)
        unit, inverse = standardise(own_cut(latents).astype(F32))
        gln = lax.dot_general(
            grad_q, w_query, (((2,), (1,)), ((), ())), preferred_element_type=F32
        )
        glats = jnp.stack(pick(1)) + standardise_back(unit, inverse, gln * gain_lat)
        glats = glats.astype(BF)
        glats_far = swap(glats, "seq", 1)
        flat = lambda a: a.reshape(-1, a.shape[-1])
        share = 1.0 / chips
        g_query = scatter_rows(tn(flat((unit * gain_lat).astype(BF)), flat(grad_q)) * share)
        rows = lambda lefts, rights: scatter_rows(
            sum(nn(x, y) for x, y in zip(lefts, rights)) * share
        )
        g_down = rows(pick(7), own_cut(cotangent))
        g_up, g_out = rows(pick(6), pick(8)), rows(pick(5), pick(9))
        g_bytes = scatter_rows(sum(tn(xns[i], dkv[i]) for i in range(items)))
        g_key, g_value = g_bytes[:, :qk], g_bytes[:, qk:]
        pad = ((0, 0), (0, width_lat - width_in))
        small = jnp.concatenate(
            [
                jnp.pad(small[: langs + 1], pad),
                jnp.sum(gln * unit, (0, 1))[None] * share,
                sum(pick(10)) * share,
            ],
            0,
        )
        small = everywhere(small)
        cut = lambda rows, count: lax.dynamic_slice_in_dim(rows, device * count, count, 1)
        g_table, g_in = cut(small[:langs], rows_in), cut(small[langs : langs + 1], rows_in)[0]
        g_lat, g_mlp = cut(small[langs + 1 :], rows_lat)
        latents_out, grad_bytes, grad_latents, _ = place(
            where,
            [
                (outs, 0, outs_far, 0, width_lat, BF),
                (gown, 0, gfar_far, 0, width_in, F32),
                (glats, 0, glats_far, 0, width_lat, F32),
            ],
            (),
        )

    return (
        latents_out,
        grad_latents,
        grad_bytes,
        g_table,
        g_in,
        g_lat,
        g_mlp,
        g_query,
        g_key,
        g_value,
        g_out,
        g_up,
        g_down,
    )


def solution(mesh):
    return jax.shard_map(
        local,
        mesh=mesh,
        in_specs=(
            P("batch", "seq", None),
            P("batch"),
            P(),
            P("batch", None, None),
            P(),
            P(),
            P(),
            P(),
            P(),
            P(),
            P(),
            P(),
            P(),
            P("batch", None, None),
        ),
        out_specs=(
            P("batch", None, None),
            P("batch", None, None),
            P("batch", "seq", None),
            P(None, ("batch", "seq")),
            P(("batch", "seq")),
            P(("batch", "seq")),
            P(("batch", "seq")),
            P(("batch", "seq"), None),
            P(("batch", "seq"), None),
            P(("batch", "seq"), None),
            P(("batch", "seq"), None),
            P(("batch", "seq"), None),
            P(("batch", "seq"), None),
        ),
        check_vma=False,
    )
```

```python
import functools
import math

import jax
import jax.numpy as jnp
from jax import lax
from jax.experimental import pallas as pl
from jax.experimental.pallas import tpu as pltpu
from jax.sharding import PartitionSpec as P

HEADS = 8
CORES = 2
EPS = 1e-05
F32 = jnp.float32
BF = jnp.bfloat16
VMEM_LIMIT = 12 * 1024 * 1024
PEAK = 1.15e9
SHORT, LONG, AHEAD = 0.001, 40, 3


def nn(a, b):
    return lax.dot_general(a, b, (((1,), (0,)), ((), ())), preferred_element_type=F32)


def nt(a, b):
    return lax.dot_general(a, b, (((1,), (1,)), ((), ())), preferred_element_type=F32)


def tn(a, b):
    return lax.dot_general(a, b, (((0,), (0,)), ((), ())), preferred_element_type=F32)


def standardise(x):
    centre = x - jnp.mean(x, -1, keepdims=True)
    inverse = lax.rsqrt(jnp.mean(centre * centre, -1, keepdims=True) + EPS)
    return centre * inverse, inverse


def standardise_back(unit, inverse, grad):
    return inverse * (
        grad - jnp.mean(grad, -1, keepdims=True) - unit * jnp.mean(grad * unit, -1, keepdims=True)
    )


def block(shape, at):
    return pl.BlockSpec(shape, lambda g: (at(g),) + (0,) * (len(shape) - 1))


ANY = pl.BlockSpec(memory_space=pl.ANY)
FAST = pl.BlockSpec(memory_space=pltpu.VMEM)
FAR = pl.BlockSpec(memory_space=pltpu.HBM)
SCALARS = pl.BlockSpec(memory_space=pltpu.SMEM)


def launch(body, name, micros, ins, outs, scratch=(), deps=(), alias=None, grid=1, far=False):
    count, extra = len(ins), len(deps)
    ins = [
        (pltpu.with_memory_space_constraint(a, pltpu.HBM) if s is FAR else a, s) for a, s in ins
    ]

    def kernel(*refs):
        body(Where(), *refs[:count], *refs[count + extra :])

    return pl.pallas_call(
        kernel,
        grid=(grid,),
        in_specs=[FAST if s is None else s for _, s in ins] + [ANY] * extra,
        out_specs=[FAST if s is None else s for _, _, s in outs],
        scratch_shapes=list(scratch),
        out_shape=[
            (jax.ShapeDtypeStruct if s is None or not far else pltpu.HBM)(shape, dtype)
            for shape, dtype, s in outs
        ],
        input_output_aliases=alias or {},
        compiler_params=pltpu.CompilerParams(vmem_limit_bytes=VMEM_LIMIT),
        cost_estimate=pl.CostEstimate(
            flops=int(micros * PEAK), bytes_accessed=1, transcendentals=0
        ),
        name=name,
    )(*[a for a, _ in ins], *deps)


class Where:
    def __getitem__(self, at):
        if at == 2:
            return lax.axis_index("batch")
        return (lax.rem, lax.div)[at](lax.axis_index("seq"), CORES)


def pick_kernel(where, own_ref, out_ref, arrived):
    items = out_ref.shape[0]
    copy = pltpu.make_async_copy(
        own_ref.at[pl.ds((1 - where[0]) * items, items)], out_ref, arrived
    )
    copy.start()
    copy.wait()


def pick_bytes(own, items):
    return launch(
        pick_kernel,
        "pick_bytes",
        AHEAD,
        [(own, FAR)],
        [((items,) + own.shape[1:], BF, None)],
        scratch=[pltpu.SemaphoreType.DMA(())],
    )[0]


def query_kernel(where, lat_ref, gain_ref, wq_ref, *outs):
    items = len(outs) // 2
    for i in range(items):
        unit, _ = standardise(lat_ref[where[0] * items + i].astype(F32))
        rows = nn((unit * gain_ref[...]).astype(BF), wq_ref[...])
        outs[2 * i][...] = rows.astype(BF)
        outs[2 * i + 1][...] = rows.T.astype(BF)


def queries(items, latents, gain, w_query, deps):
    _, count, width = latents.shape
    qk = w_query.shape[1]
    return launch(
        query_kernel,
        "queries",
        2,
        [(latents, None), (gain, None), (w_query, None)],
        [((count, qk), BF, None), ((qk, count), BF, None)] * items,
        deps=deps,
    )


SPAN = 256


def head_span(h, wide):
    begin = h * wide // 128 * 128
    return begin, h * wide - begin


def language_row(table_ref, language):
    at = lax.broadcasted_iota(jnp.int32, table_ref.shape, 0)
    table = table_ref[...].astype(F32)
    return jnp.sum(jnp.where(at == language, table, 0.0), 0, keepdims=True)


def attend_kernel(
    item, items, score_unit, where, lang_ref, own_ref, far_ref, table_ref, gain_ref, wk_ref, wv_ref, qt_ref,
    ot_ref, xn_ref, k_ref, kt_ref, v_ref,
):
    at = where[0] * items + item
    count = far_ref.shape[1]
    row = language_row(table_ref, lang_ref[at])
    gain = gain_ref[...]
    for part, rows in enumerate((own_ref[at], far_ref[item])):
        unit, _ = standardise(rows.astype(F32) + row)
        xn_ref[part * count : (part + 1) * count] = (unit * gain).astype(BF)
    xn = xn_ref[...]
    k = nn(xn, wk_ref[...]).astype(BF)
    k_ref[...] = k
    kt_ref[...] = k.T
    v = nn(xn, wv_ref[...]).astype(BF)
    v_ref[...] = v
    qt = qt_ref[...]
    depth = qt.shape[0] // HEADS
    wide = v.shape[1] // HEADS
    at = lax.broadcasted_iota(jnp.int32, qt.shape, 0) // depth

    def score_of(h):
        return nn(k, jnp.where(at == h, qt, jnp.zeros_like(qt)))

    def finish(h, weight, total):
        begin, ahead = head_span(h, wide)
        out = tn(v[:, begin : begin + SPAN], weight)[ahead : ahead + wide]
        ot_ref[h * wide : (h + 1) * wide] = (out * (1.0 / total)).astype(BF)

    lse = []
    coming, waiting = score_of(0), None
    for h in range(HEADS):
        score = coming * score_unit
        if h + 1 < HEADS:
            coming = score_of(h + 1)
        if waiting is not None:
            finish(*waiting)
        top = jnp.max(score, 0, keepdims=True)
        weight = jnp.exp2(score - top)
        total = jnp.sum(weight, 0, keepdims=True)
        lse.append(top + jnp.log2(total))
        waiting = (h, weight.astype(BF), total)
    finish(*waiting)
    lse = jnp.concatenate(lse, 0)
    high = lse.astype(BF)
    low = (lse - high.astype(F32)).astype(BF)
    ot_ref[HEADS * wide :] = jnp.concatenate([high, low], 0)


def attend(
    item, items, language, own, far, table, gain, w_key, w_value, qt, score_unit, deps
):
    _, count, width = own.shape
    qk, lat = w_key.shape[1], qt.shape[1]
    wide = w_value.shape[1]
    return launch(
        functools.partial(attend_kernel, item, items, score_unit),
        "attend",
        3.8,
        [(language, SCALARS)]
        + [(a, None) for a in (own, far, table, gain, w_key, w_value, qt)],
        [
            ((wide + 2 * HEADS, lat), BF, None),
            ((2 * count, width), BF, None),
            ((2 * count, qk), BF, None),
            ((qk, 2 * count), BF, None),
            ((2 * count, wide), BF, None),
        ],
        deps=deps,
    )


def act_back_kernel(where, cot_ref, wd_ref, gact_ref):
    items = gact_ref.shape[0]
    for i in range(items):
        gact_ref[i] = nt(cot_ref[where[0] * items + i], wd_ref[...])


def act_back(cot, w_down, items, deps):
    return launch(
        act_back_kernel,
        "act_back",
        2.5,
        [(cot, None), (w_down, None)],
        [((items, cot.shape[1], w_down.shape[0]), F32, None)],
        deps=deps,
    )[0]


GELU_A = math.sqrt(2.0 / math.pi)
GELU_B = 0.044715


def latent_kernel(
    item, items, bit, where, oa_ref, ob_ref, lat_ref, cot_ref, gact_ref, gain_ref, wo_ref, wu_ref, wd_ref,
    *refs,
):
    (
        outs_ref, gres_ref, gatt_ref, dot_ref, lse_ref, att_ref, hid_ref, act_ref, gpre_ref,
        glow_ref, ggain_ref,
    ) = refs[-11:]
    at = where[0] * items + item
    first = lax.rem(lax.div(where[1], bit), 2) == 0
    rows = gatt_ref.shape[0]
    wide = rows // HEADS
    ours = oa_ref[rows : rows + HEADS].astype(F32) + oa_ref[rows + HEADS :].astype(F32)
    theirs = ob_ref[rows : rows + HEADS].astype(F32) + ob_ref[rows + HEADS :].astype(F32)
    left = jnp.where(first, ours, theirs)
    right = jnp.where(first, theirs, ours)
    top = jnp.maximum(left, right)
    e_left, e_right = jnp.exp2(left - top), jnp.exp2(right - top)
    total = e_left + e_right
    lse_ref[...] = top + jnp.log2(total)
    scale = 1.0 / total
    e_left, e_right = e_left * scale, e_right * scale
    merged = []
    for h in range(HEADS):
        a = oa_ref[h * wide : (h + 1) * wide].astype(F32)
        b = ob_ref[h * wide : (h + 1) * wide].astype(F32)
        low, high = jnp.where(first, a, b), jnp.where(first, b, a)
        merged.append(low * e_left[h : h + 1] + high * e_right[h : h + 1])
        att_ref[h * wide : (h + 1) * wide] = merged[-1].astype(BF)
    resid = lat_ref[at].astype(F32) + tn(att_ref[...], wo_ref[...])
    unit, inverse = standardise(resid)
    gain = gain_ref[...]
    hidden = (unit * gain).astype(BF)
    hid_ref[...] = hidden.T
    pre = nn(hidden, wu_ref[...])
    square = pre * pre
    slope = jnp.tanh(GELU_A * pre * (1.0 + GELU_B * square))
    act = (0.5 * pre * (1.0 + slope)).astype(BF)
    act_ref[...] = act.T
    outs_ref[item] = (resid + nn(act, wd_ref[...])).astype(BF)
    cot = cot_ref[at]
    gelu_slope = 0.5 * (1.0 + slope) + 0.5 * pre * (1.0 - slope * slope) * GELU_A * (
        1.0 + 3.0 * GELU_B * square
    )
    gpre = (gact_ref[item] * gelu_slope).astype(BF)
    gpre_ref[...] = gpre
    ghid = nt(gpre, wu_ref[...])
    ggain_ref[...] = jnp.sum(ghid * unit, 0, keepdims=True)
    gres = cot.astype(F32) + standardise_back(unit, inverse, ghid * gain)
    gres_ref[...] = gres
    glow = gres.astype(BF)
    glow_ref[...] = glow
    gatt_ref[...] = nt(wo_ref[...], glow).astype(BF)
    for h in range(HEADS):
        dot_ref[h : h + 1] = jnp.sum(
            gatt_ref[h * wide : (h + 1) * wide].astype(F32) * merged[h], 0, keepdims=True
        )


def latent_side(
    item, items, bit, oa, ob, latents, cot, gact, gain, w_out, w_up, w_down, before, deps
):
    total, lat, width = latents.shape
    feed = w_up.shape[1]
    ins = [(a, None) for a in (oa, ob, latents, cot, gact, gain, w_out, w_up, w_down)]
    alias = {}
    if before is not None:
        alias[len(ins)] = 0
        ins.append((before, None))
    return launch(
        functools.partial(latent_kernel, item, items, bit),
        "latent_side",
        7,
        ins,
        [
            ((items, lat, width), BF, None),
            ((lat, width), F32, None),
            ((width, lat), BF, None),
            ((HEADS, lat), F32, None),
            ((HEADS, lat), F32, None),
            ((width, lat), BF, None),
            ((width, lat), BF, None),
            ((feed, lat), BF, None),
            ((lat, feed), BF, None),
            ((lat, width), BF, None),
            ((1, width), F32, None),
        ],
        alias=alias,
        deps=deps,
    )


def flipped(at, bits):
    return sum(((at >> (len(bits) - 1 - t)) & 1) * bit for t, bit in enumerate(bits))


def pick_rows(where, source, lhs_ref, lane, rows, chips, bits):
    lat = source.shape[1]
    for j in range(2 ** len(bits)):
        spot = where[2] ^ flipped(j, bits)
        begin = pl.multiple_of((spot * chips + where[1]) * rows, 16)
        lhs_ref[j * rows : (j + 1) * rows, lane : lane + lat] = source[pl.ds(begin, rows)]


def latent_weights_kernel(plan, items, chips, bits, where, *refs):
    ins, keep_ref, send_ref, lhs_ref = refs[:-3], refs[-3], refs[-2], refs[-1]
    half = keep_ref.shape[1]
    column = 0
    for w, (begin, width) in enumerate(plan):
        lefts = ins[2 * items * w : 2 * items * w + items]
        rights = ins[2 * items * w + items : 2 * items * (w + 1)]
        total = 0.0
        for i in range(items):
            lat = lefts[i].shape[1]
            pick_rows(where, lefts[i], lhs_ref, i * lat, 2 * half, chips, bits)
            right = rights[i]
            if len(right.shape) == 3:
                right = right.at[where[0] * items + i]
            total += nn(lhs_ref[:, i * lat : (i + 1) * lat], right[:, begin : begin + width])
        out = slice(column, column + width)
        for j in range(keep_ref.shape[0]):
            low = total[2 * j * half : (2 * j + 1) * half]
            high = total[(2 * j + 1) * half : (2 * j + 2) * half]
            keep_ref[j, :, out] = jnp.where(where[0] == 0, low, high).astype(BF)
            send_ref[j, :, out] = jnp.where(where[0] == 0, high, low).astype(BF)
        column += width


def latent_weights(groups, plan, chips, bits, name, deps):
    items = len(groups[0][0])
    ins = []
    for lefts, rights in groups:
        ins += [(a, None) for a in lefts + rights]
    width, lat = groups[0][0][0].shape
    count = 2 ** len(bits)
    half = width // (count * chips * CORES)
    shape = (count, half, sum(w for _, w in plan))
    return launch(
        functools.partial(latent_weights_kernel, plan, items, chips, bits),
        name,
        SHORT,
        ins,
        [(shape, BF, None), (shape, BF, None)],
        scratch=[pltpu.VMEM((width // chips, items * lat), BF)],
        deps=deps,
    )


def attend_back_kernel(
    item, score_unit, score_scale, where, q_ref, qt_ref, k_ref, kt_ref, v_ref, gatt_ref, lse_ref,
    dot_ref, *refs,
):
    dqt_ref, dkv_ref, dvt_ref = refs[-3:]
    q, qt, k = q_ref[...], qt_ref[...], k_ref[...]
    qk = qt.shape[0]
    depth = qk // HEADS
    wide = gatt_ref.shape[0] // HEADS
    lat = qt.shape[1]
    at = lax.broadcasted_iota(jnp.int32, qt.shape, 0) // depth
    across = lax.broadcasted_iota(jnp.int32, q.shape, 1) // depth

    def begin_head(h):
        score = nn(k, jnp.where(at == h, qt, jnp.zeros_like(qt)))
        grad = gatt_ref[h * wide : (h + 1) * wide]
        begin, ahead = head_span(h, wide)
        after = SPAN - ahead - wide
        pieces = [grad]
        if ahead:
            pieces = [jnp.zeros((ahead, lat), BF)] + pieces
        if after:
            pieces = pieces + [jnp.zeros((after, lat), BF)]
        return score, grad, nn(v_ref[:, begin : begin + SPAN], jnp.concatenate(pieces, 0))

    def finish(h, grad, prob, grad_score):
        dvt_ref[h * wide : (h + 1) * wide] = nt(grad, prob).astype(BF)
        dqt_ref[item, h * depth : (h + 1) * depth] = nn(
            kt_ref[h * depth : (h + 1) * depth], grad_score
        ).astype(BF)
        return nn(grad_score, jnp.where(across == h, q, jnp.zeros_like(q)))

    dk = jnp.zeros(k.shape, F32)
    coming, waiting = begin_head(0), None
    for h in range(HEADS):
        score, grad, grad_prob = coming
        if h + 1 < HEADS:
            coming = begin_head(h + 1)
        if waiting is not None:
            dk += finish(*waiting)
        prob = jnp.exp2(score * score_unit - lse_ref[h : h + 1])
        grad_score = (prob * (grad_prob - dot_ref[h : h + 1])).astype(BF)
        waiting = (h, grad, prob.astype(BF), grad_score)
    dk += finish(*waiting)
    dkv_ref[item, :, :qk] = (dk * score_scale).astype(BF)
    dkv_ref[item, :, qk:] = dvt_ref[...].T


def attend_back(
    item, items, q, qt, k, kt, v, gatt, lse, dot, score_unit, score_scale, before, deps
):
    lat, qk = q.shape
    count, wide = v.shape
    ins = [(a, None) for a in (q, qt, k, kt, v, gatt, lse, dot)]
    alias = {}
    for spot, array in enumerate(before):
        alias[len(ins)] = spot
        ins.append((array, None))
    return launch(
        functools.partial(attend_back_kernel, item, score_unit, score_scale),
        "attend_back",
        3.8 if item + 1 < items else SHORT,
        ins,
        [
            ((items, qk, lat), BF, None),
            ((items, count, qk + wide), BF, None),
        ],
        scratch=[pltpu.VMEM((wide, count), BF)],
        alias=alias,
        deps=deps,
    )


def byte_weights_kernel(bits, where, *refs):
    xn_refs, (dkv_ref, keep_ref, send_ref, all_ref) = refs[:-4], refs[-4:]
    total = 0.0
    for i, ref in enumerate(xn_refs):
        total += tn(ref[...], dkv_ref[i])
    all_ref[...] = total
    count, rows, wide = keep_ref.shape
    mine = where[2] * 2 + where[1]
    for j in range(count):
        spot = (mine ^ flipped(j, bits)) * CORES
        keep = pl.multiple_of((spot + where[0]) * rows, 8)
        send = pl.multiple_of((spot + 1 - where[0]) * rows, 8)
        keep_ref[j] = all_ref[pl.ds(keep, rows)].astype(BF)
        send_ref[j] = all_ref[pl.ds(send, rows)].astype(BF)


def byte_weights(xn, dkv, bits, deps):
    width, wide = xn[0].shape[1], dkv.shape[2]
    count = 2 ** len(bits)
    rows = width // (count * CORES)
    return launch(
        functools.partial(byte_weights_kernel, bits),
        "byte_weights",
        SHORT,
        [(a, None) for a in xn] + [(dkv, None)],
        [
            ((count, rows, wide), BF, None),
            ((count, rows, wide), BF, None),
        ],
        scratch=[pltpu.VMEM((width, wide), F32)],
        deps=deps,
    )


def bytes_back_kernel(
    item, where, lang_ref, own_ref, far_ref, table_ref, gain_ref, wk_ref, wv_ref, dkv_ref, *refs
):
    gown_ref, gfar_ref, small_ref = refs[-3:]
    items, count = gfar_ref.shape[:2]
    qk = wk_ref.shape[1]
    langs = table_ref.shape[0]
    gain = gain_ref[...]
    language = lang_ref[where[0] * items + item]
    row = language_row(table_ref, language)
    grads = nt(dkv_ref[item, :, :qk], wk_ref[...]) + nt(dkv_ref[item, :, qk:], wv_ref[...])
    gain_sum = jnp.zeros_like(row)
    byte_sum = jnp.zeros_like(row)
    for part, rows, out in (
        (0, own_ref[where[0] * items + item], gown_ref),
        (1, far_ref[item], gfar_ref),
    ):
        unit, inverse = standardise(rows.astype(F32) + row)
        grad = grads[part * count : (part + 1) * count]
        gain_sum += jnp.sum(grad * unit, 0, keepdims=True)
        back = standardise_back(unit, inverse, grad * gain)
        byte_sum += jnp.sum(back, 0, keepdims=True)
        out[item] = back.astype(out.dtype)
    at = lax.broadcasted_iota(jnp.int32, small_ref.shape, 0)
    small = jnp.where(at == language, byte_sum, 0.0) + jnp.where(at == langs, gain_sum, 0.0)
    if item:
        small += refs[2][...]
    small_ref[...] = small


def bytes_back(
    item, items, language, own, far, table, gain, w_key, w_value, dkv, before, deps
):
    shape = far.shape
    ins = [(language, SCALARS)]
    ins += [(a, None) for a in (own, far, table, gain, w_key, w_value, dkv)]
    alias = {}
    if before:
        alias = {len(ins): 0, len(ins) + 1: 1}
        ins += [(a, None) for a in before]
    return launch(
        functools.partial(bytes_back_kernel, item),
        "bytes_back",
        2.5 if item + 1 < items else SHORT,
        ins,
        [
            (shape, F32, None),
            (shape, BF, None),
            ((table.shape[0] + 8, far.shape[2]), F32, None),
        ],
        alias=alias,
        deps=deps,
    )


def latents_back_kernel(
    score_scale, chips, bits, where, da_ref, db_ref, *refs
):
    items = da_ref.shape[0]
    gres_refs, gmlp_refs, refs = refs[:items], refs[items : 2 * items], refs[2 * items :]
    gfar_ref, small_ref, lat_ref, gain_ref, wq_ref = refs[:5]
    glat_ref, keep_ref, send_ref, own_ref = refs[5:9]
    lhs_ref, rhs_ref, turn_ref = refs[9:]
    lat = lat_ref.shape[1]
    gain = gain_ref[...]
    gain_sum = jnp.zeros_like(gain)
    half = keep_ref.shape[1]
    for i in range(items):
        total = (da_ref[i].astype(F32) + db_ref[i].astype(F32)) * score_scale
        grad = total.T.astype(BF)
        rhs_ref[i * lat : (i + 1) * lat] = grad
        unit, inverse = standardise(lat_ref[where[0] * items + i].astype(F32))
        turn_ref[i] = (unit * gain).astype(BF).T
        gln = nt(grad, wq_ref[...])
        gain_sum += jnp.sum(gln * unit, 0, keepdims=True)
        out = gres_refs[i][...] + standardise_back(unit, inverse, gln * gain)
        glat_ref[i, :, : out.shape[1]] = out.astype(BF)
        glat_ref[i, :, out.shape[1] :] = gfar_ref[i]
    gmlp = functools.reduce(jnp.add, [r[...] for r in gmlp_refs])
    wide = own_ref.shape[1]
    at = lax.broadcasted_iota(jnp.int32, (8, wide), 0)
    own = jnp.concatenate(
        [
            jnp.where(at == 1, gain_sum[:, g : g + wide], 0.0)
            + jnp.where(at == 2, gmlp[:, g : g + wide], 0.0)
            for g in range(0, gain.shape[1], wide)
        ],
        0,
    )
    own_ref[...] = own
    count = keep_ref.shape[0]
    send_ref[count] = own.astype(BF)
    tall = [small_ref[:, g : g + wide] for g in range(0, small_ref.shape[1], wide)]
    rest = (send_ref.shape[0] - count - 1) * half - len(tall) * small_ref.shape[0]
    tall = jnp.concatenate(tall + [jnp.zeros((rest, wide), F32)], 0)
    for j in range(count + 1, send_ref.shape[0]):
        send_ref[j] = tall[(j - count - 1) * half : (j - count) * half].astype(BF)
    for i in range(items):
        pick_rows(where, turn_ref.at[i], lhs_ref, i * lat, 2 * half, chips, bits)
    total = nn(lhs_ref[...], rhs_ref[...])
    for j in range(keep_ref.shape[0]):
        low = total[2 * j * half : (2 * j + 1) * half]
        high = total[(2 * j + 1) * half : (2 * j + 2) * half]
        keep_ref[j] = jnp.where(where[0] == 0, low, high).astype(BF)
        send_ref[j] = jnp.where(where[0] == 0, high, low).astype(BF)


def latents_back(da, db, gres, gmlps, gfar, small, latents, gain, w_query, score_scale, chips, bits, deps):
    _, lat, width = latents.shape
    items = da.shape[0]
    qk = w_query.shape[1]
    count = 2 ** len(bits)
    half = width // (count * chips * CORES)
    small_blocks = -(-small.size // (half * qk))
    return launch(
        functools.partial(latents_back_kernel, score_scale, chips, bits),
        "latents_back",
        SHORT,
        [(da, None), (db, None)]
        + [(g, None) for g in gres + gmlps]
        + [(a, None) for a in (gfar, small, latents, gain, w_query)],
        [
            ((items, lat, width + gfar.shape[2]), BF, None),
            ((count, half, qk), BF, None),
            ((count + 1 + small_blocks, half, qk), BF, None),
            ((half, qk), F32, None),
        ],
        scratch=[
            pltpu.VMEM((width // chips, items * lat), BF),
            pltpu.VMEM((items * lat, qk), BF),
            pltpu.VMEM((items, width, lat), BF),
        ],
        deps=deps,
    )


def fold_kernel(where, keep_ref, far_ref, *outs):
    half = keep_ref.shape[0] // 2
    if len(outs) == 1:
        outs[0][...] = keep_ref[0].astype(F32) + far_ref[0].astype(F32)
        return
    for spot, out in enumerate(outs):
        for j in range(half):
            at = spot * half + j
            out[j] = (keep_ref[at].astype(F32) + far_ref[at].astype(F32)).astype(BF)


def fold(keep, far, deps, micros=SHORT):
    if keep.shape[0] == 1:
        outs = [(keep.shape[1:], F32, None)]
    else:
        shape = (keep.shape[0] // 2,) + keep.shape[1:]
        outs = [(shape, BF, None), (shape, BF, None)]
    return launch(fold_kernel, "fold", micros, [(keep, None), (far, None)], outs, deps=deps)


def side_kernel(begin, where, far_ref, small_ref, own_ref, send_ref):
    rows, width = small_ref.shape
    tall = jnp.concatenate([far_ref[j].astype(F32) for j in range(begin, far_ref.shape[0])], 0)
    pieces = [tall[rows * g : rows * (g + 1)] for g in range(width // far_ref.shape[2])]
    own = small_ref[...] + jnp.concatenate(pieces, 1)
    own_ref[...] = own
    send_ref[...] = own.astype(BF)


def side_sum(far, small, begin, deps):
    return launch(
        functools.partial(side_kernel, begin),
        "side_sum",
        1,
        [(far, None), (small, None)],
        [(small.shape, F32, None), (small.shape, BF, None)],
        deps=deps,
    )


def join_kernel(
    langs, chips, bits, where, keep_ref, far_ref, own_ref, side_ref, qkeep_ref, qfar_ref, qown_ref,
    keep_out, send_out,
):
    count, rows, wide = keep_ref.shape
    qrows, qwide = qown_ref.shape

    def across(tall):
        return jnp.concatenate([tall[r : r + 8] for r in range(0, qrows, 8)], 1)

    own = own_ref[...] + side_ref[...].astype(F32)
    gains = across(qown_ref[...] + qfar_ref[count].astype(F32))
    at = lax.broadcasted_iota(jnp.int32, (8, qwide), 1)
    half = count // 2
    for j in range(count):
        spot = where[2] ^ flipped(j, bits)
        device = (spot * chips + where[1]) * CORES + where[0]
        byte_cut = pltpu.roll(own, own.shape[1] - device * rows, 1)[:, :qwide]
        lat_cut = pltpu.roll(gains, gains.shape[1] - device * qrows, 1)[:, :qwide]
        spare = jnp.where(at < rows, byte_cut[:8], 0.0)
        for n in range(1, langs // 8 + 1):
            piece = jnp.where(at < rows, byte_cut[8 * n : 8 * n + 8], 0.0)
            spare += pltpu.roll(piece, n * rows, 1)
        spare += pltpu.roll(jnp.where(at < qrows, lat_cut, 0.0), (langs // 8 + 1) * rows, 1)
        byte = keep_ref[j].astype(F32) + far_ref[j].astype(F32)
        query = across(qkeep_ref[j].astype(F32) + qfar_ref[j].astype(F32))
        out = keep_out if j < half else send_out
        below = jnp.concatenate([query, spare], 1)
        out[j % half] = jnp.concatenate([byte, below], 0).astype(BF)


def join(keep, far, own, side, qkeep, qfar, qown, langs, chips, bits, deps):
    count, rows, wide = keep.shape
    shape = (count // 2, rows + 8, wide)
    return launch(
        functools.partial(join_kernel, langs, chips, bits),
        "join",
        LONG,
        [(a, None) for a in (keep, far, own, side, qkeep, qfar, qown)],
        [(shape, BF, None), (shape, BF, None)],
        deps=deps,
    )


def part_kernel(
    where, keep_ref, far_ref, key_ref, value_ref, query_ref, lang_ref, gin_ref, glat_ref, gmlp_ref
):
    total = keep_ref[0].astype(F32) + far_ref[0].astype(F32)
    rows, qk = key_ref.shape
    qrows, langs = query_ref.shape[0], lang_ref.shape[0]
    key_ref[...] = total[:rows, :qk]
    value_ref[...] = total[:rows, qk:]
    for r in range(0, qrows, 8):
        query_ref[r : r + 8] = total[rows:, r // 8 * qk : (r // 8 + 1) * qk]
    spare = total[rows:, qrows // 8 * qk : (qrows // 8 + 1) * qk]
    groups = langs // 8
    for n in range(groups):
        lang_ref[8 * n : 8 * n + 8] = spare[:, n * rows : (n + 1) * rows]
    gin_ref[...] = spare[:1, groups * rows : (groups + 1) * rows]
    begin = (groups + 1) * rows
    glat_ref[...] = spare[1:2, begin : begin + qrows]
    gmlp_ref[...] = spare[2:3, begin : begin + qrows]


def part(keep, far, qk, qrows, langs, deps):
    rows, wide = keep.shape[1] - 8, keep.shape[2]
    shapes = [(rows, qk), (rows, wide - qk), (qrows, qk), (langs, rows)]
    shapes += [(1, rows), (1, qrows), (1, qrows)]
    return launch(
        part_kernel,
        "part",
        SHORT,
        [(keep, None), (far, None)],
        [(shape, F32, None) for shape in shapes],
        deps=deps,
    )


def last_kernel(where, keep_a, far_a, keep_b, far_b, up_ref, down_ref, out_ref):
    wide = up_ref.shape[1]
    split = out_ref.shape[1] // 2
    first = keep_a[0].astype(F32) + far_a[0].astype(F32)
    second = keep_b[0].astype(F32) + far_b[0].astype(F32)
    up_ref[...] = first[:, :wide]
    down_ref[...] = second[:, :wide]
    out_ref[:, :split] = first[:, wide:]
    out_ref[:, split:] = second[:, wide:]


def last(keep_a, far_a, keep_b, far_b, width, deps):
    shape = (keep_a.shape[1], width)
    return launch(
        last_kernel,
        "last",
        SHORT,
        [(a, None) for a in (keep_a, far_a, keep_b, far_b)],
        [(shape, F32, None)] * 3,
        deps=deps,
    )


def place_kernel(columns, where, *refs):
    count = len(columns)
    items = pl.num_programs(0) // 2
    ours = pl.program_id(0) // items == where[0]
    for n, (left, right) in enumerate(columns):
        out = refs[2 * count + n]
        wide = out.shape[2]
        own = refs[n][:, :, left : left + wide].astype(out.dtype)
        far = refs[count + n][:, :, right : right + wide].astype(out.dtype)
        out[...] = jnp.where(ours, own, far)
    refs[-1][...] = jnp.zeros_like(refs[-1])


def place(pairs, micros, deps):
    items = pairs[0][0].shape[0]
    one = lambda a: (1,) + a.shape[1:]
    rows = lambda p: p[0].shape[1]
    outs = [
        ((2 * items, rows(p), p[4]), p[5], block((1, rows(p), p[4]), lambda g: g))
        for p in pairs
    ]
    return launch(
        functools.partial(place_kernel, [(p[1], p[3]) for p in pairs]),
        "place",
        micros,
        [(a, block(one(a), lambda g: g % items)) for a in [p[0] for p in pairs]]
        + [(a, block(one(a), lambda g: g % items)) for a in [p[2] for p in pairs]],
        outs + [((8, 128), F32, None)],
        deps=deps,
        grid=2 * items,
        far=True,
    )


def swap(value, axis, bit):
    size = lax.axis_size(axis)
    return lax.ppermute(value, axis, [(i, i ^ bit) for i in range(size)])


def bits_of(size):
    return [2**t for t in range(size.bit_length() - 1)]


def halve(value, dim, axis, bit):
    mine = (lax.axis_index(axis) // bit) % 2
    keep = lax.dynamic_index_in_dim(value, mine, dim, keepdims=False)
    send = lax.dynamic_index_in_dim(value, 1 - mine, dim, keepdims=False)
    return (keep.astype(F32) + swap(send, axis, bit).astype(F32)).astype(BF)


def scatter_rows(value):
    spots, chips = lax.axis_size("batch"), lax.axis_size("seq") // CORES
    rows = value.shape[0] // (spots * chips * CORES)
    blocks = value.astype(BF).reshape(spots, chips, CORES, rows, value.shape[1])
    blocks = halve(blocks, 2, "seq", 1)
    for bit in bits_of(chips):
        rest = blocks.shape[2:]
        blocks = blocks.reshape((spots, blocks.shape[1] // 2, 2) + rest)
        blocks = halve(blocks, 2, "seq", CORES * bit)
    blocks = blocks[:, 0]
    for bit in bits_of(spots):
        blocks = blocks.reshape((blocks.shape[0] // 2, 2) + blocks.shape[1:])
        blocks = halve(blocks, 1, "batch", bit)
    return blocks[0].astype(F32)


def everywhere(value):
    for axis in ("seq", "batch"):
        for bit in bits_of(lax.axis_size(axis)):
            value = value + swap(value, axis, bit)
    return value


def merge(oa, ob):
    rows = oa.shape[0] - 2 * HEADS
    wide = rows // HEADS
    la = oa[rows : rows + HEADS].astype(F32) + oa[rows + HEADS :].astype(F32)
    lb = ob[rows : rows + HEADS].astype(F32) + ob[rows + HEADS :].astype(F32)
    top = jnp.maximum(la, lb)
    ea, eb = jnp.exp2(la - top), jnp.exp2(lb - top)
    total = ea + eb
    lse = top + jnp.log2(total)
    out = oa[:rows].astype(F32) * jnp.repeat(ea / total, wide, 0)
    out = out + ob[:rows].astype(F32) * jnp.repeat(eb / total, wide, 0)
    high = lse.astype(BF)
    return jnp.concatenate([out.astype(BF), high, (lse - high.astype(F32)).astype(BF)], 0)


def local(
    byte_inputs,
    language,
    lang_table,
    latents,
    gain_in,
    gain_lat,
    gain_mlp,
    w_query,
    w_key,
    w_value,
    w_out,
    w_up,
    w_down,
    cotangent,
):
    items = byte_inputs.shape[0] // CORES
    width_in, width_lat = byte_inputs.shape[2], latents.shape[2]
    lat, qk = latents.shape[1], w_query.shape[1]
    langs = lang_table.shape[0]
    score_scale = 1.0 / math.sqrt(qk // HEADS)
    score_unit = score_scale * math.log2(math.e)
    spots, chips = lax.axis_size("batch"), lax.axis_size("seq") // CORES
    devices = spots * chips * CORES
    seq_at, spot = lax.axis_index("seq"), lax.axis_index("batch")
    core, side = seq_at % CORES, seq_at // CORES
    device = spot * (chips * CORES) + seq_at
    chip_bits, spot_bits = bits_of(chips), bits_of(spots)
    rows_in, rows_lat = width_in // devices, width_lat // devices
    direct = (
        chips == 2
        and rows_in == langs + 8
        and rows_lat * qk == 8 * width_lat
        and width_lat % qk == 0
        and langs % 8 == 0
        and byte_inputs.shape[1] == lat
    )
    last_bit = chip_bits[-1]
    table = lang_table
    gain_in, gain_lat, gain_mlp = gain_in[None], gain_lat[None], gain_mlp[None]

    far = swap(pick_bytes(byte_inputs, items), "seq", 1)
    asked = queries(items, latents, gain_lat, w_query, ())
    asked = [asked[2 * i : 2 * i + 2] for i in range(items)]
    xns, kept, pairs, token = [], [], [], ()
    for item in range(items):
        ot, xn, k, kt, v = attend(
            item, items, language, byte_inputs, far, table, gain_in, w_key, w_value,
            asked[item][1], score_unit, token,
        )
        xns.append(xn)
        kept.append((k, kt, v))
        token = (k,)
        for bit in chip_bits[:-1]:
            ot = merge(ot, swap(ot, "seq", CORES * bit))
        pairs.append((ot, swap(ot, "seq", CORES * last_bit)))

    gact = act_back(cotangent, w_down, items, token)
    token = (gact,)
    sides, outs, dqkv = [], None, ()

    def back(item, deps):
        gatt, dot, lse = sides[item][2:5]
        return attend_back(
            item, items, *asked[item], *kept[item], gatt, lse, dot, score_unit, score_scale, dqkv, deps
        )

    byted = ()

    def back_bytes(item, deps):
        return bytes_back(
            item, items, language, byte_inputs, far, table, gain_in, w_key, w_value,
            dqkv[1], byted, deps,
        )

    for item in range(items):
        if item:
            dqkv = back(item - 1, token)
            byted = back_bytes(item - 1, ())
            token = (byted[2],)
        side_out = latent_side(
            item, items, last_bit, *pairs[item], latents, cotangent,
            gact, gain_mlp, w_out, w_up, w_down, outs, token,
        )
        outs = side_out[0]
        sides.append(side_out)
        token = (side_out[3],)
    outs_far = swap(outs, "seq", 1)

    pick = lambda at: [s[at] for s in sides]
    down = (pick(7), [cotangent] * items)
    up = (pick(6), pick(8))
    out = (pick(5), pick(9))

    if direct:
        y_bit, z_bit, far_bit = spot_bits
        a_bits, b_bits = [y_bit, z_bit, far_bit], [z_bit, far_bit, y_bit]
        c_bits = [1] + [2 * b for b in a_bits]
        split = width_lat // 2
        keep_a, send_a = latent_weights(
            [up, out], [(0, width_lat), (0, split)], chips, a_bits, "weights_a", token
        )
        far_a = swap(send_a, "seq", 1)
        keep_b, send_b = latent_weights(
            [down, out], [(0, width_lat), (split, split)], chips, b_bits, "weights_b",
            (keep_a,),
        )
        far_b = swap(send_b, "seq", 1)
        dqkv = back(items - 1, (keep_b,))
        dqt, dkv = dqkv
        dqt_far = swap(dqt, "seq", CORES)
        keep_a, send_a = fold(keep_a, far_a, (dqt, outs_far))
        far_a = swap(send_a, "batch", a_bits[0])
        keep_b, send_b = fold(keep_b, far_b, (keep_a,))
        far_b = swap(send_b, "batch", b_bits[0])
        keep_c, send_c = byte_weights(xns, dkv, c_bits, (keep_b,))
        far_c = swap(send_c, "seq", 1)
        keep_c, send_c = fold(keep_c, far_c, ())
        far_c = swap(send_c, "seq", CORES)
        gown, gfar, small = back_bytes(items - 1, (keep_c,))
        glats, keep_q, send_q, own_q = latents_back(
            dqt, dqt_far, pick(1), pick(10), gfar, small, latents, gain_lat, w_query,
            score_scale, chips, a_bits, (),
        )
        glats_far = swap(glats, "seq", 1)
        far_q = swap(send_q, "seq", 1)
        own_s, send_s = side_sum(far_q, small, keep_q.shape[0] + 1, ())
        far_s = swap(send_s, "seq", CORES)
        keep_b, send_b = fold(keep_b, far_b, (own_s,))
        far_b = swap(send_b, "batch", b_bits[1])
        keep_a, send_a = fold(keep_a, far_a, (keep_b,))
        far_a = swap(send_a, "batch", a_bits[1])
        keep_c, send_c = join(
            keep_c, far_c, own_s, far_s, keep_q, far_q, own_q, langs, chips, a_bits,
            (keep_a,),
        )
        far_c = swap(send_c, "batch", a_bits[0])
        latents_out, grad_bytes, token = place(
            [
                (outs, 0, outs_far, 0, width_lat, BF),
                (gown, 0, glats_far, width_lat, width_in, F32),
            ],
            LONG,
            (keep_c,),
        )
        keep_c, send_c = fold(keep_c, far_c, (token,))
        far_c = swap(send_c, "batch", a_bits[1])
        keep_b, send_b = fold(keep_b, far_b, (keep_c,))
        far_b = swap(send_b, "batch", b_bits[2])
        keep_a, send_a = fold(keep_a, far_a, (keep_b,))
        far_a = swap(send_a, "batch", a_bits[2])
        grad_latents, token = place(
            [(glats, 0, glats_far, 0, width_lat, F32)], SHORT, (keep_a,)
        )
        keep_c, send_c = fold(keep_c, far_c, (token,))
        far_c = swap(send_c, "batch", a_bits[2])
        g_up, g_down, g_out = last(keep_a, far_a, keep_b, far_b, width_lat, (keep_c,))
        g_key, g_value, g_query, g_table, *gains = part(
            keep_c, far_c, qk, rows_lat, langs, ()
        )
        g_in, g_lat, g_mlp = [g[0] for g in gains]
    else:
        dqkv = back(items - 1, token)
        dqt, dkv = dqkv
        for bit in chip_bits:
            dqt = (dqt.astype(F32) + swap(dqt, "seq", CORES * bit).astype(F32)).astype(BF)
        gown, gfar, small = back_bytes(items - 1, ())
        gfar_far = swap(gfar, "seq", 1)
        own_cut = lambda a: lax.dynamic_slice_in_dim(a, core * items, items, 0)
        grad_q = (dqt.astype(F32) * score_scale).swapaxes(1, 2).astype(BF)
        unit, inverse = standardise(own_cut(latents).astype(F32))
        gln = lax.dot_general(
            grad_q, w_query, (((2,), (1,)), ((), ())), preferred_element_type=F32
        )
        glats = jnp.stack(pick(1)) + standardise_back(unit, inverse, gln * gain_lat)
        glats = glats.astype(BF)
        glats_far = swap(glats, "seq", 1)
        flat = lambda a: a.reshape(-1, a.shape[-1])
        share = 1.0 / chips
        g_query = scatter_rows(tn(flat((unit * gain_lat).astype(BF)), flat(grad_q)) * share)
        rows = lambda lefts, rights: scatter_rows(
            sum(nn(x, y) for x, y in zip(lefts, rights)) * share
        )
        g_down = rows(pick(7), own_cut(cotangent))
        g_up, g_out = rows(pick(6), pick(8)), rows(pick(5), pick(9))
        g_bytes = scatter_rows(sum(tn(xns[i], dkv[i]) for i in range(items)))
        g_key, g_value = g_bytes[:, :qk], g_bytes[:, qk:]
        pad = ((0, 0), (0, width_lat - width_in))
        small = jnp.concatenate(
            [
                jnp.pad(small[: langs + 1], pad),
                jnp.sum(gln * unit, (0, 1))[None] * share,
                sum(pick(10)) * share,
            ],
            0,
        )
        small = everywhere(small)
        cut = lambda rows, count: lax.dynamic_slice_in_dim(rows, device * count, count, 1)
        g_table, g_in = cut(small[:langs], rows_in), cut(small[langs : langs + 1], rows_in)[0]
        g_lat, g_mlp = cut(small[langs + 1 :], rows_lat)
        latents_out, grad_bytes, grad_latents, _ = place(
            [
                (outs, 0, outs_far, 0, width_lat, BF),
                (gown, 0, gfar_far, 0, width_in, F32),
                (glats, 0, glats_far, 0, width_lat, F32),
            ],
            SHORT,
            (),
        )

    return (
        latents_out,
        grad_latents,
        grad_bytes,
        g_table,
        g_in,
        g_lat,
        g_mlp,
        g_query,
        g_key,
        g_value,
        g_out,
        g_up,
        g_down,
    )


def solution(mesh):
    return jax.shard_map(
        local,
        mesh=mesh,
        in_specs=(
            P("batch", "seq", None),
            P("batch"),
            P(),
            P("batch", None, None),
            P(),
            P(),
            P(),
            P(),
            P(),
            P(),
            P(),
            P(),
            P(),
            P("batch", None, None),
        ),
        out_specs=(
            P("batch", None, None),
            P("batch", None, None),
            P("batch", "seq", None),
            P(None, ("batch", "seq")),
            P(("batch", "seq")),
            P(("batch", "seq")),
            P(("batch", "seq")),
            P(("batch", "seq"), None),
            P(("batch", "seq"), None),
            P(("batch", "seq"), None),
            P(("batch", "seq"), None),
            P(("batch", "seq"), None),
            P(("batch", "seq"), None),
        ),
        check_vma=False,
    )
```

```python
import functools
import math

import jax
import jax.numpy as jnp
from jax import lax
from jax.experimental import pallas as pl
from jax.experimental.pallas import tpu as pltpu
from jax.sharding import PartitionSpec as P

HEADS = 8
CORES = 2
EPS = 1e-05
F32 = jnp.float32
BF = jnp.bfloat16
VMEM_LIMIT = 12 * 1024 * 1024
PEAK = 1.15e9
SHORT, LONG, AHEAD = 0.001, 40, 3


def nn(a, b):
    return lax.dot_general(a, b, (((1,), (0,)), ((), ())), preferred_element_type=F32)


def nt(a, b):
    return lax.dot_general(a, b, (((1,), (1,)), ((), ())), preferred_element_type=F32)


def tn(a, b):
    return lax.dot_general(a, b, (((0,), (0,)), ((), ())), preferred_element_type=F32)


def standardise(x):
    centre = x - jnp.mean(x, -1, keepdims=True)
    inverse = lax.rsqrt(jnp.mean(centre * centre, -1, keepdims=True) + EPS)
    return centre * inverse, inverse


def standardise_back(unit, inverse, grad):
    return inverse * (
        grad - jnp.mean(grad, -1, keepdims=True) - unit * jnp.mean(grad * unit, -1, keepdims=True)
    )


def block(shape, at):
    return pl.BlockSpec(shape, lambda g: (at(g),) + (0,) * (len(shape) - 1))


ANY = pl.BlockSpec(memory_space=pl.ANY)
FAST = pl.BlockSpec(memory_space=pltpu.VMEM)
FAR = pl.BlockSpec(memory_space=pltpu.HBM)
SCALARS = pl.BlockSpec(memory_space=pltpu.SMEM)


def launch(body, name, micros, ins, outs, scratch=(), deps=(), alias=None, grid=1, far=False):
    count, extra = len(ins), len(deps)
    ins = [
        (pltpu.with_memory_space_constraint(a, pltpu.HBM) if s is FAR else a, s) for a, s in ins
    ]

    def kernel(*refs):
        body(Where(), *refs[:count], *refs[count + extra :])

    return pl.pallas_call(
        kernel,
        grid=(grid,),
        in_specs=[FAST if s is None else s for _, s in ins] + [ANY] * extra,
        out_specs=[FAST if s is None else s for _, _, s in outs],
        scratch_shapes=list(scratch),
        out_shape=[
            (jax.ShapeDtypeStruct if s is None or not far else pltpu.HBM)(shape, dtype)
            for shape, dtype, s in outs
        ],
        input_output_aliases=alias or {},
        compiler_params=pltpu.CompilerParams(vmem_limit_bytes=VMEM_LIMIT),
        cost_estimate=pl.CostEstimate(
            flops=int(micros * PEAK), bytes_accessed=1, transcendentals=0
        ),
        name=name,
    )(*[a for a, _ in ins], *deps)


class Where:
    def __getitem__(self, at):
        if at == 2:
            return lax.axis_index("batch")
        return (lax.rem, lax.div)[at](lax.axis_index("seq"), CORES)


def pick_kernel(where, own_ref, out_ref, arrived):
    items = out_ref.shape[0]
    copy = pltpu.make_async_copy(
        own_ref.at[pl.ds((1 - where[0]) * items, items)], out_ref, arrived
    )
    copy.start()
    copy.wait()


def pick_bytes(own, items):
    return launch(
        pick_kernel,
        "pick_bytes",
        AHEAD,
        [(own, FAR)],
        [((items,) + own.shape[1:], BF, None)],
        scratch=[pltpu.SemaphoreType.DMA(())],
    )[0]


def query_kernel(where, lat_ref, gain_ref, wq_ref, *outs):
    items = len(outs) // 2
    for i in range(items):
        unit, _ = standardise(lat_ref[where[0] * items + i].astype(F32))
        rows = nn((unit * gain_ref[...]).astype(BF), wq_ref[...])
        outs[2 * i][...] = rows.astype(BF)
        outs[2 * i + 1][...] = rows.T.astype(BF)


def queries(items, latents, gain, w_query, deps):
    _, count, width = latents.shape
    qk = w_query.shape[1]
    return launch(
        query_kernel,
        "queries",
        2,
        [(latents, None), (gain, None), (w_query, None)],
        [((count, qk), BF, None), ((qk, count), BF, None)] * items,
        deps=deps,
    )


SPAN = 256


def head_span(h, wide):
    begin = h * wide // 128 * 128
    return begin, h * wide - begin


def language_row(table_ref, language):
    at = lax.broadcasted_iota(jnp.int32, table_ref.shape, 0)
    table = table_ref[...].astype(F32)
    return jnp.sum(jnp.where(at == language, table, 0.0), 0, keepdims=True)


def attend_kernel(
    item, items, score_unit, where, lang_ref, own_ref, far_ref, table_ref, gain_ref, wk_ref, wv_ref, qt_ref,
    ot_ref, xn_ref, k_ref, kt_ref, v_ref,
):
    at = where[0] * items + item
    count = far_ref.shape[1]
    row = language_row(table_ref, lang_ref[at])
    gain = gain_ref[...]
    for part, rows in enumerate((own_ref[at], far_ref[item])):
        unit, _ = standardise(rows.astype(F32) + row)
        xn_ref[part * count : (part + 1) * count] = (unit * gain).astype(BF)
    xn = xn_ref[...]
    k = nn(xn, wk_ref[...]).astype(BF)
    k_ref[...] = k
    kt_ref[...] = k.T
    v = nn(xn, wv_ref[...]).astype(BF)
    v_ref[...] = v
    qt = qt_ref[...]
    depth = qt.shape[0] // HEADS
    wide = v.shape[1] // HEADS
    at = lax.broadcasted_iota(jnp.int32, qt.shape, 0) // depth

    def score_of(h):
        return nn(k, jnp.where(at == h, qt, jnp.zeros_like(qt)))

    def finish(h, weight, total):
        begin, ahead = head_span(h, wide)
        out = tn(v[:, begin : begin + SPAN], weight)[ahead : ahead + wide]
        ot_ref[h * wide : (h + 1) * wide] = (out * (1.0 / total)).astype(BF)

    lse = []
    coming, waiting = score_of(0), None
    for h in range(HEADS):
        score = coming * score_unit
        if h + 1 < HEADS:
            coming = score_of(h + 1)
        if waiting is not None:
            finish(*waiting)
        top = jnp.max(score, 0, keepdims=True)
        weight = jnp.exp2(score - top)
        total = jnp.sum(weight, 0, keepdims=True)
        lse.append(top + jnp.log2(total))
        waiting = (h, weight.astype(BF), total)
    finish(*waiting)
    lse = jnp.concatenate(lse, 0)
    high = lse.astype(BF)
    low = (lse - high.astype(F32)).astype(BF)
    ot_ref[HEADS * wide :] = jnp.concatenate([high, low], 0)


def attend(
    item, items, language, own, far, table, gain, w_key, w_value, qt, score_unit, deps
):
    _, count, width = own.shape
    qk, lat = w_key.shape[1], qt.shape[1]
    wide = w_value.shape[1]
    return launch(
        functools.partial(attend_kernel, item, items, score_unit),
        "attend",
        3.8,
        [(language, SCALARS)]
        + [(a, None) for a in (own, far, table, gain, w_key, w_value, qt)],
        [
            ((wide + 2 * HEADS, lat), BF, None),
            ((2 * count, width), BF, None),
            ((2 * count, qk), BF, None),
            ((qk, 2 * count), BF, None),
            ((2 * count, wide), BF, None),
        ],
        deps=deps,
    )


def act_back_kernel(where, cot_ref, wd_ref, gact_ref):
    items = gact_ref.shape[0]
    for i in range(items):
        gact_ref[i] = nt(cot_ref[where[0] * items + i], wd_ref[...])


def act_back(cot, w_down, items, deps):
    return launch(
        act_back_kernel,
        "act_back",
        2.5,
        [(cot, None), (w_down, None)],
        [((items, cot.shape[1], w_down.shape[0]), F32, None)],
        deps=deps,
    )[0]


GELU_A = math.sqrt(2.0 / math.pi)
GELU_B = 0.044715


def latent_kernel(
    item, items, bit, where, oa_ref, ob_ref, lat_ref, cot_ref, gact_ref, gain_ref, wo_ref, wu_ref, wd_ref,
    *refs,
):
    (
        outs_ref, gres_ref, gatt_ref, dot_ref, lse_ref, att_ref, hid_ref, act_ref, gpre_ref,
        glow_ref, ggain_ref,
    ) = refs[-11:]
    at = where[0] * items + item
    first = lax.rem(lax.div(where[1], bit), 2) == 0
    rows = gatt_ref.shape[0]
    wide = rows // HEADS
    ours = oa_ref[rows : rows + HEADS].astype(F32) + oa_ref[rows + HEADS :].astype(F32)
    theirs = ob_ref[rows : rows + HEADS].astype(F32) + ob_ref[rows + HEADS :].astype(F32)
    left = jnp.where(first, ours, theirs)
    right = jnp.where(first, theirs, ours)
    top = jnp.maximum(left, right)
    e_left, e_right = jnp.exp2(left - top), jnp.exp2(right - top)
    total = e_left + e_right
    lse_ref[...] = top + jnp.log2(total)
    scale = 1.0 / total
    e_left, e_right = e_left * scale, e_right * scale
    merged = []
    for h in range(HEADS):
        a = oa_ref[h * wide : (h + 1) * wide].astype(F32)
        b = ob_ref[h * wide : (h + 1) * wide].astype(F32)
        low, high = jnp.where(first, a, b), jnp.where(first, b, a)
        merged.append(low * e_left[h : h + 1] + high * e_right[h : h + 1])
        att_ref[h * wide : (h + 1) * wide] = merged[-1].astype(BF)
    resid = lat_ref[at].astype(F32) + tn(att_ref[...], wo_ref[...])
    unit, inverse = standardise(resid)
    gain = gain_ref[...]
    hidden = (unit * gain).astype(BF)
    hid_ref[...] = hidden.T
    pre = nn(hidden, wu_ref[...])
    square = pre * pre
    slope = jnp.tanh(GELU_A * pre * (1.0 + GELU_B * square))
    act = (0.5 * pre * (1.0 + slope)).astype(BF)
    act_ref[...] = act.T
    outs_ref[item] = (resid + nn(act, wd_ref[...])).astype(BF)
    cot = cot_ref[at]
    gelu_slope = 0.5 * (1.0 + slope) + 0.5 * pre * (1.0 - slope * slope) * GELU_A * (
        1.0 + 3.0 * GELU_B * square
    )
    gpre = (gact_ref[item] * gelu_slope).astype(BF)
    gpre_ref[...] = gpre
    ghid = nt(gpre, wu_ref[...])
    ggain_ref[...] = jnp.sum(ghid * unit, 0, keepdims=True)
    gres = cot.astype(F32) + standardise_back(unit, inverse, ghid * gain)
    gres_ref[...] = gres
    glow = gres.astype(BF)
    glow_ref[...] = glow
    gatt_ref[...] = nt(wo_ref[...], glow).astype(BF)
    for h in range(HEADS):
        dot_ref[h : h + 1] = jnp.sum(
            gatt_ref[h * wide : (h + 1) * wide].astype(F32) * merged[h], 0, keepdims=True
        )


def latent_side(
    item, items, bit, oa, ob, latents, cot, gact, gain, w_out, w_up, w_down, before, deps
):
    total, lat, width = latents.shape
    feed = w_up.shape[1]
    ins = [(a, None) for a in (oa, ob, latents, cot, gact, gain, w_out, w_up, w_down)]
    alias = {}
    if before is not None:
        alias[len(ins)] = 0
        ins.append((before, None))
    return launch(
        functools.partial(latent_kernel, item, items, bit),
        "latent_side",
        7,
        ins,
        [
            ((items, lat, width), BF, None),
            ((lat, width), F32, None),
            ((width, lat), BF, None),
            ((HEADS, lat), F32, None),
            ((HEADS, lat), F32, None),
            ((width, lat), BF, None),
            ((width, lat), BF, None),
            ((feed, lat), BF, None),
            ((lat, feed), BF, None),
            ((lat, width), BF, None),
            ((1, width), F32, None),
        ],
        alias=alias,
        deps=deps,
    )


def flipped(at, bits):
    return sum(((at >> (len(bits) - 1 - t)) & 1) * bit for t, bit in enumerate(bits))


def pick_rows(where, source, lhs_ref, lane, rows, chips, bits):
    lat = source.shape[1]
    for j in range(2 ** len(bits)):
        spot = where[2] ^ flipped(j, bits)
        begin = pl.multiple_of((spot * chips + where[1]) * rows, 16)
        lhs_ref[j * rows : (j + 1) * rows, lane : lane + lat] = source[pl.ds(begin, rows)]


def latent_weights_kernel(plan, items, chips, bits, where, *refs):
    ins, keep_ref, send_ref, lhs_ref = refs[:-3], refs[-3], refs[-2], refs[-1]
    half = keep_ref.shape[1]
    column = 0
    for w, (begin, width) in enumerate(plan):
        lefts = ins[2 * items * w : 2 * items * w + items]
        rights = ins[2 * items * w + items : 2 * items * (w + 1)]
        total = 0.0
        for i in range(items):
            lat = lefts[i].shape[1]
            pick_rows(where, lefts[i], lhs_ref, i * lat, 2 * half, chips, bits)
            right = rights[i]
            if len(right.shape) == 3:
                right = right.at[where[0] * items + i]
            total += nn(lhs_ref[:, i * lat : (i + 1) * lat], right[:, begin : begin + width])
        out = slice(column, column + width)
        for j in range(keep_ref.shape[0]):
            low = total[2 * j * half : (2 * j + 1) * half]
            high = total[(2 * j + 1) * half : (2 * j + 2) * half]
            keep_ref[j, :, out] = jnp.where(where[0] == 0, low, high).astype(BF)
            send_ref[j, :, out] = jnp.where(where[0] == 0, high, low).astype(BF)
        column += width


def latent_weights(groups, plan, chips, bits, name, deps):
    items = len(groups[0][0])
    ins = []
    for lefts, rights in groups:
        ins += [(a, None) for a in lefts + rights]
    width, lat = groups[0][0][0].shape
    count = 2 ** len(bits)
    half = width // (count * chips * CORES)
    shape = (count, half, sum(w for _, w in plan))
    return launch(
        functools.partial(latent_weights_kernel, plan, items, chips, bits),
        name,
        SHORT,
        ins,
        [(shape, BF, None), (shape, BF, None)],
        scratch=[pltpu.VMEM((width // chips, items * lat), BF)],
        deps=deps,
    )


def attend_back_kernel(
    item, score_unit, score_scale, where, q_ref, qt_ref, k_ref, kt_ref, v_ref, gatt_ref, lse_ref,
    dot_ref, *refs,
):
    dqt_ref, dkv_ref, dvt_ref = refs[-3:]
    q, qt, k = q_ref[...], qt_ref[...], k_ref[...]
    qk = qt.shape[0]
    depth = qk // HEADS
    wide = gatt_ref.shape[0] // HEADS
    lat = qt.shape[1]
    at = lax.broadcasted_iota(jnp.int32, qt.shape, 0) // depth
    across = lax.broadcasted_iota(jnp.int32, q.shape, 1) // depth

    def begin_head(h):
        score = nn(k, jnp.where(at == h, qt, jnp.zeros_like(qt)))
        grad = gatt_ref[h * wide : (h + 1) * wide]
        begin, ahead = head_span(h, wide)
        after = SPAN - ahead - wide
        pieces = [grad]
        if ahead:
            pieces = [jnp.zeros((ahead, lat), BF)] + pieces
        if after:
            pieces = pieces + [jnp.zeros((after, lat), BF)]
        return score, grad, nn(v_ref[:, begin : begin + SPAN], jnp.concatenate(pieces, 0))

    def finish(h, grad, prob, grad_score):
        dvt_ref[h * wide : (h + 1) * wide] = nt(grad, prob).astype(BF)
        dqt_ref[item, h * depth : (h + 1) * depth] = nn(
            kt_ref[h * depth : (h + 1) * depth], grad_score
        ).astype(BF)
        return nn(grad_score, jnp.where(across == h, q, jnp.zeros_like(q)))

    dk = jnp.zeros(k.shape, F32)
    coming, waiting = begin_head(0), None
    for h in range(HEADS):
        score, grad, grad_prob = coming
        if h + 1 < HEADS:
            coming = begin_head(h + 1)
        if waiting is not None:
            dk += finish(*waiting)
        prob = jnp.exp2(score * score_unit - lse_ref[h : h + 1])
        grad_score = (prob * (grad_prob - dot_ref[h : h + 1])).astype(BF)
        waiting = (h, grad, prob.astype(BF), grad_score)
    dk += finish(*waiting)
    dkv_ref[:, :qk] = (dk * score_scale).astype(BF)
    dkv_ref[:, qk:] = dvt_ref[...].T


def attend_back(
    item, items, q, qt, k, kt, v, gatt, lse, dot, score_unit, score_scale, before, deps
):
    lat, qk = q.shape
    count, wide = v.shape
    ins = [(a, None) for a in (q, qt, k, kt, v, gatt, lse, dot)]
    alias = {}
    for spot, array in enumerate(before):
        alias[len(ins)] = spot
        ins.append((array, None))
    return launch(
        functools.partial(attend_back_kernel, item, score_unit, score_scale),
        "attend_back",
        3.8 if item + 1 < items else SHORT,
        ins,
        [
            ((items, qk, lat), BF, None),
            ((count, qk + wide), BF, None),
        ],
        scratch=[pltpu.VMEM((wide, count), BF)],
        alias=alias,
        deps=deps,
    )


def turn_kernel(bits, where, *refs):
    xn_refs, (keep_ref, send_ref, all_ref) = refs[:-3], refs[-3:]
    count = 2 ** len(bits)
    rows = keep_ref.shape[1] // count
    mine = where[2] * 2 + where[1]
    for i, ref in enumerate(xn_refs):
        all_ref[i] = ref[...].astype(F32).T
    for i in range(len(xn_refs)):
        for out, core in ((keep_ref, where[0]), (send_ref, 1 - where[0])):
            for j in range(0, count, 2):
                pair = []
                for n in (j, j + 1):
                    spot = (mine ^ flipped(n, bits)) * CORES + core
                    begin = pl.multiple_of(spot * rows, 8)
                    pair.append(all_ref[i, pl.ds(begin, rows)])
                out[i, j * rows : (j + 2) * rows] = jnp.concatenate(pair, 0).astype(BF)


def turn(xns, bits, deps):
    count, width = xns[0].shape
    shape = (len(xns), width // CORES, count)
    return launch(
        functools.partial(turn_kernel, bits),
        "turn",
        3,
        [(a, None) for a in xns],
        [(shape, BF, None), (shape, BF, None)],
        scratch=[pltpu.VMEM((len(xns), width, count), F32)],
        deps=deps,
    )


def byte_part_kernel(spots, where, *refs):
    out_ref = refs[-1]
    total = refs[-2][...] if len(refs) % 2 == 0 else 0.0
    for n, spot in enumerate(spots):
        total += nn(refs[2 * n][spot], refs[2 * n + 1][...])
    out_ref[...] = total


def byte_part(pairs, before, micros, deps):
    ins = [(a, None) for turned, _, dkv in pairs for a in (turned, dkv)]
    alias = {}
    if before is not None:
        alias = {len(ins): 0}
        ins.append((before, None))
    shape = (pairs[0][0].shape[1], pairs[0][2].shape[1])
    return launch(
        functools.partial(byte_part_kernel, [p[1] for p in pairs]),
        "byte_part",
        micros,
        ins,
        [(shape, F32, None)],
        alias=alias,
        deps=deps,
    )[0]


def byte_last_kernel(spot, where, turned_ref, dkv_ref, before_ref, keep_ref, send_ref):
    total = before_ref[...] + nn(turned_ref[spot], dkv_ref[...])
    half, rows = keep_ref.shape[:2]
    for j in range(half):
        keep_ref[j] = total[j * rows : (j + 1) * rows].astype(BF)
        send_ref[j] = total[(half + j) * rows : (half + j + 1) * rows].astype(BF)


def byte_last(turned, spot, dkv, before, count, deps):
    shape = (count // 2, turned.shape[1] // count, dkv.shape[1])
    return launch(
        functools.partial(byte_last_kernel, spot),
        "byte_last",
        SHORT,
        [(turned, None), (dkv, None), (before, None)],
        [(shape, BF, None), (shape, BF, None)],
        deps=deps,
    )


def bytes_back_kernel(
    item, where, lang_ref, own_ref, far_ref, table_ref, gain_ref, wk_ref, wv_ref, dkv_ref, *refs
):
    gown_ref, gfar_ref, small_ref = refs[-3:]
    items, count = gfar_ref.shape[:2]
    qk = wk_ref.shape[1]
    langs = table_ref.shape[0]
    gain = gain_ref[...]
    language = lang_ref[where[0] * items + item]
    row = language_row(table_ref, language)
    grads = nt(dkv_ref[:, :qk], wk_ref[...]) + nt(dkv_ref[:, qk:], wv_ref[...])
    gain_sum = jnp.zeros_like(row)
    byte_sum = jnp.zeros_like(row)
    for part, rows, out in (
        (0, own_ref[where[0] * items + item], gown_ref),
        (1, far_ref[item], gfar_ref),
    ):
        unit, inverse = standardise(rows.astype(F32) + row)
        grad = grads[part * count : (part + 1) * count]
        gain_sum += jnp.sum(grad * unit, 0, keepdims=True)
        back = standardise_back(unit, inverse, grad * gain)
        byte_sum += jnp.sum(back, 0, keepdims=True)
        out[item] = back.astype(out.dtype)
    at = lax.broadcasted_iota(jnp.int32, small_ref.shape, 0)
    small = jnp.where(at == language, byte_sum, 0.0) + jnp.where(at == langs, gain_sum, 0.0)
    if item:
        small += refs[2][...]
    small_ref[...] = small


def bytes_back(
    item, items, language, own, far, table, gain, w_key, w_value, dkv, before, deps
):
    shape = far.shape
    ins = [(language, SCALARS)]
    ins += [(a, None) for a in (own, far, table, gain, w_key, w_value, dkv)]
    alias = {}
    if before:
        alias = {len(ins): 0, len(ins) + 1: 1}
        ins += [(a, None) for a in before]
    return launch(
        functools.partial(bytes_back_kernel, item),
        "bytes_back",
        2.5 if item + 1 < items else SHORT,
        ins,
        [
            (shape, F32, None),
            (shape, BF, None),
            ((table.shape[0] + 8, far.shape[2]), F32, None),
        ],
        alias=alias,
        deps=deps,
    )


def latents_back_kernel(
    score_scale, chips, bits, where, da_ref, db_ref, *refs
):
    items = da_ref.shape[0]
    gres_refs, gmlp_refs, refs = refs[:items], refs[items : 2 * items], refs[2 * items :]
    gfar_ref, small_ref, lat_ref, gain_ref, wq_ref = refs[:5]
    glat_ref, keep_ref, send_ref, own_ref = refs[5:9]
    lhs_ref, rhs_ref, turn_ref = refs[9:]
    lat = lat_ref.shape[1]
    gain = gain_ref[...]
    gain_sum = jnp.zeros_like(gain)
    half = keep_ref.shape[1]
    for i in range(items):
        total = (da_ref[i].astype(F32) + db_ref[i].astype(F32)) * score_scale
        grad = total.T.astype(BF)
        rhs_ref[i * lat : (i + 1) * lat] = grad
        unit, inverse = standardise(lat_ref[where[0] * items + i].astype(F32))
        turn_ref[i] = (unit * gain).astype(BF).T
        gln = nt(grad, wq_ref[...])
        gain_sum += jnp.sum(gln * unit, 0, keepdims=True)
        out = gres_refs[i][...] + standardise_back(unit, inverse, gln * gain)
        glat_ref[i, :, : out.shape[1]] = out.astype(BF)
        glat_ref[i, :, out.shape[1] :] = gfar_ref[i]
    gmlp = functools.reduce(jnp.add, [r[...] for r in gmlp_refs])
    wide = own_ref.shape[1]
    at = lax.broadcasted_iota(jnp.int32, (8, wide), 0)
    own = jnp.concatenate(
        [
            jnp.where(at == 1, gain_sum[:, g : g + wide], 0.0)
            + jnp.where(at == 2, gmlp[:, g : g + wide], 0.0)
            for g in range(0, gain.shape[1], wide)
        ],
        0,
    )
    own_ref[...] = own
    count = keep_ref.shape[0]
    send_ref[count] = own.astype(BF)
    tall = [small_ref[:, g : g + wide] for g in range(0, small_ref.shape[1], wide)]
    rest = (send_ref.shape[0] - count - 1) * half - len(tall) * small_ref.shape[0]
    tall = jnp.concatenate(tall + [jnp.zeros((rest, wide), F32)], 0)
    for j in range(count + 1, send_ref.shape[0]):
        send_ref[j] = tall[(j - count - 1) * half : (j - count) * half].astype(BF)
    for i in range(items):
        pick_rows(where, turn_ref.at[i], lhs_ref, i * lat, 2 * half, chips, bits)
    total = nn(lhs_ref[...], rhs_ref[...])
    for j in range(keep_ref.shape[0]):
        low = total[2 * j * half : (2 * j + 1) * half]
        high = total[(2 * j + 1) * half : (2 * j + 2) * half]
        keep_ref[j] = jnp.where(where[0] == 0, low, high).astype(BF)
        send_ref[j] = jnp.where(where[0] == 0, high, low).astype(BF)


def latents_back(da, db, gres, gmlps, gfar, small, latents, gain, w_query, score_scale, chips, bits, deps):
    _, lat, width = latents.shape
    items = da.shape[0]
    qk = w_query.shape[1]
    count = 2 ** len(bits)
    half = width // (count * chips * CORES)
    small_blocks = -(-small.size // (half * qk))
    return launch(
        functools.partial(latents_back_kernel, score_scale, chips, bits),
        "latents_back",
        SHORT,
        [(da, None), (db, None)]
        + [(g, None) for g in gres + gmlps]
        + [(a, None) for a in (gfar, small, latents, gain, w_query)],
        [
            ((items, lat, width + gfar.shape[2]), BF, None),
            ((count, half, qk), BF, None),
            ((count + 1 + small_blocks, half, qk), BF, None),
            ((half, qk), F32, None),
        ],
        scratch=[
            pltpu.VMEM((width // chips, items * lat), BF),
            pltpu.VMEM((items * lat, qk), BF),
            pltpu.VMEM((items, width, lat), BF),
        ],
        deps=deps,
    )


def fold_kernel(where, keep_ref, far_ref, *outs):
    half = keep_ref.shape[0] // 2
    if len(outs) == 1:
        outs[0][...] = keep_ref[0].astype(F32) + far_ref[0].astype(F32)
        return
    for spot, out in enumerate(outs):
        for j in range(half):
            at = spot * half + j
            out[j] = (keep_ref[at].astype(F32) + far_ref[at].astype(F32)).astype(BF)


def fold(keep, far, deps, micros=SHORT):
    if keep.shape[0] == 1:
        outs = [(keep.shape[1:], F32, None)]
    else:
        shape = (keep.shape[0] // 2,) + keep.shape[1:]
        outs = [(shape, BF, None), (shape, BF, None)]
    return launch(fold_kernel, "fold", micros, [(keep, None), (far, None)], outs, deps=deps)


def side_kernel(begin, where, far_ref, small_ref, own_ref, send_ref):
    rows, width = small_ref.shape
    tall = jnp.concatenate([far_ref[j].astype(F32) for j in range(begin, far_ref.shape[0])], 0)
    pieces = [tall[rows * g : rows * (g + 1)] for g in range(width // far_ref.shape[2])]
    own = small_ref[...] + jnp.concatenate(pieces, 1)
    own_ref[...] = own
    send_ref[...] = own.astype(BF)


def side_sum(far, small, begin, deps):
    return launch(
        functools.partial(side_kernel, begin),
        "side_sum",
        1,
        [(far, None), (small, None)],
        [(small.shape, F32, None), (small.shape, BF, None)],
        deps=deps,
    )


def join_kernel(
    langs, chips, bits, where, keep_ref, far_ref, own_ref, side_ref, qkeep_ref, qfar_ref, qown_ref,
    keep_out, send_out,
):
    count, rows, wide = keep_ref.shape
    qrows, qwide = qown_ref.shape

    def across(tall):
        return jnp.concatenate([tall[r : r + 8] for r in range(0, qrows, 8)], 1)

    own = own_ref[...] + side_ref[...].astype(F32)
    gains = across(qown_ref[...] + qfar_ref[count].astype(F32))
    at = lax.broadcasted_iota(jnp.int32, (8, qwide), 1)
    half = count // 2
    for j in range(count):
        spot = where[2] ^ flipped(j, bits)
        device = (spot * chips + where[1]) * CORES + where[0]
        byte_cut = pltpu.roll(own, own.shape[1] - device * rows, 1)[:, :qwide]
        lat_cut = pltpu.roll(gains, gains.shape[1] - device * qrows, 1)[:, :qwide]
        spare = jnp.where(at < rows, byte_cut[:8], 0.0)
        for n in range(1, langs // 8 + 1):
            piece = jnp.where(at < rows, byte_cut[8 * n : 8 * n + 8], 0.0)
            spare += pltpu.roll(piece, n * rows, 1)
        spare += pltpu.roll(jnp.where(at < qrows, lat_cut, 0.0), (langs // 8 + 1) * rows, 1)
        byte = keep_ref[j].astype(F32) + far_ref[j].astype(F32)
        query = across(qkeep_ref[j].astype(F32) + qfar_ref[j].astype(F32))
        out = keep_out if j < half else send_out
        below = jnp.concatenate([query, spare], 1)
        out[j % half] = jnp.concatenate([byte, below], 0).astype(BF)


def join(keep, far, own, side, qkeep, qfar, qown, langs, chips, bits, deps):
    count, rows, wide = keep.shape
    shape = (count // 2, rows + 8, wide)
    return launch(
        functools.partial(join_kernel, langs, chips, bits),
        "join",
        LONG,
        [(a, None) for a in (keep, far, own, side, qkeep, qfar, qown)],
        [(shape, BF, None), (shape, BF, None)],
        deps=deps,
    )


def part_kernel(
    where, keep_ref, far_ref, key_ref, value_ref, query_ref, lang_ref, gin_ref, glat_ref, gmlp_ref
):
    total = keep_ref[0].astype(F32) + far_ref[0].astype(F32)
    rows, qk = key_ref.shape
    qrows, langs = query_ref.shape[0], lang_ref.shape[0]
    key_ref[...] = total[:rows, :qk]
    value_ref[...] = total[:rows, qk:]
    for r in range(0, qrows, 8):
        query_ref[r : r + 8] = total[rows:, r // 8 * qk : (r // 8 + 1) * qk]
    spare = total[rows:, qrows // 8 * qk : (qrows // 8 + 1) * qk]
    groups = langs // 8
    for n in range(groups):
        lang_ref[8 * n : 8 * n + 8] = spare[:, n * rows : (n + 1) * rows]
    gin_ref[...] = spare[:1, groups * rows : (groups + 1) * rows]
    begin = (groups + 1) * rows
    glat_ref[...] = spare[1:2, begin : begin + qrows]
    gmlp_ref[...] = spare[2:3, begin : begin + qrows]


def part(keep, far, qk, qrows, langs, deps):
    rows, wide = keep.shape[1] - 8, keep.shape[2]
    shapes = [(rows, qk), (rows, wide - qk), (qrows, qk), (langs, rows)]
    shapes += [(1, rows), (1, qrows), (1, qrows)]
    return launch(
        part_kernel,
        "part",
        SHORT,
        [(keep, None), (far, None)],
        [(shape, F32, None) for shape in shapes],
        deps=deps,
    )


def last_kernel(where, keep_a, far_a, keep_b, far_b, up_ref, down_ref, out_ref):
    wide = up_ref.shape[1]
    split = out_ref.shape[1] // 2
    first = keep_a[0].astype(F32) + far_a[0].astype(F32)
    second = keep_b[0].astype(F32) + far_b[0].astype(F32)
    up_ref[...] = first[:, :wide]
    down_ref[...] = second[:, :wide]
    out_ref[:, :split] = first[:, wide:]
    out_ref[:, split:] = second[:, wide:]


def last(keep_a, far_a, keep_b, far_b, width, deps):
    shape = (keep_a.shape[1], width)
    return launch(
        last_kernel,
        "last",
        SHORT,
        [(a, None) for a in (keep_a, far_a, keep_b, far_b)],
        [(shape, F32, None)] * 3,
        deps=deps,
    )


def place_kernel(columns, where, *refs):
    count = len(columns)
    items = pl.num_programs(0) // 2
    ours = pl.program_id(0) // items == where[0]
    for n, (left, right) in enumerate(columns):
        out = refs[2 * count + n]
        wide = out.shape[2]
        own = refs[n][:, :, left : left + wide].astype(out.dtype)
        far = refs[count + n][:, :, right : right + wide].astype(out.dtype)
        out[...] = jnp.where(ours, own, far)
    refs[-1][...] = jnp.zeros_like(refs[-1])


def place(pairs, micros, deps):
    items = pairs[0][0].shape[0]
    one = lambda a: (1,) + a.shape[1:]
    rows = lambda p: p[0].shape[1]
    outs = [
        ((2 * items, rows(p), p[4]), p[5], block((1, rows(p), p[4]), lambda g: g))
        for p in pairs
    ]
    return launch(
        functools.partial(place_kernel, [(p[1], p[3]) for p in pairs]),
        "place",
        micros,
        [(a, block(one(a), lambda g: g % items)) for a in [p[0] for p in pairs]]
        + [(a, block(one(a), lambda g: g % items)) for a in [p[2] for p in pairs]],
        outs + [((8, 128), F32, None)],
        deps=deps,
        grid=2 * items,
        far=True,
    )


def swap(value, axis, bit):
    size = lax.axis_size(axis)
    return lax.ppermute(value, axis, [(i, i ^ bit) for i in range(size)])


def bits_of(size):
    return [2**t for t in range(size.bit_length() - 1)]


def halve(value, dim, axis, bit):
    mine = (lax.axis_index(axis) // bit) % 2
    keep = lax.dynamic_index_in_dim(value, mine, dim, keepdims=False)
    send = lax.dynamic_index_in_dim(value, 1 - mine, dim, keepdims=False)
    return (keep.astype(F32) + swap(send, axis, bit).astype(F32)).astype(BF)


def scatter_rows(value):
    spots, chips = lax.axis_size("batch"), lax.axis_size("seq") // CORES
    rows = value.shape[0] // (spots * chips * CORES)
    blocks = value.astype(BF).reshape(spots, chips, CORES, rows, value.shape[1])
    blocks = halve(blocks, 2, "seq", 1)
    for bit in bits_of(chips):
        rest = blocks.shape[2:]
        blocks = blocks.reshape((spots, blocks.shape[1] // 2, 2) + rest)
        blocks = halve(blocks, 2, "seq", CORES * bit)
    blocks = blocks[:, 0]
    for bit in bits_of(spots):
        blocks = blocks.reshape((blocks.shape[0] // 2, 2) + blocks.shape[1:])
        blocks = halve(blocks, 1, "batch", bit)
    return blocks[0].astype(F32)


def everywhere(value):
    for axis in ("seq", "batch"):
        for bit in bits_of(lax.axis_size(axis)):
            value = value + swap(value, axis, bit)
    return value


def merge(oa, ob):
    rows = oa.shape[0] - 2 * HEADS
    wide = rows // HEADS
    la = oa[rows : rows + HEADS].astype(F32) + oa[rows + HEADS :].astype(F32)
    lb = ob[rows : rows + HEADS].astype(F32) + ob[rows + HEADS :].astype(F32)
    top = jnp.maximum(la, lb)
    ea, eb = jnp.exp2(la - top), jnp.exp2(lb - top)
    total = ea + eb
    lse = top + jnp.log2(total)
    out = oa[:rows].astype(F32) * jnp.repeat(ea / total, wide, 0)
    out = out + ob[:rows].astype(F32) * jnp.repeat(eb / total, wide, 0)
    high = lse.astype(BF)
    return jnp.concatenate([out.astype(BF), high, (lse - high.astype(F32)).astype(BF)], 0)


def local(
    byte_inputs,
    language,
    lang_table,
    latents,
    gain_in,
    gain_lat,
    gain_mlp,
    w_query,
    w_key,
    w_value,
    w_out,
    w_up,
    w_down,
    cotangent,
):
    items = byte_inputs.shape[0] // CORES
    width_in, width_lat = byte_inputs.shape[2], latents.shape[2]
    lat, qk = latents.shape[1], w_query.shape[1]
    langs = lang_table.shape[0]
    score_scale = 1.0 / math.sqrt(qk // HEADS)
    score_unit = score_scale * math.log2(math.e)
    spots, chips = lax.axis_size("batch"), lax.axis_size("seq") // CORES
    devices = spots * chips * CORES
    seq_at, spot = lax.axis_index("seq"), lax.axis_index("batch")
    core, side = seq_at % CORES, seq_at // CORES
    device = spot * (chips * CORES) + seq_at
    chip_bits, spot_bits = bits_of(chips), bits_of(spots)
    rows_in, rows_lat = width_in // devices, width_lat // devices
    direct = (
        chips == 2
        and rows_in == langs + 8
        and rows_lat * qk == 8 * width_lat
        and width_lat % qk == 0
        and langs % 8 == 0
        and byte_inputs.shape[1] == lat
    )
    last_bit = chip_bits[-1]
    table = lang_table
    gain_in, gain_lat, gain_mlp = gain_in[None], gain_lat[None], gain_mlp[None]

    far = swap(pick_bytes(byte_inputs, items), "seq", 1)
    asked = queries(items, latents, gain_lat, w_query, ())
    asked = [asked[2 * i : 2 * i + 2] for i in range(items)]
    xns, kept, pairs, token = [], [], [], ()
    for item in range(items):
        ot, xn, k, kt, v = attend(
            item, items, language, byte_inputs, far, table, gain_in, w_key, w_value,
            asked[item][1], score_unit, token,
        )
        xns.append(xn)
        kept.append((k, kt, v))
        token = (k,)
        for bit in chip_bits[:-1]:
            ot = merge(ot, swap(ot, "seq", CORES * bit))
        pairs.append((ot, swap(ot, "seq", CORES * last_bit)))

    gact = act_back(cotangent, w_down, items, token)
    token = (gact,)
    sides, outs, dqkv, dkvs = [], None, (), []
    if direct:
        y_bit, z_bit, far_bit = spot_bits
        a_bits, b_bits = [y_bit, z_bit, far_bit], [z_bit, far_bit, y_bit]
        c_bits = [1] + [2 * b for b in a_bits]
        turned, turned_send = turn(xns, c_bits, token)
        turned_far = swap(turned_send, "seq", 1)
        part_c, far_pairs = None, []

    def back(item, deps):
        gatt, dot, lse = sides[item][2:5]
        return attend_back(
            item, items, *asked[item], *kept[item], gatt, lse, dot, score_unit, score_scale, dqkv, deps
        )

    byted = ()

    def back_bytes(item, deps):
        return bytes_back(
            item, items, language, byte_inputs, far, table, gain_in, w_key, w_value,
            dkvs[item], byted, deps,
        )

    for item in range(items):
        if item:
            *dqkv, dkv = back(item - 1, token)
            dkvs.append(dkv)
            byted = back_bytes(item - 1, ())
            token = (byted[2],)
            if direct:
                dkv_far = swap(dkv, "seq", 1)
                part_c = byte_part([(turned, item - 1, dkv)], part_c, 1, token)
                far_pairs.append((turned_far, item - 1, dkv_far))
                token = (part_c,)
        side_out = latent_side(
            item, items, last_bit, *pairs[item], latents, cotangent,
            gact, gain_mlp, w_out, w_up, w_down, outs, token,
        )
        outs = side_out[0]
        sides.append(side_out)
        token = (side_out[3],)
    outs_far = swap(outs, "seq", 1)

    pick = lambda at: [s[at] for s in sides]
    down = (pick(7), [cotangent] * items)
    up = (pick(6), pick(8))
    out = (pick(5), pick(9))

    if direct:
        split = width_lat // 2
        keep_a, send_a = latent_weights(
            [up, out], [(0, width_lat), (0, split)], chips, a_bits, "weights_a", token
        )
        far_a = swap(send_a, "seq", 1)
        keep_b, send_b = latent_weights(
            [down, out], [(0, width_lat), (split, split)], chips, b_bits, "weights_b",
            (keep_a,),
        )
        far_b = swap(send_b, "seq", 1)
        early = [a for pair in far_pairs for a in (pair[0], pair[2])]
        dqt, dkv = back(items - 1, (keep_b, *early))
        dkvs.append(dkv)
        dkv_far = swap(dkv, "seq", 1)
        dqt_far = swap(dqt, "seq", CORES)
        keep_a, send_a = fold(keep_a, far_a, (dqt, outs_far), 5)
        far_a = swap(send_a, "batch", a_bits[0])
        keep_b, send_b = fold(keep_b, far_b, (keep_a,), 5)
        far_b = swap(send_b, "batch", b_bits[0])
        part_c = byte_part(
            far_pairs + [(turned, items - 1, dkv)], part_c, SHORT, (keep_b,)
        )
        keep_c, send_c = byte_last(
            turned_far, items - 1, dkv_far, part_c, 2 ** len(c_bits), ()
        )
        far_c = swap(send_c, "seq", CORES)
        gown, gfar, small = back_bytes(items - 1, (keep_c,))
        glats, keep_q, send_q, own_q = latents_back(
            dqt, dqt_far, pick(1), pick(10), gfar, small, latents, gain_lat, w_query,
            score_scale, chips, a_bits, (),
        )
        glats_far = swap(glats, "seq", 1)
        far_q = swap(send_q, "seq", 1)
        own_s, send_s = side_sum(far_q, small, keep_q.shape[0] + 1, ())
        far_s = swap(send_s, "seq", CORES)
        keep_b, send_b = fold(keep_b, far_b, (own_s,))
        far_b = swap(send_b, "batch", b_bits[1])
        keep_a, send_a = fold(keep_a, far_a, (keep_b,))
        far_a = swap(send_a, "batch", a_bits[1])
        keep_c, send_c = join(
            keep_c, far_c, own_s, far_s, keep_q, far_q, own_q, langs, chips, a_bits,
            (keep_a,),
        )
        far_c = swap(send_c, "batch", a_bits[0])
        latents_out, grad_bytes, token = place(
            [
                (outs, 0, outs_far, 0, width_lat, BF),
                (gown, 0, glats_far, width_lat, width_in, F32),
            ],
            LONG,
            (keep_c,),
        )
        keep_c, send_c = fold(keep_c, far_c, (token,))
        far_c = swap(send_c, "batch", a_bits[1])
        keep_b, send_b = fold(keep_b, far_b, (keep_c,))
        far_b = swap(send_b, "batch", b_bits[2])
        keep_a, send_a = fold(keep_a, far_a, (keep_b,))
        far_a = swap(send_a, "batch", a_bits[2])
        grad_latents, token = place(
            [(glats, 0, glats_far, 0, width_lat, F32)], SHORT, (keep_a,)
        )
        keep_c, send_c = fold(keep_c, far_c, (token,))
        far_c = swap(send_c, "batch", a_bits[2])
        g_up, g_down, g_out = last(keep_a, far_a, keep_b, far_b, width_lat, (keep_c,))
        g_key, g_value, g_query, g_table, *gains = part(
            keep_c, far_c, qk, rows_lat, langs, ()
        )
        g_in, g_lat, g_mlp = [g[0] for g in gains]
    else:
        dqt, dkv = back(items - 1, token)
        dkvs.append(dkv)
        for bit in chip_bits:
            dqt = (dqt.astype(F32) + swap(dqt, "seq", CORES * bit).astype(F32)).astype(BF)
        gown, gfar, small = back_bytes(items - 1, ())
        gfar_far = swap(gfar, "seq", 1)
        own_cut = lambda a: lax.dynamic_slice_in_dim(a, core * items, items, 0)
        grad_q = (dqt.astype(F32) * score_scale).swapaxes(1, 2).astype(BF)
        unit, inverse = standardise(own_cut(latents).astype(F32))
        gln = lax.dot_general(
            grad_q, w_query, (((2,), (1,)), ((), ())), preferred_element_type=F32
        )
        glats = jnp.stack(pick(1)) + standardise_back(unit, inverse, gln * gain_lat)
        glats = glats.astype(BF)
        glats_far = swap(glats, "seq", 1)
        flat = lambda a: a.reshape(-1, a.shape[-1])
        share = 1.0 / chips
        g_query = scatter_rows(tn(flat((unit * gain_lat).astype(BF)), flat(grad_q)) * share)
        rows = lambda lefts, rights: scatter_rows(
            sum(nn(x, y) for x, y in zip(lefts, rights)) * share
        )
        g_down = rows(pick(7), own_cut(cotangent))
        g_up, g_out = rows(pick(6), pick(8)), rows(pick(5), pick(9))
        g_bytes = scatter_rows(sum(tn(xns[i], dkvs[i]) for i in range(items)))
        g_key, g_value = g_bytes[:, :qk], g_bytes[:, qk:]
        pad = ((0, 0), (0, width_lat - width_in))
        small = jnp.concatenate(
            [
                jnp.pad(small[: langs + 1], pad),
                jnp.sum(gln * unit, (0, 1))[None] * share,
                sum(pick(10)) * share,
            ],
            0,
        )
        small = everywhere(small)
        cut = lambda rows, count: lax.dynamic_slice_in_dim(rows, device * count, count, 1)
        g_table, g_in = cut(small[:langs], rows_in), cut(small[langs : langs + 1], rows_in)[0]
        g_lat, g_mlp = cut(small[langs + 1 :], rows_lat)
        latents_out, grad_bytes, grad_latents, _ = place(
            [
                (outs, 0, outs_far, 0, width_lat, BF),
                (gown, 0, gfar_far, 0, width_in, F32),
                (glats, 0, glats_far, 0, width_lat, F32),
            ],
            SHORT,
            (),
        )

    return (
        latents_out,
        grad_latents,
        grad_bytes,
        g_table,
        g_in,
        g_lat,
        g_mlp,
        g_query,
        g_key,
        g_value,
        g_out,
        g_up,
        g_down,
    )


def solution(mesh):
    return jax.shard_map(
        local,
        mesh=mesh,
        in_specs=(
            P("batch", "seq", None),
            P("batch"),
            P(),
            P("batch", None, None),
            P(),
            P(),
            P(),
            P(),
            P(),
            P(),
            P(),
            P(),
            P(),
            P("batch", None, None),
        ),
        out_specs=(
            P("batch", None, None),
            P("batch", None, None),
            P("batch", "seq", None),
            P(None, ("batch", "seq")),
            P(("batch", "seq")),
            P(("batch", "seq")),
            P(("batch", "seq")),
            P(("batch", "seq"), None),
            P(("batch", "seq"), None),
            P(("batch", "seq"), None),
            P(("batch", "seq"), None),
            P(("batch", "seq"), None),
            P(("batch", "seq"), None),
        ),
        check_vma=False,
    )
```

```python
import functools
import math

import jax
import jax.numpy as jnp
from jax import lax
from jax.experimental import pallas as pl
from jax.experimental.pallas import tpu as pltpu
from jax.sharding import PartitionSpec as P

HEADS = 8
CORES = 2
EPS = 1e-05
F32 = jnp.float32
BF = jnp.bfloat16
VMEM_LIMIT = 12 * 1024 * 1024
PEAK = 1.15e9
SHORT, LONG, AHEAD = 0.001, 40, 3


def nn(a, b):
    return lax.dot_general(a, b, (((1,), (0,)), ((), ())), preferred_element_type=F32)


def nt(a, b):
    return lax.dot_general(a, b, (((1,), (1,)), ((), ())), preferred_element_type=F32)


def tn(a, b):
    return lax.dot_general(a, b, (((0,), (0,)), ((), ())), preferred_element_type=F32)


def standardise(x):
    centre = x - jnp.mean(x, -1, keepdims=True)
    inverse = lax.rsqrt(jnp.mean(centre * centre, -1, keepdims=True) + EPS)
    return centre * inverse, inverse


def standardise_back(unit, inverse, grad):
    return inverse * (
        grad - jnp.mean(grad, -1, keepdims=True) - unit * jnp.mean(grad * unit, -1, keepdims=True)
    )


def block(shape, at):
    return pl.BlockSpec(shape, lambda g: (at(g),) + (0,) * (len(shape) - 1))


ANY = pl.BlockSpec(memory_space=pl.ANY)
FAST = pl.BlockSpec(memory_space=pltpu.VMEM)
FAR = pl.BlockSpec(memory_space=pltpu.HBM)
SCALARS = pl.BlockSpec(memory_space=pltpu.SMEM)


def launch(body, name, micros, ins, outs, scratch=(), deps=(), alias=None, grid=1, far=False):
    count, extra = len(ins), len(deps)
    ins = [
        (pltpu.with_memory_space_constraint(a, pltpu.HBM) if s is FAR else a, s) for a, s in ins
    ]

    def kernel(*refs):
        body(Where(), *refs[:count], *refs[count + extra :])

    return pl.pallas_call(
        kernel,
        grid=(grid,),
        in_specs=[FAST if s is None else s for _, s in ins] + [ANY] * extra,
        out_specs=[FAST if s is None else s for _, _, s in outs],
        scratch_shapes=list(scratch),
        out_shape=[
            (jax.ShapeDtypeStruct if s is None or not far else pltpu.HBM)(shape, dtype)
            for shape, dtype, s in outs
        ],
        input_output_aliases=alias or {},
        compiler_params=pltpu.CompilerParams(vmem_limit_bytes=VMEM_LIMIT),
        cost_estimate=pl.CostEstimate(
            flops=int(micros * PEAK), bytes_accessed=1, transcendentals=0
        ),
        name=name,
    )(*[a for a, _ in ins], *deps)


class Where:
    def __getitem__(self, at):
        if at == 2:
            return lax.axis_index("batch")
        return (lax.rem, lax.div)[at](lax.axis_index("seq"), CORES)


def pick_kernel(where, own_ref, out_ref, arrived):
    items = out_ref.shape[0]
    copy = pltpu.make_async_copy(
        own_ref.at[pl.ds((1 - where[0]) * items, items)], out_ref, arrived
    )
    copy.start()
    copy.wait()


def pick_bytes(own, items):
    return launch(
        pick_kernel,
        "pick_bytes",
        AHEAD,
        [(own, FAR)],
        [((items,) + own.shape[1:], BF, None)],
        scratch=[pltpu.SemaphoreType.DMA(())],
    )[0]


def query_kernel(where, lat_ref, gain_ref, wq_ref, *outs):
    items = len(outs) // 2
    for i in range(items):
        unit, _ = standardise(lat_ref[where[0] * items + i].astype(F32))
        rows = nn((unit * gain_ref[...]).astype(BF), wq_ref[...])
        outs[2 * i][...] = rows.astype(BF)
        outs[2 * i + 1][...] = rows.T.astype(BF)


def queries(items, latents, gain, w_query, deps):
    _, count, width = latents.shape
    qk = w_query.shape[1]
    return launch(
        query_kernel,
        "queries",
        2,
        [(latents, None), (gain, None), (w_query, None)],
        [((count, qk), BF, None), ((qk, count), BF, None)] * items,
        deps=deps,
    )


SPAN = 256


def head_span(h, wide):
    begin = h * wide // 128 * 128
    return begin, h * wide - begin


def language_row(table_ref, language):
    at = lax.broadcasted_iota(jnp.int32, table_ref.shape, 0)
    table = table_ref[...].astype(F32)
    return jnp.sum(jnp.where(at == language, table, 0.0), 0, keepdims=True)


PARTS = 2
SHARE = HEADS // PARTS


def heads_out(part, score_unit, k, v, qt, ot_ref):
    depth = qt.shape[0] // HEADS
    wide = v.shape[1] // SHARE
    at = lax.broadcasted_iota(jnp.int32, qt.shape, 0) // depth

    def score_of(h):
        return nn(k, jnp.where(at == part * SHARE + h, qt, jnp.zeros_like(qt)))

    def finish(h, weight, total):
        begin, ahead = head_span(h, wide)
        out = tn(v[:, begin : begin + SPAN], weight)[ahead : ahead + wide]
        ot_ref[h * wide : (h + 1) * wide] = (out * (1.0 / total)).astype(BF)

    lse = []
    coming, waiting = score_of(0), None
    for h in range(SHARE):
        score = coming * score_unit
        if h + 1 < SHARE:
            coming = score_of(h + 1)
        if waiting is not None:
            finish(*waiting)
        top = jnp.max(score, 0, keepdims=True)
        weight = jnp.exp2(score - top)
        total = jnp.sum(weight, 0, keepdims=True)
        lse.append(top + jnp.log2(total))
        waiting = (h, weight.astype(BF), total)
    finish(*waiting)
    lse = jnp.concatenate(lse, 0)
    high = lse.astype(BF).astype(F32)
    rest = jnp.zeros((16 - 2 * SHARE, lse.shape[1]), F32)
    ot_ref[SHARE * wide :] = jnp.concatenate([high, lse - high, rest], 0).astype(BF)


def attend_kernel(
    item, items, score_unit, where, lang_ref, own_ref, far_ref, table_ref, gain_ref, wk_ref,
    wv_ref, qt_ref, ot_ref, xn_ref, k_ref, kt_ref, v_ref,
):
    at = where[0] * items + item
    count = far_ref.shape[1]
    row = language_row(table_ref, lang_ref[at])
    gain = gain_ref[...]
    for part, rows in enumerate((own_ref[at], far_ref[item])):
        unit, _ = standardise(rows.astype(F32) + row)
        xn_ref[part * count : (part + 1) * count] = (unit * gain).astype(BF)
    xn = xn_ref[...]
    k = nn(xn, wk_ref[...]).astype(BF)
    k_ref[...] = k
    kt_ref[...] = k.T
    v = nn(xn, wv_ref[:, : v_ref.shape[1]]).astype(BF)
    v_ref[...] = v
    heads_out(0, score_unit, k, v, qt_ref[...], ot_ref)


def attend_more_kernel(part, score_unit, where, xn_ref, k_ref, wv_ref, qt_ref, ot_ref, v_ref):
    wide = v_ref.shape[1]
    v = nn(xn_ref[...], wv_ref[:, part * wide : (part + 1) * wide]).astype(BF)
    v_ref[...] = v
    heads_out(part, score_unit, k_ref[...], v, qt_ref[...], ot_ref)


def attend(
    item, items, language, own, far, table, gain, w_key, w_value, qt, score_unit, deps
):
    _, count, width = own.shape
    qk, lat = w_key.shape[1], qt.shape[1]
    wide = w_value.shape[1] // PARTS
    out = ((wide + 16, lat), BF, None)
    values = ((2 * count, wide), BF, None)
    first, xn, k, kt, v = launch(
        functools.partial(attend_kernel, item, items, score_unit),
        "attend",
        2.4,
        [(language, SCALARS)]
        + [(a, None) for a in (own, far, table, gain, w_key, w_value, qt)],
        [
            out,
            ((2 * count, width), BF, None),
            ((2 * count, qk), BF, None),
            ((qk, 2 * count), BF, None),
            values,
        ],
        deps=deps,
    )
    outs, vs = [first], [v]
    for part in range(1, PARTS):
        more, v = launch(
            functools.partial(attend_more_kernel, part, score_unit),
            "attend_more",
            1.9,
            [(a, None) for a in (xn, k, w_value, qt)],
            [out, values],
        )
        outs.append(more)
        vs.append(v)
    return outs, xn, k, kt, vs


def act_back_kernel(where, cot_ref, wd_ref, gact_ref):
    items = gact_ref.shape[0]
    for i in range(items):
        gact_ref[i] = nt(cot_ref[where[0] * items + i], wd_ref[...])


def act_back(cot, w_down, items, deps):
    return launch(
        act_back_kernel,
        "act_back",
        2.5,
        [(cot, None), (w_down, None)],
        [((items, cot.shape[1], w_down.shape[0]), F32, None)],
        deps=deps,
    )[0]


GELU_A = math.sqrt(2.0 / math.pi)
GELU_B = 0.044715


def part_sums(two):
    return two[:SHARE] + two[SHARE : 2 * SHARE]


def latent_kernel(
    item, items, bit, where, *refs
):
    oa_refs, ob_refs, refs = refs[:PARTS], refs[PARTS : 2 * PARTS], refs[2 * PARTS :]
    lat_ref, cot_ref, gact_ref, gain_ref, wo_ref, wu_ref, wd_ref = refs[:7]
    (
        outs_ref, gres_ref, gatt_ref, dot_ref, lse_ref, att_ref, hid_ref, act_ref, gpre_ref,
        glow_ref, ggain_ref,
    ) = refs[-11:]
    at = where[0] * items + item
    first = lax.rem(lax.div(where[1], bit), 2) == 0
    rows = gatt_ref.shape[0]
    wide = rows // HEADS
    ours, theirs = (
        jnp.concatenate(
            [part_sums(ref[rows // PARTS :].astype(F32)) for ref in refs_], 0
        )
        for refs_ in (oa_refs, ob_refs)
    )
    left = jnp.where(first, ours, theirs)
    right = jnp.where(first, theirs, ours)
    top = jnp.maximum(left, right)
    e_left, e_right = jnp.exp2(left - top), jnp.exp2(right - top)
    total = e_left + e_right
    lse_ref[...] = top + jnp.log2(total)
    scale = 1.0 / total
    e_left, e_right = e_left * scale, e_right * scale
    merged = []
    for h in range(HEADS):
        cut = slice(h % SHARE * wide, (h % SHARE + 1) * wide)
        a = oa_refs[h // SHARE][cut].astype(F32)
        b = ob_refs[h // SHARE][cut].astype(F32)
        low, high = jnp.where(first, a, b), jnp.where(first, b, a)
        merged.append(low * e_left[h : h + 1] + high * e_right[h : h + 1])
        att_ref[h * wide : (h + 1) * wide] = merged[-1].astype(BF)
    resid = lat_ref[at].astype(F32) + tn(att_ref[...], wo_ref[...])
    unit, inverse = standardise(resid)
    gain = gain_ref[...]
    hidden = (unit * gain).astype(BF)
    hid_ref[...] = hidden.T
    pre = nn(hidden, wu_ref[...])
    square = pre * pre
    slope = jnp.tanh(GELU_A * pre * (1.0 + GELU_B * square))
    act = (0.5 * pre * (1.0 + slope)).astype(BF)
    act_ref[...] = act.T
    outs_ref[item] = (resid + nn(act, wd_ref[...])).astype(BF)
    cot = cot_ref[at]
    gelu_slope = 0.5 * (1.0 + slope) + 0.5 * pre * (1.0 - slope * slope) * GELU_A * (
        1.0 + 3.0 * GELU_B * square
    )
    gpre = (gact_ref[item] * gelu_slope).astype(BF)
    gpre_ref[...] = gpre
    ghid = nt(gpre, wu_ref[...])
    ggain_ref[...] = jnp.sum(ghid * unit, 0, keepdims=True)
    gres = cot.astype(F32) + standardise_back(unit, inverse, ghid * gain)
    gres_ref[...] = gres
    glow = gres.astype(BF)
    glow_ref[...] = glow
    gatt_ref[...] = nt(wo_ref[...], glow).astype(BF)
    for h in range(HEADS):
        dot_ref[h : h + 1] = jnp.sum(
            gatt_ref[h * wide : (h + 1) * wide].astype(F32) * merged[h], 0, keepdims=True
        )


def latent_side(
    item, items, bit, oa, ob, latents, cot, gact, gain, w_out, w_up, w_down, before, deps
):
    total, lat, width = latents.shape
    feed = w_up.shape[1]
    ins = [(a, None) for a in (*oa, *ob, latents, cot, gact, gain, w_out, w_up, w_down)]
    alias = {}
    if before is not None:
        alias[len(ins)] = 0
        ins.append((before, None))
    return launch(
        functools.partial(latent_kernel, item, items, bit),
        "latent_side",
        7,
        ins,
        [
            ((items, lat, width), BF, None),
            ((lat, width), F32, None),
            ((width, lat), BF, None),
            ((HEADS, lat), F32, None),
            ((HEADS, lat), F32, None),
            ((width, lat), BF, None),
            ((width, lat), BF, None),
            ((feed, lat), BF, None),
            ((lat, feed), BF, None),
            ((lat, width), BF, None),
            ((1, width), F32, None),
        ],
        alias=alias,
        deps=deps,
    )


def flipped(at, bits):
    return sum(((at >> (len(bits) - 1 - t)) & 1) * bit for t, bit in enumerate(bits))


def pick_rows(where, source, lhs_ref, lane, rows, chips, bits):
    lat = source.shape[1]
    for j in range(2 ** len(bits)):
        spot = where[2] ^ flipped(j, bits)
        begin = pl.multiple_of((spot * chips + where[1]) * rows, 16)
        lhs_ref[j * rows : (j + 1) * rows, lane : lane + lat] = source[pl.ds(begin, rows)]


def latent_weights_kernel(plan, items, chips, bits, where, *refs):
    ins, keep_ref, send_ref, lhs_ref = refs[:-3], refs[-3], refs[-2], refs[-1]
    half = keep_ref.shape[1]
    column = 0
    for w, (begin, width) in enumerate(plan):
        lefts = ins[2 * items * w : 2 * items * w + items]
        rights = ins[2 * items * w + items : 2 * items * (w + 1)]
        total = 0.0
        for i in range(items):
            lat = lefts[i].shape[1]
            pick_rows(where, lefts[i], lhs_ref, i * lat, 2 * half, chips, bits)
            right = rights[i]
            if len(right.shape) == 3:
                right = right.at[where[0] * items + i]
            total += nn(lhs_ref[:, i * lat : (i + 1) * lat], right[:, begin : begin + width])
        out = slice(column, column + width)
        for j in range(keep_ref.shape[0]):
            low = total[2 * j * half : (2 * j + 1) * half]
            high = total[(2 * j + 1) * half : (2 * j + 2) * half]
            keep_ref[j, :, out] = jnp.where(where[0] == 0, low, high).astype(BF)
            send_ref[j, :, out] = jnp.where(where[0] == 0, high, low).astype(BF)
        column += width


def latent_weights(groups, plan, chips, bits, name, deps):
    items = len(groups[0][0])
    ins = []
    for lefts, rights in groups:
        ins += [(a, None) for a in lefts + rights]
    width, lat = groups[0][0][0].shape
    count = 2 ** len(bits)
    half = width // (count * chips * CORES)
    shape = (count, half, sum(w for _, w in plan))
    return launch(
        functools.partial(latent_weights_kernel, plan, items, chips, bits),
        name,
        SHORT,
        ins,
        [(shape, BF, None), (shape, BF, None)],
        scratch=[pltpu.VMEM((width // chips, items * lat), BF)],
        deps=deps,
    )


def attend_back_kernel(
    item, score_unit, score_scale, where, q_ref, qt_ref, k_ref, kt_ref, *refs
):
    v_refs, (gatt_ref, lse_ref, dot_ref) = refs[:PARTS], refs[PARTS : PARTS + 3]
    dqt_ref, dkv_ref, dvt_ref = refs[-3:]
    q, qt, k = q_ref[...], qt_ref[...], k_ref[...]
    qk = qt.shape[0]
    depth = qk // HEADS
    wide = gatt_ref.shape[0] // HEADS
    lat = qt.shape[1]
    at = lax.broadcasted_iota(jnp.int32, qt.shape, 0) // depth
    across = lax.broadcasted_iota(jnp.int32, q.shape, 1) // depth

    def begin_head(h):
        score = nn(k, jnp.where(at == h, qt, jnp.zeros_like(qt)))
        grad = gatt_ref[h * wide : (h + 1) * wide]
        begin, ahead = head_span(h % SHARE, wide)
        after = SPAN - ahead - wide
        pieces = [grad]
        if ahead:
            pieces = [jnp.zeros((ahead, lat), BF)] + pieces
        if after:
            pieces = pieces + [jnp.zeros((after, lat), BF)]
        values = v_refs[h // SHARE][:, begin : begin + SPAN]
        return score, grad, nn(values, jnp.concatenate(pieces, 0))

    def finish(h, grad, prob, grad_score):
        dvt_ref[h * wide : (h + 1) * wide] = nt(grad, prob).astype(BF)
        dqt_ref[item, h * depth : (h + 1) * depth] = nn(
            kt_ref[h * depth : (h + 1) * depth], grad_score
        ).astype(BF)
        return nn(grad_score, jnp.where(across == h, q, jnp.zeros_like(q)))

    dk = jnp.zeros(k.shape, F32)
    coming, waiting = begin_head(0), None
    for h in range(HEADS):
        score, grad, grad_prob = coming
        if h + 1 < HEADS:
            coming = begin_head(h + 1)
        if waiting is not None:
            dk += finish(*waiting)
        prob = jnp.exp2(score * score_unit - lse_ref[h : h + 1])
        grad_score = (prob * (grad_prob - dot_ref[h : h + 1])).astype(BF)
        waiting = (h, grad, prob.astype(BF), grad_score)
    dk += finish(*waiting)
    dkv_ref[:, :qk] = (dk * score_scale).astype(BF)
    dkv_ref[:, qk:] = dvt_ref[...].T


def attend_back(
    item, items, q, qt, k, kt, v, gatt, lse, dot, score_unit, score_scale, before, deps
):
    lat, qk = q.shape
    count, wide = v[0].shape[0], gatt.shape[0]
    ins = [(a, None) for a in (q, qt, k, kt, *v, gatt, lse, dot)]
    alias = {}
    for spot, array in enumerate(before):
        alias[len(ins)] = spot
        ins.append((array, None))
    return launch(
        functools.partial(attend_back_kernel, item, score_unit, score_scale),
        "attend_back",
        3.8 if item + 1 < items else SHORT,
        ins,
        [
            ((items, qk, lat), BF, None),
            ((count, qk + wide), BF, None),
        ],
        scratch=[pltpu.VMEM((wide, count), BF)],
        alias=alias,
        deps=deps,
    )


def turn_kernel(bits, where, *refs):
    xn_refs, (keep_ref, send_ref, all_ref) = refs[:-3], refs[-3:]
    count = 2 ** len(bits)
    rows = keep_ref.shape[1] // count
    mine = where[2] * 2 + where[1]
    for i, ref in enumerate(xn_refs):
        all_ref[i] = ref[...].astype(F32).T
    for i in range(len(xn_refs)):
        for out, core in ((keep_ref, where[0]), (send_ref, 1 - where[0])):
            for j in range(0, count, 2):
                pair = []
                for n in (j, j + 1):
                    spot = (mine ^ flipped(n, bits)) * CORES + core
                    begin = pl.multiple_of(spot * rows, 8)
                    pair.append(all_ref[i, pl.ds(begin, rows)])
                out[i, j * rows : (j + 2) * rows] = jnp.concatenate(pair, 0).astype(BF)


def turn(xns, bits, deps):
    count, width = xns[0].shape
    shape = (len(xns), width // CORES, count)
    return launch(
        functools.partial(turn_kernel, bits),
        "turn",
        3,
        [(a, None) for a in xns],
        [(shape, BF, None), (shape, BF, None)],
        scratch=[pltpu.VMEM((len(xns), width, count), F32)],
        deps=deps,
    )


def byte_part_kernel(spots, where, *refs):
    out_ref = refs[-1]
    total = refs[-2][...] if len(refs) % 2 == 0 else 0.0
    for n, spot in enumerate(spots):
        total += nn(refs[2 * n][spot], refs[2 * n + 1][...])
    out_ref[...] = total


def byte_part(pairs, before, micros, deps):
    ins = [(a, None) for turned, _, dkv in pairs for a in (turned, dkv)]
    alias = {}
    if before is not None:
        alias = {len(ins): 0}
        ins.append((before, None))
    shape = (pairs[0][0].shape[1], pairs[0][2].shape[1])
    return launch(
        functools.partial(byte_part_kernel, [p[1] for p in pairs]),
        "byte_part",
        micros,
        ins,
        [(shape, F32, None)],
        alias=alias,
        deps=deps,
    )[0]


def byte_last_kernel(spot, where, turned_ref, dkv_ref, before_ref, keep_ref, send_ref):
    total = before_ref[...] + nn(turned_ref[spot], dkv_ref[...])
    half, rows = keep_ref.shape[:2]
    for j in range(half):
        keep_ref[j] = total[j * rows : (j + 1) * rows].astype(BF)
        send_ref[j] = total[(half + j) * rows : (half + j + 1) * rows].astype(BF)


def byte_last(turned, spot, dkv, before, count, deps):
    shape = (count // 2, turned.shape[1] // count, dkv.shape[1])
    return launch(
        functools.partial(byte_last_kernel, spot),
        "byte_last",
        SHORT,
        [(turned, None), (dkv, None), (before, None)],
        [(shape, BF, None), (shape, BF, None)],
        deps=deps,
    )


def bytes_back_kernel(
    item, where, lang_ref, own_ref, far_ref, table_ref, gain_ref, wk_ref, wv_ref, dkv_ref, *refs
):
    gown_ref, gfar_ref, small_ref = refs[-3:]
    items, count = gfar_ref.shape[:2]
    qk = wk_ref.shape[1]
    langs = table_ref.shape[0]
    gain = gain_ref[...]
    language = lang_ref[where[0] * items + item]
    row = language_row(table_ref, language)
    grads = nt(dkv_ref[:, :qk], wk_ref[...]) + nt(dkv_ref[:, qk:], wv_ref[...])
    gain_sum = jnp.zeros_like(row)
    byte_sum = jnp.zeros_like(row)
    for part, rows, out in (
        (0, own_ref[where[0] * items + item], gown_ref),
        (1, far_ref[item], gfar_ref),
    ):
        unit, inverse = standardise(rows.astype(F32) + row)
        grad = grads[part * count : (part + 1) * count]
        gain_sum += jnp.sum(grad * unit, 0, keepdims=True)
        back = standardise_back(unit, inverse, grad * gain)
        byte_sum += jnp.sum(back, 0, keepdims=True)
        out[item] = back.astype(out.dtype)
    at = lax.broadcasted_iota(jnp.int32, small_ref.shape, 0)
    small = jnp.where(at == language, byte_sum, 0.0) + jnp.where(at == langs, gain_sum, 0.0)
    if item:
        small += refs[2][...]
    small_ref[...] = small


def bytes_back(
    item, items, language, own, far, table, gain, w_key, w_value, dkv, before, deps
):
    shape = far.shape
    ins = [(language, SCALARS)]
    ins += [(a, None) for a in (own, far, table, gain, w_key, w_value, dkv)]
    alias = {}
    if before:
        alias = {len(ins): 0, len(ins) + 1: 1}
        ins += [(a, None) for a in before]
    return launch(
        functools.partial(bytes_back_kernel, item),
        "bytes_back",
        2.5 if item + 1 < items else SHORT,
        ins,
        [
            (shape, F32, None),
            (shape, BF, None),
            ((table.shape[0] + 8, far.shape[2]), F32, None),
        ],
        alias=alias,
        deps=deps,
    )


def latents_back_kernel(
    score_scale, chips, bits, where, da_ref, db_ref, *refs
):
    items = da_ref.shape[0]
    gres_refs, gmlp_refs, refs = refs[:items], refs[items : 2 * items], refs[2 * items :]
    gfar_ref, small_ref, lat_ref, gain_ref, wq_ref = refs[:5]
    glat_ref, keep_ref, send_ref, own_ref = refs[5:9]
    lhs_ref, rhs_ref, turn_ref = refs[9:]
    lat = lat_ref.shape[1]
    gain = gain_ref[...]
    gain_sum = jnp.zeros_like(gain)
    half = keep_ref.shape[1]
    for i in range(items):
        total = (da_ref[i].astype(F32) + db_ref[i].astype(F32)) * score_scale
        grad = total.T.astype(BF)
        rhs_ref[i * lat : (i + 1) * lat] = grad
        unit, inverse = standardise(lat_ref[where[0] * items + i].astype(F32))
        turn_ref[i] = (unit * gain).astype(BF).T
        gln = nt(grad, wq_ref[...])
        gain_sum += jnp.sum(gln * unit, 0, keepdims=True)
        out = gres_refs[i][...] + standardise_back(unit, inverse, gln * gain)
        glat_ref[i, :, : out.shape[1]] = out.astype(BF)
        glat_ref[i, :, out.shape[1] :] = gfar_ref[i]
    gmlp = functools.reduce(jnp.add, [r[...] for r in gmlp_refs])
    wide = own_ref.shape[1]
    at = lax.broadcasted_iota(jnp.int32, (8, wide), 0)
    own = jnp.concatenate(
        [
            jnp.where(at == 1, gain_sum[:, g : g + wide], 0.0)
            + jnp.where(at == 2, gmlp[:, g : g + wide], 0.0)
            for g in range(0, gain.shape[1], wide)
        ],
        0,
    )
    own_ref[...] = own
    count = keep_ref.shape[0]
    send_ref[count] = own.astype(BF)
    tall = [small_ref[:, g : g + wide] for g in range(0, small_ref.shape[1], wide)]
    rest = (send_ref.shape[0] - count - 1) * half - len(tall) * small_ref.shape[0]
    tall = jnp.concatenate(tall + [jnp.zeros((rest, wide), F32)], 0)
    for j in range(count + 1, send_ref.shape[0]):
        send_ref[j] = tall[(j - count - 1) * half : (j - count) * half].astype(BF)
    for i in range(items):
        pick_rows(where, turn_ref.at[i], lhs_ref, i * lat, 2 * half, chips, bits)
    total = nn(lhs_ref[...], rhs_ref[...])
    for j in range(keep_ref.shape[0]):
        low = total[2 * j * half : (2 * j + 1) * half]
        high = total[(2 * j + 1) * half : (2 * j + 2) * half]
        keep_ref[j] = jnp.where(where[0] == 0, low, high).astype(BF)
        send_ref[j] = jnp.where(where[0] == 0, high, low).astype(BF)


def latents_back(da, db, gres, gmlps, gfar, small, latents, gain, w_query, score_scale, chips, bits, deps):
    _, lat, width = latents.shape
    items = da.shape[0]
    qk = w_query.shape[1]
    count = 2 ** len(bits)
    half = width // (count * chips * CORES)
    small_blocks = -(-small.size // (half * qk))
    return launch(
        functools.partial(latents_back_kernel, score_scale, chips, bits),
        "latents_back",
        SHORT,
        [(da, None), (db, None)]
        + [(g, None) for g in gres + gmlps]
        + [(a, None) for a in (gfar, small, latents, gain, w_query)],
        [
            ((items, lat, width + gfar.shape[2]), BF, None),
            ((count, half, qk), BF, None),
            ((count + 1 + small_blocks, half, qk), BF, None),
            ((half, qk), F32, None),
        ],
        scratch=[
            pltpu.VMEM((width // chips, items * lat), BF),
            pltpu.VMEM((items * lat, qk), BF),
            pltpu.VMEM((items, width, lat), BF),
        ],
        deps=deps,
    )


def fold_kernel(where, keep_ref, far_ref, *outs):
    half = keep_ref.shape[0] // 2
    if len(outs) == 1:
        outs[0][...] = keep_ref[0].astype(F32) + far_ref[0].astype(F32)
        return
    for spot, out in enumerate(outs):
        for j in range(half):
            at = spot * half + j
            out[j] = (keep_ref[at].astype(F32) + far_ref[at].astype(F32)).astype(BF)


def fold(keep, far, deps, micros=SHORT):
    if keep.shape[0] == 1:
        outs = [(keep.shape[1:], F32, None)]
    else:
        shape = (keep.shape[0] // 2,) + keep.shape[1:]
        outs = [(shape, BF, None), (shape, BF, None)]
    return launch(fold_kernel, "fold", micros, [(keep, None), (far, None)], outs, deps=deps)


def side_kernel(begin, where, far_ref, small_ref, own_ref, send_ref):
    rows, width = small_ref.shape
    tall = jnp.concatenate([far_ref[j].astype(F32) for j in range(begin, far_ref.shape[0])], 0)
    pieces = [tall[rows * g : rows * (g + 1)] for g in range(width // far_ref.shape[2])]
    own = small_ref[...] + jnp.concatenate(pieces, 1)
    own_ref[...] = own
    send_ref[...] = own.astype(BF)


def side_sum(far, small, begin, deps):
    return launch(
        functools.partial(side_kernel, begin),
        "side_sum",
        1,
        [(far, None), (small, None)],
        [(small.shape, F32, None), (small.shape, BF, None)],
        deps=deps,
    )


def join_kernel(
    langs, chips, bits, where, keep_ref, far_ref, own_ref, side_ref, qkeep_ref, qfar_ref, qown_ref,
    keep_out, send_out,
):
    count, rows, wide = keep_ref.shape
    qrows, qwide = qown_ref.shape

    def across(tall):
        return jnp.concatenate([tall[r : r + 8] for r in range(0, qrows, 8)], 1)

    own = own_ref[...] + side_ref[...].astype(F32)
    gains = across(qown_ref[...] + qfar_ref[count].astype(F32))
    at = lax.broadcasted_iota(jnp.int32, (8, qwide), 1)
    half = count // 2
    for j in range(count):
        spot = where[2] ^ flipped(j, bits)
        device = (spot * chips + where[1]) * CORES + where[0]
        byte_cut = pltpu.roll(own, own.shape[1] - device * rows, 1)[:, :qwide]
        lat_cut = pltpu.roll(gains, gains.shape[1] - device * qrows, 1)[:, :qwide]
        spare = jnp.where(at < rows, byte_cut[:8], 0.0)
        for n in range(1, langs // 8 + 1):
            piece = jnp.where(at < rows, byte_cut[8 * n : 8 * n + 8], 0.0)
            spare += pltpu.roll(piece, n * rows, 1)
        spare += pltpu.roll(jnp.where(at < qrows, lat_cut, 0.0), (langs // 8 + 1) * rows, 1)
        byte = keep_ref[j].astype(F32) + far_ref[j].astype(F32)
        query = across(qkeep_ref[j].astype(F32) + qfar_ref[j].astype(F32))
        out = keep_out if j < half else send_out
        below = jnp.concatenate([query, spare], 1)
        out[j % half] = jnp.concatenate([byte, below], 0).astype(BF)


def join(keep, far, own, side, qkeep, qfar, qown, langs, chips, bits, deps):
    count, rows, wide = keep.shape
    shape = (count // 2, rows + 8, wide)
    return launch(
        functools.partial(join_kernel, langs, chips, bits),
        "join",
        LONG,
        [(a, None) for a in (keep, far, own, side, qkeep, qfar, qown)],
        [(shape, BF, None), (shape, BF, None)],
        deps=deps,
    )


def part_kernel(
    where, keep_ref, far_ref, key_ref, value_ref, query_ref, lang_ref, gin_ref, glat_ref, gmlp_ref
):
    total = keep_ref[0].astype(F32) + far_ref[0].astype(F32)
    rows, qk = key_ref.shape
    qrows, langs = query_ref.shape[0], lang_ref.shape[0]
    key_ref[...] = total[:rows, :qk]
    value_ref[...] = total[:rows, qk:]
    for r in range(0, qrows, 8):
        query_ref[r : r + 8] = total[rows:, r // 8 * qk : (r // 8 + 1) * qk]
    spare = total[rows:, qrows // 8 * qk : (qrows // 8 + 1) * qk]
    groups = langs // 8
    for n in range(groups):
        lang_ref[8 * n : 8 * n + 8] = spare[:, n * rows : (n + 1) * rows]
    gin_ref[...] = spare[:1, groups * rows : (groups + 1) * rows]
    begin = (groups + 1) * rows
    glat_ref[...] = spare[1:2, begin : begin + qrows]
    gmlp_ref[...] = spare[2:3, begin : begin + qrows]


def part(keep, far, qk, qrows, langs, deps):
    rows, wide = keep.shape[1] - 8, keep.shape[2]
    shapes = [(rows, qk), (rows, wide - qk), (qrows, qk), (langs, rows)]
    shapes += [(1, rows), (1, qrows), (1, qrows)]
    return launch(
        part_kernel,
        "part",
        SHORT,
        [(keep, None), (far, None)],
        [(shape, F32, None) for shape in shapes],
        deps=deps,
    )


def last_kernel(where, keep_a, far_a, keep_b, far_b, up_ref, down_ref, out_ref):
    wide = up_ref.shape[1]
    split = out_ref.shape[1] // 2
    first = keep_a[0].astype(F32) + far_a[0].astype(F32)
    second = keep_b[0].astype(F32) + far_b[0].astype(F32)
    up_ref[...] = first[:, :wide]
    down_ref[...] = second[:, :wide]
    out_ref[:, :split] = first[:, wide:]
    out_ref[:, split:] = second[:, wide:]


def last(keep_a, far_a, keep_b, far_b, width, deps):
    shape = (keep_a.shape[1], width)
    return launch(
        last_kernel,
        "last",
        SHORT,
        [(a, None) for a in (keep_a, far_a, keep_b, far_b)],
        [(shape, F32, None)] * 3,
        deps=deps,
    )


def place_kernel(columns, where, *refs):
    count = len(columns)
    items = pl.num_programs(0) // 2
    ours = pl.program_id(0) // items == where[0]
    for n, (left, right) in enumerate(columns):
        out = refs[2 * count + n]
        wide = out.shape[2]
        own = refs[n][:, :, left : left + wide].astype(out.dtype)
        far = refs[count + n][:, :, right : right + wide].astype(out.dtype)
        out[...] = jnp.where(ours, own, far)
    refs[-1][...] = jnp.zeros_like(refs[-1])


def place(pairs, micros, deps):
    items = pairs[0][0].shape[0]
    one = lambda a: (1,) + a.shape[1:]
    rows = lambda p: p[0].shape[1]
    outs = [
        ((2 * items, rows(p), p[4]), p[5], block((1, rows(p), p[4]), lambda g: g))
        for p in pairs
    ]
    return launch(
        functools.partial(place_kernel, [(p[1], p[3]) for p in pairs]),
        "place",
        micros,
        [(a, block(one(a), lambda g: g % items)) for a in [p[0] for p in pairs]]
        + [(a, block(one(a), lambda g: g % items)) for a in [p[2] for p in pairs]],
        outs + [((8, 128), F32, None)],
        deps=deps,
        grid=2 * items,
        far=True,
    )


def swap(value, axis, bit):
    size = lax.axis_size(axis)
    return lax.ppermute(value, axis, [(i, i ^ bit) for i in range(size)])


def bits_of(size):
    return [2**t for t in range(size.bit_length() - 1)]


def halve(value, dim, axis, bit):
    mine = (lax.axis_index(axis) // bit) % 2
    keep = lax.dynamic_index_in_dim(value, mine, dim, keepdims=False)
    send = lax.dynamic_index_in_dim(value, 1 - mine, dim, keepdims=False)
    return (keep.astype(F32) + swap(send, axis, bit).astype(F32)).astype(BF)


def scatter_rows(value):
    spots, chips = lax.axis_size("batch"), lax.axis_size("seq") // CORES
    rows = value.shape[0] // (spots * chips * CORES)
    blocks = value.astype(BF).reshape(spots, chips, CORES, rows, value.shape[1])
    blocks = halve(blocks, 2, "seq", 1)
    for bit in bits_of(chips):
        rest = blocks.shape[2:]
        blocks = blocks.reshape((spots, blocks.shape[1] // 2, 2) + rest)
        blocks = halve(blocks, 2, "seq", CORES * bit)
    blocks = blocks[:, 0]
    for bit in bits_of(spots):
        blocks = blocks.reshape((blocks.shape[0] // 2, 2) + blocks.shape[1:])
        blocks = halve(blocks, 1, "batch", bit)
    return blocks[0].astype(F32)


def everywhere(value):
    for axis in ("seq", "batch"):
        for bit in bits_of(lax.axis_size(axis)):
            value = value + swap(value, axis, bit)
    return value


def merge(oa, ob):
    rows = oa.shape[0] - 16
    wide = rows // SHARE
    la, lb = part_sums(oa[rows:].astype(F32)), part_sums(ob[rows:].astype(F32))
    top = jnp.maximum(la, lb)
    ea, eb = jnp.exp2(la - top), jnp.exp2(lb - top)
    total = ea + eb
    lse = top + jnp.log2(total)
    out = oa[:rows].astype(F32) * jnp.repeat(ea / total, wide, 0)
    out = out + ob[:rows].astype(F32) * jnp.repeat(eb / total, wide, 0)
    high = lse.astype(BF)
    low = (lse - high.astype(F32)).astype(BF)
    rest = jnp.zeros((16 - 2 * SHARE, lse.shape[1]), BF)
    return jnp.concatenate([out.astype(BF), high, low, rest], 0)


def local(
    byte_inputs,
    language,
    lang_table,
    latents,
    gain_in,
    gain_lat,
    gain_mlp,
    w_query,
    w_key,
    w_value,
    w_out,
    w_up,
    w_down,
    cotangent,
):
    items = byte_inputs.shape[0] // CORES
    width_in, width_lat = byte_inputs.shape[2], latents.shape[2]
    lat, qk = latents.shape[1], w_query.shape[1]
    langs = lang_table.shape[0]
    score_scale = 1.0 / math.sqrt(qk // HEADS)
    score_unit = score_scale * math.log2(math.e)
    spots, chips = lax.axis_size("batch"), lax.axis_size("seq") // CORES
    devices = spots * chips * CORES
    seq_at, spot = lax.axis_index("seq"), lax.axis_index("batch")
    core, side = seq_at % CORES, seq_at // CORES
    device = spot * (chips * CORES) + seq_at
    chip_bits, spot_bits = bits_of(chips), bits_of(spots)
    rows_in, rows_lat = width_in // devices, width_lat // devices
    direct = (
        chips == 2
        and rows_in == langs + 8
        and rows_lat * qk == 8 * width_lat
        and width_lat % qk == 0
        and langs % 8 == 0
        and byte_inputs.shape[1] == lat
    )
    last_bit = chip_bits[-1]
    table = lang_table
    gain_in, gain_lat, gain_mlp = gain_in[None], gain_lat[None], gain_mlp[None]

    far = swap(pick_bytes(byte_inputs, items), "seq", 1)
    asked = queries(items, latents, gain_lat, w_query, ())
    asked = [asked[2 * i : 2 * i + 2] for i in range(items)]
    xns, kept, pairs, token = [], [], [], ()
    for item in range(items):
        ots, xn, k, kt, v = attend(
            item, items, language, byte_inputs, far, table, gain_in, w_key, w_value,
            asked[item][1], score_unit, token,
        )
        xns.append(xn)
        kept.append((k, kt, v))
        token = (v[-1],)
        for bit in chip_bits[:-1]:
            ots = [merge(ot, swap(ot, "seq", CORES * bit)) for ot in ots]
        pairs.append((ots, [swap(ot, "seq", CORES * last_bit) for ot in ots]))

    gact = act_back(cotangent, w_down, items, token)
    token = (gact,)
    sides, outs, dqkv, dkvs = [], None, (), []
    if direct:
        y_bit, z_bit, far_bit = spot_bits
        a_bits, b_bits = [y_bit, z_bit, far_bit], [z_bit, far_bit, y_bit]
        c_bits = [1] + [2 * b for b in a_bits]
        turned, turned_send = turn(xns, c_bits, token)
        turned_far = swap(turned_send, "seq", 1)
        part_c, far_pairs = None, []

    def back(item, deps):
        gatt, dot, lse = sides[item][2:5]
        return attend_back(
            item, items, *asked[item], *kept[item], gatt, lse, dot, score_unit, score_scale, dqkv, deps
        )

    byted = ()

    def back_bytes(item, deps):
        return bytes_back(
            item, items, language, byte_inputs, far, table, gain_in, w_key, w_value,
            dkvs[item], byted, deps,
        )

    for item in range(items):
        if item:
            *dqkv, dkv = back(item - 1, token)
            dkvs.append(dkv)
            byted = back_bytes(item - 1, ())
            token = (byted[2],)
            if direct:
                dkv_far = swap(dkv, "seq", 1)
                part_c = byte_part([(turned, item - 1, dkv)], part_c, 1, token)
                far_pairs.append((turned_far, item - 1, dkv_far))
                token = (part_c,)
        side_out = latent_side(
            item, items, last_bit, *pairs[item], latents, cotangent,
            gact, gain_mlp, w_out, w_up, w_down, outs, token,
        )
        outs = side_out[0]
        sides.append(side_out)
        token = (side_out[3],)
    outs_far = swap(outs, "seq", 1)

    pick = lambda at: [s[at] for s in sides]
    down = (pick(7), [cotangent] * items)
    up = (pick(6), pick(8))
    out = (pick(5), pick(9))

    if direct:
        split = width_lat // 2
        keep_a, send_a = latent_weights(
            [up, out], [(0, width_lat), (0, split)], chips, a_bits, "weights_a", token
        )
        far_a = swap(send_a, "seq", 1)
        keep_b, send_b = latent_weights(
            [down, out], [(0, width_lat), (split, split)], chips, b_bits, "weights_b",
            (keep_a,),
        )
        far_b = swap(send_b, "seq", 1)
        early = [a for pair in far_pairs for a in (pair[0], pair[2])]
        dqt, dkv = back(items - 1, (keep_b, *early))
        dkvs.append(dkv)
        dkv_far = swap(dkv, "seq", 1)
        dqt_far = swap(dqt, "seq", CORES)
        keep_a, send_a = fold(keep_a, far_a, (dqt, outs_far), 5)
        far_a = swap(send_a, "batch", a_bits[0])
        keep_b, send_b = fold(keep_b, far_b, (keep_a,), 5)
        far_b = swap(send_b, "batch", b_bits[0])
        part_c = byte_part(
            far_pairs + [(turned, items - 1, dkv)], part_c, SHORT, (keep_b,)
        )
        keep_c, send_c = byte_last(
            turned_far, items - 1, dkv_far, part_c, 2 ** len(c_bits), ()
        )
        far_c = swap(send_c, "seq", CORES)
        gown, gfar, small = back_bytes(items - 1, (keep_c,))
        glats, keep_q, send_q, own_q = latents_back(
            dqt, dqt_far, pick(1), pick(10), gfar, small, latents, gain_lat, w_query,
            score_scale, chips, a_bits, (),
        )
        glats_far = swap(glats, "seq", 1)
        far_q = swap(send_q, "seq", 1)
        own_s, send_s = side_sum(far_q, small, keep_q.shape[0] + 1, ())
        far_s = swap(send_s, "seq", CORES)
        keep_b, send_b = fold(keep_b, far_b, (own_s,))
        far_b = swap(send_b, "batch", b_bits[1])
        keep_a, send_a = fold(keep_a, far_a, (keep_b,))
        far_a = swap(send_a, "batch", a_bits[1])
        keep_c, send_c = join(
            keep_c, far_c, own_s, far_s, keep_q, far_q, own_q, langs, chips, a_bits,
            (keep_a,),
        )
        far_c = swap(send_c, "batch", a_bits[0])
        latents_out, grad_bytes, token = place(
            [
                (outs, 0, outs_far, 0, width_lat, BF),
                (gown, 0, glats_far, width_lat, width_in, F32),
            ],
            LONG,
            (keep_c,),
        )
        keep_c, send_c = fold(keep_c, far_c, (token,))
        far_c = swap(send_c, "batch", a_bits[1])
        keep_b, send_b = fold(keep_b, far_b, (keep_c,))
        far_b = swap(send_b, "batch", b_bits[2])
        keep_a, send_a = fold(keep_a, far_a, (keep_b,))
        far_a = swap(send_a, "batch", a_bits[2])
        grad_latents, token = place(
            [(glats, 0, glats_far, 0, width_lat, F32)], SHORT, (keep_a,)
        )
        keep_c, send_c = fold(keep_c, far_c, (token,))
        far_c = swap(send_c, "batch", a_bits[2])
        g_up, g_down, g_out = last(keep_a, far_a, keep_b, far_b, width_lat, (keep_c,))
        g_key, g_value, g_query, g_table, *gains = part(
            keep_c, far_c, qk, rows_lat, langs, ()
        )
        g_in, g_lat, g_mlp = [g[0] for g in gains]
    else:
        dqt, dkv = back(items - 1, token)
        dkvs.append(dkv)
        for bit in chip_bits:
            dqt = (dqt.astype(F32) + swap(dqt, "seq", CORES * bit).astype(F32)).astype(BF)
        gown, gfar, small = back_bytes(items - 1, ())
        gfar_far = swap(gfar, "seq", 1)
        own_cut = lambda a: lax.dynamic_slice_in_dim(a, core * items, items, 0)
        grad_q = (dqt.astype(F32) * score_scale).swapaxes(1, 2).astype(BF)
        unit, inverse = standardise(own_cut(latents).astype(F32))
        gln = lax.dot_general(
            grad_q, w_query, (((2,), (1,)), ((), ())), preferred_element_type=F32
        )
        glats = jnp.stack(pick(1)) + standardise_back(unit, inverse, gln * gain_lat)
        glats = glats.astype(BF)
        glats_far = swap(glats, "seq", 1)
        flat = lambda a: a.reshape(-1, a.shape[-1])
        share = 1.0 / chips
        g_query = scatter_rows(tn(flat((unit * gain_lat).astype(BF)), flat(grad_q)) * share)
        rows = lambda lefts, rights: scatter_rows(
            sum(nn(x, y) for x, y in zip(lefts, rights)) * share
        )
        g_down = rows(pick(7), own_cut(cotangent))
        g_up, g_out = rows(pick(6), pick(8)), rows(pick(5), pick(9))
        g_bytes = scatter_rows(sum(tn(xns[i], dkvs[i]) for i in range(items)))
        g_key, g_value = g_bytes[:, :qk], g_bytes[:, qk:]
        pad = ((0, 0), (0, width_lat - width_in))
        small = jnp.concatenate(
            [
                jnp.pad(small[: langs + 1], pad),
                jnp.sum(gln * unit, (0, 1))[None] * share,
                sum(pick(10)) * share,
            ],
            0,
        )
        small = everywhere(small)
        cut = lambda rows, count: lax.dynamic_slice_in_dim(rows, device * count, count, 1)
        g_table, g_in = cut(small[:langs], rows_in), cut(small[langs : langs + 1], rows_in)[0]
        g_lat, g_mlp = cut(small[langs + 1 :], rows_lat)
        latents_out, grad_bytes, grad_latents, _ = place(
            [
                (outs, 0, outs_far, 0, width_lat, BF),
                (gown, 0, gfar_far, 0, width_in, F32),
                (glats, 0, glats_far, 0, width_lat, F32),
            ],
            SHORT,
            (),
        )

    return (
        latents_out,
        grad_latents,
        grad_bytes,
        g_table,
        g_in,
        g_lat,
        g_mlp,
        g_query,
        g_key,
        g_value,
        g_out,
        g_up,
        g_down,
    )


def solution(mesh):
    return jax.shard_map(
        local,
        mesh=mesh,
        in_specs=(
            P("batch", "seq", None),
            P("batch"),
            P(),
            P("batch", None, None),
            P(),
            P(),
            P(),
            P(),
            P(),
            P(),
            P(),
            P(),
            P(),
            P("batch", None, None),
        ),
        out_specs=(
            P("batch", None, None),
            P("batch", None, None),
            P("batch", "seq", None),
            P(None, ("batch", "seq")),
            P(("batch", "seq")),
            P(("batch", "seq")),
            P(("batch", "seq")),
            P(("batch", "seq"), None),
            P(("batch", "seq"), None),
            P(("batch", "seq"), None),
            P(("batch", "seq"), None),
            P(("batch", "seq"), None),
            P(("batch", "seq"), None),
        ),
        check_vma=False,
    )
```

```python
import functools
import math

import jax
import jax.numpy as jnp
from jax import lax
from jax.experimental import pallas as pl
from jax.experimental.pallas import tpu as pltpu
from jax.sharding import PartitionSpec as P

HEADS = 8
CORES = 2
EPS = 1e-05
F32 = jnp.float32
BF = jnp.bfloat16
VMEM_LIMIT = 12 * 1024 * 1024
PEAK = 1.15e9
SHORT, LONG, AHEAD = 0.001, 40, 3


def nn(a, b):
    return lax.dot_general(a, b, (((1,), (0,)), ((), ())), preferred_element_type=F32)


def nt(a, b):
    return lax.dot_general(a, b, (((1,), (1,)), ((), ())), preferred_element_type=F32)


def tn(a, b):
    return lax.dot_general(a, b, (((0,), (0,)), ((), ())), preferred_element_type=F32)


def standardise(x):
    centre = x - jnp.mean(x, -1, keepdims=True)
    inverse = lax.rsqrt(jnp.mean(centre * centre, -1, keepdims=True) + EPS)
    return centre * inverse, inverse


def standardise_back(unit, inverse, grad):
    return inverse * (
        grad - jnp.mean(grad, -1, keepdims=True) - unit * jnp.mean(grad * unit, -1, keepdims=True)
    )


def block(shape, at):
    return pl.BlockSpec(shape, lambda g: (at(g),) + (0,) * (len(shape) - 1))


ANY = pl.BlockSpec(memory_space=pl.ANY)
FAST = pl.BlockSpec(memory_space=pltpu.VMEM)
FAR = pl.BlockSpec(memory_space=pltpu.HBM)
SCALARS = pl.BlockSpec(memory_space=pltpu.SMEM)


def launch(body, name, micros, ins, outs, scratch=(), deps=(), alias=None, grid=1, far=False):
    count, extra = len(ins), len(deps)
    ins = [
        (pltpu.with_memory_space_constraint(a, pltpu.HBM) if s is FAR else a, s) for a, s in ins
    ]

    def kernel(*refs):
        body(Where(), *refs[:count], *refs[count + extra :])

    return pl.pallas_call(
        kernel,
        grid=(grid,),
        in_specs=[FAST if s is None else s for _, s in ins] + [ANY] * extra,
        out_specs=[FAST if s is None else s for _, _, s in outs],
        scratch_shapes=list(scratch),
        out_shape=[
            (jax.ShapeDtypeStruct if s is None or not far else pltpu.HBM)(shape, dtype)
            for shape, dtype, s in outs
        ],
        input_output_aliases=alias or {},
        compiler_params=pltpu.CompilerParams(vmem_limit_bytes=VMEM_LIMIT),
        cost_estimate=pl.CostEstimate(
            flops=int(micros * PEAK), bytes_accessed=1, transcendentals=0
        ),
        name=name,
    )(*[a for a, _ in ins], *deps)


class Where:
    def __getitem__(self, at):
        if at == 2:
            return lax.axis_index("batch")
        return (lax.rem, lax.div)[at](lax.axis_index("seq"), CORES)


def pick_kernel(where, own_ref, out_ref, arrived):
    items = out_ref.shape[0]
    copy = pltpu.make_async_copy(
        own_ref.at[pl.ds((1 - where[0]) * items, items)], out_ref, arrived
    )
    copy.start()
    copy.wait()


def pick_bytes(own, items):
    return launch(
        pick_kernel,
        "pick_bytes",
        AHEAD,
        [(own, FAR)],
        [((items,) + own.shape[1:], BF, None)],
        scratch=[pltpu.SemaphoreType.DMA(())],
    )[0]


def query_kernel(where, lat_ref, gain_ref, wq_ref, *outs):
    items = len(outs) // 2
    for i in range(items):
        unit, _ = standardise(lat_ref[where[0] * items + i].astype(F32))
        rows = nn((unit * gain_ref[...]).astype(BF), wq_ref[...])
        outs[2 * i][...] = rows.astype(BF)
        outs[2 * i + 1][...] = rows.T.astype(BF)


def queries(items, latents, gain, w_query, deps):
    _, count, width = latents.shape
    qk = w_query.shape[1]
    return launch(
        query_kernel,
        "queries",
        2,
        [(latents, None), (gain, None), (w_query, None)],
        [((count, qk), BF, None), ((qk, count), BF, None)] * items,
        deps=deps,
    )


SPAN = 256


def head_span(h, wide):
    begin = h * wide // 128 * 128
    return begin, h * wide - begin


def language_row(table_ref, language):
    at = lax.broadcasted_iota(jnp.int32, table_ref.shape, 0)
    table = table_ref[...].astype(F32)
    return jnp.sum(jnp.where(at == language, table, 0.0), 0, keepdims=True)


PARTS = 2
SHARE = HEADS // PARTS


def heads_out(part, score_unit, k, v, qt, ot_ref):
    depth = qt.shape[0] // HEADS
    wide = v.shape[1] // SHARE
    at = lax.broadcasted_iota(jnp.int32, qt.shape, 0) // depth

    def score_of(h):
        return nn(k, jnp.where(at == part * SHARE + h, qt, jnp.zeros_like(qt)))

    def finish(h, weight, total):
        begin, ahead = head_span(h, wide)
        out = tn(v[:, begin : begin + SPAN], weight)[ahead : ahead + wide]
        ot_ref[h * wide : (h + 1) * wide] = (out * (1.0 / total)).astype(BF)

    lse = []
    coming, waiting = score_of(0), None
    for h in range(SHARE):
        score = coming * score_unit
        if h + 1 < SHARE:
            coming = score_of(h + 1)
        if waiting is not None:
            finish(*waiting)
        top = jnp.max(score, 0, keepdims=True)
        weight = jnp.exp2(score - top)
        total = jnp.sum(weight, 0, keepdims=True)
        lse.append(top + jnp.log2(total))
        waiting = (h, weight.astype(BF), total)
    finish(*waiting)
    lse = jnp.concatenate(lse, 0)
    high = lse.astype(BF).astype(F32)
    rest = jnp.zeros((16 - 2 * SHARE, lse.shape[1]), F32)
    ot_ref[SHARE * wide :] = jnp.concatenate([high, lse - high, rest], 0).astype(BF)


def attend_kernel(
    item, items, score_unit, where, lang_ref, own_ref, far_ref, table_ref, gain_ref, wk_ref,
    wv_ref, qt_ref, ot_ref, xn_ref, k_ref, kt_ref, v_ref,
):
    at = where[0] * items + item
    count = far_ref.shape[1]
    row = language_row(table_ref, lang_ref[at])
    gain = gain_ref[...]
    for part, rows in enumerate((own_ref[at], far_ref[item])):
        unit, _ = standardise(rows.astype(F32) + row)
        xn_ref[part * count : (part + 1) * count] = (unit * gain).astype(BF)
    xn = xn_ref[...]
    k = nn(xn, wk_ref[...]).astype(BF)
    k_ref[...] = k
    kt_ref[...] = k.T
    v = nn(xn, wv_ref[:, : v_ref.shape[1]]).astype(BF)
    v_ref[...] = v
    heads_out(0, score_unit, k, v, qt_ref[...], ot_ref)


def attend_more_kernel(part, score_unit, where, xn_ref, k_ref, wv_ref, qt_ref, ot_ref, v_ref):
    wide = v_ref.shape[1]
    v = nn(xn_ref[...], wv_ref[:, part * wide : (part + 1) * wide]).astype(BF)
    v_ref[...] = v
    heads_out(part, score_unit, k_ref[...], v, qt_ref[...], ot_ref)


def attend(
    item, items, language, own, far, table, gain, w_key, w_value, qt, score_unit, deps
):
    _, count, width = own.shape
    qk, lat = w_key.shape[1], qt.shape[1]
    wide = w_value.shape[1] // PARTS
    out = ((wide + 16, lat), BF, None)
    values = ((2 * count, wide), BF, None)
    first, xn, k, kt, v = launch(
        functools.partial(attend_kernel, item, items, score_unit),
        "attend",
        2.4,
        [(language, SCALARS)]
        + [(a, None) for a in (own, far, table, gain, w_key, w_value, qt)],
        [
            out,
            ((2 * count, width), BF, None),
            ((2 * count, qk), BF, None),
            ((qk, 2 * count), BF, None),
            values,
        ],
        deps=deps,
    )
    outs, vs = [first], [v]
    for part in range(1, PARTS):
        more, v = launch(
            functools.partial(attend_more_kernel, part, score_unit),
            "attend_more",
            1.9,
            [(a, None) for a in (xn, k, w_value, qt)],
            [out, values],
        )
        outs.append(more)
        vs.append(v)
    return outs, xn, k, kt, vs


def act_back_kernel(where, cot_ref, wd_ref, gact_ref):
    items = gact_ref.shape[0]
    for i in range(items):
        gact_ref[i] = nt(cot_ref[where[0] * items + i], wd_ref[...])


def act_back(cot, w_down, items, deps):
    return launch(
        act_back_kernel,
        "act_back",
        2.5,
        [(cot, None), (w_down, None)],
        [((items, cot.shape[1], w_down.shape[0]), F32, None)],
        deps=deps,
    )[0]


GELU_A = math.sqrt(2.0 / math.pi)
GELU_B = 0.044715


def part_sums(two):
    return two[:SHARE] + two[SHARE : 2 * SHARE]


def latent_kernel(
    item, items, bit, where, *refs
):
    oa_refs, ob_refs, refs = refs[:PARTS], refs[PARTS : 2 * PARTS], refs[2 * PARTS :]
    lat_ref, cot_ref, gact_ref, gain_ref, wo_ref, wu_ref = refs[:6]
    (
        resid_ref, gres_ref, gatt_ref, dot_ref, lse_ref, att_ref, hid_ref, act_ref, gpre_ref,
        glow_ref, ggain_ref,
    ) = refs[-11:]
    at = where[0] * items + item
    first = lax.rem(lax.div(where[1], bit), 2) == 0
    rows = gatt_ref.shape[0]
    wide = rows // HEADS
    ours, theirs = (
        jnp.concatenate(
            [part_sums(ref[rows // PARTS :].astype(F32)) for ref in refs_], 0
        )
        for refs_ in (oa_refs, ob_refs)
    )
    left = jnp.where(first, ours, theirs)
    right = jnp.where(first, theirs, ours)
    top = jnp.maximum(left, right)
    e_left, e_right = jnp.exp2(left - top), jnp.exp2(right - top)
    total = e_left + e_right
    lse_ref[...] = top + jnp.log2(total)
    scale = 1.0 / total
    e_left, e_right = e_left * scale, e_right * scale
    merged = []
    for h in range(HEADS):
        cut = slice(h % SHARE * wide, (h % SHARE + 1) * wide)
        a = oa_refs[h // SHARE][cut].astype(F32)
        b = ob_refs[h // SHARE][cut].astype(F32)
        low, high = jnp.where(first, a, b), jnp.where(first, b, a)
        merged.append(low * e_left[h : h + 1] + high * e_right[h : h + 1])
        att_ref[h * wide : (h + 1) * wide] = merged[-1].astype(BF)
    resid = lat_ref[at].astype(F32) + tn(att_ref[...], wo_ref[...])
    unit, inverse = standardise(resid)
    gain = gain_ref[...]
    hidden = (unit * gain).astype(BF)
    hid_ref[...] = hidden.T
    pre = nn(hidden, wu_ref[...])
    square = pre * pre
    slope = jnp.tanh(GELU_A * pre * (1.0 + GELU_B * square))
    act = (0.5 * pre * (1.0 + slope)).astype(BF)
    act_ref[...] = act.T
    resid_ref[...] = resid
    cot = cot_ref[at]
    gelu_slope = 0.5 * (1.0 + slope) + 0.5 * pre * (1.0 - slope * slope) * GELU_A * (
        1.0 + 3.0 * GELU_B * square
    )
    gpre = (gact_ref[item] * gelu_slope).astype(BF)
    gpre_ref[...] = gpre
    ghid = nt(gpre, wu_ref[...])
    ggain_ref[...] = jnp.sum(ghid * unit, 0, keepdims=True)
    gres = cot.astype(F32) + standardise_back(unit, inverse, ghid * gain)
    gres_ref[...] = gres
    glow = gres.astype(BF)
    glow_ref[...] = glow
    gatt_ref[...] = nt(wo_ref[...], glow).astype(BF)
    for h in range(HEADS):
        dot_ref[h : h + 1] = jnp.sum(
            gatt_ref[h * wide : (h + 1) * wide].astype(F32) * merged[h], 0, keepdims=True
        )


def latent_side(
    item, items, bit, oa, ob, latents, cot, gact, gain, w_out, w_up, deps
):
    total, lat, width = latents.shape
    feed = w_up.shape[1]
    ins = [(a, None) for a in (*oa, *ob, latents, cot, gact, gain, w_out, w_up)]
    return launch(
        functools.partial(latent_kernel, item, items, bit),
        "latent_side",
        7,
        ins,
        [
            ((lat, width), F32, None),
            ((lat, width), F32, None),
            ((width, lat), BF, None),
            ((HEADS, lat), F32, None),
            ((HEADS, lat), F32, None),
            ((width, lat), BF, None),
            ((width, lat), BF, None),
            ((feed, lat), BF, None),
            ((lat, feed), BF, None),
            ((lat, width), BF, None),
            ((1, width), F32, None),
        ],
        deps=deps,
    )


def out_rows_kernel(where, *refs):
    wd_ref, outs_ref = refs[-2:]
    for i in range(outs_ref.shape[0]):
        outs_ref[i] = (refs[2 * i][...] + tn(refs[2 * i + 1][...], wd_ref[...])).astype(BF)


def out_rows(resids, acts, w_down, deps):
    lat, width = resids[0].shape
    return launch(
        out_rows_kernel,
        "out_rows",
        SHORT,
        [(a, None) for pair in zip(resids, acts) for a in pair] + [(w_down, None)],
        [((len(resids), lat, width), BF, None)],
        deps=deps,
    )[0]


def flipped(at, bits):
    return sum(((at >> (len(bits) - 1 - t)) & 1) * bit for t, bit in enumerate(bits))


def pick_rows(where, source, lhs_ref, lane, rows, chips, bits):
    lat = source.shape[1]
    for j in range(2 ** len(bits)):
        spot = where[2] ^ flipped(j, bits)
        begin = pl.multiple_of((spot * chips + where[1]) * rows, 16)
        lhs_ref[j * rows : (j + 1) * rows, lane : lane + lat] = source[pl.ds(begin, rows)]


def latent_weights_kernel(plan, items, chips, bits, where, *refs):
    ins, keep_ref, send_ref, lhs_ref = refs[:-3], refs[-3], refs[-2], refs[-1]
    half = keep_ref.shape[1]
    column = 0
    for w, (begin, width) in enumerate(plan):
        lefts = ins[2 * items * w : 2 * items * w + items]
        rights = ins[2 * items * w + items : 2 * items * (w + 1)]
        total = 0.0
        for i in range(items):
            lat = lefts[i].shape[1]
            pick_rows(where, lefts[i], lhs_ref, i * lat, 2 * half, chips, bits)
            right = rights[i]
            if len(right.shape) == 3:
                right = right.at[where[0] * items + i]
            total += nn(lhs_ref[:, i * lat : (i + 1) * lat], right[:, begin : begin + width])
        out = slice(column, column + width)
        for j in range(keep_ref.shape[0]):
            low = total[2 * j * half : (2 * j + 1) * half]
            high = total[(2 * j + 1) * half : (2 * j + 2) * half]
            keep_ref[j, :, out] = jnp.where(where[0] == 0, low, high).astype(BF)
            send_ref[j, :, out] = jnp.where(where[0] == 0, high, low).astype(BF)
        column += width


def latent_weights(groups, plan, chips, bits, name, deps):
    items = len(groups[0][0])
    ins = []
    for lefts, rights in groups:
        ins += [(a, None) for a in lefts + rights]
    width, lat = groups[0][0][0].shape
    count = 2 ** len(bits)
    half = width // (count * chips * CORES)
    shape = (count, half, sum(w for _, w in plan))
    return launch(
        functools.partial(latent_weights_kernel, plan, items, chips, bits),
        name,
        SHORT,
        ins,
        [(shape, BF, None), (shape, BF, None)],
        scratch=[pltpu.VMEM((width // chips, items * lat), BF)],
        deps=deps,
    )


def attend_back_kernel(
    item, score_unit, score_scale, where, q_ref, qt_ref, k_ref, kt_ref, *refs
):
    v_refs, (gatt_ref, lse_ref, dot_ref) = refs[:PARTS], refs[PARTS : PARTS + 3]
    dqt_ref, dkv_ref, dvt_ref = refs[-3:]
    q, qt, k = q_ref[...], qt_ref[...], k_ref[...]
    qk = qt.shape[0]
    depth = qk // HEADS
    wide = gatt_ref.shape[0] // HEADS
    lat = qt.shape[1]
    at = lax.broadcasted_iota(jnp.int32, qt.shape, 0) // depth
    across = lax.broadcasted_iota(jnp.int32, q.shape, 1) // depth

    def begin_head(h):
        score = nn(k, jnp.where(at == h, qt, jnp.zeros_like(qt)))
        grad = gatt_ref[h * wide : (h + 1) * wide]
        begin, ahead = head_span(h % SHARE, wide)
        after = SPAN - ahead - wide
        pieces = [grad]
        if ahead:
            pieces = [jnp.zeros((ahead, lat), BF)] + pieces
        if after:
            pieces = pieces + [jnp.zeros((after, lat), BF)]
        values = v_refs[h // SHARE][:, begin : begin + SPAN]
        return score, grad, nn(values, jnp.concatenate(pieces, 0))

    def finish(h, grad, prob, grad_score):
        dvt_ref[h * wide : (h + 1) * wide] = nt(grad, prob).astype(BF)
        dqt_ref[item, h * depth : (h + 1) * depth] = nn(
            kt_ref[h * depth : (h + 1) * depth], grad_score
        ).astype(BF)
        return nn(grad_score, jnp.where(across == h, q, jnp.zeros_like(q)))

    dk = jnp.zeros(k.shape, F32)
    coming, waiting = begin_head(0), None
    for h in range(HEADS):
        score, grad, grad_prob = coming
        if h + 1 < HEADS:
            coming = begin_head(h + 1)
        if waiting is not None:
            dk += finish(*waiting)
        prob = jnp.exp2(score * score_unit - lse_ref[h : h + 1])
        grad_score = (prob * (grad_prob - dot_ref[h : h + 1])).astype(BF)
        waiting = (h, grad, prob.astype(BF), grad_score)
    dk += finish(*waiting)
    dkv_ref[:, :qk] = (dk * score_scale).astype(BF)
    dkv_ref[:, qk:] = dvt_ref[...].T


def attend_back(
    item, items, q, qt, k, kt, v, gatt, lse, dot, score_unit, score_scale, before, deps
):
    lat, qk = q.shape
    count, wide = v[0].shape[0], gatt.shape[0]
    ins = [(a, None) for a in (q, qt, k, kt, *v, gatt, lse, dot)]
    alias = {}
    for spot, array in enumerate(before):
        alias[len(ins)] = spot
        ins.append((array, None))
    return launch(
        functools.partial(attend_back_kernel, item, score_unit, score_scale),
        "attend_back",
        3.8 if item + 1 < items else SHORT,
        ins,
        [
            ((items, qk, lat), BF, None),
            ((count, qk + wide), BF, None),
        ],
        scratch=[pltpu.VMEM((wide, count), BF)],
        alias=alias,
        deps=deps,
    )


def turn_kernel(bits, where, *refs):
    xn_refs, (keep_ref, send_ref, all_ref) = refs[:-3], refs[-3:]
    count = 2 ** len(bits)
    rows = keep_ref.shape[1] // count
    mine = where[2] * 2 + where[1]
    for i, ref in enumerate(xn_refs):
        all_ref[i] = ref[...].astype(F32).T
    for i in range(len(xn_refs)):
        for out, core in ((keep_ref, where[0]), (send_ref, 1 - where[0])):
            for j in range(0, count, 2):
                pair = []
                for n in (j, j + 1):
                    spot = (mine ^ flipped(n, bits)) * CORES + core
                    begin = pl.multiple_of(spot * rows, 8)
                    pair.append(all_ref[i, pl.ds(begin, rows)])
                out[i, j * rows : (j + 2) * rows] = jnp.concatenate(pair, 0).astype(BF)


def turn(xns, bits, deps):
    count, width = xns[0].shape
    shape = (len(xns), width // CORES, count)
    return launch(
        functools.partial(turn_kernel, bits),
        "turn",
        3,
        [(a, None) for a in xns],
        [(shape, BF, None), (shape, BF, None)],
        scratch=[pltpu.VMEM((len(xns), width, count), F32)],
        deps=deps,
    )


def byte_part_kernel(spots, where, *refs):
    out_ref = refs[-1]
    total = refs[-2][...] if len(refs) % 2 == 0 else 0.0
    for n, spot in enumerate(spots):
        total += nn(refs[2 * n][spot], refs[2 * n + 1][...])
    out_ref[...] = total


def byte_part(pairs, before, micros, deps):
    ins = [(a, None) for turned, _, dkv in pairs for a in (turned, dkv)]
    alias = {}
    if before is not None:
        alias = {len(ins): 0}
        ins.append((before, None))
    shape = (pairs[0][0].shape[1], pairs[0][2].shape[1])
    return launch(
        functools.partial(byte_part_kernel, [p[1] for p in pairs]),
        "byte_part",
        micros,
        ins,
        [(shape, F32, None)],
        alias=alias,
        deps=deps,
    )[0]


def byte_last_kernel(spot, where, turned_ref, dkv_ref, before_ref, keep_ref, send_ref):
    total = before_ref[...] + nn(turned_ref[spot], dkv_ref[...])
    half, rows = keep_ref.shape[:2]
    for j in range(half):
        keep_ref[j] = total[j * rows : (j + 1) * rows].astype(BF)
        send_ref[j] = total[(half + j) * rows : (half + j + 1) * rows].astype(BF)


def byte_last(turned, spot, dkv, before, count, deps):
    shape = (count // 2, turned.shape[1] // count, dkv.shape[1])
    return launch(
        functools.partial(byte_last_kernel, spot),
        "byte_last",
        SHORT,
        [(turned, None), (dkv, None), (before, None)],
        [(shape, BF, None), (shape, BF, None)],
        deps=deps,
    )


def bytes_back_kernel(
    item, where, lang_ref, own_ref, far_ref, table_ref, gain_ref, wk_ref, wv_ref, dkv_ref, *refs
):
    gown_ref, gfar_ref, small_ref = refs[-3:]
    items, count = gfar_ref.shape[:2]
    qk = wk_ref.shape[1]
    langs = table_ref.shape[0]
    gain = gain_ref[...]
    language = lang_ref[where[0] * items + item]
    row = language_row(table_ref, language)
    grads = nt(dkv_ref[:, :qk], wk_ref[...]) + nt(dkv_ref[:, qk:], wv_ref[...])
    gain_sum = jnp.zeros_like(row)
    byte_sum = jnp.zeros_like(row)
    for part, rows, out in (
        (0, own_ref[where[0] * items + item], gown_ref),
        (1, far_ref[item], gfar_ref),
    ):
        unit, inverse = standardise(rows.astype(F32) + row)
        grad = grads[part * count : (part + 1) * count]
        gain_sum += jnp.sum(grad * unit, 0, keepdims=True)
        back = standardise_back(unit, inverse, grad * gain)
        byte_sum += jnp.sum(back, 0, keepdims=True)
        out[item] = back.astype(out.dtype)
    at = lax.broadcasted_iota(jnp.int32, small_ref.shape, 0)
    small = jnp.where(at == language, byte_sum, 0.0) + jnp.where(at == langs, gain_sum, 0.0)
    if item:
        small += refs[2][...]
    small_ref[...] = small


def bytes_back(
    item, items, language, own, far, table, gain, w_key, w_value, dkv, before, deps
):
    shape = far.shape
    ins = [(language, SCALARS)]
    ins += [(a, None) for a in (own, far, table, gain, w_key, w_value, dkv)]
    alias = {}
    if before:
        alias = {len(ins): 0, len(ins) + 1: 1}
        ins += [(a, None) for a in before]
    return launch(
        functools.partial(bytes_back_kernel, item),
        "bytes_back",
        2.5 if item + 1 < items else SHORT,
        ins,
        [
            (shape, F32, None),
            (shape, BF, None),
            ((table.shape[0] + 8, far.shape[2]), F32, None),
        ],
        alias=alias,
        deps=deps,
    )


def latents_back_kernel(
    score_scale, chips, bits, where, da_ref, db_ref, *refs
):
    items = da_ref.shape[0]
    gres_refs, gmlp_refs, refs = refs[:items], refs[items : 2 * items], refs[2 * items :]
    gfar_ref, small_ref, lat_ref, gain_ref, wq_ref = refs[:5]
    glat_ref, keep_ref, send_ref, own_ref = refs[5:9]
    lhs_ref, rhs_ref, turn_ref = refs[9:]
    lat = lat_ref.shape[1]
    gain = gain_ref[...]
    gain_sum = jnp.zeros_like(gain)
    half = keep_ref.shape[1]
    for i in range(items):
        total = (da_ref[i].astype(F32) + db_ref[i].astype(F32)) * score_scale
        grad = total.T.astype(BF)
        rhs_ref[i * lat : (i + 1) * lat] = grad
        unit, inverse = standardise(lat_ref[where[0] * items + i].astype(F32))
        turn_ref[i] = (unit * gain).astype(BF).T
        gln = nt(grad, wq_ref[...])
        gain_sum += jnp.sum(gln * unit, 0, keepdims=True)
        out = gres_refs[i][...] + standardise_back(unit, inverse, gln * gain)
        glat_ref[i, :, : out.shape[1]] = out.astype(BF)
        glat_ref[i, :, out.shape[1] :] = gfar_ref[i]
    gmlp = functools.reduce(jnp.add, [r[...] for r in gmlp_refs])
    wide = own_ref.shape[1]
    at = lax.broadcasted_iota(jnp.int32, (8, wide), 0)
    own = jnp.concatenate(
        [
            jnp.where(at == 1, gain_sum[:, g : g + wide], 0.0)
            + jnp.where(at == 2, gmlp[:, g : g + wide], 0.0)
            for g in range(0, gain.shape[1], wide)
        ],
        0,
    )
    own_ref[...] = own
    count = keep_ref.shape[0]
    send_ref[count] = own.astype(BF)
    tall = [small_ref[:, g : g + wide] for g in range(0, small_ref.shape[1], wide)]
    rest = (send_ref.shape[0] - count - 1) * half - len(tall) * small_ref.shape[0]
    tall = jnp.concatenate(tall + [jnp.zeros((rest, wide), F32)], 0)
    for j in range(count + 1, send_ref.shape[0]):
        send_ref[j] = tall[(j - count - 1) * half : (j - count) * half].astype(BF)
    for i in range(items):
        pick_rows(where, turn_ref.at[i], lhs_ref, i * lat, 2 * half, chips, bits)
    total = nn(lhs_ref[...], rhs_ref[...])
    for j in range(keep_ref.shape[0]):
        low = total[2 * j * half : (2 * j + 1) * half]
        high = total[(2 * j + 1) * half : (2 * j + 2) * half]
        keep_ref[j] = jnp.where(where[0] == 0, low, high).astype(BF)
        send_ref[j] = jnp.where(where[0] == 0, high, low).astype(BF)


def latents_back(da, db, gres, gmlps, gfar, small, latents, gain, w_query, score_scale, chips, bits, deps):
    _, lat, width = latents.shape
    items = da.shape[0]
    qk = w_query.shape[1]
    count = 2 ** len(bits)
    half = width // (count * chips * CORES)
    small_blocks = -(-small.size // (half * qk))
    return launch(
        functools.partial(latents_back_kernel, score_scale, chips, bits),
        "latents_back",
        SHORT,
        [(da, None), (db, None)]
        + [(g, None) for g in gres + gmlps]
        + [(a, None) for a in (gfar, small, latents, gain, w_query)],
        [
            ((items, lat, width + gfar.shape[2]), BF, None),
            ((count, half, qk), BF, None),
            ((count + 1 + small_blocks, half, qk), BF, None),
            ((half, qk), F32, None),
        ],
        scratch=[
            pltpu.VMEM((width // chips, items * lat), BF),
            pltpu.VMEM((items * lat, qk), BF),
            pltpu.VMEM((items, width, lat), BF),
        ],
        deps=deps,
    )


def fold_kernel(where, keep_ref, far_ref, *outs):
    half = keep_ref.shape[0] // 2
    if len(outs) == 1:
        outs[0][...] = keep_ref[0].astype(F32) + far_ref[0].astype(F32)
        return
    for spot, out in enumerate(outs):
        for j in range(half):
            at = spot * half + j
            out[j] = (keep_ref[at].astype(F32) + far_ref[at].astype(F32)).astype(BF)


def fold(keep, far, deps, micros=SHORT):
    if keep.shape[0] == 1:
        outs = [(keep.shape[1:], F32, None)]
    else:
        shape = (keep.shape[0] // 2,) + keep.shape[1:]
        outs = [(shape, BF, None), (shape, BF, None)]
    return launch(fold_kernel, "fold", micros, [(keep, None), (far, None)], outs, deps=deps)


def side_kernel(begin, where, far_ref, small_ref, own_ref, send_ref):
    rows, width = small_ref.shape
    tall = jnp.concatenate([far_ref[j].astype(F32) for j in range(begin, far_ref.shape[0])], 0)
    pieces = [tall[rows * g : rows * (g + 1)] for g in range(width // far_ref.shape[2])]
    own = small_ref[...] + jnp.concatenate(pieces, 1)
    own_ref[...] = own
    send_ref[...] = own.astype(BF)


def side_sum(far, small, begin, deps):
    return launch(
        functools.partial(side_kernel, begin),
        "side_sum",
        1,
        [(far, None), (small, None)],
        [(small.shape, F32, None), (small.shape, BF, None)],
        deps=deps,
    )


def join_kernel(
    langs, chips, bits, where, keep_ref, far_ref, own_ref, side_ref, qkeep_ref, qfar_ref, qown_ref,
    keep_out, send_out,
):
    count, rows, wide = keep_ref.shape
    qrows, qwide = qown_ref.shape

    def across(tall):
        return jnp.concatenate([tall[r : r + 8] for r in range(0, qrows, 8)], 1)

    own = own_ref[...] + side_ref[...].astype(F32)
    gains = across(qown_ref[...] + qfar_ref[count].astype(F32))
    at = lax.broadcasted_iota(jnp.int32, (8, qwide), 1)
    half = count // 2
    for j in range(count):
        spot = where[2] ^ flipped(j, bits)
        device = (spot * chips + where[1]) * CORES + where[0]
        byte_cut = pltpu.roll(own, own.shape[1] - device * rows, 1)[:, :qwide]
        lat_cut = pltpu.roll(gains, gains.shape[1] - device * qrows, 1)[:, :qwide]
        spare = jnp.where(at < rows, byte_cut[:8], 0.0)
        for n in range(1, langs // 8 + 1):
            piece = jnp.where(at < rows, byte_cut[8 * n : 8 * n + 8], 0.0)
            spare += pltpu.roll(piece, n * rows, 1)
        spare += pltpu.roll(jnp.where(at < qrows, lat_cut, 0.0), (langs // 8 + 1) * rows, 1)
        byte = keep_ref[j].astype(F32) + far_ref[j].astype(F32)
        query = across(qkeep_ref[j].astype(F32) + qfar_ref[j].astype(F32))
        out = keep_out if j < half else send_out
        below = jnp.concatenate([query, spare], 1)
        out[j % half] = jnp.concatenate([byte, below], 0).astype(BF)


def join(keep, far, own, side, qkeep, qfar, qown, langs, chips, bits, deps):
    count, rows, wide = keep.shape
    shape = (count // 2, rows + 8, wide)
    return launch(
        functools.partial(join_kernel, langs, chips, bits),
        "join",
        LONG,
        [(a, None) for a in (keep, far, own, side, qkeep, qfar, qown)],
        [(shape, BF, None), (shape, BF, None)],
        deps=deps,
    )


def part_kernel(
    where, keep_ref, far_ref, key_ref, value_ref, query_ref, lang_ref, gin_ref, glat_ref, gmlp_ref
):
    total = keep_ref[0].astype(F32) + far_ref[0].astype(F32)
    rows, qk = key_ref.shape
    qrows, langs = query_ref.shape[0], lang_ref.shape[0]
    key_ref[...] = total[:rows, :qk]
    value_ref[...] = total[:rows, qk:]
    for r in range(0, qrows, 8):
        query_ref[r : r + 8] = total[rows:, r // 8 * qk : (r // 8 + 1) * qk]
    spare = total[rows:, qrows // 8 * qk : (qrows // 8 + 1) * qk]
    groups = langs // 8
    for n in range(groups):
        lang_ref[8 * n : 8 * n + 8] = spare[:, n * rows : (n + 1) * rows]
    gin_ref[...] = spare[:1, groups * rows : (groups + 1) * rows]
    begin = (groups + 1) * rows
    glat_ref[...] = spare[1:2, begin : begin + qrows]
    gmlp_ref[...] = spare[2:3, begin : begin + qrows]


def part(keep, far, qk, qrows, langs, deps):
    rows, wide = keep.shape[1] - 8, keep.shape[2]
    shapes = [(rows, qk), (rows, wide - qk), (qrows, qk), (langs, rows)]
    shapes += [(1, rows), (1, qrows), (1, qrows)]
    return launch(
        part_kernel,
        "part",
        SHORT,
        [(keep, None), (far, None)],
        [(shape, F32, None) for shape in shapes],
        deps=deps,
    )


def last_kernel(where, keep_a, far_a, keep_b, far_b, up_ref, down_ref, out_ref):
    wide = up_ref.shape[1]
    split = out_ref.shape[1] // 2
    first = keep_a[0].astype(F32) + far_a[0].astype(F32)
    second = keep_b[0].astype(F32) + far_b[0].astype(F32)
    up_ref[...] = first[:, :wide]
    down_ref[...] = second[:, :wide]
    out_ref[:, :split] = first[:, wide:]
    out_ref[:, split:] = second[:, wide:]


def last(keep_a, far_a, keep_b, far_b, width, deps):
    shape = (keep_a.shape[1], width)
    return launch(
        last_kernel,
        "last",
        SHORT,
        [(a, None) for a in (keep_a, far_a, keep_b, far_b)],
        [(shape, F32, None)] * 3,
        deps=deps,
    )


def place_kernel(columns, where, *refs):
    count = len(columns)
    items = pl.num_programs(0) // 2
    ours = pl.program_id(0) // items == where[0]
    for n, (left, right) in enumerate(columns):
        out = refs[2 * count + n]
        wide = out.shape[2]
        own = refs[n][:, :, left : left + wide].astype(out.dtype)
        far = refs[count + n][:, :, right : right + wide].astype(out.dtype)
        out[...] = jnp.where(ours, own, far)
    refs[-1][...] = jnp.zeros_like(refs[-1])


def place(pairs, micros, deps):
    items = pairs[0][0].shape[0]
    one = lambda a: (1,) + a.shape[1:]
    rows = lambda p: p[0].shape[1]
    outs = [
        ((2 * items, rows(p), p[4]), p[5], block((1, rows(p), p[4]), lambda g: g))
        for p in pairs
    ]
    return launch(
        functools.partial(place_kernel, [(p[1], p[3]) for p in pairs]),
        "place",
        micros,
        [(a, block(one(a), lambda g: g % items)) for a in [p[0] for p in pairs]]
        + [(a, block(one(a), lambda g: g % items)) for a in [p[2] for p in pairs]],
        outs + [((8, 128), F32, None)],
        deps=deps,
        grid=2 * items,
        far=True,
    )


def swap(value, axis, bit):
    size = lax.axis_size(axis)
    return lax.ppermute(value, axis, [(i, i ^ bit) for i in range(size)])


def bits_of(size):
    return [2**t for t in range(size.bit_length() - 1)]


def halve(value, dim, axis, bit):
    mine = (lax.axis_index(axis) // bit) % 2
    keep = lax.dynamic_index_in_dim(value, mine, dim, keepdims=False)
    send = lax.dynamic_index_in_dim(value, 1 - mine, dim, keepdims=False)
    return (keep.astype(F32) + swap(send, axis, bit).astype(F32)).astype(BF)


def scatter_rows(value):
    spots, chips = lax.axis_size("batch"), lax.axis_size("seq") // CORES
    rows = value.shape[0] // (spots * chips * CORES)
    blocks = value.astype(BF).reshape(spots, chips, CORES, rows, value.shape[1])
    blocks = halve(blocks, 2, "seq", 1)
    for bit in bits_of(chips):
        rest = blocks.shape[2:]
        blocks = blocks.reshape((spots, blocks.shape[1] // 2, 2) + rest)
        blocks = halve(blocks, 2, "seq", CORES * bit)
    blocks = blocks[:, 0]
    for bit in bits_of(spots):
        blocks = blocks.reshape((blocks.shape[0] // 2, 2) + blocks.shape[1:])
        blocks = halve(blocks, 1, "batch", bit)
    return blocks[0].astype(F32)


def everywhere(value):
    for axis in ("seq", "batch"):
        for bit in bits_of(lax.axis_size(axis)):
            value = value + swap(value, axis, bit)
    return value


def merge(oa, ob):
    rows = oa.shape[0] - 16
    wide = rows // SHARE
    la, lb = part_sums(oa[rows:].astype(F32)), part_sums(ob[rows:].astype(F32))
    top = jnp.maximum(la, lb)
    ea, eb = jnp.exp2(la - top), jnp.exp2(lb - top)
    total = ea + eb
    lse = top + jnp.log2(total)
    out = oa[:rows].astype(F32) * jnp.repeat(ea / total, wide, 0)
    out = out + ob[:rows].astype(F32) * jnp.repeat(eb / total, wide, 0)
    high = lse.astype(BF)
    low = (lse - high.astype(F32)).astype(BF)
    rest = jnp.zeros((16 - 2 * SHARE, lse.shape[1]), BF)
    return jnp.concatenate([out.astype(BF), high, low, rest], 0)


def local(
    byte_inputs,
    language,
    lang_table,
    latents,
    gain_in,
    gain_lat,
    gain_mlp,
    w_query,
    w_key,
    w_value,
    w_out,
    w_up,
    w_down,
    cotangent,
):
    items = byte_inputs.shape[0] // CORES
    width_in, width_lat = byte_inputs.shape[2], latents.shape[2]
    lat, qk = latents.shape[1], w_query.shape[1]
    langs = lang_table.shape[0]
    score_scale = 1.0 / math.sqrt(qk // HEADS)
    score_unit = score_scale * math.log2(math.e)
    spots, chips = lax.axis_size("batch"), lax.axis_size("seq") // CORES
    devices = spots * chips * CORES
    seq_at, spot = lax.axis_index("seq"), lax.axis_index("batch")
    core, side = seq_at % CORES, seq_at // CORES
    device = spot * (chips * CORES) + seq_at
    chip_bits, spot_bits = bits_of(chips), bits_of(spots)
    rows_in, rows_lat = width_in // devices, width_lat // devices
    direct = (
        chips == 2
        and rows_in == langs + 8
        and rows_lat * qk == 8 * width_lat
        and width_lat % qk == 0
        and langs % 8 == 0
        and byte_inputs.shape[1] == lat
    )
    last_bit = chip_bits[-1]
    table = lang_table
    gain_in, gain_lat, gain_mlp = gain_in[None], gain_lat[None], gain_mlp[None]

    far = swap(pick_bytes(byte_inputs, items), "seq", 1)
    asked = queries(items, latents, gain_lat, w_query, ())
    asked = [asked[2 * i : 2 * i + 2] for i in range(items)]
    xns, kept, pairs, token = [], [], [], ()
    for item in range(items):
        ots, xn, k, kt, v = attend(
            item, items, language, byte_inputs, far, table, gain_in, w_key, w_value,
            asked[item][1], score_unit, token,
        )
        xns.append(xn)
        kept.append((k, kt, v))
        token = (v[-1],)
        for bit in chip_bits[:-1]:
            ots = [merge(ot, swap(ot, "seq", CORES * bit)) for ot in ots]
        pairs.append((ots, [swap(ot, "seq", CORES * last_bit) for ot in ots]))

    gact = act_back(cotangent, w_down, items, token)
    token = (gact,)
    sides, dqkv, dkvs = [], (), []
    if direct:
        y_bit, z_bit, far_bit = spot_bits
        a_bits, b_bits = [y_bit, z_bit, far_bit], [z_bit, far_bit, y_bit]
        c_bits = [1] + [2 * b for b in a_bits]
        turned, turned_send = turn(xns, c_bits, token)
        turned_far = swap(turned_send, "seq", 1)
        part_c, far_pairs = None, []

    def back(item, deps):
        gatt, dot, lse = sides[item][2:5]
        return attend_back(
            item, items, *asked[item], *kept[item], gatt, lse, dot, score_unit, score_scale, dqkv, deps
        )

    byted = ()

    def back_bytes(item, deps):
        return bytes_back(
            item, items, language, byte_inputs, far, table, gain_in, w_key, w_value,
            dkvs[item], byted, deps,
        )

    for item in range(items):
        if item:
            *dqkv, dkv = back(item - 1, token)
            dkvs.append(dkv)
            byted = back_bytes(item - 1, ())
            token = (byted[2],)
            if direct:
                dkv_far = swap(dkv, "seq", 1)
                part_c = byte_part([(turned, item - 1, dkv)], part_c, 1, token)
                far_pairs.append((turned_far, item - 1, dkv_far))
                token = (part_c,)
        side_out = latent_side(
            item, items, last_bit, *pairs[item], latents, cotangent,
            gact, gain_mlp, w_out, w_up, token,
        )
        sides.append(side_out)
        token = (side_out[3],)

    pick = lambda at: [s[at] for s in sides]
    down = (pick(7), [cotangent] * items)
    up = (pick(6), pick(8))
    out = (pick(5), pick(9))

    if direct:
        split = width_lat // 2
        keep_a, send_a = latent_weights(
            [up, out], [(0, width_lat), (0, split)], chips, a_bits, "weights_a", token
        )
        far_a = swap(send_a, "seq", 1)
        keep_b, send_b = latent_weights(
            [down, out], [(0, width_lat), (split, split)], chips, b_bits, "weights_b",
            (keep_a,),
        )
        far_b = swap(send_b, "seq", 1)
        early = [a for pair in far_pairs for a in (pair[0], pair[2])]
        dqt, dkv = back(items - 1, (keep_b, *early))
        dkvs.append(dkv)
        dkv_far = swap(dkv, "seq", 1)
        dqt_far = swap(dqt, "seq", CORES)
        keep_a, send_a = fold(keep_a, far_a, (dqt,), 5)
        far_a = swap(send_a, "batch", a_bits[0])
        keep_b, send_b = fold(keep_b, far_b, (keep_a,), 5)
        far_b = swap(send_b, "batch", b_bits[0])
        part_c = byte_part(
            far_pairs + [(turned, items - 1, dkv)], part_c, SHORT, (keep_b,)
        )
        keep_c, send_c = byte_last(
            turned_far, items - 1, dkv_far, part_c, 2 ** len(c_bits), ()
        )
        far_c = swap(send_c, "seq", CORES)
        gown, gfar, small = back_bytes(items - 1, (keep_c,))
        glats, keep_q, send_q, own_q = latents_back(
            dqt, dqt_far, pick(1), pick(10), gfar, small, latents, gain_lat, w_query,
            score_scale, chips, a_bits, (),
        )
        glats_far = swap(glats, "seq", 1)
        far_q = swap(send_q, "seq", 1)
        own_s, send_s = side_sum(far_q, small, keep_q.shape[0] + 1, ())
        far_s = swap(send_s, "seq", CORES)
        keep_b, send_b = fold(keep_b, far_b, (own_s,))
        far_b = swap(send_b, "batch", b_bits[1])
        keep_a, send_a = fold(keep_a, far_a, (keep_b,))
        far_a = swap(send_a, "batch", a_bits[1])
        keep_c, send_c = join(
            keep_c, far_c, own_s, far_s, keep_q, far_q, own_q, langs, chips, a_bits,
            (keep_a,),
        )
        far_c = swap(send_c, "batch", a_bits[0])
        outs = out_rows(pick(0), pick(7), w_down, (keep_c,))
        outs_far = swap(outs, "seq", 1)
        grad_bytes, grad_latents, token = place(
            [
                (gown, 0, glats_far, width_lat, width_in, F32),
                (glats, 0, glats_far, 0, width_lat, F32),
            ],
            LONG,
            (outs,),
        )
        keep_c, send_c = fold(keep_c, far_c, (token,))
        far_c = swap(send_c, "batch", a_bits[1])
        keep_b, send_b = fold(keep_b, far_b, (keep_c,))
        far_b = swap(send_b, "batch", b_bits[2])
        keep_a, send_a = fold(keep_a, far_a, (keep_b,))
        far_a = swap(send_a, "batch", a_bits[2])
        latents_out, token = place(
            [(outs, 0, outs_far, 0, width_lat, BF)], SHORT, (keep_a,)
        )
        keep_c, send_c = fold(keep_c, far_c, (token,))
        far_c = swap(send_c, "batch", a_bits[2])
        g_up, g_down, g_out = last(keep_a, far_a, keep_b, far_b, width_lat, (keep_c,))
        g_key, g_value, g_query, g_table, *gains = part(
            keep_c, far_c, qk, rows_lat, langs, ()
        )
        g_in, g_lat, g_mlp = [g[0] for g in gains]
    else:
        outs = out_rows(pick(0), pick(7), w_down, ())
        outs_far = swap(outs, "seq", 1)
        dqt, dkv = back(items - 1, token)
        dkvs.append(dkv)
        for bit in chip_bits:
            dqt = (dqt.astype(F32) + swap(dqt, "seq", CORES * bit).astype(F32)).astype(BF)
        gown, gfar, small = back_bytes(items - 1, ())
        gfar_far = swap(gfar, "seq", 1)
        own_cut = lambda a: lax.dynamic_slice_in_dim(a, core * items, items, 0)
        grad_q = (dqt.astype(F32) * score_scale).swapaxes(1, 2).astype(BF)
        unit, inverse = standardise(own_cut(latents).astype(F32))
        gln = lax.dot_general(
            grad_q, w_query, (((2,), (1,)), ((), ())), preferred_element_type=F32
        )
        glats = jnp.stack(pick(1)) + standardise_back(unit, inverse, gln * gain_lat)
        glats = glats.astype(BF)
        glats_far = swap(glats, "seq", 1)
        flat = lambda a: a.reshape(-1, a.shape[-1])
        share = 1.0 / chips
        g_query = scatter_rows(tn(flat((unit * gain_lat).astype(BF)), flat(grad_q)) * share)
        rows = lambda lefts, rights: scatter_rows(
            sum(nn(x, y) for x, y in zip(lefts, rights)) * share
        )
        g_down = rows(pick(7), own_cut(cotangent))
        g_up, g_out = rows(pick(6), pick(8)), rows(pick(5), pick(9))
        g_bytes = scatter_rows(sum(tn(xns[i], dkvs[i]) for i in range(items)))
        g_key, g_value = g_bytes[:, :qk], g_bytes[:, qk:]
        pad = ((0, 0), (0, width_lat - width_in))
        small = jnp.concatenate(
            [
                jnp.pad(small[: langs + 1], pad),
                jnp.sum(gln * unit, (0, 1))[None] * share,
                sum(pick(10)) * share,
            ],
            0,
        )
        small = everywhere(small)
        cut = lambda rows, count: lax.dynamic_slice_in_dim(rows, device * count, count, 1)
        g_table, g_in = cut(small[:langs], rows_in), cut(small[langs : langs + 1], rows_in)[0]
        g_lat, g_mlp = cut(small[langs + 1 :], rows_lat)
        latents_out, grad_bytes, grad_latents, _ = place(
            [
                (outs, 0, outs_far, 0, width_lat, BF),
                (gown, 0, gfar_far, 0, width_in, F32),
                (glats, 0, glats_far, 0, width_lat, F32),
            ],
            SHORT,
            (),
        )

    return (
        latents_out,
        grad_latents,
        grad_bytes,
        g_table,
        g_in,
        g_lat,
        g_mlp,
        g_query,
        g_key,
        g_value,
        g_out,
        g_up,
        g_down,
    )


def solution(mesh):
    return jax.shard_map(
        local,
        mesh=mesh,
        in_specs=(
            P("batch", "seq", None),
            P("batch"),
            P(),
            P("batch", None, None),
            P(),
            P(),
            P(),
            P(),
            P(),
            P(),
            P(),
            P(),
            P(),
            P("batch", None, None),
        ),
        out_specs=(
            P("batch", None, None),
            P("batch", None, None),
            P("batch", "seq", None),
            P(None, ("batch", "seq")),
            P(("batch", "seq")),
            P(("batch", "seq")),
            P(("batch", "seq")),
            P(("batch", "seq"), None),
            P(("batch", "seq"), None),
            P(("batch", "seq"), None),
            P(("batch", "seq"), None),
            P(("batch", "seq"), None),
            P(("batch", "seq"), None),
        ),
        check_vma=False,
    )
```

```python
import functools
import math

import jax
import jax.numpy as jnp
from jax import lax
from jax.experimental import pallas as pl
from jax.experimental.pallas import tpu as pltpu
from jax.sharding import PartitionSpec as P

HEADS = 8
CORES = 2
EPS = 1e-05
F32 = jnp.float32
BF = jnp.bfloat16
VMEM_LIMIT = 12 * 1024 * 1024
PEAK = 1.15e9
SHORT, LONG, AHEAD = 0.001, 40, 3


def nn(a, b):
    return lax.dot_general(a, b, (((1,), (0,)), ((), ())), preferred_element_type=F32)


def nt(a, b):
    return lax.dot_general(a, b, (((1,), (1,)), ((), ())), preferred_element_type=F32)


def tn(a, b):
    return lax.dot_general(a, b, (((0,), (0,)), ((), ())), preferred_element_type=F32)


def standardise(x):
    centre = x - jnp.mean(x, -1, keepdims=True)
    inverse = lax.rsqrt(jnp.mean(centre * centre, -1, keepdims=True) + EPS)
    return centre * inverse, inverse


def standardise_back(unit, inverse, grad):
    return inverse * (
        grad - jnp.mean(grad, -1, keepdims=True) - unit * jnp.mean(grad * unit, -1, keepdims=True)
    )


def block(shape, at):
    return pl.BlockSpec(shape, lambda g: (at(g),) + (0,) * (len(shape) - 1))


ANY = pl.BlockSpec(memory_space=pl.ANY)
FAST = pl.BlockSpec(memory_space=pltpu.VMEM)
FAR = pl.BlockSpec(memory_space=pltpu.HBM)
SCALARS = pl.BlockSpec(memory_space=pltpu.SMEM)


def launch(body, name, micros, ins, outs, scratch=(), deps=(), alias=None, grid=1, far=False):
    count, extra = len(ins), len(deps)
    ins = [
        (pltpu.with_memory_space_constraint(a, pltpu.HBM) if s is FAR else a, s) for a, s in ins
    ]

    def kernel(*refs):
        body(Where(), *refs[:count], *refs[count + extra :])

    return pl.pallas_call(
        kernel,
        grid=(grid,),
        in_specs=[FAST if s is None else s for _, s in ins] + [ANY] * extra,
        out_specs=[FAST if s is None else s for _, _, s in outs],
        scratch_shapes=list(scratch),
        out_shape=[
            (jax.ShapeDtypeStruct if s is None or not far else pltpu.HBM)(shape, dtype)
            for shape, dtype, s in outs
        ],
        input_output_aliases=alias or {},
        compiler_params=pltpu.CompilerParams(vmem_limit_bytes=VMEM_LIMIT),
        cost_estimate=pl.CostEstimate(
            flops=int(micros * PEAK), bytes_accessed=1, transcendentals=0
        ),
        name=name,
    )(*[a for a, _ in ins], *deps)


class Where:
    def __getitem__(self, at):
        if at == 2:
            return lax.axis_index("batch")
        return (lax.rem, lax.div)[at](lax.axis_index("seq"), CORES)


def pick_kernel(where, own_ref, out_ref, arrived):
    items = out_ref.shape[0]
    copy = pltpu.make_async_copy(
        own_ref.at[pl.ds((1 - where[0]) * items, items)], out_ref, arrived
    )
    copy.start()
    copy.wait()


def pick_bytes(own, items):
    return launch(
        pick_kernel,
        "pick_bytes",
        AHEAD,
        [(own, FAR)],
        [((items,) + own.shape[1:], BF, None)],
        scratch=[pltpu.SemaphoreType.DMA(())],
    )[0]


def query_kernel(where, lat_ref, gain_ref, wq_ref, *outs):
    items = len(outs) // 2
    for i in range(items):
        unit, _ = standardise(lat_ref[where[0] * items + i].astype(F32))
        rows = nn((unit * gain_ref[...]).astype(BF), wq_ref[...])
        outs[2 * i][...] = rows.astype(BF)
        outs[2 * i + 1][...] = rows.T.astype(BF)


def queries(items, latents, gain, w_query, deps):
    _, count, width = latents.shape
    qk = w_query.shape[1]
    return launch(
        query_kernel,
        "queries",
        2,
        [(latents, None), (gain, None), (w_query, None)],
        [((count, qk), BF, None), ((qk, count), BF, None)] * items,
        deps=deps,
    )


SPAN = 256


def head_span(h, wide):
    begin = h * wide // 128 * 128
    return begin, h * wide - begin


def language_row(table_ref, language):
    at = lax.broadcasted_iota(jnp.int32, table_ref.shape, 0)
    table = table_ref[...].astype(F32)
    return jnp.sum(jnp.where(at == language, table, 0.0), 0, keepdims=True)


PARTS = 2
SHARE = HEADS // PARTS
TERMS = 4


def part_terms(lse):
    terms, left = [], lse
    for _ in range(TERMS):
        terms.append(left.astype(BF).astype(F32))
        left = left - terms[-1]
    return jnp.concatenate(terms, 0).astype(BF)


def part_sums(terms):
    total = terms[(TERMS - 1) * SHARE :]
    for n in reversed(range(TERMS - 1)):
        total = terms[n * SHARE : (n + 1) * SHARE] + total
    return total


def heads_out(part, score_unit, k, v, qt, ot_ref):
    depth = qt.shape[0] // HEADS
    wide = v.shape[1] // SHARE
    at = lax.broadcasted_iota(jnp.int32, qt.shape, 0) // depth

    def score_of(h):
        return nn(k, jnp.where(at == part * SHARE + h, qt, jnp.zeros_like(qt)))

    def finish(h, weight, total):
        begin, ahead = head_span(h, wide)
        out = tn(v[:, begin : begin + SPAN], weight)[ahead : ahead + wide]
        ot_ref[h * wide : (h + 1) * wide] = (out * (1.0 / total)).astype(BF)

    lse = []
    coming, waiting = score_of(0), None
    for h in range(SHARE):
        score = coming * score_unit
        if h + 1 < SHARE:
            coming = score_of(h + 1)
        if waiting is not None:
            finish(*waiting)
        top = jnp.max(score, 0, keepdims=True)
        weight = jnp.exp2(score - top)
        total = jnp.sum(weight, 0, keepdims=True)
        lse.append(top + jnp.log2(total))
        waiting = (h, weight.astype(BF), total)
    finish(*waiting)
    lse = jnp.concatenate(lse, 0)
    ot_ref[SHARE * wide :] = part_terms(lse)


def attend_kernel(
    item, items, score_unit, where, lang_ref, own_ref, far_ref, table_ref, gain_ref, wk_ref,
    wv_ref, qt_ref, ot_ref, xn_ref, k_ref, kt_ref, v_ref,
):
    at = where[0] * items + item
    count = far_ref.shape[1]
    row = language_row(table_ref, lang_ref[at])
    gain = gain_ref[...]
    for part, rows in enumerate((own_ref[at], far_ref[item])):
        unit, _ = standardise(rows.astype(F32) + row)
        xn_ref[part * count : (part + 1) * count] = (unit * gain).astype(BF)
    xn = xn_ref[...]
    k = nn(xn, wk_ref[...]).astype(BF)
    k_ref[...] = k
    kt_ref[...] = k.T
    v = nn(xn, wv_ref[:, : v_ref.shape[1]]).astype(BF)
    v_ref[...] = v
    heads_out(0, score_unit, k, v, qt_ref[...], ot_ref)


def attend_more_kernel(part, score_unit, where, xn_ref, k_ref, wv_ref, qt_ref, ot_ref, v_ref):
    wide = v_ref.shape[1]
    v = nn(xn_ref[...], wv_ref[:, part * wide : (part + 1) * wide]).astype(BF)
    v_ref[...] = v
    heads_out(part, score_unit, k_ref[...], v, qt_ref[...], ot_ref)


def attend(
    item, items, language, own, far, table, gain, w_key, w_value, qt, score_unit, deps
):
    _, count, width = own.shape
    qk, lat = w_key.shape[1], qt.shape[1]
    wide = w_value.shape[1] // PARTS
    out = ((wide + TERMS * SHARE, lat), BF, None)
    values = ((2 * count, wide), BF, None)
    first, xn, k, kt, v = launch(
        functools.partial(attend_kernel, item, items, score_unit),
        "attend",
        2.4,
        [(language, SCALARS)]
        + [(a, None) for a in (own, far, table, gain, w_key, w_value, qt)],
        [
            out,
            ((2 * count, width), BF, None),
            ((2 * count, qk), BF, None),
            ((qk, 2 * count), BF, None),
            values,
        ],
        deps=deps,
    )
    outs, vs = [first], [v]
    for part in range(1, PARTS):
        more, v = launch(
            functools.partial(attend_more_kernel, part, score_unit),
            "attend_more",
            1.9,
            [(a, None) for a in (xn, k, w_value, qt)],
            [out, values],
        )
        outs.append(more)
        vs.append(v)
    return outs, xn, k, kt, vs


def act_back_kernel(where, cot_ref, wd_ref, gact_ref):
    items = gact_ref.shape[0]
    for i in range(items):
        gact_ref[i] = nt(cot_ref[where[0] * items + i], wd_ref[...])


def act_back(cot, w_down, items, deps):
    return launch(
        act_back_kernel,
        "act_back",
        2.5,
        [(cot, None), (w_down, None)],
        [((items, cot.shape[1], w_down.shape[0]), F32, None)],
        deps=deps,
    )[0]


GELU_A = math.sqrt(2.0 / math.pi)
GELU_B = 0.044715


def latent_kernel(
    item, items, bit, where, *refs
):
    oa_refs, ob_refs, refs = refs[:PARTS], refs[PARTS : 2 * PARTS], refs[2 * PARTS :]
    lat_ref, cot_ref, gact_ref, gain_ref, wo_ref, wu_ref, wd_ref = refs[:7]
    (
        outs_ref, gres_ref, gatt_ref, dot_ref, lse_ref, att_ref, hid_ref, act_ref, gpre_ref,
        glow_ref, ggain_ref,
    ) = refs[-11:]
    at = where[0] * items + item
    first = lax.rem(lax.div(where[1], bit), 2) == 0
    rows = gatt_ref.shape[0]
    wide = rows // HEADS
    ours, theirs = (
        jnp.concatenate(
            [part_sums(ref[rows // PARTS :].astype(F32)) for ref in refs_], 0
        )
        for refs_ in (oa_refs, ob_refs)
    )
    left = jnp.where(first, ours, theirs)
    right = jnp.where(first, theirs, ours)
    top = jnp.maximum(left, right)
    e_left, e_right = jnp.exp2(left - top), jnp.exp2(right - top)
    total = e_left + e_right
    lse_ref[...] = top + jnp.log2(total)
    scale = 1.0 / total
    e_left, e_right = e_left * scale, e_right * scale
    merged = []
    for h in range(HEADS):
        cut = slice(h % SHARE * wide, (h % SHARE + 1) * wide)
        a = oa_refs[h // SHARE][cut].astype(F32)
        b = ob_refs[h // SHARE][cut].astype(F32)
        low, high = jnp.where(first, a, b), jnp.where(first, b, a)
        merged.append(low * e_left[h : h + 1] + high * e_right[h : h + 1])
        att_ref[h * wide : (h + 1) * wide] = merged[-1].astype(BF)
    resid = lat_ref[at].astype(F32) + tn(att_ref[...], wo_ref[...])
    unit, inverse = standardise(resid)
    gain = gain_ref[...]
    hidden = (unit * gain).astype(BF)
    hid_ref[...] = hidden.T
    pre = nn(hidden, wu_ref[...])
    square = pre * pre
    slope = jnp.tanh(GELU_A * pre * (1.0 + GELU_B * square))
    act = (0.5 * pre * (1.0 + slope)).astype(BF)
    act_ref[...] = act.T
    outs_ref[item] = (resid + nn(act, wd_ref[...])).astype(BF)
    cot = cot_ref[at]
    gelu_slope = 0.5 * (1.0 + slope) + 0.5 * pre * (1.0 - slope * slope) * GELU_A * (
        1.0 + 3.0 * GELU_B * square
    )
    gpre = (gact_ref[item] * gelu_slope).astype(BF)
    gpre_ref[...] = gpre
    ghid = nt(gpre, wu_ref[...])
    ggain_ref[...] = jnp.sum(ghid * unit, 0, keepdims=True)
    gres = cot.astype(F32) + standardise_back(unit, inverse, ghid * gain)
    gres_ref[...] = gres
    glow = gres.astype(BF)
    glow_ref[...] = glow
    gatt_ref[...] = nt(wo_ref[...], glow).astype(BF)
    for h in range(HEADS):
        dot_ref[h : h + 1] = jnp.sum(
            gatt_ref[h * wide : (h + 1) * wide].astype(F32) * merged[h], 0, keepdims=True
        )


def latent_side(
    item, items, bit, oa, ob, latents, cot, gact, gain, w_out, w_up, w_down, before, deps
):
    total, lat, width = latents.shape
    feed = w_up.shape[1]
    ins = [(a, None) for a in (*oa, *ob, latents, cot, gact, gain, w_out, w_up, w_down)]
    alias = {}
    if before is not None:
        alias[len(ins)] = 0
        ins.append((before, None))
    return launch(
        functools.partial(latent_kernel, item, items, bit),
        "latent_side",
        7,
        ins,
        [
            ((items, lat, width), BF, None),
            ((lat, width), F32, None),
            ((width, lat), BF, None),
            ((HEADS, lat), F32, None),
            ((HEADS, lat), F32, None),
            ((width, lat), BF, None),
            ((width, lat), BF, None),
            ((feed, lat), BF, None),
            ((lat, feed), BF, None),
            ((lat, width), BF, None),
            ((1, width), F32, None),
        ],
        alias=alias,
        deps=deps,
    )


def flipped(at, bits):
    return sum(((at >> (len(bits) - 1 - t)) & 1) * bit for t, bit in enumerate(bits))


def pick_rows(where, source, lhs_ref, lane, rows, chips, bits):
    lat = source.shape[1]
    for j in range(2 ** len(bits)):
        spot = where[2] ^ flipped(j, bits)
        begin = pl.multiple_of((spot * chips + where[1]) * rows, 16)
        lhs_ref[j * rows : (j + 1) * rows, lane : lane + lat] = source[pl.ds(begin, rows)]


def latent_weights_kernel(plan, items, chips, bits, where, *refs):
    ins, keep_ref, send_ref, lhs_ref = refs[:-3], refs[-3], refs[-2], refs[-1]
    half = keep_ref.shape[1]
    column = 0
    for w, (begin, width) in enumerate(plan):
        lefts = ins[2 * items * w : 2 * items * w + items]
        rights = ins[2 * items * w + items : 2 * items * (w + 1)]
        total = 0.0
        for i in range(items):
            lat = lefts[i].shape[1]
            pick_rows(where, lefts[i], lhs_ref, i * lat, 2 * half, chips, bits)
            right = rights[i]
            if len(right.shape) == 3:
                right = right.at[where[0] * items + i]
            total += nn(lhs_ref[:, i * lat : (i + 1) * lat], right[:, begin : begin + width])
        out = slice(column, column + width)
        for j in range(keep_ref.shape[0]):
            low = total[2 * j * half : (2 * j + 1) * half]
            high = total[(2 * j + 1) * half : (2 * j + 2) * half]
            keep_ref[j, :, out] = jnp.where(where[0] == 0, low, high).astype(BF)
            send_ref[j, :, out] = jnp.where(where[0] == 0, high, low).astype(BF)
        column += width


def latent_weights(groups, plan, chips, bits, name, deps):
    items = len(groups[0][0])
    ins = []
    for lefts, rights in groups:
        ins += [(a, None) for a in lefts + rights]
    width, lat = groups[0][0][0].shape
    count = 2 ** len(bits)
    half = width // (count * chips * CORES)
    shape = (count, half, sum(w for _, w in plan))
    return launch(
        functools.partial(latent_weights_kernel, plan, items, chips, bits),
        name,
        SHORT,
        ins,
        [(shape, BF, None), (shape, BF, None)],
        scratch=[pltpu.VMEM((width // chips, items * lat), BF)],
        deps=deps,
    )


def attend_back_kernel(
    item, score_unit, score_scale, where, q_ref, qt_ref, k_ref, kt_ref, *refs
):
    v_refs, (gatt_ref, lse_ref, dot_ref) = refs[:PARTS], refs[PARTS : PARTS + 3]
    dqt_ref, dkv_ref, dvt_ref = refs[-3:]
    q, qt, k = q_ref[...], qt_ref[...], k_ref[...]
    qk = qt.shape[0]
    depth = qk // HEADS
    wide = gatt_ref.shape[0] // HEADS
    lat = qt.shape[1]
    at = lax.broadcasted_iota(jnp.int32, qt.shape, 0) // depth
    across = lax.broadcasted_iota(jnp.int32, q.shape, 1) // depth

    def begin_head(h):
        score = nn(k, jnp.where(at == h, qt, jnp.zeros_like(qt)))
        grad = gatt_ref[h * wide : (h + 1) * wide]
        begin, ahead = head_span(h % SHARE, wide)
        after = SPAN - ahead - wide
        pieces = [grad]
        if ahead:
            pieces = [jnp.zeros((ahead, lat), BF)] + pieces
        if after:
            pieces = pieces + [jnp.zeros((after, lat), BF)]
        values = v_refs[h // SHARE][:, begin : begin + SPAN]
        return score, grad, nn(values, jnp.concatenate(pieces, 0))

    def finish(h, grad, prob, grad_score):
        dvt_ref[h * wide : (h + 1) * wide] = nt(grad, prob).astype(BF)
        dqt_ref[item, h * depth : (h + 1) * depth] = nn(
            kt_ref[h * depth : (h + 1) * depth], grad_score
        ).astype(BF)
        return nn(grad_score, jnp.where(across == h, q, jnp.zeros_like(q)))

    dk = jnp.zeros(k.shape, F32)
    coming, waiting = begin_head(0), None
    for h in range(HEADS):
        score, grad, grad_prob = coming
        if h + 1 < HEADS:
            coming = begin_head(h + 1)
        if waiting is not None:
            dk += finish(*waiting)
        prob = jnp.exp2(score * score_unit - lse_ref[h : h + 1])
        grad_score = (prob * (grad_prob - dot_ref[h : h + 1])).astype(BF)
        waiting = (h, grad, prob.astype(BF), grad_score)
    dk += finish(*waiting)
    dkv_ref[:, :qk] = (dk * score_scale).astype(BF)
    dkv_ref[:, qk:] = dvt_ref[...].T


def attend_back(
    item, items, q, qt, k, kt, v, gatt, lse, dot, score_unit, score_scale, before, deps
):
    lat, qk = q.shape
    count, wide = v[0].shape[0], gatt.shape[0]
    ins = [(a, None) for a in (q, qt, k, kt, *v, gatt, lse, dot)]
    alias = {}
    for spot, array in enumerate(before):
        alias[len(ins)] = spot
        ins.append((array, None))
    return launch(
        functools.partial(attend_back_kernel, item, score_unit, score_scale),
        "attend_back",
        3.8 if item + 1 < items else SHORT,
        ins,
        [
            ((items, qk, lat), BF, None),
            ((count, qk + wide), BF, None),
        ],
        scratch=[pltpu.VMEM((wide, count), BF)],
        alias=alias,
        deps=deps,
    )


def turn_kernel(bits, where, *refs):
    xn_refs, (keep_ref, send_ref, all_ref) = refs[:-3], refs[-3:]
    count = 2 ** len(bits)
    rows = keep_ref.shape[1] // count
    mine = where[2] * 2 + where[1]
    for i, ref in enumerate(xn_refs):
        all_ref[i] = ref[...].astype(F32).T
    for i in range(len(xn_refs)):
        for out, core in ((keep_ref, where[0]), (send_ref, 1 - where[0])):
            for j in range(0, count, 2):
                pair = []
                for n in (j, j + 1):
                    spot = (mine ^ flipped(n, bits)) * CORES + core
                    begin = pl.multiple_of(spot * rows, 8)
                    pair.append(all_ref[i, pl.ds(begin, rows)])
                out[i, j * rows : (j + 2) * rows] = jnp.concatenate(pair, 0).astype(BF)


def turn(xns, bits, deps):
    count, width = xns[0].shape
    shape = (len(xns), width // CORES, count)
    return launch(
        functools.partial(turn_kernel, bits),
        "turn",
        3,
        [(a, None) for a in xns],
        [(shape, BF, None), (shape, BF, None)],
        scratch=[pltpu.VMEM((len(xns), width, count), F32)],
        deps=deps,
    )


def byte_part_kernel(spots, where, *refs):
    out_ref = refs[-1]
    total = refs[-2][...] if len(refs) % 2 == 0 else 0.0
    for n, spot in enumerate(spots):
        total += nn(refs[2 * n][spot], refs[2 * n + 1][...])
    out_ref[...] = total


def byte_part(pairs, before, micros, deps):
    ins = [(a, None) for turned, _, dkv in pairs for a in (turned, dkv)]
    alias = {}
    if before is not None:
        alias = {len(ins): 0}
        ins.append((before, None))
    shape = (pairs[0][0].shape[1], pairs[0][2].shape[1])
    return launch(
        functools.partial(byte_part_kernel, [p[1] for p in pairs]),
        "byte_part",
        micros,
        ins,
        [(shape, F32, None)],
        alias=alias,
        deps=deps,
    )[0]


def byte_last_kernel(spot, where, turned_ref, dkv_ref, before_ref, keep_ref, send_ref):
    total = before_ref[...] + nn(turned_ref[spot], dkv_ref[...])
    half, rows = keep_ref.shape[:2]
    for j in range(half):
        keep_ref[j] = total[j * rows : (j + 1) * rows].astype(BF)
        send_ref[j] = total[(half + j) * rows : (half + j + 1) * rows].astype(BF)


def byte_last(turned, spot, dkv, before, count, deps):
    shape = (count // 2, turned.shape[1] // count, dkv.shape[1])
    return launch(
        functools.partial(byte_last_kernel, spot),
        "byte_last",
        SHORT,
        [(turned, None), (dkv, None), (before, None)],
        [(shape, BF, None), (shape, BF, None)],
        deps=deps,
    )


def bytes_back_kernel(
    item, where, lang_ref, own_ref, far_ref, table_ref, gain_ref, wk_ref, wv_ref, dkv_ref, *refs
):
    gown_ref, gfar_ref, small_ref = refs[-3:]
    items, count = gfar_ref.shape[:2]
    qk = wk_ref.shape[1]
    langs = table_ref.shape[0]
    gain = gain_ref[...]
    language = lang_ref[where[0] * items + item]
    row = language_row(table_ref, language)
    grads = nt(dkv_ref[:, :qk], wk_ref[...]) + nt(dkv_ref[:, qk:], wv_ref[...])
    gain_sum = jnp.zeros_like(row)
    byte_sum = jnp.zeros_like(row)
    for part, rows, out in (
        (0, own_ref[where[0] * items + item], gown_ref),
        (1, far_ref[item], gfar_ref),
    ):
        unit, inverse = standardise(rows.astype(F32) + row)
        grad = grads[part * count : (part + 1) * count]
        gain_sum += jnp.sum(grad * unit, 0, keepdims=True)
        back = standardise_back(unit, inverse, grad * gain)
        byte_sum += jnp.sum(back, 0, keepdims=True)
        out[item] = back.astype(out.dtype)
    at = lax.broadcasted_iota(jnp.int32, small_ref.shape, 0)
    small = jnp.where(at == language, byte_sum, 0.0) + jnp.where(at == langs, gain_sum, 0.0)
    if item:
        small += refs[2][...]
    small_ref[...] = small


def bytes_back(
    item, items, language, own, far, table, gain, w_key, w_value, dkv, before, deps
):
    shape = far.shape
    ins = [(language, SCALARS)]
    ins += [(a, None) for a in (own, far, table, gain, w_key, w_value, dkv)]
    alias = {}
    if before:
        alias = {len(ins): 0, len(ins) + 1: 1}
        ins += [(a, None) for a in before]
    return launch(
        functools.partial(bytes_back_kernel, item),
        "bytes_back",
        2.5 if item + 1 < items else SHORT,
        ins,
        [
            (shape, F32, None),
            (shape, BF, None),
            ((table.shape[0] + 8, far.shape[2]), F32, None),
        ],
        alias=alias,
        deps=deps,
    )


def latents_back_kernel(
    score_scale, chips, bits, where, da_ref, db_ref, *refs
):
    items = da_ref.shape[0]
    gres_refs, gmlp_refs, refs = refs[:items], refs[items : 2 * items], refs[2 * items :]
    gfar_ref, small_ref, lat_ref, gain_ref, wq_ref = refs[:5]
    glat_ref, keep_ref, send_ref, own_ref = refs[5:9]
    lhs_ref, rhs_ref, turn_ref = refs[9:]
    lat = lat_ref.shape[1]
    gain = gain_ref[...]
    gain_sum = jnp.zeros_like(gain)
    half = keep_ref.shape[1]
    for i in range(items):
        total = (da_ref[i].astype(F32) + db_ref[i].astype(F32)) * score_scale
        grad = total.T.astype(BF)
        rhs_ref[i * lat : (i + 1) * lat] = grad
        unit, inverse = standardise(lat_ref[where[0] * items + i].astype(F32))
        turn_ref[i] = (unit * gain).astype(BF).T
        gln = nt(grad, wq_ref[...])
        gain_sum += jnp.sum(gln * unit, 0, keepdims=True)
        out = gres_refs[i][...] + standardise_back(unit, inverse, gln * gain)
        glat_ref[i, :, : out.shape[1]] = out.astype(BF)
        glat_ref[i, :, out.shape[1] :] = gfar_ref[i]
    gmlp = functools.reduce(jnp.add, [r[...] for r in gmlp_refs])
    wide = own_ref.shape[1]
    at = lax.broadcasted_iota(jnp.int32, (8, wide), 0)
    own = jnp.concatenate(
        [
            jnp.where(at == 1, gain_sum[:, g : g + wide], 0.0)
            + jnp.where(at == 2, gmlp[:, g : g + wide], 0.0)
            for g in range(0, gain.shape[1], wide)
        ],
        0,
    )
    own_ref[...] = own
    count = keep_ref.shape[0]
    send_ref[count] = own.astype(BF)
    tall = [small_ref[:, g : g + wide] for g in range(0, small_ref.shape[1], wide)]
    rest = (send_ref.shape[0] - count - 1) * half - len(tall) * small_ref.shape[0]
    tall = jnp.concatenate(tall + [jnp.zeros((rest, wide), F32)], 0)
    for j in range(count + 1, send_ref.shape[0]):
        send_ref[j] = tall[(j - count - 1) * half : (j - count) * half].astype(BF)
    for i in range(items):
        pick_rows(where, turn_ref.at[i], lhs_ref, i * lat, 2 * half, chips, bits)
    total = nn(lhs_ref[...], rhs_ref[...])
    for j in range(keep_ref.shape[0]):
        low = total[2 * j * half : (2 * j + 1) * half]
        high = total[(2 * j + 1) * half : (2 * j + 2) * half]
        keep_ref[j] = jnp.where(where[0] == 0, low, high).astype(BF)
        send_ref[j] = jnp.where(where[0] == 0, high, low).astype(BF)


def latents_back(da, db, gres, gmlps, gfar, small, latents, gain, w_query, score_scale, chips, bits, deps):
    _, lat, width = latents.shape
    items = da.shape[0]
    qk = w_query.shape[1]
    count = 2 ** len(bits)
    half = width // (count * chips * CORES)
    small_blocks = -(-small.size // (half * qk))
    return launch(
        functools.partial(latents_back_kernel, score_scale, chips, bits),
        "latents_back",
        SHORT,
        [(da, None), (db, None)]
        + [(g, None) for g in gres + gmlps]
        + [(a, None) for a in (gfar, small, latents, gain, w_query)],
        [
            ((items, lat, width + gfar.shape[2]), BF, None),
            ((count, half, qk), BF, None),
            ((count + 1 + small_blocks, half, qk), BF, None),
            ((half, qk), F32, None),
        ],
        scratch=[
            pltpu.VMEM((width // chips, items * lat), BF),
            pltpu.VMEM((items * lat, qk), BF),
            pltpu.VMEM((items, width, lat), BF),
        ],
        deps=deps,
    )


def fold_kernel(where, keep_ref, far_ref, *outs):
    half = keep_ref.shape[0] // 2
    if len(outs) == 1:
        outs[0][...] = keep_ref[0].astype(F32) + far_ref[0].astype(F32)
        return
    for spot, out in enumerate(outs):
        for j in range(half):
            at = spot * half + j
            out[j] = (keep_ref[at].astype(F32) + far_ref[at].astype(F32)).astype(BF)


def fold(keep, far, deps, micros=SHORT):
    if keep.shape[0] == 1:
        outs = [(keep.shape[1:], F32, None)]
    else:
        shape = (keep.shape[0] // 2,) + keep.shape[1:]
        outs = [(shape, BF, None), (shape, BF, None)]
    return launch(fold_kernel, "fold", micros, [(keep, None), (far, None)], outs, deps=deps)


def side_kernel(begin, where, far_ref, small_ref, own_ref, send_ref):
    rows, width = small_ref.shape
    tall = jnp.concatenate([far_ref[j].astype(F32) for j in range(begin, far_ref.shape[0])], 0)
    pieces = [tall[rows * g : rows * (g + 1)] for g in range(width // far_ref.shape[2])]
    own = small_ref[...] + jnp.concatenate(pieces, 1)
    own_ref[...] = own
    send_ref[...] = own.astype(BF)


def side_sum(far, small, begin, deps):
    return launch(
        functools.partial(side_kernel, begin),
        "side_sum",
        1,
        [(far, None), (small, None)],
        [(small.shape, F32, None), (small.shape, BF, None)],
        deps=deps,
    )


def join_kernel(
    langs, chips, bits, where, keep_ref, far_ref, own_ref, side_ref, qkeep_ref, qfar_ref, qown_ref,
    keep_out, send_out,
):
    count, rows, wide = keep_ref.shape
    qrows, qwide = qown_ref.shape

    def across(tall):
        return jnp.concatenate([tall[r : r + 8] for r in range(0, qrows, 8)], 1)

    own = own_ref[...] + side_ref[...].astype(F32)
    gains = across(qown_ref[...] + qfar_ref[count].astype(F32))
    at = lax.broadcasted_iota(jnp.int32, (8, qwide), 1)
    half = count // 2
    for j in range(count):
        spot = where[2] ^ flipped(j, bits)
        device = (spot * chips + where[1]) * CORES + where[0]
        byte_cut = pltpu.roll(own, own.shape[1] - device * rows, 1)[:, :qwide]
        lat_cut = pltpu.roll(gains, gains.shape[1] - device * qrows, 1)[:, :qwide]
        spare = jnp.where(at < rows, byte_cut[:8], 0.0)
        for n in range(1, langs // 8 + 1):
            piece = jnp.where(at < rows, byte_cut[8 * n : 8 * n + 8], 0.0)
            spare += pltpu.roll(piece, n * rows, 1)
        spare += pltpu.roll(jnp.where(at < qrows, lat_cut, 0.0), (langs // 8 + 1) * rows, 1)
        byte = keep_ref[j].astype(F32) + far_ref[j].astype(F32)
        query = across(qkeep_ref[j].astype(F32) + qfar_ref[j].astype(F32))
        out = keep_out if j < half else send_out
        below = jnp.concatenate([query, spare], 1)
        out[j % half] = jnp.concatenate([byte, below], 0).astype(BF)


def join(keep, far, own, side, qkeep, qfar, qown, langs, chips, bits, deps):
    count, rows, wide = keep.shape
    shape = (count // 2, rows + 8, wide)
    return launch(
        functools.partial(join_kernel, langs, chips, bits),
        "join",
        LONG,
        [(a, None) for a in (keep, far, own, side, qkeep, qfar, qown)],
        [(shape, BF, None), (shape, BF, None)],
        deps=deps,
    )


def part_kernel(
    where, keep_ref, far_ref, key_ref, value_ref, query_ref, lang_ref, gin_ref, glat_ref, gmlp_ref
):
    total = keep_ref[0].astype(F32) + far_ref[0].astype(F32)
    rows, qk = key_ref.shape
    qrows, langs = query_ref.shape[0], lang_ref.shape[0]
    key_ref[...] = total[:rows, :qk]
    value_ref[...] = total[:rows, qk:]
    for r in range(0, qrows, 8):
        query_ref[r : r + 8] = total[rows:, r // 8 * qk : (r // 8 + 1) * qk]
    spare = total[rows:, qrows // 8 * qk : (qrows // 8 + 1) * qk]
    groups = langs // 8
    for n in range(groups):
        lang_ref[8 * n : 8 * n + 8] = spare[:, n * rows : (n + 1) * rows]
    gin_ref[...] = spare[:1, groups * rows : (groups + 1) * rows]
    begin = (groups + 1) * rows
    glat_ref[...] = spare[1:2, begin : begin + qrows]
    gmlp_ref[...] = spare[2:3, begin : begin + qrows]


def part(keep, far, qk, qrows, langs, deps):
    rows, wide = keep.shape[1] - 8, keep.shape[2]
    shapes = [(rows, qk), (rows, wide - qk), (qrows, qk), (langs, rows)]
    shapes += [(1, rows), (1, qrows), (1, qrows)]
    return launch(
        part_kernel,
        "part",
        SHORT,
        [(keep, None), (far, None)],
        [(shape, F32, None) for shape in shapes],
        deps=deps,
    )


def last_kernel(where, keep_a, far_a, keep_b, far_b, up_ref, down_ref, out_ref):
    wide = up_ref.shape[1]
    split = out_ref.shape[1] // 2
    first = keep_a[0].astype(F32) + far_a[0].astype(F32)
    second = keep_b[0].astype(F32) + far_b[0].astype(F32)
    up_ref[...] = first[:, :wide]
    down_ref[...] = second[:, :wide]
    out_ref[:, :split] = first[:, wide:]
    out_ref[:, split:] = second[:, wide:]


def last(keep_a, far_a, keep_b, far_b, width, deps):
    shape = (keep_a.shape[1], width)
    return launch(
        last_kernel,
        "last",
        SHORT,
        [(a, None) for a in (keep_a, far_a, keep_b, far_b)],
        [(shape, F32, None)] * 3,
        deps=deps,
    )


def place_kernel(columns, where, *refs):
    count = len(columns)
    items = pl.num_programs(0) // 2
    ours = pl.program_id(0) // items == where[0]
    for n, (left, right) in enumerate(columns):
        out = refs[2 * count + n]
        wide = out.shape[2]
        own = refs[n][:, :, left : left + wide].astype(out.dtype)
        far = refs[count + n][:, :, right : right + wide].astype(out.dtype)
        out[...] = jnp.where(ours, own, far)
    refs[-1][...] = jnp.zeros_like(refs[-1])


def place(pairs, micros, deps):
    items = pairs[0][0].shape[0]
    one = lambda a: (1,) + a.shape[1:]
    rows = lambda p: p[0].shape[1]
    outs = [
        ((2 * items, rows(p), p[4]), p[5], block((1, rows(p), p[4]), lambda g: g))
        for p in pairs
    ]
    return launch(
        functools.partial(place_kernel, [(p[1], p[3]) for p in pairs]),
        "place",
        micros,
        [(a, block(one(a), lambda g: g % items)) for a in [p[0] for p in pairs]]
        + [(a, block(one(a), lambda g: g % items)) for a in [p[2] for p in pairs]],
        outs + [((8, 128), F32, None)],
        deps=deps,
        grid=2 * items,
        far=True,
    )


def swap(value, axis, bit):
    size = lax.axis_size(axis)
    return lax.ppermute(value, axis, [(i, i ^ bit) for i in range(size)])


def bits_of(size):
    return [2**t for t in range(size.bit_length() - 1)]


def halve(value, dim, axis, bit):
    mine = (lax.axis_index(axis) // bit) % 2
    keep = lax.dynamic_index_in_dim(value, mine, dim, keepdims=False)
    send = lax.dynamic_index_in_dim(value, 1 - mine, dim, keepdims=False)
    return (keep.astype(F32) + swap(send, axis, bit).astype(F32)).astype(BF)


def scatter_rows(value):
    spots, chips = lax.axis_size("batch"), lax.axis_size("seq") // CORES
    rows = value.shape[0] // (spots * chips * CORES)
    blocks = value.astype(BF).reshape(spots, chips, CORES, rows, value.shape[1])
    blocks = halve(blocks, 2, "seq", 1)
    for bit in bits_of(chips):
        rest = blocks.shape[2:]
        blocks = blocks.reshape((spots, blocks.shape[1] // 2, 2) + rest)
        blocks = halve(blocks, 2, "seq", CORES * bit)
    blocks = blocks[:, 0]
    for bit in bits_of(spots):
        blocks = blocks.reshape((blocks.shape[0] // 2, 2) + blocks.shape[1:])
        blocks = halve(blocks, 1, "batch", bit)
    return blocks[0].astype(F32)


def everywhere(value):
    for axis in ("seq", "batch"):
        for bit in bits_of(lax.axis_size(axis)):
            value = value + swap(value, axis, bit)
    return value


def merge(oa, ob):
    rows = oa.shape[0] - TERMS * SHARE
    wide = rows // SHARE
    la, lb = part_sums(oa[rows:].astype(F32)), part_sums(ob[rows:].astype(F32))
    top = jnp.maximum(la, lb)
    ea, eb = jnp.exp2(la - top), jnp.exp2(lb - top)
    total = ea + eb
    lse = top + jnp.log2(total)
    out = oa[:rows].astype(F32) * jnp.repeat(ea / total, wide, 0)
    out = out + ob[:rows].astype(F32) * jnp.repeat(eb / total, wide, 0)
    return jnp.concatenate([out.astype(BF), part_terms(lse)], 0)


def local(
    byte_inputs,
    language,
    lang_table,
    latents,
    gain_in,
    gain_lat,
    gain_mlp,
    w_query,
    w_key,
    w_value,
    w_out,
    w_up,
    w_down,
    cotangent,
):
    items = byte_inputs.shape[0] // CORES
    width_in, width_lat = byte_inputs.shape[2], latents.shape[2]
    lat, qk = latents.shape[1], w_query.shape[1]
    langs = lang_table.shape[0]
    score_scale = 1.0 / math.sqrt(qk // HEADS)
    score_unit = score_scale * math.log2(math.e)
    spots, chips = lax.axis_size("batch"), lax.axis_size("seq") // CORES
    devices = spots * chips * CORES
    seq_at, spot = lax.axis_index("seq"), lax.axis_index("batch")
    core, side = seq_at % CORES, seq_at // CORES
    device = spot * (chips * CORES) + seq_at
    chip_bits, spot_bits = bits_of(chips), bits_of(spots)
    rows_in, rows_lat = width_in // devices, width_lat // devices
    direct = (
        chips == 2
        and rows_in == langs + 8
        and rows_lat * qk == 8 * width_lat
        and width_lat % qk == 0
        and langs % 8 == 0
        and byte_inputs.shape[1] == lat
    )
    last_bit = chip_bits[-1]
    table = lang_table
    gain_in, gain_lat, gain_mlp = gain_in[None], gain_lat[None], gain_mlp[None]

    far = swap(pick_bytes(byte_inputs, items), "seq", 1)
    asked = queries(items, latents, gain_lat, w_query, ())
    asked = [asked[2 * i : 2 * i + 2] for i in range(items)]
    xns, kept, pairs, token = [], [], [], ()
    for item in range(items):
        ots, xn, k, kt, v = attend(
            item, items, language, byte_inputs, far, table, gain_in, w_key, w_value,
            asked[item][1], score_unit, token,
        )
        xns.append(xn)
        kept.append((k, kt, v))
        token = (v[-1],)
        for bit in chip_bits[:-1]:
            ots = [merge(ot, swap(ot, "seq", CORES * bit)) for ot in ots]
        pairs.append((ots, [swap(ot, "seq", CORES * last_bit) for ot in ots]))

    gact = act_back(cotangent, w_down, items, token)
    token = (gact,)
    sides, outs, dqkv, dkvs = [], None, (), []
    if direct:
        y_bit, z_bit, far_bit = spot_bits
        a_bits, b_bits = [y_bit, z_bit, far_bit], [z_bit, far_bit, y_bit]
        c_bits = [1] + [2 * b for b in a_bits]
        turned, turned_send = turn(xns, c_bits, token)
        turned_far = swap(turned_send, "seq", 1)
        part_c, far_pairs = None, []

    def back(item, deps):
        gatt, dot, lse = sides[item][2:5]
        return attend_back(
            item, items, *asked[item], *kept[item], gatt, lse, dot, score_unit, score_scale, dqkv, deps
        )

    byted = ()

    def back_bytes(item, deps):
        return bytes_back(
            item, items, language, byte_inputs, far, table, gain_in, w_key, w_value,
            dkvs[item], byted, deps,
        )

    for item in range(items):
        if item:
            *dqkv, dkv = back(item - 1, token)
            dkvs.append(dkv)
            byted = back_bytes(item - 1, ())
            token = (byted[2],)
            if direct:
                dkv_far = swap(dkv, "seq", 1)
                part_c = byte_part([(turned, item - 1, dkv)], part_c, 1, token)
                far_pairs.append((turned_far, item - 1, dkv_far))
                token = (part_c,)
        side_out = latent_side(
            item, items, last_bit, *pairs[item], latents, cotangent,
            gact, gain_mlp, w_out, w_up, w_down, outs, token,
        )
        outs = side_out[0]
        sides.append(side_out)
        token = (side_out[3],)
    outs_far = swap(outs, "seq", 1)

    pick = lambda at: [s[at] for s in sides]
    down = (pick(7), [cotangent] * items)
    up = (pick(6), pick(8))
    out = (pick(5), pick(9))

    if direct:
        split = width_lat // 2
        keep_a, send_a = latent_weights(
            [up, out], [(0, width_lat), (0, split)], chips, a_bits, "weights_a", token
        )
        far_a = swap(send_a, "seq", 1)
        keep_b, send_b = latent_weights(
            [down, out], [(0, width_lat), (split, split)], chips, b_bits, "weights_b",
            (keep_a,),
        )
        far_b = swap(send_b, "seq", 1)
        early = [a for pair in far_pairs for a in (pair[0], pair[2])]
        dqt, dkv = back(items - 1, (keep_b, *early))
        dkvs.append(dkv)
        dkv_far = swap(dkv, "seq", 1)
        dqt_far = swap(dqt, "seq", CORES)
        keep_a, send_a = fold(keep_a, far_a, (dqt, outs_far), 5)
        far_a = swap(send_a, "batch", a_bits[0])
        keep_b, send_b = fold(keep_b, far_b, (keep_a,), 5)
        far_b = swap(send_b, "batch", b_bits[0])
        part_c = byte_part(
            far_pairs + [(turned, items - 1, dkv)], part_c, SHORT, (keep_b,)
        )
        keep_c, send_c = byte_last(
            turned_far, items - 1, dkv_far, part_c, 2 ** len(c_bits), ()
        )
        far_c = swap(send_c, "seq", CORES)
        gown, gfar, small = back_bytes(items - 1, (keep_c,))
        glats, keep_q, send_q, own_q = latents_back(
            dqt, dqt_far, pick(1), pick(10), gfar, small, latents, gain_lat, w_query,
            score_scale, chips, a_bits, (),
        )
        glats_far = swap(glats, "seq", 1)
        far_q = swap(send_q, "seq", 1)
        own_s, send_s = side_sum(far_q, small, keep_q.shape[0] + 1, ())
        far_s = swap(send_s, "seq", CORES)
        keep_b, send_b = fold(keep_b, far_b, (own_s,))
        far_b = swap(send_b, "batch", b_bits[1])
        keep_a, send_a = fold(keep_a, far_a, (keep_b,))
        far_a = swap(send_a, "batch", a_bits[1])
        keep_c, send_c = join(
            keep_c, far_c, own_s, far_s, keep_q, far_q, own_q, langs, chips, a_bits,
            (keep_a,),
        )
        far_c = swap(send_c, "batch", a_bits[0])
        latents_out, grad_bytes, token = place(
            [
                (outs, 0, outs_far, 0, width_lat, BF),
                (gown, 0, glats_far, width_lat, width_in, F32),
            ],
            LONG,
            (keep_c,),
        )
        keep_c, send_c = fold(keep_c, far_c, (token,))
        far_c = swap(send_c, "batch", a_bits[1])
        keep_b, send_b = fold(keep_b, far_b, (keep_c,))
        far_b = swap(send_b, "batch", b_bits[2])
        keep_a, send_a = fold(keep_a, far_a, (keep_b,))
        far_a = swap(send_a, "batch", a_bits[2])
        grad_latents, token = place(
            [(glats, 0, glats_far, 0, width_lat, F32)], SHORT, (keep_a,)
        )
        keep_c, send_c = fold(keep_c, far_c, (token,))
        far_c = swap(send_c, "batch", a_bits[2])
        g_up, g_down, g_out = last(keep_a, far_a, keep_b, far_b, width_lat, (keep_c,))
        g_key, g_value, g_query, g_table, *gains = part(
            keep_c, far_c, qk, rows_lat, langs, ()
        )
        g_in, g_lat, g_mlp = [g[0] for g in gains]
    else:
        dqt, dkv = back(items - 1, token)
        dkvs.append(dkv)
        for bit in chip_bits:
            dqt = (dqt.astype(F32) + swap(dqt, "seq", CORES * bit).astype(F32)).astype(BF)
        gown, gfar, small = back_bytes(items - 1, ())
        gfar_far = swap(gfar, "seq", 1)
        own_cut = lambda a: lax.dynamic_slice_in_dim(a, core * items, items, 0)
        grad_q = (dqt.astype(F32) * score_scale).swapaxes(1, 2).astype(BF)
        unit, inverse = standardise(own_cut(latents).astype(F32))
        gln = lax.dot_general(
            grad_q, w_query, (((2,), (1,)), ((), ())), preferred_element_type=F32
        )
        glats = jnp.stack(pick(1)) + standardise_back(unit, inverse, gln * gain_lat)
        glats = glats.astype(BF)
        glats_far = swap(glats, "seq", 1)
        flat = lambda a: a.reshape(-1, a.shape[-1])
        share = 1.0 / chips
        g_query = scatter_rows(tn(flat((unit * gain_lat).astype(BF)), flat(grad_q)) * share)
        rows = lambda lefts, rights: scatter_rows(
            sum(nn(x, y) for x, y in zip(lefts, rights)) * share
        )
        g_down = rows(pick(7), own_cut(cotangent))
        g_up, g_out = rows(pick(6), pick(8)), rows(pick(5), pick(9))
        g_bytes = scatter_rows(sum(tn(xns[i], dkvs[i]) for i in range(items)))
        g_key, g_value = g_bytes[:, :qk], g_bytes[:, qk:]
        pad = ((0, 0), (0, width_lat - width_in))
        small = jnp.concatenate(
            [
                jnp.pad(small[: langs + 1], pad),
                jnp.sum(gln * unit, (0, 1))[None] * share,
                sum(pick(10)) * share,
            ],
            0,
        )
        small = everywhere(small)
        cut = lambda rows, count: lax.dynamic_slice_in_dim(rows, device * count, count, 1)
        g_table, g_in = cut(small[:langs], rows_in), cut(small[langs : langs + 1], rows_in)[0]
        g_lat, g_mlp = cut(small[langs + 1 :], rows_lat)
        latents_out, grad_bytes, grad_latents, _ = place(
            [
                (outs, 0, outs_far, 0, width_lat, BF),
                (gown, 0, gfar_far, 0, width_in, F32),
                (glats, 0, glats_far, 0, width_lat, F32),
            ],
            SHORT,
            (),
        )

    return (
        latents_out,
        grad_latents,
        grad_bytes,
        g_table,
        g_in,
        g_lat,
        g_mlp,
        g_query,
        g_key,
        g_value,
        g_out,
        g_up,
        g_down,
    )


def solution(mesh):
    return jax.shard_map(
        local,
        mesh=mesh,
        in_specs=(
            P("batch", "seq", None),
            P("batch"),
            P(),
            P("batch", None, None),
            P(),
            P(),
            P(),
            P(),
            P(),
            P(),
            P(),
            P(),
            P(),
            P("batch", None, None),
        ),
        out_specs=(
            P("batch", None, None),
            P("batch", None, None),
            P("batch", "seq", None),
            P(None, ("batch", "seq")),
            P(("batch", "seq")),
            P(("batch", "seq")),
            P(("batch", "seq")),
            P(("batch", "seq"), None),
            P(("batch", "seq"), None),
            P(("batch", "seq"), None),
            P(("batch", "seq"), None),
            P(("batch", "seq"), None),
            P(("batch", "seq"), None),
        ),
        check_vma=False,
    )
```

```python
import functools
import math

import jax
import jax.numpy as jnp
from jax import lax
from jax.experimental import pallas as pl
from jax.experimental.pallas import tpu as pltpu
from jax.sharding import PartitionSpec as P

HEADS = 8
CORES = 2
EPS = 1e-05
F32 = jnp.float32
BF = jnp.bfloat16
VMEM_LIMIT = 12 * 1024 * 1024
PEAK = 1.15e9
SHORT, LONG, AHEAD = 0.001, 40, 3


def nn(a, b):
    return lax.dot_general(a, b, (((1,), (0,)), ((), ())), preferred_element_type=F32)


def nt(a, b):
    return lax.dot_general(a, b, (((1,), (1,)), ((), ())), preferred_element_type=F32)


def tn(a, b):
    return lax.dot_general(a, b, (((0,), (0,)), ((), ())), preferred_element_type=F32)


def standardise(x):
    centre = x - jnp.mean(x, -1, keepdims=True)
    inverse = lax.rsqrt(jnp.mean(centre * centre, -1, keepdims=True) + EPS)
    return centre * inverse, inverse


def standardise_back(unit, inverse, grad):
    return inverse * (
        grad - jnp.mean(grad, -1, keepdims=True) - unit * jnp.mean(grad * unit, -1, keepdims=True)
    )


def block(shape, at):
    return pl.BlockSpec(shape, lambda g: (at(g),) + (0,) * (len(shape) - 1))


ANY = pl.BlockSpec(memory_space=pl.ANY)
FAST = pl.BlockSpec(memory_space=pltpu.VMEM)
FAR = pl.BlockSpec(memory_space=pltpu.HBM)
SCALARS = pl.BlockSpec(memory_space=pltpu.SMEM)


def launch(body, name, micros, ins, outs, scratch=(), deps=(), alias=None, grid=1, far=False):
    count, extra = len(ins), len(deps)
    ins = [
        (pltpu.with_memory_space_constraint(a, pltpu.HBM) if s is FAR else a, s) for a, s in ins
    ]

    def kernel(*refs):
        body(Where(), *refs[:count], *refs[count + extra :])

    return pl.pallas_call(
        kernel,
        grid=(grid,),
        in_specs=[FAST if s is None else s for _, s in ins] + [ANY] * extra,
        out_specs=[FAST if s is None else s for _, _, s in outs],
        scratch_shapes=list(scratch),
        out_shape=[
            (jax.ShapeDtypeStruct if s is None or not far else pltpu.HBM)(shape, dtype)
            for shape, dtype, s in outs
        ],
        input_output_aliases=alias or {},
        compiler_params=pltpu.CompilerParams(vmem_limit_bytes=VMEM_LIMIT),
        cost_estimate=pl.CostEstimate(
            flops=int(micros * PEAK), bytes_accessed=1, transcendentals=0
        ),
        name=name,
    )(*[a for a, _ in ins], *deps)


class Where:
    def __getitem__(self, at):
        if at == 2:
            return lax.axis_index("batch")
        return (lax.rem, lax.div)[at](lax.axis_index("seq"), CORES)


def pick_kernel(where, own_ref, out_ref, arrived):
    items = out_ref.shape[0]
    copy = pltpu.make_async_copy(
        own_ref.at[pl.ds((1 - where[0]) * items, items)], out_ref, arrived
    )
    copy.start()
    copy.wait()


def pick_bytes(own, items):
    return launch(
        pick_kernel,
        "pick_bytes",
        AHEAD,
        [(own, FAR)],
        [((items,) + own.shape[1:], BF, None)],
        scratch=[pltpu.SemaphoreType.DMA(())],
    )[0]


def query_kernel(where, lang_ref, table_ref, lat_ref, gain_ref, wq_ref, *outs):
    outs, rows_ref = outs[:-1], outs[-1]
    items = len(outs) // 2
    for i in range(items):
        row = language_row(table_ref, lang_ref[where[0] * items + i])
        rows_ref[i] = jnp.broadcast_to(row, rows_ref.shape[1:])
        unit, _ = standardise(lat_ref[where[0] * items + i].astype(F32))
        rows = nn((unit * gain_ref[...]).astype(BF), wq_ref[...])
        outs[2 * i][...] = rows.astype(BF)
        outs[2 * i + 1][...] = rows.T.astype(BF)


def queries(items, language, table, latents, gain, w_query, deps):
    _, count, width = latents.shape
    qk = w_query.shape[1]
    return launch(
        query_kernel,
        "queries",
        2,
        [(language, SCALARS), (table, None), (latents, None), (gain, None), (w_query, None)],
        [((count, qk), BF, None), ((qk, count), BF, None)] * items
        + [((items, 8, table.shape[1]), F32, None)],
        deps=deps,
    )


SPAN = 256


def head_span(h, wide):
    begin = h * wide // 128 * 128
    return begin, h * wide - begin


def language_row(table_ref, language):
    at = lax.broadcasted_iota(jnp.int32, table_ref.shape, 0)
    table = table_ref[...].astype(F32)
    return jnp.sum(jnp.where(at == language, table, 0.0), 0, keepdims=True)


PARTS = 2
SHARE = HEADS // PARTS
TERMS = 4


def part_terms(lse):
    terms, left = [], lse
    for _ in range(TERMS):
        terms.append(left.astype(BF).astype(F32))
        left = left - terms[-1]
    return jnp.concatenate(terms, 0).astype(BF)


def part_sums(terms):
    total = terms[(TERMS - 1) * SHARE :]
    for n in reversed(range(TERMS - 1)):
        total = terms[n * SHARE : (n + 1) * SHARE] + total
    return total


def heads_out(part, score_unit, k, v, qt, ot_ref):
    depth = qt.shape[0] // HEADS
    wide = v.shape[1] // SHARE
    at = lax.broadcasted_iota(jnp.int32, qt.shape, 0) // depth

    def score_of(h):
        return nn(k, jnp.where(at == part * SHARE + h, qt, jnp.zeros_like(qt)))

    def finish(h, weight, total):
        begin, ahead = head_span(h, wide)
        out = tn(v[:, begin : begin + SPAN], weight)[ahead : ahead + wide]
        ot_ref[h * wide : (h + 1) * wide] = (out * (1.0 / total)).astype(BF)

    lse = []
    coming, waiting = score_of(0), None
    for h in range(SHARE):
        score = coming * score_unit
        if h + 1 < SHARE:
            coming = score_of(h + 1)
        if waiting is not None:
            finish(*waiting)
        top = jnp.max(score, 0, keepdims=True)
        weight = jnp.exp2(score - top)
        total = jnp.sum(weight, 0, keepdims=True)
        lse.append(top + jnp.log2(total))
        waiting = (h, weight.astype(BF), total)
    finish(*waiting)
    lse = jnp.concatenate(lse, 0)
    ot_ref[SHARE * wide :] = part_terms(lse)


def attend_kernel(
    item, items, score_unit, where, own_ref, far_ref, rows_ref, gain_ref, wk_ref,
    wv_ref, qt_ref, ot_ref, xn_ref, k_ref, kt_ref, v_ref,
):
    at = where[0] * items + item
    count = far_ref.shape[1]
    row = rows_ref[item, :1]
    gain = gain_ref[...]
    for part, rows in enumerate((own_ref[at], far_ref[item])):
        unit, _ = standardise(rows.astype(F32) + row)
        xn_ref[part * count : (part + 1) * count] = (unit * gain).astype(BF)
    xn = xn_ref[...]
    k = nn(xn, wk_ref[...]).astype(BF)
    k_ref[...] = k
    kt_ref[...] = k.T
    v = nn(xn, wv_ref[:, : v_ref.shape[1]]).astype(BF)
    v_ref[...] = v
    heads_out(0, score_unit, k, v, qt_ref[...], ot_ref)


def attend_more_kernel(part, score_unit, where, xn_ref, k_ref, wv_ref, qt_ref, ot_ref, v_ref):
    wide = v_ref.shape[1]
    v = nn(xn_ref[...], wv_ref[:, part * wide : (part + 1) * wide]).astype(BF)
    v_ref[...] = v
    heads_out(part, score_unit, k_ref[...], v, qt_ref[...], ot_ref)


def attend(
    item, items, own, far, rows, gain, w_key, w_value, qt, score_unit, deps
):
    _, count, width = own.shape
    qk, lat = w_key.shape[1], qt.shape[1]
    wide = w_value.shape[1] // PARTS
    out = ((wide + TERMS * SHARE, lat), BF, None)
    values = ((2 * count, wide), BF, None)
    first, xn, k, kt, v = launch(
        functools.partial(attend_kernel, item, items, score_unit),
        "attend",
        2.4,
        [(a, None) for a in (own, far, rows, gain, w_key, w_value, qt)],
        [
            out,
            ((2 * count, width), BF, None),
            ((2 * count, qk), BF, None),
            ((qk, 2 * count), BF, None),
            values,
        ],
        deps=deps,
    )
    outs, vs = [first], [v]
    for part in range(1, PARTS):
        more, v = launch(
            functools.partial(attend_more_kernel, part, score_unit),
            "attend_more",
            1.9,
            [(a, None) for a in (xn, k, w_value, qt)],
            [out, values],
        )
        outs.append(more)
        vs.append(v)
    return outs, xn, k, kt, vs


def act_back_kernel(where, cot_ref, wd_ref, gact_ref):
    items = gact_ref.shape[0]
    for i in range(items):
        gact_ref[i] = nt(cot_ref[where[0] * items + i], wd_ref[...])


def act_back(cot, w_down, items, deps):
    return launch(
        act_back_kernel,
        "act_back",
        2.5,
        [(cot, None), (w_down, None)],
        [((items, cot.shape[1], w_down.shape[0]), F32, None)],
        deps=deps,
    )[0]


GELU_A = math.sqrt(2.0 / math.pi)
GELU_B = 0.044715


def latent_kernel(
    item, items, bit, where, *refs
):
    oa_refs, ob_refs, refs = refs[:PARTS], refs[PARTS : 2 * PARTS], refs[2 * PARTS :]
    lat_ref, cot_ref, gact_ref, gain_ref, wo_ref, wu_ref, wd_ref = refs[:7]
    (
        outs_ref, gres_ref, gatt_ref, dot_ref, lse_ref, att_ref, hid_ref, act_ref, gpre_ref,
        glow_ref, ggain_ref,
    ) = refs[-11:]
    at = where[0] * items + item
    first = lax.rem(lax.div(where[1], bit), 2) == 0
    rows = gatt_ref.shape[0]
    wide = rows // HEADS
    ours, theirs = (
        jnp.concatenate(
            [part_sums(ref[rows // PARTS :].astype(F32)) for ref in refs_], 0
        )
        for refs_ in (oa_refs, ob_refs)
    )
    left = jnp.where(first, ours, theirs)
    right = jnp.where(first, theirs, ours)
    top = jnp.maximum(left, right)
    e_left, e_right = jnp.exp2(left - top), jnp.exp2(right - top)
    total = e_left + e_right
    lse_ref[...] = top + jnp.log2(total)
    scale = 1.0 / total
    e_left, e_right = e_left * scale, e_right * scale
    merged = []
    for h in range(HEADS):
        cut = slice(h % SHARE * wide, (h % SHARE + 1) * wide)
        a = oa_refs[h // SHARE][cut].astype(F32)
        b = ob_refs[h // SHARE][cut].astype(F32)
        low, high = jnp.where(first, a, b), jnp.where(first, b, a)
        merged.append(low * e_left[h : h + 1] + high * e_right[h : h + 1])
        att_ref[h * wide : (h + 1) * wide] = merged[-1].astype(BF)
    resid = lat_ref[at].astype(F32) + tn(att_ref[...], wo_ref[...])
    unit, inverse = standardise(resid)
    gain = gain_ref[...]
    hidden = (unit * gain).astype(BF)
    hid_ref[...] = hidden.T
    pre = nn(hidden, wu_ref[...])
    square = pre * pre
    slope = jnp.tanh(GELU_A * pre * (1.0 + GELU_B * square))
    act = (0.5 * pre * (1.0 + slope)).astype(BF)
    act_ref[...] = act.T
    outs_ref[item] = (resid + nn(act, wd_ref[...])).astype(BF)
    cot = cot_ref[at]
    gelu_slope = 0.5 * (1.0 + slope) + 0.5 * pre * (1.0 - slope * slope) * GELU_A * (
        1.0 + 3.0 * GELU_B * square
    )
    gpre = (gact_ref[item] * gelu_slope).astype(BF)
    gpre_ref[...] = gpre
    ghid = nt(gpre, wu_ref[...])
    ggain_ref[...] = jnp.sum(ghid * unit, 0, keepdims=True)
    gres = cot.astype(F32) + standardise_back(unit, inverse, ghid * gain)
    gres_ref[...] = gres
    glow = gres.astype(BF)
    glow_ref[...] = glow
    gatt_ref[...] = nt(wo_ref[...], glow).astype(BF)
    for h in range(HEADS):
        dot_ref[h : h + 1] = jnp.sum(
            gatt_ref[h * wide : (h + 1) * wide].astype(F32) * merged[h], 0, keepdims=True
        )


def latent_side(
    item, items, bit, oa, ob, latents, cot, gact, gain, w_out, w_up, w_down, before, deps
):
    total, lat, width = latents.shape
    feed = w_up.shape[1]
    ins = [(a, None) for a in (*oa, *ob, latents, cot, gact, gain, w_out, w_up, w_down)]
    alias = {}
    if before is not None:
        alias[len(ins)] = 0
        ins.append((before, None))
    return launch(
        functools.partial(latent_kernel, item, items, bit),
        "latent_side",
        7,
        ins,
        [
            ((items, lat, width), BF, None),
            ((lat, width), F32, None),
            ((width, lat), BF, None),
            ((HEADS, lat), F32, None),
            ((HEADS, lat), F32, None),
            ((width, lat), BF, None),
            ((width, lat), BF, None),
            ((feed, lat), BF, None),
            ((lat, feed), BF, None),
            ((lat, width), BF, None),
            ((1, width), F32, None),
        ],
        alias=alias,
        deps=deps,
    )


def flipped(at, bits):
    return sum(((at >> (len(bits) - 1 - t)) & 1) * bit for t, bit in enumerate(bits))


def pick_rows(where, source, lhs_ref, lane, rows, chips, bits):
    lat = source.shape[1]
    for j in range(2 ** len(bits)):
        spot = where[2] ^ flipped(j, bits)
        begin = pl.multiple_of((spot * chips + where[1]) * rows, 16)
        lhs_ref[j * rows : (j + 1) * rows, lane : lane + lat] = source[pl.ds(begin, rows)]


def latent_weights_kernel(plan, items, chips, bits, where, *refs):
    ins, keep_ref, send_ref, lhs_ref = refs[:-3], refs[-3], refs[-2], refs[-1]
    half = keep_ref.shape[1]
    column = 0
    for w, (begin, width) in enumerate(plan):
        lefts = ins[2 * items * w : 2 * items * w + items]
        rights = ins[2 * items * w + items : 2 * items * (w + 1)]
        total = 0.0
        for i in range(items):
            lat = lefts[i].shape[1]
            pick_rows(where, lefts[i], lhs_ref, i * lat, 2 * half, chips, bits)
            right = rights[i]
            if len(right.shape) == 3:
                right = right.at[where[0] * items + i]
            total += nn(lhs_ref[:, i * lat : (i + 1) * lat], right[:, begin : begin + width])
        out = slice(column, column + width)
        for j in range(keep_ref.shape[0]):
            low = total[2 * j * half : (2 * j + 1) * half]
            high = total[(2 * j + 1) * half : (2 * j + 2) * half]
            keep_ref[j, :, out] = jnp.where(where[0] == 0, low, high).astype(BF)
            send_ref[j, :, out] = jnp.where(where[0] == 0, high, low).astype(BF)
        column += width


def latent_weights(groups, plan, chips, bits, name, deps):
    items = len(groups[0][0])
    ins = []
    for lefts, rights in groups:
        ins += [(a, None) for a in lefts + rights]
    width, lat = groups[0][0][0].shape
    count = 2 ** len(bits)
    half = width // (count * chips * CORES)
    shape = (count, half, sum(w for _, w in plan))
    return launch(
        functools.partial(latent_weights_kernel, plan, items, chips, bits),
        name,
        SHORT,
        ins,
        [(shape, BF, None), (shape, BF, None)],
        scratch=[pltpu.VMEM((width // chips, items * lat), BF)],
        deps=deps,
    )


def attend_back_kernel(
    item, score_unit, score_scale, where, q_ref, qt_ref, k_ref, kt_ref, *refs
):
    v_refs, (gatt_ref, lse_ref, dot_ref) = refs[:PARTS], refs[PARTS : PARTS + 3]
    dqt_ref, dkv_ref, dvt_ref = refs[-3:]
    q, qt, k = q_ref[...], qt_ref[...], k_ref[...]
    qk = qt.shape[0]
    depth = qk // HEADS
    wide = gatt_ref.shape[0] // HEADS
    lat = qt.shape[1]
    at = lax.broadcasted_iota(jnp.int32, qt.shape, 0) // depth
    across = lax.broadcasted_iota(jnp.int32, q.shape, 1) // depth

    def begin_head(h):
        score = nn(k, jnp.where(at == h, qt, jnp.zeros_like(qt)))
        grad = gatt_ref[h * wide : (h + 1) * wide]
        begin, ahead = head_span(h % SHARE, wide)
        after = SPAN - ahead - wide
        pieces = [grad]
        if ahead:
            pieces = [jnp.zeros((ahead, lat), BF)] + pieces
        if after:
            pieces = pieces + [jnp.zeros((after, lat), BF)]
        values = v_refs[h // SHARE][:, begin : begin + SPAN]
        return score, grad, nn(values, jnp.concatenate(pieces, 0))

    def finish(h, grad, prob, grad_score):
        dvt_ref[h * wide : (h + 1) * wide] = nt(grad, prob).astype(BF)
        dqt_ref[item, h * depth : (h + 1) * depth] = nn(
            kt_ref[h * depth : (h + 1) * depth], grad_score
        ).astype(BF)
        return nn(grad_score, jnp.where(across == h, q, jnp.zeros_like(q)))

    dk = jnp.zeros(k.shape, F32)
    coming, waiting = begin_head(0), None
    for h in range(HEADS):
        score, grad, grad_prob = coming
        if h + 1 < HEADS:
            coming = begin_head(h + 1)
        if waiting is not None:
            dk += finish(*waiting)
        prob = jnp.exp2(score * score_unit - lse_ref[h : h + 1])
        grad_score = (prob * (grad_prob - dot_ref[h : h + 1])).astype(BF)
        waiting = (h, grad, prob.astype(BF), grad_score)
    dk += finish(*waiting)
    dkv_ref[:, :qk] = (dk * score_scale).astype(BF)
    dkv_ref[:, qk:] = dvt_ref[...].T


def attend_back(
    item, items, q, qt, k, kt, v, gatt, lse, dot, score_unit, score_scale, before, deps
):
    lat, qk = q.shape
    count, wide = v[0].shape[0], gatt.shape[0]
    ins = [(a, None) for a in (q, qt, k, kt, *v, gatt, lse, dot)]
    alias = {}
    for spot, array in enumerate(before):
        alias[len(ins)] = spot
        ins.append((array, None))
    return launch(
        functools.partial(attend_back_kernel, item, score_unit, score_scale),
        "attend_back",
        3.8 if item + 1 < items else SHORT,
        ins,
        [
            ((items, qk, lat), BF, None),
            ((count, qk + wide), BF, None),
        ],
        scratch=[pltpu.VMEM((wide, count), BF)],
        alias=alias,
        deps=deps,
    )


def turn_kernel(bits, where, *refs):
    xn_refs, (keep_ref, send_ref, all_ref) = refs[:-3], refs[-3:]
    count = 2 ** len(bits)
    rows = keep_ref.shape[1] // count
    mine = where[2] * 2 + where[1]
    for i, ref in enumerate(xn_refs):
        all_ref[i] = ref[...].astype(F32).T
    for i in range(len(xn_refs)):
        for out, core in ((keep_ref, where[0]), (send_ref, 1 - where[0])):
            for j in range(0, count, 2):
                pair = []
                for n in (j, j + 1):
                    spot = (mine ^ flipped(n, bits)) * CORES + core
                    begin = pl.multiple_of(spot * rows, 8)
                    pair.append(all_ref[i, pl.ds(begin, rows)])
                out[i, j * rows : (j + 2) * rows] = jnp.concatenate(pair, 0).astype(BF)


def turn(xns, bits, deps):
    count, width = xns[0].shape
    shape = (len(xns), width // CORES, count)
    return launch(
        functools.partial(turn_kernel, bits),
        "turn",
        3,
        [(a, None) for a in xns],
        [(shape, BF, None), (shape, BF, None)],
        scratch=[pltpu.VMEM((len(xns), width, count), F32)],
        deps=deps,
    )


def byte_part_kernel(spots, where, *refs):
    out_ref = refs[-1]
    total = refs[-2][...] if len(refs) % 2 == 0 else 0.0
    for n, spot in enumerate(spots):
        total += nn(refs[2 * n][spot], refs[2 * n + 1][...])
    out_ref[...] = total


def byte_part(pairs, before, micros, deps):
    ins = [(a, None) for turned, _, dkv in pairs for a in (turned, dkv)]
    alias = {}
    if before is not None:
        alias = {len(ins): 0}
        ins.append((before, None))
    shape = (pairs[0][0].shape[1], pairs[0][2].shape[1])
    return launch(
        functools.partial(byte_part_kernel, [p[1] for p in pairs]),
        "byte_part",
        micros,
        ins,
        [(shape, F32, None)],
        alias=alias,
        deps=deps,
    )[0]


def byte_last_kernel(spot, where, turned_ref, dkv_ref, before_ref, keep_ref, send_ref):
    total = before_ref[...] + nn(turned_ref[spot], dkv_ref[...])
    half, rows = keep_ref.shape[:2]
    for j in range(half):
        keep_ref[j] = total[j * rows : (j + 1) * rows].astype(BF)
        send_ref[j] = total[(half + j) * rows : (half + j + 1) * rows].astype(BF)


def byte_last(turned, spot, dkv, before, count, deps):
    shape = (count // 2, turned.shape[1] // count, dkv.shape[1])
    return launch(
        functools.partial(byte_last_kernel, spot),
        "byte_last",
        SHORT,
        [(turned, None), (dkv, None), (before, None)],
        [(shape, BF, None), (shape, BF, None)],
        deps=deps,
    )


def bytes_back_kernel(
    item, where, lang_ref, own_ref, far_ref, table_ref, gain_ref, wk_ref, wv_ref, dkv_ref, *refs
):
    gown_ref, gfar_ref, small_ref = refs[-3:]
    items, count = gfar_ref.shape[:2]
    qk = wk_ref.shape[1]
    langs = table_ref.shape[0]
    gain = gain_ref[...]
    language = lang_ref[where[0] * items + item]
    row = language_row(table_ref, language)
    grads = nt(dkv_ref[:, :qk], wk_ref[...]) + nt(dkv_ref[:, qk:], wv_ref[...])
    gain_sum = jnp.zeros_like(row)
    byte_sum = jnp.zeros_like(row)
    for part, rows, out in (
        (0, own_ref[where[0] * items + item], gown_ref),
        (1, far_ref[item], gfar_ref),
    ):
        unit, inverse = standardise(rows.astype(F32) + row)
        grad = grads[part * count : (part + 1) * count]
        gain_sum += jnp.sum(grad * unit, 0, keepdims=True)
        back = standardise_back(unit, inverse, grad * gain)
        byte_sum += jnp.sum(back, 0, keepdims=True)
        out[item] = back.astype(out.dtype)
    at = lax.broadcasted_iota(jnp.int32, small_ref.shape, 0)
    small = jnp.where(at == language, byte_sum, 0.0) + jnp.where(at == langs, gain_sum, 0.0)
    if item:
        small += refs[2][...]
    small_ref[...] = small


def bytes_back(
    item, items, language, own, far, table, gain, w_key, w_value, dkv, before, deps
):
    shape = far.shape
    ins = [(language, SCALARS)]
    ins += [(a, None) for a in (own, far, table, gain, w_key, w_value, dkv)]
    alias = {}
    if before:
        alias = {len(ins): 0, len(ins) + 1: 1}
        ins += [(a, None) for a in before]
    return launch(
        functools.partial(bytes_back_kernel, item),
        "bytes_back",
        2.5 if item + 1 < items else SHORT,
        ins,
        [
            (shape, F32, None),
            (shape, BF, None),
            ((table.shape[0] + 8, far.shape[2]), F32, None),
        ],
        alias=alias,
        deps=deps,
    )


def latents_back_kernel(
    score_scale, chips, bits, where, da_ref, db_ref, *refs
):
    items = da_ref.shape[0]
    gres_refs, gmlp_refs, refs = refs[:items], refs[items : 2 * items], refs[2 * items :]
    gfar_ref, small_ref, lat_ref, gain_ref, wq_ref = refs[:5]
    glat_ref, keep_ref, send_ref, own_ref = refs[5:9]
    lhs_ref, rhs_ref, turn_ref = refs[9:]
    lat = lat_ref.shape[1]
    gain = gain_ref[...]
    gain_sum = jnp.zeros_like(gain)
    half = keep_ref.shape[1]
    for i in range(items):
        total = (da_ref[i].astype(F32) + db_ref[i].astype(F32)) * score_scale
        grad = total.T.astype(BF)
        rhs_ref[i * lat : (i + 1) * lat] = grad
        unit, inverse = standardise(lat_ref[where[0] * items + i].astype(F32))
        turn_ref[i] = (unit * gain).astype(BF).T
        gln = nt(grad, wq_ref[...])
        gain_sum += jnp.sum(gln * unit, 0, keepdims=True)
        out = gres_refs[i][...] + standardise_back(unit, inverse, gln * gain)
        glat_ref[i, :, : out.shape[1]] = out.astype(BF)
        glat_ref[i, :, out.shape[1] :] = gfar_ref[i]
    gmlp = functools.reduce(jnp.add, [r[...] for r in gmlp_refs])
    wide = own_ref.shape[1]
    at = lax.broadcasted_iota(jnp.int32, (8, wide), 0)
    own = jnp.concatenate(
        [
            jnp.where(at == 1, gain_sum[:, g : g + wide], 0.0)
            + jnp.where(at == 2, gmlp[:, g : g + wide], 0.0)
            for g in range(0, gain.shape[1], wide)
        ],
        0,
    )
    own_ref[...] = own
    count = keep_ref.shape[0]
    send_ref[count] = own.astype(BF)
    tall = [small_ref[:, g : g + wide] for g in range(0, small_ref.shape[1], wide)]
    rest = (send_ref.shape[0] - count - 1) * half - len(tall) * small_ref.shape[0]
    tall = jnp.concatenate(tall + [jnp.zeros((rest, wide), F32)], 0)
    for j in range(count + 1, send_ref.shape[0]):
        send_ref[j] = tall[(j - count - 1) * half : (j - count) * half].astype(BF)
    for i in range(items):
        pick_rows(where, turn_ref.at[i], lhs_ref, i * lat, 2 * half, chips, bits)
    total = nn(lhs_ref[...], rhs_ref[...])
    for j in range(keep_ref.shape[0]):
        low = total[2 * j * half : (2 * j + 1) * half]
        high = total[(2 * j + 1) * half : (2 * j + 2) * half]
        keep_ref[j] = jnp.where(where[0] == 0, low, high).astype(BF)
        send_ref[j] = jnp.where(where[0] == 0, high, low).astype(BF)


def latents_back(da, db, gres, gmlps, gfar, small, latents, gain, w_query, score_scale, chips, bits, deps):
    _, lat, width = latents.shape
    items = da.shape[0]
    qk = w_query.shape[1]
    count = 2 ** len(bits)
    half = width // (count * chips * CORES)
    small_blocks = -(-small.size // (half * qk))
    return launch(
        functools.partial(latents_back_kernel, score_scale, chips, bits),
        "latents_back",
        SHORT,
        [(da, None), (db, None)]
        + [(g, None) for g in gres + gmlps]
        + [(a, None) for a in (gfar, small, latents, gain, w_query)],
        [
            ((items, lat, width + gfar.shape[2]), BF, None),
            ((count, half, qk), BF, None),
            ((count + 1 + small_blocks, half, qk), BF, None),
            ((half, qk), F32, None),
        ],
        scratch=[
            pltpu.VMEM((width // chips, items * lat), BF),
            pltpu.VMEM((items * lat, qk), BF),
            pltpu.VMEM((items, width, lat), BF),
        ],
        deps=deps,
    )


def fold_kernel(where, keep_ref, far_ref, *outs):
    half = keep_ref.shape[0] // 2
    if len(outs) == 1:
        outs[0][...] = keep_ref[0].astype(F32) + far_ref[0].astype(F32)
        return
    for spot, out in enumerate(outs):
        for j in range(half):
            at = spot * half + j
            out[j] = (keep_ref[at].astype(F32) + far_ref[at].astype(F32)).astype(BF)


def fold(keep, far, deps, micros=SHORT):
    if keep.shape[0] == 1:
        outs = [(keep.shape[1:], F32, None)]
    else:
        shape = (keep.shape[0] // 2,) + keep.shape[1:]
        outs = [(shape, BF, None), (shape, BF, None)]
    return launch(fold_kernel, "fold", micros, [(keep, None), (far, None)], outs, deps=deps)


def side_kernel(begin, where, far_ref, small_ref, own_ref, send_ref):
    rows, width = small_ref.shape
    tall = jnp.concatenate([far_ref[j].astype(F32) for j in range(begin, far_ref.shape[0])], 0)
    pieces = [tall[rows * g : rows * (g + 1)] for g in range(width // far_ref.shape[2])]
    own = small_ref[...] + jnp.concatenate(pieces, 1)
    own_ref[...] = own
    send_ref[...] = own.astype(BF)


def side_sum(far, small, begin, deps):
    return launch(
        functools.partial(side_kernel, begin),
        "side_sum",
        1,
        [(far, None), (small, None)],
        [(small.shape, F32, None), (small.shape, BF, None)],
        deps=deps,
    )


def join_kernel(
    langs, chips, bits, where, keep_ref, far_ref, own_ref, side_ref, qkeep_ref, qfar_ref, qown_ref,
    keep_out, send_out,
):
    count, rows, wide = keep_ref.shape
    qrows, qwide = qown_ref.shape

    def across(tall):
        return jnp.concatenate([tall[r : r + 8] for r in range(0, qrows, 8)], 1)

    own = own_ref[...] + side_ref[...].astype(F32)
    gains = across(qown_ref[...] + qfar_ref[count].astype(F32))
    at = lax.broadcasted_iota(jnp.int32, (8, qwide), 1)
    half = count // 2
    for j in range(count):
        spot = where[2] ^ flipped(j, bits)
        device = (spot * chips + where[1]) * CORES + where[0]
        byte_cut = pltpu.roll(own, own.shape[1] - device * rows, 1)[:, :qwide]
        lat_cut = pltpu.roll(gains, gains.shape[1] - device * qrows, 1)[:, :qwide]
        spare = jnp.where(at < rows, byte_cut[:8], 0.0)
        for n in range(1, langs // 8 + 1):
            piece = jnp.where(at < rows, byte_cut[8 * n : 8 * n + 8], 0.0)
            spare += pltpu.roll(piece, n * rows, 1)
        spare += pltpu.roll(jnp.where(at < qrows, lat_cut, 0.0), (langs // 8 + 1) * rows, 1)
        byte = keep_ref[j].astype(F32) + far_ref[j].astype(F32)
        query = across(qkeep_ref[j].astype(F32) + qfar_ref[j].astype(F32))
        out = keep_out if j < half else send_out
        below = jnp.concatenate([query, spare], 1)
        out[j % half] = jnp.concatenate([byte, below], 0).astype(BF)


def join(keep, far, own, side, qkeep, qfar, qown, langs, chips, bits, deps):
    count, rows, wide = keep.shape
    shape = (count // 2, rows + 8, wide)
    return launch(
        functools.partial(join_kernel, langs, chips, bits),
        "join",
        LONG,
        [(a, None) for a in (keep, far, own, side, qkeep, qfar, qown)],
        [(shape, BF, None), (shape, BF, None)],
        deps=deps,
    )


def part_kernel(
    where, keep_ref, far_ref, key_ref, value_ref, query_ref, lang_ref, gin_ref, glat_ref, gmlp_ref
):
    total = keep_ref[0].astype(F32) + far_ref[0].astype(F32)
    rows, qk = key_ref.shape
    qrows, langs = query_ref.shape[0], lang_ref.shape[0]
    key_ref[...] = total[:rows, :qk]
    value_ref[...] = total[:rows, qk:]
    for r in range(0, qrows, 8):
        query_ref[r : r + 8] = total[rows:, r // 8 * qk : (r // 8 + 1) * qk]
    spare = total[rows:, qrows // 8 * qk : (qrows // 8 + 1) * qk]
    groups = langs // 8
    for n in range(groups):
        lang_ref[8 * n : 8 * n + 8] = spare[:, n * rows : (n + 1) * rows]
    gin_ref[...] = spare[:1, groups * rows : (groups + 1) * rows]
    begin = (groups + 1) * rows
    glat_ref[...] = spare[1:2, begin : begin + qrows]
    gmlp_ref[...] = spare[2:3, begin : begin + qrows]


def part(keep, far, qk, qrows, langs, deps):
    rows, wide = keep.shape[1] - 8, keep.shape[2]
    shapes = [(rows, qk), (rows, wide - qk), (qrows, qk), (langs, rows)]
    shapes += [(1, rows), (1, qrows), (1, qrows)]
    return launch(
        part_kernel,
        "part",
        SHORT,
        [(keep, None), (far, None)],
        [(shape, F32, None) for shape in shapes],
        deps=deps,
    )


def last_kernel(where, keep_a, far_a, keep_b, far_b, up_ref, down_ref, out_ref):
    wide = up_ref.shape[1]
    split = out_ref.shape[1] // 2
    first = keep_a[0].astype(F32) + far_a[0].astype(F32)
    second = keep_b[0].astype(F32) + far_b[0].astype(F32)
    up_ref[...] = first[:, :wide]
    down_ref[...] = second[:, :wide]
    out_ref[:, :split] = first[:, wide:]
    out_ref[:, split:] = second[:, wide:]


def last(keep_a, far_a, keep_b, far_b, width, deps):
    shape = (keep_a.shape[1], width)
    return launch(
        last_kernel,
        "last",
        SHORT,
        [(a, None) for a in (keep_a, far_a, keep_b, far_b)],
        [(shape, F32, None)] * 3,
        deps=deps,
    )


def place_kernel(columns, where, *refs):
    count = len(columns)
    items = pl.num_programs(0) // 2
    ours = pl.program_id(0) // items == where[0]
    for n, (left, right) in enumerate(columns):
        out = refs[2 * count + n]
        wide = out.shape[2]
        own = refs[n][:, :, left : left + wide].astype(out.dtype)
        far = refs[count + n][:, :, right : right + wide].astype(out.dtype)
        out[...] = jnp.where(ours, own, far)
    refs[-1][...] = jnp.zeros_like(refs[-1])


def place(pairs, micros, deps):
    items = pairs[0][0].shape[0]
    one = lambda a: (1,) + a.shape[1:]
    rows = lambda p: p[0].shape[1]
    outs = [
        ((2 * items, rows(p), p[4]), p[5], block((1, rows(p), p[4]), lambda g: g))
        for p in pairs
    ]
    return launch(
        functools.partial(place_kernel, [(p[1], p[3]) for p in pairs]),
        "place",
        micros,
        [(a, block(one(a), lambda g: g % items)) for a in [p[0] for p in pairs]]
        + [(a, block(one(a), lambda g: g % items)) for a in [p[2] for p in pairs]],
        outs + [((8, 128), F32, None)],
        deps=deps,
        grid=2 * items,
        far=True,
    )


def swap(value, axis, bit):
    size = lax.axis_size(axis)
    return lax.ppermute(value, axis, [(i, i ^ bit) for i in range(size)])


def bits_of(size):
    return [2**t for t in range(size.bit_length() - 1)]


def halve(value, dim, axis, bit):
    mine = (lax.axis_index(axis) // bit) % 2
    keep = lax.dynamic_index_in_dim(value, mine, dim, keepdims=False)
    send = lax.dynamic_index_in_dim(value, 1 - mine, dim, keepdims=False)
    return (keep.astype(F32) + swap(send, axis, bit).astype(F32)).astype(BF)


def scatter_rows(value):
    spots, chips = lax.axis_size("batch"), lax.axis_size("seq") // CORES
    rows = value.shape[0] // (spots * chips * CORES)
    blocks = value.astype(BF).reshape(spots, chips, CORES, rows, value.shape[1])
    blocks = halve(blocks, 2, "seq", 1)
    for bit in bits_of(chips):
        rest = blocks.shape[2:]
        blocks = blocks.reshape((spots, blocks.shape[1] // 2, 2) + rest)
        blocks = halve(blocks, 2, "seq", CORES * bit)
    blocks = blocks[:, 0]
    for bit in bits_of(spots):
        blocks = blocks.reshape((blocks.shape[0] // 2, 2) + blocks.shape[1:])
        blocks = halve(blocks, 1, "batch", bit)
    return blocks[0].astype(F32)


def everywhere(value):
    for axis in ("seq", "batch"):
        for bit in bits_of(lax.axis_size(axis)):
            value = value + swap(value, axis, bit)
    return value


def merge(oa, ob):
    rows = oa.shape[0] - TERMS * SHARE
    wide = rows // SHARE
    la, lb = part_sums(oa[rows:].astype(F32)), part_sums(ob[rows:].astype(F32))
    top = jnp.maximum(la, lb)
    ea, eb = jnp.exp2(la - top), jnp.exp2(lb - top)
    total = ea + eb
    lse = top + jnp.log2(total)
    out = oa[:rows].astype(F32) * jnp.repeat(ea / total, wide, 0)
    out = out + ob[:rows].astype(F32) * jnp.repeat(eb / total, wide, 0)
    return jnp.concatenate([out.astype(BF), part_terms(lse)], 0)


def local(
    byte_inputs,
    language,
    lang_table,
    latents,
    gain_in,
    gain_lat,
    gain_mlp,
    w_query,
    w_key,
    w_value,
    w_out,
    w_up,
    w_down,
    cotangent,
):
    items = byte_inputs.shape[0] // CORES
    width_in, width_lat = byte_inputs.shape[2], latents.shape[2]
    lat, qk = latents.shape[1], w_query.shape[1]
    langs = lang_table.shape[0]
    score_scale = 1.0 / math.sqrt(qk // HEADS)
    score_unit = score_scale * math.log2(math.e)
    spots, chips = lax.axis_size("batch"), lax.axis_size("seq") // CORES
    devices = spots * chips * CORES
    seq_at, spot = lax.axis_index("seq"), lax.axis_index("batch")
    core, side = seq_at % CORES, seq_at // CORES
    device = spot * (chips * CORES) + seq_at
    chip_bits, spot_bits = bits_of(chips), bits_of(spots)
    rows_in, rows_lat = width_in // devices, width_lat // devices
    direct = (
        chips == 2
        and rows_in == langs + 8
        and rows_lat * qk == 8 * width_lat
        and width_lat % qk == 0
        and langs % 8 == 0
        and byte_inputs.shape[1] == lat
    )
    last_bit = chip_bits[-1]
    table = lang_table
    gain_in, gain_lat, gain_mlp = gain_in[None], gain_lat[None], gain_mlp[None]

    far = swap(pick_bytes(byte_inputs, items), "seq", 1)
    *asked, rows = queries(items, language, table, latents, gain_lat, w_query, ())
    asked = [asked[2 * i : 2 * i + 2] for i in range(items)]
    xns, kept, pairs, token = [], [], [], ()
    for item in range(items):
        ots, xn, k, kt, v = attend(
            item, items, byte_inputs, far, rows, gain_in, w_key, w_value,
            asked[item][1], score_unit, token,
        )
        xns.append(xn)
        kept.append((k, kt, v))
        token = (v[-1],)
        for bit in chip_bits[:-1]:
            ots = [merge(ot, swap(ot, "seq", CORES * bit)) for ot in ots]
        pairs.append((ots, [swap(ot, "seq", CORES * last_bit) for ot in ots]))

    gact = act_back(cotangent, w_down, items, token)
    token = (gact,)
    sides, outs, dqkv, dkvs = [], None, (), []
    if direct:
        y_bit, z_bit, far_bit = spot_bits
        a_bits, b_bits = [y_bit, z_bit, far_bit], [z_bit, far_bit, y_bit]
        c_bits = [1] + [2 * b for b in a_bits]
        turned, turned_send = turn(xns, c_bits, token)
        turned_far = swap(turned_send, "seq", 1)
        part_c, far_pairs = None, []

    def back(item, deps):
        gatt, dot, lse = sides[item][2:5]
        return attend_back(
            item, items, *asked[item], *kept[item], gatt, lse, dot, score_unit, score_scale, dqkv, deps
        )

    byted = ()

    def back_bytes(item, deps):
        return bytes_back(
            item, items, language, byte_inputs, far, table, gain_in, w_key, w_value,
            dkvs[item], byted, deps,
        )

    for item in range(items):
        if item:
            *dqkv, dkv = back(item - 1, token)
            dkvs.append(dkv)
            byted = back_bytes(item - 1, ())
            token = (byted[2],)
            if direct:
                dkv_far = swap(dkv, "seq", 1)
                part_c = byte_part([(turned, item - 1, dkv)], part_c, 1, token)
                far_pairs.append((turned_far, item - 1, dkv_far))
                token = (part_c,)
        side_out = latent_side(
            item, items, last_bit, *pairs[item], latents, cotangent,
            gact, gain_mlp, w_out, w_up, w_down, outs, token,
        )
        outs = side_out[0]
        sides.append(side_out)
        token = (side_out[3],)
    outs_far = swap(outs, "seq", 1)

    pick = lambda at: [s[at] for s in sides]
    down = (pick(7), [cotangent] * items)
    up = (pick(6), pick(8))
    out = (pick(5), pick(9))

    if direct:
        split = width_lat // 2
        keep_a, send_a = latent_weights(
            [up, out], [(0, width_lat), (0, split)], chips, a_bits, "weights_a", token
        )
        far_a = swap(send_a, "seq", 1)
        keep_b, send_b = latent_weights(
            [down, out], [(0, width_lat), (split, split)], chips, b_bits, "weights_b",
            (keep_a,),
        )
        far_b = swap(send_b, "seq", 1)
        early = [a for pair in far_pairs for a in (pair[0], pair[2])]
        dqt, dkv = back(items - 1, (keep_b, *early))
        dkvs.append(dkv)
        dkv_far = swap(dkv, "seq", 1)
        dqt_far = swap(dqt, "seq", CORES)
        keep_a, send_a = fold(keep_a, far_a, (dqt, outs_far), 5)
        far_a = swap(send_a, "batch", a_bits[0])
        keep_b, send_b = fold(keep_b, far_b, (keep_a,), 5)
        far_b = swap(send_b, "batch", b_bits[0])
        part_c = byte_part(
            far_pairs + [(turned, items - 1, dkv)], part_c, SHORT, (keep_b,)
        )
        keep_c, send_c = byte_last(
            turned_far, items - 1, dkv_far, part_c, 2 ** len(c_bits), ()
        )
        far_c = swap(send_c, "seq", CORES)
        gown, gfar, small = back_bytes(items - 1, (keep_c,))
        glats, keep_q, send_q, own_q = latents_back(
            dqt, dqt_far, pick(1), pick(10), gfar, small, latents, gain_lat, w_query,
            score_scale, chips, a_bits, (),
        )
        glats_far = swap(glats, "seq", 1)
        far_q = swap(send_q, "seq", 1)
        own_s, send_s = side_sum(far_q, small, keep_q.shape[0] + 1, ())
        far_s = swap(send_s, "seq", CORES)
        keep_b, send_b = fold(keep_b, far_b, (own_s,))
        far_b = swap(send_b, "batch", b_bits[1])
        keep_a, send_a = fold(keep_a, far_a, (keep_b,))
        far_a = swap(send_a, "batch", a_bits[1])
        keep_c, send_c = join(
            keep_c, far_c, own_s, far_s, keep_q, far_q, own_q, langs, chips, a_bits,
            (keep_a,),
        )
        far_c = swap(send_c, "batch", a_bits[0])
        latents_out, grad_bytes, token = place(
            [
                (outs, 0, outs_far, 0, width_lat, BF),
                (gown, 0, glats_far, width_lat, width_in, F32),
            ],
            LONG,
            (keep_c,),
        )
        keep_c, send_c = fold(keep_c, far_c, (token,))
        far_c = swap(send_c, "batch", a_bits[1])
        keep_b, send_b = fold(keep_b, far_b, (keep_c,))
        far_b = swap(send_b, "batch", b_bits[2])
        keep_a, send_a = fold(keep_a, far_a, (keep_b,))
        far_a = swap(send_a, "batch", a_bits[2])
        grad_latents, token = place(
            [(glats, 0, glats_far, 0, width_lat, F32)], SHORT, (keep_a,)
        )
        keep_c, send_c = fold(keep_c, far_c, (token,))
        far_c = swap(send_c, "batch", a_bits[2])
        g_up, g_down, g_out = last(keep_a, far_a, keep_b, far_b, width_lat, (keep_c,))
        g_key, g_value, g_query, g_table, *gains = part(
            keep_c, far_c, qk, rows_lat, langs, ()
        )
        g_in, g_lat, g_mlp = [g[0] for g in gains]
    else:
        dqt, dkv = back(items - 1, token)
        dkvs.append(dkv)
        for bit in chip_bits:
            dqt = (dqt.astype(F32) + swap(dqt, "seq", CORES * bit).astype(F32)).astype(BF)
        gown, gfar, small = back_bytes(items - 1, ())
        gfar_far = swap(gfar, "seq", 1)
        own_cut = lambda a: lax.dynamic_slice_in_dim(a, core * items, items, 0)
        grad_q = (dqt.astype(F32) * score_scale).swapaxes(1, 2).astype(BF)
        unit, inverse = standardise(own_cut(latents).astype(F32))
        gln = lax.dot_general(
            grad_q, w_query, (((2,), (1,)), ((), ())), preferred_element_type=F32
        )
        glats = jnp.stack(pick(1)) + standardise_back(unit, inverse, gln * gain_lat)
        glats = glats.astype(BF)
        glats_far = swap(glats, "seq", 1)
        flat = lambda a: a.reshape(-1, a.shape[-1])
        share = 1.0 / chips
        g_query = scatter_rows(tn(flat((unit * gain_lat).astype(BF)), flat(grad_q)) * share)
        rows = lambda lefts, rights: scatter_rows(
            sum(nn(x, y) for x, y in zip(lefts, rights)) * share
        )
        g_down = rows(pick(7), own_cut(cotangent))
        g_up, g_out = rows(pick(6), pick(8)), rows(pick(5), pick(9))
        g_bytes = scatter_rows(sum(tn(xns[i], dkvs[i]) for i in range(items)))
        g_key, g_value = g_bytes[:, :qk], g_bytes[:, qk:]
        pad = ((0, 0), (0, width_lat - width_in))
        small = jnp.concatenate(
            [
                jnp.pad(small[: langs + 1], pad),
                jnp.sum(gln * unit, (0, 1))[None] * share,
                sum(pick(10)) * share,
            ],
            0,
        )
        small = everywhere(small)
        cut = lambda rows, count: lax.dynamic_slice_in_dim(rows, device * count, count, 1)
        g_table, g_in = cut(small[:langs], rows_in), cut(small[langs : langs + 1], rows_in)[0]
        g_lat, g_mlp = cut(small[langs + 1 :], rows_lat)
        latents_out, grad_bytes, grad_latents, _ = place(
            [
                (outs, 0, outs_far, 0, width_lat, BF),
                (gown, 0, gfar_far, 0, width_in, F32),
                (glats, 0, glats_far, 0, width_lat, F32),
            ],
            SHORT,
            (),
        )

    return (
        latents_out,
        grad_latents,
        grad_bytes,
        g_table,
        g_in,
        g_lat,
        g_mlp,
        g_query,
        g_key,
        g_value,
        g_out,
        g_up,
        g_down,
    )


def solution(mesh):
    return jax.shard_map(
        local,
        mesh=mesh,
        in_specs=(
            P("batch", "seq", None),
            P("batch"),
            P(),
            P("batch", None, None),
            P(),
            P(),
            P(),
            P(),
            P(),
            P(),
            P(),
            P(),
            P(),
            P("batch", None, None),
        ),
        out_specs=(
            P("batch", None, None),
            P("batch", None, None),
            P("batch", "seq", None),
            P(None, ("batch", "seq")),
            P(("batch", "seq")),
            P(("batch", "seq")),
            P(("batch", "seq")),
            P(("batch", "seq"), None),
            P(("batch", "seq"), None),
            P(("batch", "seq"), None),
            P(("batch", "seq"), None),
            P(("batch", "seq"), None),
            P(("batch", "seq"), None),
        ),
        check_vma=False,
    )
```

```python
import functools
import math

import jax
import jax.numpy as jnp
from jax import lax
from jax.experimental import pallas as pl
from jax.experimental.pallas import tpu as pltpu
from jax.sharding import PartitionSpec as P

HEADS = 8
CORES = 2
EPS = 1e-05
F32 = jnp.float32
BF = jnp.bfloat16
VMEM_LIMIT = 12 * 1024 * 1024
PEAK = 1.15e9
SHORT, LONG, AHEAD = 0.001, 40, 3


def nn(a, b):
    return lax.dot_general(a, b, (((1,), (0,)), ((), ())), preferred_element_type=F32)


def nt(a, b):
    return lax.dot_general(a, b, (((1,), (1,)), ((), ())), preferred_element_type=F32)


def tn(a, b):
    return lax.dot_general(a, b, (((0,), (0,)), ((), ())), preferred_element_type=F32)


def standardise(x):
    centre = x - jnp.mean(x, -1, keepdims=True)
    inverse = lax.rsqrt(jnp.mean(centre * centre, -1, keepdims=True) + EPS)
    return centre * inverse, inverse


def standardise_back(unit, inverse, grad):
    return inverse * (
        grad - jnp.mean(grad, -1, keepdims=True) - unit * jnp.mean(grad * unit, -1, keepdims=True)
    )


def block(shape, at):
    return pl.BlockSpec(shape, lambda g: (at(g),) + (0,) * (len(shape) - 1))


ANY = pl.BlockSpec(memory_space=pl.ANY)
FAST = pl.BlockSpec(memory_space=pltpu.VMEM)
FAR = pl.BlockSpec(memory_space=pltpu.HBM)
SCALARS = pl.BlockSpec(memory_space=pltpu.SMEM)


def launch(body, name, micros, ins, outs, scratch=(), deps=(), alias=None, grid=1, far=False):
    count, extra = len(ins), len(deps)
    ins = [
        (pltpu.with_memory_space_constraint(a, pltpu.HBM) if s is FAR else a, s) for a, s in ins
    ]

    def kernel(*refs):
        body(Where(), *refs[:count], *refs[count + extra :])

    return pl.pallas_call(
        kernel,
        grid=(grid,),
        in_specs=[FAST if s is None else s for _, s in ins] + [ANY] * extra,
        out_specs=[FAST if s is None else s for _, _, s in outs],
        scratch_shapes=list(scratch),
        out_shape=[
            (jax.ShapeDtypeStruct if s is None or not far else pltpu.HBM)(shape, dtype)
            for shape, dtype, s in outs
        ],
        input_output_aliases=alias or {},
        compiler_params=pltpu.CompilerParams(vmem_limit_bytes=VMEM_LIMIT),
        cost_estimate=pl.CostEstimate(
            flops=int(micros * PEAK), bytes_accessed=1, transcendentals=0
        ),
        name=name,
    )(*[a for a, _ in ins], *deps)


class Where:
    def __getitem__(self, at):
        if at == 2:
            return lax.axis_index("batch")
        return (lax.rem, lax.div)[at](lax.axis_index("seq"), CORES)


def pick_kernel(where, own_ref, out_ref, arrived):
    items = out_ref.shape[0]
    copy = pltpu.make_async_copy(
        own_ref.at[pl.ds((1 - where[0]) * items, items)], out_ref, arrived
    )
    copy.start()
    copy.wait()


def pick_bytes(own, items):
    return launch(
        pick_kernel,
        "pick_bytes",
        AHEAD,
        [(own, FAR)],
        [((items,) + own.shape[1:], BF, None)],
        scratch=[pltpu.SemaphoreType.DMA(())],
    )[0]


def query_kernel(where, lang_ref, table_ref, lat_ref, gain_ref, wq_ref, *outs):
    outs, rows_ref = outs[:-1], outs[-1]
    items = len(outs) // 2
    for i in range(items):
        row = language_row(table_ref, lang_ref[where[0] * items + i])
        rows_ref[i] = jnp.broadcast_to(row, rows_ref.shape[1:])
        unit, _ = standardise(lat_ref[where[0] * items + i].astype(F32))
        rows = nn((unit * gain_ref[...]).astype(BF), wq_ref[...])
        outs[2 * i][...] = rows.astype(BF)
        outs[2 * i + 1][...] = rows.T.astype(BF)


def queries(items, language, table, latents, gain, w_query, deps):
    _, count, width = latents.shape
    qk = w_query.shape[1]
    return launch(
        query_kernel,
        "queries",
        2,
        [(language, SCALARS), (table, None), (latents, None), (gain, None), (w_query, None)],
        [((count, qk), BF, None), ((qk, count), BF, None)] * items
        + [((items, 8, table.shape[1]), F32, None)],
        deps=deps,
    )


SPAN = 256


def head_span(h, wide):
    begin = h * wide // 128 * 128
    return begin, h * wide - begin


def language_row(table_ref, language):
    at = lax.broadcasted_iota(jnp.int32, table_ref.shape, 0)
    table = table_ref[...].astype(F32)
    return jnp.sum(jnp.where(at == language, table, 0.0), 0, keepdims=True)


PARTS = 2
SHARE = HEADS // PARTS
TERMS = 4


def part_terms(lse):
    terms, left = [], lse
    for _ in range(TERMS):
        terms.append(left.astype(BF).astype(F32))
        left = left - terms[-1]
    return jnp.concatenate(terms, 0).astype(BF)


def part_sums(terms):
    total = terms[(TERMS - 1) * SHARE :]
    for n in reversed(range(TERMS - 1)):
        total = terms[n * SHARE : (n + 1) * SHARE] + total
    return total


def heads_out(part, score_unit, k, v, qt, ot_ref):
    depth = qt.shape[0] // HEADS
    wide = v.shape[1] // SHARE
    at = lax.broadcasted_iota(jnp.int32, qt.shape, 0) // depth

    def score_of(h):
        return nn(k, jnp.where(at == part * SHARE + h, qt, jnp.zeros_like(qt)))

    def finish(h, weight, total):
        begin, ahead = head_span(h, wide)
        out = tn(v[:, begin : begin + SPAN], weight)[ahead : ahead + wide]
        ot_ref[h * wide : (h + 1) * wide] = (out * (1.0 / total)).astype(BF)

    lse = []
    coming, waiting = score_of(0), None
    for h in range(SHARE):
        score = coming * score_unit
        if h + 1 < SHARE:
            coming = score_of(h + 1)
        if waiting is not None:
            finish(*waiting)
        top = jnp.max(score, 0, keepdims=True)
        weight = jnp.exp2(score - top)
        total = jnp.sum(weight, 0, keepdims=True)
        lse.append(top + jnp.log2(total))
        waiting = (h, weight.astype(BF), total)
    finish(*waiting)
    lse = jnp.concatenate(lse, 0)
    ot_ref[SHARE * wide :] = part_terms(lse)


def attend_kernel(
    item, items, score_unit, where, own_ref, far_ref, rows_ref, gain_ref, wk_ref,
    wv_ref, qt_ref, ot_ref, xn_ref, k_ref, kt_ref, v_ref,
):
    at = where[0] * items + item
    count = far_ref.shape[1]
    row = rows_ref[item, :1]
    gain = gain_ref[...]
    for part, rows in enumerate((own_ref[at], far_ref[item])):
        unit, _ = standardise(rows.astype(F32) + row)
        xn_ref[part * count : (part + 1) * count] = (unit * gain).astype(BF)
    xn = xn_ref[...]
    k = nn(xn, wk_ref[...]).astype(BF)
    k_ref[...] = k
    kt_ref[...] = k.T
    v = nn(xn, wv_ref[:, : v_ref.shape[1]]).astype(BF)
    v_ref[...] = v
    heads_out(0, score_unit, k, v, qt_ref[...], ot_ref)


def attend_more_kernel(part, score_unit, where, xn_ref, k_ref, wv_ref, qt_ref, ot_ref, v_ref):
    wide = v_ref.shape[1]
    v = nn(xn_ref[...], wv_ref[:, part * wide : (part + 1) * wide]).astype(BF)
    v_ref[...] = v
    heads_out(part, score_unit, k_ref[...], v, qt_ref[...], ot_ref)


def attend(
    item, items, own, far, rows, gain, w_key, w_value, qt, score_unit, deps
):
    _, count, width = own.shape
    qk, lat = w_key.shape[1], qt.shape[1]
    wide = w_value.shape[1] // PARTS
    out = ((wide + TERMS * SHARE, lat), BF, None)
    values = ((2 * count, wide), BF, None)
    first, xn, k, kt, v = launch(
        functools.partial(attend_kernel, item, items, score_unit),
        "attend",
        2.4,
        [(a, None) for a in (own, far, rows, gain, w_key, w_value, qt)],
        [
            out,
            ((2 * count, width), BF, None),
            ((2 * count, qk), BF, None),
            ((qk, 2 * count), BF, None),
            values,
        ],
        deps=deps,
    )
    outs, vs = [first], [v]
    for part in range(1, PARTS):
        more, v = launch(
            functools.partial(attend_more_kernel, part, score_unit),
            "attend_more",
            1.9,
            [(a, None) for a in (xn, k, w_value, qt)],
            [out, values],
        )
        outs.append(more)
        vs.append(v)
    return outs, xn, k, kt, vs


def act_back_kernel(where, cot_ref, wd_ref, gact_ref):
    items = gact_ref.shape[0]
    for i in range(items):
        gact_ref[i] = nt(cot_ref[where[0] * items + i], wd_ref[...])


def act_back(cot, w_down, items, deps):
    return launch(
        act_back_kernel,
        "act_back",
        2.5,
        [(cot, None), (w_down, None)],
        [((items, cot.shape[1], w_down.shape[0]), F32, None)],
        deps=deps,
    )[0]


GELU_A = math.sqrt(2.0 / math.pi)
GELU_B = 0.044715


def latent_kernel(
    item, items, bit, where, *refs
):
    oa_refs, ob_refs, refs = refs[:PARTS], refs[PARTS : 2 * PARTS], refs[2 * PARTS :]
    lat_ref, cot_ref, gact_ref, gain_ref, wo_ref, wu_ref, wd_ref = refs[:7]
    (
        outs_ref, gres_ref, gatt_ref, dot_ref, lse_ref, att_ref, hid_ref, act_ref, gpre_ref,
        glow_ref, ggain_ref,
    ) = refs[-11:]
    at = where[0] * items + item
    first = lax.rem(lax.div(where[1], bit), 2) == 0
    rows = gatt_ref.shape[0]
    wide = rows // HEADS
    ours, theirs = (
        jnp.concatenate(
            [part_sums(ref[rows // PARTS :].astype(F32)) for ref in refs_], 0
        )
        for refs_ in (oa_refs, ob_refs)
    )
    left = jnp.where(first, ours, theirs)
    right = jnp.where(first, theirs, ours)
    top = jnp.maximum(left, right)
    e_left, e_right = jnp.exp2(left - top), jnp.exp2(right - top)
    total = e_left + e_right
    lse_ref[...] = top + jnp.log2(total)
    scale = 1.0 / total
    e_left, e_right = e_left * scale, e_right * scale
    merged = []
    for h in range(HEADS):
        cut = slice(h % SHARE * wide, (h % SHARE + 1) * wide)
        a = oa_refs[h // SHARE][cut].astype(F32)
        b = ob_refs[h // SHARE][cut].astype(F32)
        low, high = jnp.where(first, a, b), jnp.where(first, b, a)
        merged.append(low * e_left[h : h + 1] + high * e_right[h : h + 1])
        att_ref[h * wide : (h + 1) * wide] = merged[-1].astype(BF)
    resid = lat_ref[at].astype(F32) + tn(att_ref[...], wo_ref[...])
    unit, inverse = standardise(resid)
    gain = gain_ref[...]
    hidden = (unit * gain).astype(BF)
    hid_ref[...] = hidden.T
    pre = nn(hidden, wu_ref[...])
    square = pre * pre
    slope = jnp.tanh(GELU_A * pre * (1.0 + GELU_B * square))
    act = (0.5 * pre * (1.0 + slope)).astype(BF)
    act_ref[...] = act.T
    outs_ref[item] = (resid + nn(act, wd_ref[...])).astype(BF)
    cot = cot_ref[at]
    gelu_slope = 0.5 * (1.0 + slope) + 0.5 * pre * (1.0 - slope * slope) * GELU_A * (
        1.0 + 3.0 * GELU_B * square
    )
    gpre = (gact_ref[item] * gelu_slope).astype(BF)
    gpre_ref[...] = gpre
    ghid = nt(gpre, wu_ref[...])
    ggain_ref[...] = jnp.sum(ghid * unit, 0, keepdims=True)
    gres = cot.astype(F32) + standardise_back(unit, inverse, ghid * gain)
    gres_ref[...] = gres
    glow = gres.astype(BF)
    glow_ref[...] = glow
    gatt_ref[...] = nt(wo_ref[...], glow).astype(BF)
    for h in range(HEADS):
        dot_ref[h : h + 1] = jnp.sum(
            gatt_ref[h * wide : (h + 1) * wide].astype(F32) * merged[h], 0, keepdims=True
        )


def latent_side(
    item, items, bit, oa, ob, latents, cot, gact, gain, w_out, w_up, w_down, before, deps
):
    total, lat, width = latents.shape
    feed = w_up.shape[1]
    ins = [(a, None) for a in (*oa, *ob, latents, cot, gact, gain, w_out, w_up, w_down)]
    alias = {}
    if before is not None:
        alias[len(ins)] = 0
        ins.append((before, None))
    return launch(
        functools.partial(latent_kernel, item, items, bit),
        "latent_side",
        7,
        ins,
        [
            ((items, lat, width), BF, None),
            ((lat, width), F32, None),
            ((width, lat), BF, None),
            ((HEADS, lat), F32, None),
            ((HEADS, lat), F32, None),
            ((width, lat), BF, None),
            ((width, lat), BF, None),
            ((feed, lat), BF, None),
            ((lat, feed), BF, None),
            ((lat, width), BF, None),
            ((1, width), F32, None),
        ],
        alias=alias,
        deps=deps,
    )


def flipped(at, bits):
    return sum(((at >> (len(bits) - 1 - t)) & 1) * bit for t, bit in enumerate(bits))


def pick_rows(where, source, lhs_ref, lane, rows, chips, bits):
    lat = source.shape[1]
    for j in range(2 ** len(bits)):
        spot = where[2] ^ flipped(j, bits)
        begin = pl.multiple_of((spot * chips + where[1]) * rows, 16)
        lhs_ref[j * rows : (j + 1) * rows, lane : lane + lat] = source[pl.ds(begin, rows)]


def latent_weights_kernel(plan, items, chips, bits, where, *refs):
    ins, keep_ref, send_ref, lhs_ref = refs[:-3], refs[-3], refs[-2], refs[-1]
    half = keep_ref.shape[1]
    column = 0
    for w, (begin, width) in enumerate(plan):
        lefts = ins[2 * items * w : 2 * items * w + items]
        rights = ins[2 * items * w + items : 2 * items * (w + 1)]
        total = 0.0
        for i in range(items):
            lat = lefts[i].shape[1]
            pick_rows(where, lefts[i], lhs_ref, i * lat, 2 * half, chips, bits)
            right = rights[i]
            if len(right.shape) == 3:
                right = right.at[where[0] * items + i]
            total += nn(lhs_ref[:, i * lat : (i + 1) * lat], right[:, begin : begin + width])
        out = slice(column, column + width)
        for j in range(keep_ref.shape[0]):
            low = total[2 * j * half : (2 * j + 1) * half]
            high = total[(2 * j + 1) * half : (2 * j + 2) * half]
            keep_ref[j, :, out] = jnp.where(where[0] == 0, low, high).astype(BF)
            send_ref[j, :, out] = jnp.where(where[0] == 0, high, low).astype(BF)
        column += width


def latent_weights(groups, plan, chips, bits, name, deps):
    items = len(groups[0][0])
    ins = []
    for lefts, rights in groups:
        ins += [(a, None) for a in lefts + rights]
    width, lat = groups[0][0][0].shape
    count = 2 ** len(bits)
    half = width // (count * chips * CORES)
    shape = (count, half, sum(w for _, w in plan))
    return launch(
        functools.partial(latent_weights_kernel, plan, items, chips, bits),
        name,
        SHORT,
        ins,
        [(shape, BF, None), (shape, BF, None)],
        scratch=[pltpu.VMEM((width // chips, items * lat), BF)],
        deps=deps,
    )


def attend_back_kernel(
    item, score_unit, score_scale, where, q_ref, qt_ref, k_ref, kt_ref, *refs
):
    v_refs, (gatt_ref, lse_ref, dot_ref) = refs[:PARTS], refs[PARTS : PARTS + 3]
    dqt_ref, dkv_ref, dvt_ref = refs[-3:]
    q, qt, k = q_ref[...], qt_ref[...], k_ref[...]
    qk = qt.shape[0]
    depth = qk // HEADS
    wide = gatt_ref.shape[0] // HEADS
    lat = qt.shape[1]
    at = lax.broadcasted_iota(jnp.int32, qt.shape, 0) // depth
    across = lax.broadcasted_iota(jnp.int32, q.shape, 1) // depth

    def begin_head(h):
        score = nn(k, jnp.where(at == h, qt, jnp.zeros_like(qt)))
        grad = gatt_ref[h * wide : (h + 1) * wide]
        begin, ahead = head_span(h % SHARE, wide)
        after = SPAN - ahead - wide
        pieces = [grad]
        if ahead:
            pieces = [jnp.zeros((ahead, lat), BF)] + pieces
        if after:
            pieces = pieces + [jnp.zeros((after, lat), BF)]
        values = v_refs[h // SHARE][:, begin : begin + SPAN]
        return score, grad, nn(values, jnp.concatenate(pieces, 0))

    def finish(h, grad, prob, grad_score):
        dvt_ref[h * wide : (h + 1) * wide] = nt(grad, prob).astype(BF)
        dqt_ref[item, h * depth : (h + 1) * depth] = nn(
            kt_ref[h * depth : (h + 1) * depth], grad_score
        ).astype(BF)
        return nn(grad_score, jnp.where(across == h, q, jnp.zeros_like(q)))

    dk = jnp.zeros(k.shape, F32)
    coming, waiting = begin_head(0), None
    for h in range(HEADS):
        score, grad, grad_prob = coming
        if h + 1 < HEADS:
            coming = begin_head(h + 1)
        if waiting is not None:
            dk += finish(*waiting)
        prob = jnp.exp2(score * score_unit - lse_ref[h : h + 1])
        grad_score = (prob * (grad_prob - dot_ref[h : h + 1])).astype(BF)
        waiting = (h, grad, prob.astype(BF), grad_score)
    dk += finish(*waiting)
    dkv_ref[:, :qk] = (dk * score_scale).astype(BF)
    dkv_ref[:, qk:] = dvt_ref[...].T


def attend_back(
    item, items, q, qt, k, kt, v, gatt, lse, dot, score_unit, score_scale, before, deps
):
    lat, qk = q.shape
    count, wide = v[0].shape[0], gatt.shape[0]
    ins = [(a, None) for a in (q, qt, k, kt, *v, gatt, lse, dot)]
    alias = {}
    for spot, array in enumerate(before):
        alias[len(ins)] = spot
        ins.append((array, None))
    return launch(
        functools.partial(attend_back_kernel, item, score_unit, score_scale),
        "attend_back",
        3.8 if item + 1 < items else SHORT,
        ins,
        [
            ((items, qk, lat), BF, None),
            ((count, qk + wide), BF, None),
        ],
        scratch=[pltpu.VMEM((wide, count), BF)],
        alias=alias,
        deps=deps,
    )


def turn_kernel(bits, where, *refs):
    xn_refs, (keep_ref, send_ref, all_ref) = refs[:-3], refs[-3:]
    count = 2 ** len(bits)
    rows = keep_ref.shape[1] // count
    mine = where[2] * 2 + where[1]
    for i, ref in enumerate(xn_refs):
        all_ref[i] = ref[...].astype(F32).T
    for i in range(len(xn_refs)):
        for out, core in ((keep_ref, where[0]), (send_ref, 1 - where[0])):
            for j in range(0, count, 2):
                pair = []
                for n in (j, j + 1):
                    spot = (mine ^ flipped(n, bits)) * CORES + core
                    begin = pl.multiple_of(spot * rows, 8)
                    pair.append(all_ref[i, pl.ds(begin, rows)])
                out[i, j * rows : (j + 2) * rows] = jnp.concatenate(pair, 0).astype(BF)


def turn(xns, bits, deps):
    count, width = xns[0].shape
    shape = (len(xns), width // CORES, count)
    return launch(
        functools.partial(turn_kernel, bits),
        "turn",
        3,
        [(a, None) for a in xns],
        [(shape, BF, None), (shape, BF, None)],
        scratch=[pltpu.VMEM((len(xns), width, count), F32)],
        deps=deps,
    )


def byte_part_kernel(spots, where, *refs):
    out_ref = refs[-1]
    total = refs[-2][...] if len(refs) % 2 == 0 else 0.0
    for n, spot in enumerate(spots):
        total += nn(refs[2 * n][spot], refs[2 * n + 1][...])
    out_ref[...] = total


def byte_part(pairs, before, micros, deps):
    ins = [(a, None) for turned, _, dkv in pairs for a in (turned, dkv)]
    alias = {}
    if before is not None:
        alias = {len(ins): 0}
        ins.append((before, None))
    shape = (pairs[0][0].shape[1], pairs[0][2].shape[1])
    return launch(
        functools.partial(byte_part_kernel, [p[1] for p in pairs]),
        "byte_part",
        micros,
        ins,
        [(shape, F32, None)],
        alias=alias,
        deps=deps,
    )[0]


def byte_last_kernel(spot, where, turned_ref, dkv_ref, before_ref, keep_ref, send_ref):
    total = before_ref[...] + nn(turned_ref[spot], dkv_ref[...])
    half, rows = keep_ref.shape[:2]
    for j in range(half):
        keep_ref[j] = total[j * rows : (j + 1) * rows].astype(BF)
        send_ref[j] = total[(half + j) * rows : (half + j + 1) * rows].astype(BF)


def byte_last(turned, spot, dkv, before, count, deps):
    shape = (count // 2, turned.shape[1] // count, dkv.shape[1])
    return launch(
        functools.partial(byte_last_kernel, spot),
        "byte_last",
        SHORT,
        [(turned, None), (dkv, None), (before, None)],
        [(shape, BF, None), (shape, BF, None)],
        deps=deps,
    )


def bytes_back_kernel(
    item, where, lang_ref, own_ref, far_ref, table_ref, gain_ref, wk_ref, wv_ref, dkv_ref, *refs
):
    gown_ref, gfar_ref, small_ref = refs[-3:]
    items, count = gfar_ref.shape[:2]
    qk = wk_ref.shape[1]
    langs = table_ref.shape[0]
    gain = gain_ref[...]
    language = lang_ref[where[0] * items + item]
    row = language_row(table_ref, language)
    grads = nt(dkv_ref[:, :qk], wk_ref[...]) + nt(dkv_ref[:, qk:], wv_ref[...])
    gain_sum = jnp.zeros_like(row)
    byte_sum = jnp.zeros_like(row)
    for part, rows, out in (
        (0, own_ref[where[0] * items + item], gown_ref),
        (1, far_ref[item], gfar_ref),
    ):
        unit, inverse = standardise(rows.astype(F32) + row)
        grad = grads[part * count : (part + 1) * count]
        gain_sum += jnp.sum(grad * unit, 0, keepdims=True)
        back = standardise_back(unit, inverse, grad * gain)
        byte_sum += jnp.sum(back, 0, keepdims=True)
        out[item] = back.astype(out.dtype)
    at = lax.broadcasted_iota(jnp.int32, small_ref.shape, 0)
    small = jnp.where(at == language, byte_sum, 0.0) + jnp.where(at == langs, gain_sum, 0.0)
    if item:
        small += refs[2][...]
    small_ref[...] = small


def bytes_back(
    item, items, language, own, far, table, gain, w_key, w_value, dkv, before, deps
):
    shape = far.shape
    ins = [(language, SCALARS)]
    ins += [(a, None) for a in (own, far, table, gain, w_key, w_value, dkv)]
    alias = {}
    if before:
        alias = {len(ins): 0, len(ins) + 1: 1}
        ins += [(a, None) for a in before]
    return launch(
        functools.partial(bytes_back_kernel, item),
        "bytes_back",
        2.5 if item + 1 < items else SHORT,
        ins,
        [
            (shape, F32, None),
            (shape, BF, None),
            ((table.shape[0] + 8, far.shape[2]), F32, None),
        ],
        alias=alias,
        deps=deps,
    )


def latents_back_kernel(
    score_scale, chips, bits, where, da_ref, db_ref, *refs
):
    items = da_ref.shape[0]
    gres_refs, gmlp_refs, refs = refs[:items], refs[items : 2 * items], refs[2 * items :]
    gfar_ref, small_ref, lat_ref, gain_ref, wq_ref = refs[:5]
    glat_ref, keep_ref, send_ref, own_ref = refs[5:9]
    lhs_ref, rhs_ref, turn_ref = refs[9:]
    lat = lat_ref.shape[1]
    gain = gain_ref[...]
    gain_sum = jnp.zeros_like(gain)
    half = keep_ref.shape[1]
    for i in range(items):
        total = (da_ref[i].astype(F32) + db_ref[i].astype(F32)) * score_scale
        grad = total.T.astype(BF)
        rhs_ref[i * lat : (i + 1) * lat] = grad
        unit, inverse = standardise(lat_ref[where[0] * items + i].astype(F32))
        turn_ref[i] = (unit * gain).astype(BF).T
        gln = nt(grad, wq_ref[...])
        gain_sum += jnp.sum(gln * unit, 0, keepdims=True)
        out = gres_refs[i][...] + standardise_back(unit, inverse, gln * gain)
        glat_ref[i, :, : out.shape[1]] = out.astype(BF)
        glat_ref[i, :, out.shape[1] :] = gfar_ref[i]
    gmlp = functools.reduce(jnp.add, [r[...] for r in gmlp_refs])
    wide = own_ref.shape[1]
    at = lax.broadcasted_iota(jnp.int32, (8, wide), 0)
    own = jnp.concatenate(
        [
            jnp.where(at == 1, gain_sum[:, g : g + wide], 0.0)
            + jnp.where(at == 2, gmlp[:, g : g + wide], 0.0)
            for g in range(0, gain.shape[1], wide)
        ],
        0,
    )
    own_ref[...] = own
    count = keep_ref.shape[0]
    send_ref[count] = own.astype(BF)
    tall = [small_ref[:, g : g + wide] for g in range(0, small_ref.shape[1], wide)]
    rest = (send_ref.shape[0] - count - 1) * half - len(tall) * small_ref.shape[0]
    tall = jnp.concatenate(tall + [jnp.zeros((rest, wide), F32)], 0)
    for j in range(count + 1, send_ref.shape[0]):
        send_ref[j] = tall[(j - count - 1) * half : (j - count) * half].astype(BF)
    for i in range(items):
        pick_rows(where, turn_ref.at[i], lhs_ref, i * lat, 2 * half, chips, bits)
    total = nn(lhs_ref[...], rhs_ref[...])
    for j in range(keep_ref.shape[0]):
        low = total[2 * j * half : (2 * j + 1) * half]
        high = total[(2 * j + 1) * half : (2 * j + 2) * half]
        keep_ref[j] = jnp.where(where[0] == 0, low, high).astype(BF)
        send_ref[j] = jnp.where(where[0] == 0, high, low).astype(BF)


def latents_back(da, db, gres, gmlps, gfar, small, latents, gain, w_query, score_scale, chips, bits, deps):
    _, lat, width = latents.shape
    items = da.shape[0]
    qk = w_query.shape[1]
    count = 2 ** len(bits)
    half = width // (count * chips * CORES)
    small_blocks = -(-small.size // (half * qk))
    return launch(
        functools.partial(latents_back_kernel, score_scale, chips, bits),
        "latents_back",
        SHORT,
        [(da, None), (db, None)]
        + [(g, None) for g in gres + gmlps]
        + [(a, None) for a in (gfar, small, latents, gain, w_query)],
        [
            ((items, lat, width + gfar.shape[2]), BF, None),
            ((count, half, qk), BF, None),
            ((count + 1 + small_blocks, half, qk), BF, None),
            ((half, qk), F32, None),
        ],
        scratch=[
            pltpu.VMEM((width // chips, items * lat), BF),
            pltpu.VMEM((items * lat, qk), BF),
            pltpu.VMEM((items, width, lat), BF),
        ],
        deps=deps,
    )


def fold_kernel(where, keep_ref, far_ref, *outs):
    half = keep_ref.shape[0] // 2
    if len(outs) == 1:
        outs[0][...] = keep_ref[0].astype(F32) + far_ref[0].astype(F32)
        return
    for spot, out in enumerate(outs):
        for j in range(half):
            at = spot * half + j
            out[j] = (keep_ref[at].astype(F32) + far_ref[at].astype(F32)).astype(BF)


def fold(keep, far, deps, micros=SHORT):
    if keep.shape[0] == 1:
        outs = [(keep.shape[1:], F32, None)]
    else:
        shape = (keep.shape[0] // 2,) + keep.shape[1:]
        outs = [(shape, BF, None), (shape, BF, None)]
    return launch(fold_kernel, "fold", micros, [(keep, None), (far, None)], outs, deps=deps)


def side_kernel(begin, where, far_ref, small_ref, own_ref, send_ref):
    rows, width = small_ref.shape
    tall = jnp.concatenate([far_ref[j].astype(F32) for j in range(begin, far_ref.shape[0])], 0)
    pieces = [tall[rows * g : rows * (g + 1)] for g in range(width // far_ref.shape[2])]
    own = small_ref[...] + jnp.concatenate(pieces, 1)
    own_ref[...] = own
    send_ref[...] = own.astype(BF)


def side_sum(far, small, begin, deps):
    return launch(
        functools.partial(side_kernel, begin),
        "side_sum",
        1,
        [(far, None), (small, None)],
        [(small.shape, F32, None), (small.shape, BF, None)],
        deps=deps,
    )


def join_kernel(
    langs, chips, bits, where, keep_ref, far_ref, own_ref, side_ref, qkeep_ref, qfar_ref, qown_ref,
    keep_out, send_out,
):
    count, rows, wide = keep_ref.shape
    qrows, qwide = qown_ref.shape

    def across(tall):
        return jnp.concatenate([tall[r : r + 8] for r in range(0, qrows, 8)], 1)

    own = own_ref[...] + side_ref[...].astype(F32)
    gains = across(qown_ref[...] + qfar_ref[count].astype(F32))
    at = lax.broadcasted_iota(jnp.int32, (8, qwide), 1)
    half = count // 2
    for j in range(count):
        spot = where[2] ^ flipped(j, bits)
        device = (spot * chips + where[1]) * CORES + where[0]
        byte_cut = pltpu.roll(own, own.shape[1] - device * rows, 1)[:, :qwide]
        lat_cut = pltpu.roll(gains, gains.shape[1] - device * qrows, 1)[:, :qwide]
        spare = jnp.where(at < rows, byte_cut[:8], 0.0)
        for n in range(1, langs // 8 + 1):
            piece = jnp.where(at < rows, byte_cut[8 * n : 8 * n + 8], 0.0)
            spare += pltpu.roll(piece, n * rows, 1)
        spare += pltpu.roll(jnp.where(at < qrows, lat_cut, 0.0), (langs // 8 + 1) * rows, 1)
        byte = keep_ref[j].astype(F32) + far_ref[j].astype(F32)
        query = across(qkeep_ref[j].astype(F32) + qfar_ref[j].astype(F32))
        out = keep_out if j < half else send_out
        below = jnp.concatenate([query, spare], 1)
        out[j % half] = jnp.concatenate([byte, below], 0).astype(BF)


def join(keep, far, own, side, qkeep, qfar, qown, langs, chips, bits, deps):
    count, rows, wide = keep.shape
    shape = (count // 2, rows + 8, wide)
    return launch(
        functools.partial(join_kernel, langs, chips, bits),
        "join",
        LONG,
        [(a, None) for a in (keep, far, own, side, qkeep, qfar, qown)],
        [(shape, BF, None), (shape, BF, None)],
        deps=deps,
    )


def part_kernel(
    where, keep_ref, far_ref, key_ref, value_ref, query_ref, lang_ref, gin_ref, glat_ref, gmlp_ref
):
    total = keep_ref[0].astype(F32) + far_ref[0].astype(F32)
    rows, qk = key_ref.shape
    qrows, langs = query_ref.shape[0], lang_ref.shape[0]
    key_ref[...] = total[:rows, :qk]
    value_ref[...] = total[:rows, qk:]
    for r in range(0, qrows, 8):
        query_ref[r : r + 8] = total[rows:, r // 8 * qk : (r // 8 + 1) * qk]
    spare = total[rows:, qrows // 8 * qk : (qrows // 8 + 1) * qk]
    groups = langs // 8
    for n in range(groups):
        lang_ref[8 * n : 8 * n + 8] = spare[:, n * rows : (n + 1) * rows]
    gin_ref[...] = spare[:1, groups * rows : (groups + 1) * rows]
    begin = (groups + 1) * rows
    glat_ref[...] = spare[1:2, begin : begin + qrows]
    gmlp_ref[...] = spare[2:3, begin : begin + qrows]


def part(keep, far, qk, qrows, langs, deps):
    rows, wide = keep.shape[1] - 8, keep.shape[2]
    shapes = [(rows, qk), (rows, wide - qk), (qrows, qk), (langs, rows)]
    shapes += [(1, rows), (1, qrows), (1, qrows)]
    return launch(
        part_kernel,
        "part",
        SHORT,
        [(keep, None), (far, None)],
        [(shape, F32, None) for shape in shapes],
        deps=deps,
    )


def last_kernel(where, keep_a, far_a, keep_b, far_b, up_ref, down_ref, out_ref):
    wide = up_ref.shape[1]
    split = out_ref.shape[1] // 2
    first = keep_a[0].astype(F32) + far_a[0].astype(F32)
    second = keep_b[0].astype(F32) + far_b[0].astype(F32)
    up_ref[...] = first[:, :wide]
    down_ref[...] = second[:, :wide]
    out_ref[:, :split] = first[:, wide:]
    out_ref[:, split:] = second[:, wide:]


def last(keep_a, far_a, keep_b, far_b, width, deps):
    shape = (keep_a.shape[1], width)
    return launch(
        last_kernel,
        "last",
        SHORT,
        [(a, None) for a in (keep_a, far_a, keep_b, far_b)],
        [(shape, F32, None)] * 3,
        deps=deps,
    )


def place_kernel(columns, where, *refs):
    count = len(columns)
    items = pl.num_programs(0) // 2
    ours = pl.program_id(0) // items == where[0]
    for n, (left, right) in enumerate(columns):
        out = refs[2 * count + n]
        wide = out.shape[2]
        own = refs[n][:, :, left : left + wide].astype(out.dtype)
        far = refs[count + n][:, :, right : right + wide].astype(out.dtype)
        out[...] = jnp.where(ours, own, far)
    refs[-1][...] = jnp.zeros_like(refs[-1])


def place(pairs, micros, deps):
    items = pairs[0][0].shape[0]
    one = lambda a: (1,) + a.shape[1:]
    rows = lambda p: p[0].shape[1]
    outs = [
        ((2 * items, rows(p), p[4]), p[5], block((1, rows(p), p[4]), lambda g: g))
        for p in pairs
    ]
    return launch(
        functools.partial(place_kernel, [(p[1], p[3]) for p in pairs]),
        "place",
        micros,
        [(a, block(one(a), lambda g: g % items)) for a in [p[0] for p in pairs]]
        + [(a, block(one(a), lambda g: g % items)) for a in [p[2] for p in pairs]],
        outs + [((8, 128), F32, None)],
        deps=deps,
        grid=2 * items,
        far=True,
    )


def swap(value, axis, bit):
    size = lax.axis_size(axis)
    return lax.ppermute(value, axis, [(i, i ^ bit) for i in range(size)])


def bits_of(size):
    return [2**t for t in range(size.bit_length() - 1)]


def halve(value, dim, axis, bit):
    mine = (lax.axis_index(axis) // bit) % 2
    keep = lax.dynamic_index_in_dim(value, mine, dim, keepdims=False)
    send = lax.dynamic_index_in_dim(value, 1 - mine, dim, keepdims=False)
    return (keep.astype(F32) + swap(send, axis, bit).astype(F32)).astype(BF)


def scatter_rows(value):
    spots, chips = lax.axis_size("batch"), lax.axis_size("seq") // CORES
    rows = value.shape[0] // (spots * chips * CORES)
    blocks = value.astype(BF).reshape(spots, chips, CORES, rows, value.shape[1])
    blocks = halve(blocks, 2, "seq", 1)
    for bit in bits_of(chips):
        rest = blocks.shape[2:]
        blocks = blocks.reshape((spots, blocks.shape[1] // 2, 2) + rest)
        blocks = halve(blocks, 2, "seq", CORES * bit)
    blocks = blocks[:, 0]
    for bit in bits_of(spots):
        blocks = blocks.reshape((blocks.shape[0] // 2, 2) + blocks.shape[1:])
        blocks = halve(blocks, 1, "batch", bit)
    return blocks[0].astype(F32)


def everywhere(value):
    for axis in ("seq", "batch"):
        for bit in bits_of(lax.axis_size(axis)):
            value = value + swap(value, axis, bit)
    return value


def merge(oa, ob):
    rows = oa.shape[0] - TERMS * SHARE
    wide = rows // SHARE
    la, lb = part_sums(oa[rows:].astype(F32)), part_sums(ob[rows:].astype(F32))
    top = jnp.maximum(la, lb)
    ea, eb = jnp.exp2(la - top), jnp.exp2(lb - top)
    total = ea + eb
    lse = top + jnp.log2(total)
    out = oa[:rows].astype(F32) * jnp.repeat(ea / total, wide, 0)
    out = out + ob[:rows].astype(F32) * jnp.repeat(eb / total, wide, 0)
    return jnp.concatenate([out.astype(BF), part_terms(lse)], 0)


def local(
    byte_inputs,
    language,
    lang_table,
    latents,
    gain_in,
    gain_lat,
    gain_mlp,
    w_query,
    w_key,
    w_value,
    w_out,
    w_up,
    w_down,
    cotangent,
):
    items = byte_inputs.shape[0] // CORES
    width_in, width_lat = byte_inputs.shape[2], latents.shape[2]
    lat, qk = latents.shape[1], w_query.shape[1]
    langs = lang_table.shape[0]
    score_scale = 1.0 / math.sqrt(qk // HEADS)
    score_unit = score_scale * math.log2(math.e)
    spots, chips = lax.axis_size("batch"), lax.axis_size("seq") // CORES
    devices = spots * chips * CORES
    seq_at, spot = lax.axis_index("seq"), lax.axis_index("batch")
    core, side = seq_at % CORES, seq_at // CORES
    device = spot * (chips * CORES) + seq_at
    chip_bits, spot_bits = bits_of(chips), bits_of(spots)
    rows_in, rows_lat = width_in // devices, width_lat // devices
    direct = (
        chips == 2
        and rows_in == langs + 8
        and rows_lat * qk == 8 * width_lat
        and width_lat % qk == 0
        and langs % 8 == 0
        and byte_inputs.shape[1] == lat
    )
    last_bit = chip_bits[-1]
    table = lang_table
    gain_in, gain_lat, gain_mlp = gain_in[None], gain_lat[None], gain_mlp[None]

    far = swap(pick_bytes(byte_inputs, items), "seq", 1)
    *asked, rows = queries(items, language, table, latents, gain_lat, w_query, ())
    asked = [asked[2 * i : 2 * i + 2] for i in range(items)]
    xns, kept, pairs, token = [], [], [], ()
    for item in range(items):
        ots, xn, k, kt, v = attend(
            item, items, byte_inputs, far, rows, gain_in, w_key, w_value,
            asked[item][1], score_unit, token,
        )
        xns.append(xn)
        kept.append((k, kt, v))
        token = (v[-1],)
        for bit in chip_bits[:-1]:
            ots = [merge(ot, swap(ot, "seq", CORES * bit)) for ot in ots]
        pairs.append((ots, [swap(ot, "seq", CORES * last_bit) for ot in ots]))

    gact = act_back(cotangent, w_down, items, token)
    token = (gact,)
    sides, outs, dqkv, dkvs = [], None, (), []
    if direct:
        y_bit, z_bit, far_bit = spot_bits
        a_bits, b_bits = [y_bit, z_bit, far_bit], [z_bit, far_bit, y_bit]
        c_bits = [1] + [2 * b for b in a_bits]
        turned, turned_send = turn(xns, c_bits, token)
        turned_far = swap(turned_send, "seq", 1)
        part_c, far_pairs = None, []

    def back(item, deps):
        gatt, dot, lse = sides[item][2:5]
        return attend_back(
            item, items, *asked[item], *kept[item], gatt, lse, dot, score_unit, score_scale, dqkv, deps
        )

    byted = ()

    def back_bytes(item, deps):
        return bytes_back(
            item, items, language, byte_inputs, far, table, gain_in, w_key, w_value,
            dkvs[item], byted, deps,
        )

    for item in range(items):
        if item:
            *dqkv, dkv = back(item - 1, token)
            dkvs.append(dkv)
            byted = back_bytes(item - 1, ())
            token = (byted[2],)
            if direct:
                dkv_far = swap(dkv, "seq", 1)
                part_c = byte_part([(turned, item - 1, dkv)], part_c, 1, token)
                far_pairs.append((turned_far, item - 1, dkv_far))
                token = (part_c,)
        side_out = latent_side(
            item, items, last_bit, *pairs[item], latents, cotangent,
            gact, gain_mlp, w_out, w_up, w_down, outs, token,
        )
        outs = side_out[0]
        sides.append(side_out)
        token = (side_out[3],)
    outs_far = swap(outs, "seq", 1)

    pick = lambda at: [s[at] for s in sides]
    down = (pick(7), [cotangent] * items)
    up = (pick(6), pick(8))
    out = (pick(5), pick(9))

    if direct:
        split = width_lat // 2
        keep_b, send_b = latent_weights(
            [down, out], [(0, width_lat), (split, split)], chips, b_bits, "weights_b", token
        )
        far_b = swap(send_b, "seq", 1)
        keep_a, send_a = latent_weights(
            [up, out], [(0, width_lat), (0, split)], chips, a_bits, "weights_a", (keep_b,)
        )
        far_a = swap(send_a, "seq", 1)
        early = [a for pair in far_pairs for a in (pair[0], pair[2])]
        dqt, dkv = back(items - 1, (keep_a, *early))
        dkvs.append(dkv)
        dkv_far = swap(dkv, "seq", 1)
        dqt_far = swap(dqt, "seq", CORES)
        keep_b, send_b = fold(keep_b, far_b, (dqt, outs_far), 5)
        far_b = swap(send_b, "batch", b_bits[0])
        keep_a, send_a = fold(keep_a, far_a, (keep_b,), 5)
        far_a = swap(send_a, "batch", a_bits[0])
        part_c = byte_part(
            far_pairs + [(turned, items - 1, dkv)], part_c, SHORT, (keep_a,)
        )
        keep_c, send_c = byte_last(
            turned_far, items - 1, dkv_far, part_c, 2 ** len(c_bits), ()
        )
        far_c = swap(send_c, "seq", CORES)
        gown, gfar, small = back_bytes(items - 1, (keep_c,))
        glats, keep_q, send_q, own_q = latents_back(
            dqt, dqt_far, pick(1), pick(10), gfar, small, latents, gain_lat, w_query,
            score_scale, chips, a_bits, (),
        )
        glats_far = swap(glats, "seq", 1)
        far_q = swap(send_q, "seq", 1)
        own_s, send_s = side_sum(far_q, small, keep_q.shape[0] + 1, ())
        far_s = swap(send_s, "seq", CORES)
        keep_b, send_b = fold(keep_b, far_b, (own_s,))
        far_b = swap(send_b, "batch", b_bits[1])
        keep_a, send_a = fold(keep_a, far_a, (keep_b,))
        far_a = swap(send_a, "batch", a_bits[1])
        keep_c, send_c = join(
            keep_c, far_c, own_s, far_s, keep_q, far_q, own_q, langs, chips, a_bits,
            (keep_a,),
        )
        far_c = swap(send_c, "batch", a_bits[0])
        latents_out, grad_bytes, token = place(
            [
                (outs, 0, outs_far, 0, width_lat, BF),
                (gown, 0, glats_far, width_lat, width_in, F32),
            ],
            LONG,
            (keep_c,),
        )
        keep_c, send_c = fold(keep_c, far_c, (token,))
        far_c = swap(send_c, "batch", a_bits[1])
        keep_b, send_b = fold(keep_b, far_b, (keep_c,))
        far_b = swap(send_b, "batch", b_bits[2])
        keep_a, send_a = fold(keep_a, far_a, (keep_b,))
        far_a = swap(send_a, "batch", a_bits[2])
        grad_latents, token = place(
            [(glats, 0, glats_far, 0, width_lat, F32)], SHORT, (keep_a,)
        )
        keep_c, send_c = fold(keep_c, far_c, (token,))
        far_c = swap(send_c, "batch", a_bits[2])
        g_up, g_down, g_out = last(keep_a, far_a, keep_b, far_b, width_lat, (keep_c,))
        g_key, g_value, g_query, g_table, *gains = part(
            keep_c, far_c, qk, rows_lat, langs, ()
        )
        g_in, g_lat, g_mlp = [g[0] for g in gains]
    else:
        dqt, dkv = back(items - 1, token)
        dkvs.append(dkv)
        for bit in chip_bits:
            dqt = (dqt.astype(F32) + swap(dqt, "seq", CORES * bit).astype(F32)).astype(BF)
        gown, gfar, small = back_bytes(items - 1, ())
        gfar_far = swap(gfar, "seq", 1)
        own_cut = lambda a: lax.dynamic_slice_in_dim(a, core * items, items, 0)
        grad_q = (dqt.astype(F32) * score_scale).swapaxes(1, 2).astype(BF)
        unit, inverse = standardise(own_cut(latents).astype(F32))
        gln = lax.dot_general(
            grad_q, w_query, (((2,), (1,)), ((), ())), preferred_element_type=F32
        )
        glats = jnp.stack(pick(1)) + standardise_back(unit, inverse, gln * gain_lat)
        glats = glats.astype(BF)
        glats_far = swap(glats, "seq", 1)
        flat = lambda a: a.reshape(-1, a.shape[-1])
        share = 1.0 / chips
        g_query = scatter_rows(tn(flat((unit * gain_lat).astype(BF)), flat(grad_q)) * share)
        rows = lambda lefts, rights: scatter_rows(
            sum(nn(x, y) for x, y in zip(lefts, rights)) * share
        )
        g_down = rows(pick(7), own_cut(cotangent))
        g_up, g_out = rows(pick(6), pick(8)), rows(pick(5), pick(9))
        g_bytes = scatter_rows(sum(tn(xns[i], dkvs[i]) for i in range(items)))
        g_key, g_value = g_bytes[:, :qk], g_bytes[:, qk:]
        pad = ((0, 0), (0, width_lat - width_in))
        small = jnp.concatenate(
            [
                jnp.pad(small[: langs + 1], pad),
                jnp.sum(gln * unit, (0, 1))[None] * share,
                sum(pick(10)) * share,
            ],
            0,
        )
        small = everywhere(small)
        cut = lambda rows, count: lax.dynamic_slice_in_dim(rows, device * count, count, 1)
        g_table, g_in = cut(small[:langs], rows_in), cut(small[langs : langs + 1], rows_in)[0]
        g_lat, g_mlp = cut(small[langs + 1 :], rows_lat)
        latents_out, grad_bytes, grad_latents, _ = place(
            [
                (outs, 0, outs_far, 0, width_lat, BF),
                (gown, 0, gfar_far, 0, width_in, F32),
                (glats, 0, glats_far, 0, width_lat, F32),
            ],
            SHORT,
            (),
        )

    return (
        latents_out,
        grad_latents,
        grad_bytes,
        g_table,
        g_in,
        g_lat,
        g_mlp,
        g_query,
        g_key,
        g_value,
        g_out,
        g_up,
        g_down,
    )


def solution(mesh):
    return jax.shard_map(
        local,
        mesh=mesh,
        in_specs=(
            P("batch", "seq", None),
            P("batch"),
            P(),
            P("batch", None, None),
            P(),
            P(),
            P(),
            P(),
            P(),
            P(),
            P(),
            P(),
            P(),
            P("batch", None, None),
        ),
        out_specs=(
            P("batch", None, None),
            P("batch", None, None),
            P("batch", "seq", None),
            P(None, ("batch", "seq")),
            P(("batch", "seq")),
            P(("batch", "seq")),
            P(("batch", "seq")),
            P(("batch", "seq"), None),
            P(("batch", "seq"), None),
            P(("batch", "seq"), None),
            P(("batch", "seq"), None),
            P(("batch", "seq"), None),
            P(("batch", "seq"), None),
        ),
        check_vma=False,
    )
```
